128 devices in a mesh: ctx: 32 (over y, x, core), fsdp: 4 (over z).
Axes of the slice: x: 4, y: 4, z: 4, core: 2. Of those that a mesh axis runs over, the one named last changes fastest.
Arguments:
- tokens: bfloat16 [4, 4096, 768], P('fsdp', 'ctx'), may hold values from -6 to 6
- query_key_value_weight: bfloat16 [768, 2304], P('fsdp'), may hold values from -0.21875 to 0.21875
- output_weight: bfloat16 [768, 768], P('fsdp'), may hold values from -3 to 3
- up_weight: bfloat16 [768, 3072], P('fsdp'), may hold values from -0.21875 to 0.21875
- down_weight: bfloat16 [3072, 768], P('fsdp'), may hold values from -0.109375 to 0.109375
- norm_gains: bfloat16 [2, 768], P(None, 'fsdp'), may hold values from 0.5 to 1.5
- biases: bfloat16 [5, 768], P(None, 'fsdp'), may hold values from -1.1953125 to 1.1953125
- value_bias: bfloat16 [768], P('fsdp'), may hold values from -0.119628906 to 0.119628906
- feedforward_up_bias: bfloat16 [3072], P('fsdp'), may hold values from -1.1953125 to 1.1953125
- cotangent: bfloat16 [4, 4096, 768], P('fsdp', 'ctx'), may hold values from -6 to 6
- block_place: int32 [64], replicated, may hold values from 0 to 63, as said below
Outputs:
- layer_out: bfloat16 [4, 4096, 768], P('fsdp', 'ctx')
- input_grad: bfloat16 [4, 4096, 768], P('fsdp', 'ctx')
- grad_qkv: float32 [768, 2304], P('fsdp')
- grad_out: float32 [768, 768], P('fsdp')
- grad_up: float32 [768, 3072], P('fsdp')
- grad_down: float32 [3072, 768], P('fsdp')
- grad_gains: float32 [2, 768], P(None, 'fsdp')
- grad_biases: float32 [5, 768], P(None, 'fsdp')
- grad_value_bias: float32 [768], P('fsdp')
- grad_up_bias: float32 [3072], P('fsdp')
The draws below stay inside these ranges and needn't reach their ends.
Inputs may be any that keep to these rules, and one draw needn't show every extreme that they name: `block_place`: each place 0 to 63 appears once; stored blocks 2c and 2c + 1 hold places j and 63 - j for some j.
All inputs are finite; a program needn't handle non-finite values.
Results may differ from the reference program's by a relative error of at most 0.025.
Values may be sent and summed in bfloat16 or wider, within the bound.
No kernel may reach another device: no remote copies, remote signals or barrier semaphores. Data moves between devices by JAX's collectives and lax.ppermute only.
A program may use at most 192 MiB of HBM per device.

```python
import math
import jax
import jax.numpy as jnp
from jax import lax

D = 768
HEADS = 12
HD = 64
FF = 3072
LEN = 4096
SEQS = 4
PAIRS = 32
BLK = 64


def draw_block_place(key, part):
    key = jax.random.fold_in(key, 7)
    order_key, reverse_key = jax.random.split(key)
    pair_order = jax.random.permutation(order_key, PAIRS).astype(jnp.int32)
    reverse_bits = jax.random.randint(reverse_key, (PAIRS,), 0, 2, dtype=jnp.int32)
    top_place = 2 * PAIRS - 1 - pair_order
    first_place = jnp.where(reverse_bits == 1, top_place, pair_order)
    second_place = 2 * PAIRS - 1 - first_place
    return jnp.stack([first_place, second_place], axis=1).reshape(2 * PAIRS).astype(jnp.int32)


def steps_of(stream_key, shape, pieces, least, high):
    def one(axis_at, shards_of):
        draws = jax.random.uniform(jax.random.fold_in(jax.random.fold_in(stream_key, 6), axis_at), (shards_of,), jnp.float32, least / len(pieces), high / len(pieces))
        return jnp.repeat(jnp.exp(draws), shape[axis_at] // shards_of).reshape((-1,) + (1,) * (len(shape) - axis_at - 1))

    factor_of = one(*pieces[0])
    for cut in pieces[1:]:
        factor_of = factor_of * one(*cut)
    return factor_of


def normal_values(key, shape, deviation, most, shards=(), held_as=jnp.bfloat16):
    level = steps_of(key, shape, shards, -0.22, 0.18) if shards else 1.0
    array = jax.random.normal(key, shape, jnp.float32) * deviation * level
    return jnp.minimum(jnp.maximum(array, -most), most).astype(held_as)


def setup_inputs(seed: int = 0) -> dict:
    arg_keys = jax.random.split(jax.random.key(seed), 12)
    return {
        "tokens": normal_values(arg_keys[0], (SEQS, LEN, D), 1.0, 6.0, ((0, 4), (1, 32))),
        "query_key_value_weight": normal_values(arg_keys[1], (D, 3 * D), D ** -0.5, 0.21875, ((0, 4),)),
        "output_weight": normal_values(arg_keys[2], (D, D), 4 ** -0.5, 3.0, ((0, 4),)),
        "up_weight": normal_values(arg_keys[3], (D, FF), D ** -0.5, 0.21875, ((0, 4),)),
        "down_weight": normal_values(arg_keys[4], (FF, D), FF ** -0.5, 0.109375, ((0, 4),)),
        "norm_gains": jnp.clip(1.0 + 0.1 * jax.random.normal(arg_keys[5], (2, D), jnp.float32), 0.5, 1.5).astype(jnp.bfloat16),
        "biases": normal_values(arg_keys[6], (5, D), 0.2, 1.1953125, ((1, 4),)),
        "value_bias": normal_values(arg_keys[7], (D,), 0.02, 0.119628906, ((0, 4),)),
        "feedforward_up_bias": normal_values(arg_keys[8], (FF,), 0.2, 1.1953125, ((0, 4),)),
        "cotangent": normal_values(arg_keys[9], (SEQS, LEN, D), 1.0, 6.0, ((0, 4), (1, 32))),
        "block_place": draw_block_place(jax.random.fold_in(arg_keys[11], 71), 0),
    }


@jax.custom_vjp
def low(v):
    return lax.optimization_barrier(v.astype(jnp.bfloat16)).astype(jnp.float32)

@jax.custom_vjp
def reduced_backward(v):
    return v

def low_keep(v):
    return (low(v), None)

def low_pass(kept, grad):
    return (grad,)

def back_keep(v):
    return (v, None)

def back_low(kept, grad):
    return (low(grad),)
low.defvjp(low_keep, low_pass)
reduced_backward.defvjp(back_keep, back_low)
EPS = 1e-05
HIGH_PRECISION = lax.Precision.HIGHEST

def layer_norm(value, gain, shift):
    center = value - lax.optimization_barrier(jnp.mean(value, axis=-1, keepdims=True))
    spread = lax.optimization_barrier(jnp.mean(center * center, axis=-1, keepdims=True))
    return center * lax.rsqrt(spread + EPS) * gain + shift

def positions(block_place):
    rows = jnp.arange(LEN, dtype=jnp.int32)
    return block_place[rows // BLK] * BLK + rows % BLK

def attend_block(query, qpos, keys, values, kpos):
    raw = jnp.einsum('qhd,khd->hqk', query, keys, precision=HIGH_PRECISION)
    raw = reduced_backward(raw)
    scores = jnp.where(kpos[None, None, :] <= qpos[None, :, None], raw * 0.125, -1e+30)
    peak = lax.optimization_barrier(jnp.max(scores, axis=-1, keepdims=True))
    expo = jnp.exp(scores - peak)
    prob = expo / lax.optimization_barrier(jnp.sum(expo, axis=-1, keepdims=True))
    return jnp.einsum('hqk,khd->qhd', low(prob), values, precision=HIGH_PRECISION)

def attend_sequence(query, keys, values, pos):
    qblock = math.gcd(LEN, 512)
    query_blocks = query.reshape(LEN // qblock, qblock, HEADS, HD)
    pos_blocks = pos.reshape(LEN // qblock, qblock)
    block_fn = jax.checkpoint(lambda item: attend_block(item[0], item[1], keys, values, pos))
    result = lax.map(block_fn, (query_blocks, pos_blocks))
    return result.reshape(LEN, D)

def forward(tokens, query_key_value_weight, output_weight, up_weight, down_weight, norm_gains, biases, value_bias, feedforward_up_bias, pos):
    hidden_first = low(layer_norm(tokens, norm_gains[0], biases[0]))
    query_key_value_bias = jnp.concatenate([biases[1], jnp.zeros_like(biases[1]), value_bias])
    query_key_value = jnp.einsum('inj,jg->ing', hidden_first, query_key_value_weight, precision=HIGH_PRECISION) + query_key_value_bias
    query_key_value = low(reduced_backward(query_key_value))
    query = query_key_value[..., :D].reshape(SEQS, LEN, HEADS, HD)
    keys = query_key_value[..., D:2 * D].reshape(SEQS, LEN, HEADS, HD)
    values = query_key_value[..., 2 * D:].reshape(SEQS, LEN, HEADS, HD)
    attention_result = lax.map(lambda item: attend_sequence(item[0], item[1], item[2], pos), (query, keys, values))
    attention_result = low(reduced_backward(attention_result))
    residual_branch = reduced_backward(jnp.einsum('inj,jg->ing', attention_result, output_weight, precision=HIGH_PRECISION) + biases[2])
    mixed_heads_output = tokens + residual_branch
    hidden_second = low(layer_norm(mixed_heads_output, norm_gains[1], biases[3]))
    upper_triangle = reduced_backward(jnp.einsum('kha,ac->khc', hidden_second, up_weight, precision=HIGH_PRECISION) + feedforward_up_bias)
    activation_value = low(jax.nn.gelu(upper_triangle))
    return mixed_heads_output + jnp.einsum('goh,hy->goy', activation_value, down_weight, precision=HIGH_PRECISION) + biases[4]

def reference(tokens, query_key_value_weight, output_weight, up_weight, down_weight, norm_gains, biases, value_bias, feedforward_up_bias, cotangent, block_place):
    pos = positions(block_place)
    inputs = tuple((a.astype(jnp.float32) for a in (tokens, query_key_value_weight, output_weight, up_weight, down_weight, norm_gains, biases, value_bias, feedforward_up_bias)))
    result, pull = jax.vjp(lambda *a: forward(*a, pos), *inputs)
    grads = pull(cotangent.astype(jnp.float32))
    return (result.astype(jnp.bfloat16), grads[0].astype(jnp.bfloat16), grads[1], grads[2], grads[3], grads[4], grads[5], grads[6], grads[7], grads[8])
```

```python
import functools

import jax
import jax.numpy as jnp
from jax import lax
from jax.experimental import pallas as pl
from jax.experimental.pallas import tpu as pltpu
from jax.sharding import Mesh
from jax.sharding import PartitionSpec as P

EPS = 1e-05
D = 768
GD = 192
NH = 3
HD = 64
ROWS = 512
LEN = 4096
BLK = 64
NBLK = 64
EXT = 256
TILE = 512
CHUNK = 128
BF = jnp.bfloat16
F32 = jnp.float32
XC = ("x", "core")
CTX = ("y", "x", "core")
VMEM_LIMIT = 48 * 1024 * 1024


def dot(a, b):
    return lax.dot_general(a, b, (((1,), (0,)), ((), ())), preferred_element_type=F32)


def dot_t(a, b):
    return lax.dot_general(a, b, (((1,), (1,)), ((), ())), preferred_element_type=F32)


def t_dot(a, b):
    return lax.dot_general(a, b, (((0,), (0,)), ((), ())), preferred_element_type=F32)


def normalize(value):
    center = value - jnp.mean(value, axis=-1, keepdims=True)
    factor = lax.rsqrt(jnp.mean(center * center, axis=-1, keepdims=True) + EPS)
    return (center * factor, factor)


def norm_back(scaled, normed, factor):
    return factor * (
        scaled
        - jnp.mean(scaled, axis=-1, keepdims=True)
        - normed * jnp.mean(scaled * normed, axis=-1, keepdims=True)
    )


def lanes(rows):
    return lax.broadcasted_iota(jnp.int32, (rows, EXT), 1)


def head_mask(rows, h, high):
    lane = lanes(rows)
    if high:
        feat = (lane >= 64 + HD * h) & (lane < 64 + HD * (h + 1))
        ext = (lane >= 3 * h) & (lane < 3 * h + 3)
    else:
        feat = (lane >= HD * h) & (lane < HD * (h + 1))
        ext = (lane >= GD + 3 * h) & (lane < GD + 3 * h + 3)
    return feat | ext


def feature_mask(rows, h, high):
    lane = lanes(rows) - (64 if high else 0)
    return (lane >= HD * h) & (lane < HD * (h + 1))


def stack_heads(value, high):
    rows = value.shape[0]
    zero = jnp.zeros_like(value)
    return jnp.concatenate(
        [jnp.where(head_mask(rows, h, high), value, zero) for h in range(NH)], axis=0
    )


def merge_heads(stacked, high):
    rows = stacked.shape[0] // NH
    out = jnp.zeros((rows, EXT), F32)
    for h in range(NH):
        out = out + jnp.where(feature_mask(rows, h, high), stacked[h * rows : (h + 1) * rows], 0.0)
    return out


def pieces(value):
    first = value.astype(BF).astype(F32)
    second = (value - first).astype(BF).astype(F32)
    third = (value - first - second).astype(BF).astype(F32)
    return (first, second, third)


def add_extras(base, columns, high):
    rows = base.shape[0]
    lane = lanes(rows)
    start = 0 if high else GD
    for h in range(NH):
        for i, piece in enumerate(pieces(columns[h])):
            base = jnp.where(lane == start + 3 * h + i, piece, base)
    return base


def key_form(kv):
    lane = lanes(kv.shape[0])
    one = jnp.ones((kv.shape[0], EXT), BF)
    zero = jnp.zeros((kv.shape[0], EXT), BF)
    low = jnp.where(lane < GD, kv[:, :EXT], jnp.where(lane < GD + 9, one, zero))
    high = jnp.where(lane >= 64, kv[:, 128:384], jnp.where(lane < 9, one, zero))
    return (low, high)


def block_rows(index):
    return pl.ds(pl.multiple_of(index * BLK, BLK), BLK)


def stacked_pos(place_a, place_b):
    row = lax.broadcasted_iota(jnp.int32, (NH * CHUNK, 1), 0)
    place = jnp.where(row % CHUNK < BLK, place_a, place_b)
    return place * BLK + row % BLK


def col_pos(tile):
    return tile * TILE + lax.broadcasted_iota(jnp.int32, (NH * CHUNK, TILE), 1)


def fold(value, op):
    out = value[:, :128]
    for i in range(1, value.shape[1] // 128):
        out = op(out, value[:, i * 128 : (i + 1) * 128])
    return out


def tile_rows(t):
    return pl.ds(pl.multiple_of(t * TILE, TILE), TILE)


def fwd_kernel(
    kplace_ref, own_ref, place_ref, qkv_ref, *refs
):
    kv_refs, (attn_ref, o_ref, qe_ref, ks_ref, vs_ref, s_scr, m_scr, l_scr, acc_scr) = refs[:8], refs[8:]
    for k in range(8):
        for b in range(8):
            low, high = key_form(kv_refs[k][b * BLK : (b + 1) * BLK, :])
            dst = block_rows(kplace_ref[8 * k + b])
            ks_ref[dst, :] = low
            vs_ref[dst, :] = high

    for c in range(ROWS // CHUNK):
        place_a, place_b = place_ref[2 * c], place_ref[2 * c + 1]
        blocks = (own_ref[2 * c], own_ref[2 * c + 1])
        query = jnp.concatenate([qkv_ref[block_rows(b), 2 * GD :] for b in blocks], axis=0)
        query = query * jnp.asarray(0.125, BF)
        query = jnp.concatenate([query, jnp.zeros((CHUNK, EXT - GD), BF)], axis=1)
        stacked = stack_heads(query, False)
        qpos = stacked_pos(place_a, place_b)
        tiles = place_a // (TILE // BLK) + 1
        m_scr[...] = jnp.full(m_scr.shape, -1e30, F32)

        def score_step(t, _):
            scores = dot_t(stacked, ks_ref[tile_rows(t), :])
            scores = jnp.where(col_pos(t) <= qpos, scores, -1e30)
            s_scr[t] = scores
            m_scr[...] = jnp.maximum(m_scr[...], fold(scores, jnp.maximum))
            return 0

        lax.fori_loop(0, tiles, score_step, 0)
        peak = jnp.max(m_scr[...], axis=1, keepdims=True)
        l_scr[...] = jnp.zeros(l_scr.shape, F32)
        acc_scr[...] = jnp.zeros(acc_scr.shape, F32)

        def value_step(t, _):
            prob = jnp.exp(s_scr[t] - peak)
            l_scr[...] = l_scr[...] + fold(prob, jnp.add)
            acc_scr[...] = acc_scr[...] + dot(prob.astype(BF), vs_ref[tile_rows(t), :])
            return 0

        lax.fori_loop(0, tiles, value_step, 0)
        total = jnp.sum(l_scr[...], axis=1, keepdims=True)
        log_total = peak + jnp.log(total)
        out = merge_heads(acc_scr[...] / total, True)
        ext = add_extras(
            query.astype(F32),
            [-log_total[h * CHUNK : (h + 1) * CHUNK] for h in range(NH)],
            False,
        ).astype(BF)
        for i, b in enumerate(blocks):
            rows = slice(i * BLK, (i + 1) * BLK)
            o_ref[block_rows(b), :] = out[rows]
            attn_ref[block_rows(b), :] = out[rows].astype(BF)
            qe_ref[block_rows(b), :] = ext[rows]


def dq_kernel(own_ref, place_ref, qe_ref, de_ref, ks_ref, vs_ref, dq_ref, acc_scr):
    for c in range(ROWS // CHUNK):
        place_a, place_b = place_ref[2 * c], place_ref[2 * c + 1]
        blocks = (own_ref[2 * c], own_ref[2 * c + 1])
        query = stack_heads(jnp.concatenate([qe_ref[block_rows(b), :] for b in blocks], axis=0), False)
        d_out = stack_heads(jnp.concatenate([de_ref[block_rows(b), :] for b in blocks], axis=0), True)
        qpos = stacked_pos(place_a, place_b)
        tiles = place_a // (TILE // BLK) + 1
        acc_scr[...] = jnp.zeros(acc_scr.shape, F32)

        def step(t, _):
            keys = ks_ref[tile_rows(t), :]
            prob = jnp.where(col_pos(t) <= qpos, jnp.exp(dot_t(query, keys)), 0.0)
            d_raw = (prob * dot_t(d_out, vs_ref[tile_rows(t), :])).astype(BF)
            acc_scr[...] = acc_scr[...] + dot(d_raw, keys)
            return 0

        lax.fori_loop(0, tiles, step, 0)
        out = (merge_heads(acc_scr[...], False) * 0.125).astype(BF)
        for i, b in enumerate(blocks):
            dq_ref[block_rows(b), :] = out[i * BLK : (i + 1) * BLK]


def dkv_kernel(qplace_ref, kplace_ref, own_ref, place_ref, kv_ref, qe_ref, *refs):
    de_refs, (dkv_ref, qs_scr, ds_scr, dk_scr, dv_scr) = refs[:8], refs[8:]
    for k in range(8):
        for b in range(8):
            qs_scr[block_rows(qplace_ref[8 * k + b]), :] = qe_ref[(8 * k + b) * BLK : (8 * k + b + 1) * BLK, :]
            ds_scr[block_rows(kplace_ref[8 * k + b]), :] = de_refs[k][b * BLK : (b + 1) * BLK, :]

    for c in range(ROWS // CHUNK):
        place_a, place_b = place_ref[2 * c], place_ref[2 * c + 1]
        blocks = (own_ref[2 * c], own_ref[2 * c + 1])
        low, high = key_form(jnp.concatenate([kv_ref[block_rows(b), :] for b in blocks], axis=0))
        keys = stack_heads(low, False)
        values = stack_heads(high, True)
        kpos = stacked_pos(place_a, place_b)
        dk_scr[...] = jnp.zeros(dk_scr.shape, F32)
        dv_scr[...] = jnp.zeros(dv_scr.shape, F32)

        def step(t, _):
            query = qs_scr[tile_rows(t), :]
            d_out = ds_scr[tile_rows(t), :]
            prob = jnp.where(col_pos(t) >= kpos, jnp.exp(dot_t(keys, query)), 0.0)
            d_raw = (prob * dot_t(values, d_out)).astype(BF)
            dv_scr[...] = dv_scr[...] + dot(prob.astype(BF), d_out)
            dk_scr[...] = dk_scr[...] + dot(d_raw, query)
            return 0

        lax.fori_loop(place_b // (TILE // BLK), LEN // TILE, step, 0)
        d_keys = merge_heads(dk_scr[...], False)
        d_values = merge_heads(dv_scr[...], True)
        out = jnp.concatenate(
            [d_keys[:, :128], d_keys[:, 128:] + d_values[:, :128], d_values[:, 128:]], axis=1
        ).astype(BF)
        for i, b in enumerate(blocks):
            dkv_ref[block_rows(b), :] = out[i * BLK : (i + 1) * BLK]


def delta_kernel(d_ref, o_ref, de_ref):
    d_out = jnp.concatenate([jnp.zeros((ROWS, 64), F32), d_ref[...].astype(F32)], axis=1)
    product = d_out * o_ref[...]
    sums = [
        -jnp.sum(jnp.where(feature_mask(ROWS, h, True), product, 0.0), axis=1, keepdims=True)
        for h in range(NH)
    ]
    de_ref[...] = add_extras(d_out, sums, True).astype(BF)


SMEM = pl.BlockSpec(memory_space=pltpu.SMEM)
VM = pl.BlockSpec(memory_space=pltpu.VMEM)
PARAMS = pltpu.CompilerParams(vmem_limit_bytes=VMEM_LIMIT)


def shape(*dims, dtype=BF):
    return jax.ShapeDtypeStruct(dims, dtype)


def attention_forward(kplace, own, place, qkv, kv):
    return pl.pallas_call(
        fwd_kernel,
        out_shape=(
            shape(ROWS, EXT), shape(ROWS, EXT, dtype=F32), shape(ROWS, EXT),
            shape(LEN, EXT), shape(LEN, EXT),
        ),
        in_specs=[SMEM] * 3 + [VM] * 9,
        out_specs=(VM,) * 5,
        scratch_shapes=[
            pltpu.VMEM((LEN // TILE, NH * CHUNK, TILE), F32),
            pltpu.VMEM((NH * CHUNK, 128), F32),
            pltpu.VMEM((NH * CHUNK, 128), F32),
            pltpu.VMEM((NH * CHUNK, EXT), F32),
        ],
        compiler_params=PARAMS,
        cost_estimate=pl.CostEstimate(flops=4 * 10**9, bytes_accessed=10**7, transcendentals=4 * 10**6),
    )(kplace, own, place, qkv, *kv)


def attention_dq(own, place, qe, de, ks, vs):
    return pl.pallas_call(
        dq_kernel,
        out_shape=shape(ROWS, EXT),
        in_specs=[SMEM] * 2 + [VM] * 4,
        out_specs=VM,
        scratch_shapes=[pltpu.VMEM((NH * CHUNK, EXT), F32)],
        compiler_params=PARAMS,
        cost_estimate=pl.CostEstimate(flops=6 * 10**9, bytes_accessed=10**7, transcendentals=4 * 10**6),
    )(own, place, qe, de, ks, vs)


def attention_dkv(qplace, kplace, own, place, kv, qe, de):
    return pl.pallas_call(
        dkv_kernel,
        out_shape=shape(ROWS, 2 * GD),
        in_specs=[SMEM] * 4 + [VM] * 10,
        out_specs=VM,
        scratch_shapes=[
            pltpu.VMEM((LEN, EXT), BF),
            pltpu.VMEM((LEN, EXT), BF),
            pltpu.VMEM((NH * CHUNK, EXT), F32),
            pltpu.VMEM((NH * CHUNK, EXT), F32),
        ],
        compiler_params=PARAMS,
        cost_estimate=pl.CostEstimate(flops=8 * 10**9, bytes_accessed=10**7, transcendentals=4 * 10**6),
    )(qplace, kplace, own, place, kv, qe, *de)


def delta_rows(d_attn, o):
    return pl.pallas_call(
        delta_kernel,
        out_shape=shape(ROWS, EXT),
        in_specs=[VM] * 2,
        out_specs=VM,
        compiler_params=PARAMS,
        cost_estimate=pl.CostEstimate(flops=10**6, bytes_accessed=10**6, transcendentals=0),
    )(d_attn, o)


def final_kernel(at_ref, *refs):
    slots, (grad_ref, vec_ref, scr) = refs[:4], refs[4:]
    for s in range(4):
        for c in range(2):
            scr[s, c] = slots[s][c]
    yi, ci = at_ref[0], at_ref[1]
    for c in range(2):
        rows = slice(96 * c, 96 * (c + 1))
        total = []
        for g in range(4):
            value = scr[(yi - g + 4) % 4, (ci + c) % 2].astype(F32)
            for i, part in enumerate((1, 2, 0)):
                start = part * D + g * GD
                grad_ref[rows, start : start + GD] = value[:, i * GD : (i + 1) * GD]
            total.append(value[:, 512:])
        vec_ref[rows, :] = (total[0] + total[1]) + (total[2] + total[3])


def final_rows(at, slots):
    return pl.pallas_call(
        final_kernel,
        out_shape=(shape(GD, 3 * D, dtype=F32), shape(GD, 128, dtype=F32)),
        in_specs=[SMEM] + [VM] * 4,
        out_specs=(VM, VM),
        scratch_shapes=[pltpu.VMEM((4, 2, 96, 640), BF)],
        compiler_params=PARAMS,
        cost_estimate=pl.CostEstimate(flops=10**6, bytes_accessed=3 * 10**6, transcendentals=0),
    )(at, *slots)


def gather(value, axes, axis=0):
    return lax.all_gather(value, axes, axis=axis, tiled=True)


def swap(value, axes):
    return lax.all_to_all(value, axes, 0, 0)


def send(value, axis, step):
    n = lax.axis_size(axis)
    return lax.ppermute(value, axis, [(i, (i + step) % n) for i in range(n)])


def spread(value, axis):
    return [value] + [send(value, axis, s) for s in range(1, 4)]


def exchange(slots, axis, step):
    return [slots[0]] + [send(slots[s], axis, s * step) for s in range(1, 4)]


def add_slots(slots):
    a, b, c, d = (v.astype(F32) for v in slots)
    return (a + c) + (b + d)


def ordered(slots, index):
    both = jnp.concatenate(slots[:1] + slots[:0:-1] + slots[:1] + slots[:0:-1], axis=0)
    rows = slots[0].shape[0]
    return lax.dynamic_slice_in_dim(both, ((4 - index) % 4) * rows, 4 * rows, 0)


def group_of(value, index, size, axis=0):
    return lax.dynamic_slice_in_dim(value, (index % 4) * size, size, axis)


def local(
    tokens, qkv_w, out_w, up_w, down_w, norm_gains, biases, value_bias, up_bias, cotangent, block_place
):
    xi = lax.axis_index("x")
    yi = lax.axis_index("y")
    ci = lax.axis_index("core")
    zi = lax.axis_index("fsdp")
    tok_own = tokens[0]
    cot_own = cotangent[0]

    own_cols = lax.dynamic_index_in_dim(qkv_w.reshape(GD, 3, 4, GD), yi, 2, keepdims=False)
    own_cols = jnp.concatenate([own_cols[:, 1], own_cols[:, 2], own_cols[:, 0]], axis=1)
    small = jnp.concatenate([norm_gains, biases, value_bias[None]], axis=0)
    small = spread(small, "fsdp")
    tok_y = jnp.concatenate(spread(tok_own, "y"), axis=0)
    w_qkv = ordered(spread(own_cols, "fsdp"), zi)
    small = ordered([v.T for v in small], zi).T.astype(F32)
    gain1, gain2 = small[0], small[1]
    shift1, q_bias, out_bias, shift2, down_bias, v_bias = (small[i] for i in range(2, 8))

    ids = jnp.arange(NBLK, dtype=jnp.int32)
    slot_x, slot_c, slot_y, blk = ids // 16, (ids // 8) % 2, (ids // 2) % 4, ids % 2
    pick = lambda at: jnp.sum(jnp.where(at[:, None] == ids[None, :], block_place[None, :], 0), axis=1)
    at_y = (yi - slot_y + 4) % 4
    key_place = pick(at_y * 16 + ((xi - slot_x + 4) % 4) * 4 + ((ci + slot_c) % 2) * 2 + blk)
    query_place = pick(at_y * 16 + slot_x * 4 + slot_c * 2 + blk)
    own_place = key_place[:8]
    rank = jnp.sum((own_place[None, :] > own_place[:, None]).astype(jnp.int32), axis=1)
    order = jnp.arange(8, dtype=jnp.int32)
    hit = rank[None, :] == order[:, None]
    own = jnp.sum(jnp.where(hit, order[None, :], 0), axis=1)
    place = jnp.sum(jnp.where(hit, own_place[None, :], 0), axis=1)

    w_out = gather(out_w, "fsdp")
    w_out = jnp.concatenate([group_of(w_out, yi + s, GD) for s in range(4)], axis=0)
    w_up = swap(up_w.reshape(GD, 4, D).transpose(1, 0, 2), "fsdp").reshape(D, D)
    w_down = down_w
    ub = up_bias.astype(F32)
    cot_z = jnp.concatenate(spread(cot_own, "fsdp"), axis=0)

    n1y, _ = normalize(tok_y.astype(F32))
    h1 = (n1y * gain1 + shift1).astype(BF)
    own_q_bias = lax.dynamic_slice(q_bias, (yi * GD,), (GD,))
    own_v_bias = lax.dynamic_slice(v_bias, (yi * GD,), (GD,))
    qkv_bias = jnp.concatenate([jnp.zeros_like(own_q_bias), own_v_bias, own_q_bias])
    qkv = (dot(h1, w_qkv) + qkv_bias).astype(BF)
    kv_own = qkv[:, : 2 * GD]
    kv_all = [p for v in spread(kv_own, "x") for p in (v, send(v, "core", 1))]
    attn, o_exact, qe, ks, vs = attention_forward(key_place, own, place, qkv, kv_all)
    qe_all = gather(qe, XC)

    attn = attn[:, 64:]
    attn_own = exchange([attn[128 * s : 128 * (s + 1)] for s in range(4)], "y", -1)
    attn_own = jnp.concatenate(attn_own, axis=1)
    x2 = tok_own.astype(F32) + (dot(attn_own, w_out) + out_bias)
    n2, s2 = normalize(x2)
    h2_own = (n2 * gain2 + shift2).astype(BF)
    h2 = jnp.concatenate(spread(h2_own, "fsdp"), axis=0)

    up = dot(h2, w_up) + ub
    act32, gelu_pull = jax.vjp(jax.nn.gelu, up)
    act = act32.astype(BF)
    d_act = dot_t(cot_z, w_down)
    d_up = gelu_pull(d_act)[0].astype(BF)
    d_h2_part = dot_t(d_up, w_up).astype(BF)
    back = lambda v: add_slots(exchange([v[128 * s : 128 * (s + 1)] for s in range(4)], "fsdp", -1))
    d_h2 = back(d_h2_part)
    cot32 = cot_own.astype(F32)
    d_x2 = cot32 + norm_back(d_h2 * gain2, n2, s2)
    d_branch = d_x2.astype(BF)
    d_attn = dot_t(d_branch, w_out).astype(BF)
    d_attn_own = exchange([d_attn[:, GD * s : GD * (s + 1)] for s in range(4)], "y", 1)
    d_attn_own = jnp.concatenate(d_attn_own, axis=0)
    de = delta_rows(d_attn_own, o_exact)
    de_all = [p for v in spread(de, "x") for p in (v, send(v, "core", 1))]
    d_q = attention_dq(own, place, qe, de, ks, vs)[:, :GD]
    d_kv = attention_dkv(query_place, key_place, own, place, kv_own, qe_all, de_all)

    layer_out = (x2 + back(dot(act, w_down).astype(BF)) + down_bias).astype(BF)

    g_down = t_dot(act, cot_z).astype(BF)
    g_up = t_dot(h2, d_up).astype(BF)
    g_up = swap(g_up.reshape(4, GD, D), "fsdp").reshape(D, D)
    d_branch_y = jnp.concatenate(spread(d_branch, "y"), axis=0)
    g_out = t_dot(attn, d_branch_y).astype(BF)
    g_out = lax.ppermute(
        g_out, ("y", "fsdp"), [(a * 4 + b, b * 4 + a) for a in range(4) for b in range(4)]
    )
    g_up_bias = jnp.sum(d_up.astype(F32), axis=0)
    g_down_bias = jnp.sum(cot_z.astype(F32), axis=0)
    g_down_bias = lax.dynamic_slice(g_down_bias, (zi * GD,), (GD,))
    vec = jnp.concatenate([g_up_bias, g_down_bias, jnp.zeros((576,), F32)]).astype(BF).reshape(2, D)
    mid = jnp.concatenate([g_up, g_down, g_out, vec, jnp.zeros((62, D), BF)], axis=0)
    mid = lax.psum_scatter(mid, "y", scatter_dimension=0, tiled=True)
    mid = lax.psum_scatter(mid, XC, scatter_dimension=0, tiled=True)
    mid = gather(gather(mid, XC), "y").astype(F32)
    grad_up = mid[:D].reshape(4, GD, D).transpose(1, 0, 2).reshape(GD, 4 * D)
    grad_down = mid[D : 2 * D]
    grad_out = mid[2 * D : 2 * D + GD]
    grad_up_bias = mid[2 * D + GD]
    grad_down_bias = mid[2 * D + GD + 1, :GD]

    d_qkv = jnp.concatenate([d_kv, d_q], axis=1)
    d_h1_part = dot_t(d_qkv, w_qkv)
    d_h1_send = d_h1_part.astype(BF)
    d_h1 = add_slots(exchange([d_h1_send[128 * s : 128 * (s + 1)] for s in range(4)], "y", -1))
    n1, s1 = normalize(tok_own.astype(F32))
    input_grad = (d_x2 + norm_back(d_h1 * gain1, n1, s1)).astype(BF)

    g_qkv = t_dot(h1, d_qkv)
    dq_sum = jnp.sum(d_q.astype(F32), axis=0)
    dv_sum = jnp.sum(d_kv[:, GD:].astype(F32), axis=0)
    at_own = lambda v: lax.dynamic_update_slice(jnp.zeros((D,), F32), v, (yi * GD,))
    columns = jnp.stack(
        [
            jnp.sum(d_h1_part * n1y, axis=0),
            jnp.sum(d_h2 * n2, axis=0),
            jnp.sum(d_h1_part, axis=0),
            at_own(dq_sum),
            jnp.sum(d_branch.astype(F32), axis=0),
            jnp.sum(d_h2, axis=0),
            at_own(dv_sum),
        ],
        axis=1,
    )
    tail = jnp.concatenate([g_qkv, columns, jnp.zeros((D, 57), F32)], axis=1).astype(BF)
    tail = add_slots(exchange([group_of(tail, zi + s, GD) for s in range(4)], "fsdp", 1)).astype(BF)
    kept = lax.dynamic_slice_in_dim(tail, ci * 96, 96, 0)
    given = lax.dynamic_slice_in_dim(tail, (1 - ci) * 96, 96, 0)
    tail = (kept.astype(F32) + send(given, "core", 1).astype(F32)).astype(BF)
    tail = add_slots(spread(tail, "x")).astype(BF)
    tail = [jnp.stack([v, send(v, "core", 1)]) for v in spread(tail, "y")]
    grad_qkv, vectors = final_rows(jnp.stack([yi, ci]), tail)
    vectors = vectors[:, 64:71].T
    grad_gains = vectors[:2]
    grad_biases = jnp.concatenate([vectors[2:6], grad_down_bias[None]], axis=0)
    grad_value_bias = vectors[6]
    return (
        layer_out[None], input_grad[None], grad_qkv, grad_out, grad_up, grad_down,
        grad_gains, grad_biases, grad_value_bias, grad_up_bias,
    )


def solution(mesh):
    grid = Mesh(mesh.devices.reshape(4, 4, 2, 4), ("y", "x", "core", "fsdp"))
    rows = P("fsdp", CTX, None)
    in_specs = (
        rows, P("fsdp", None), P("fsdp", None), P("fsdp", None), P("fsdp", None),
        P(None, "fsdp"), P(None, "fsdp"), P("fsdp"), P("fsdp"), rows, P(),
    )
    out_specs = (
        rows, rows, P("fsdp", None), P("fsdp", None), P("fsdp", None), P("fsdp", None),
        P(None, "fsdp"), P(None, "fsdp"), P("fsdp"), P("fsdp"),
    )
    return jax.shard_map(local, mesh=grid, in_specs=in_specs, out_specs=out_specs, check_vma=False)
```

```python
import functools

import jax
import jax.numpy as jnp
from jax import lax
from jax.experimental import pallas as pl
from jax.experimental.pallas import tpu as pltpu
from jax.sharding import Mesh
from jax.sharding import PartitionSpec as P

EPS = 1e-05
D = 768
GD = 192
NH = 3
HD = 64
ROWS = 512
LEN = 4096
BLK = 64
NBLK = 64
EXT = 256
TILE = 512
CHUNK = 128
BF = jnp.bfloat16
F32 = jnp.float32
XC = ("x", "core")
CTX = ("y", "x", "core")
VMEM_LIMIT = 48 * 1024 * 1024


def dot(a, b):
    return lax.dot_general(a, b, (((1,), (0,)), ((), ())), preferred_element_type=F32)


def dot_t(a, b):
    return lax.dot_general(a, b, (((1,), (1,)), ((), ())), preferred_element_type=F32)


def t_dot(a, b):
    return lax.dot_general(a, b, (((0,), (0,)), ((), ())), preferred_element_type=F32)


def normalize(value):
    center = value - jnp.mean(value, axis=-1, keepdims=True)
    factor = lax.rsqrt(jnp.mean(center * center, axis=-1, keepdims=True) + EPS)
    return (center * factor, factor)


def norm_back(scaled, normed, factor):
    return factor * (
        scaled
        - jnp.mean(scaled, axis=-1, keepdims=True)
        - normed * jnp.mean(scaled * normed, axis=-1, keepdims=True)
    )


def lanes(rows):
    return lax.broadcasted_iota(jnp.int32, (rows, EXT), 1)


def head_mask(rows, h, high):
    lane = lanes(rows)
    if high:
        feat = (lane >= 64 + HD * h) & (lane < 64 + HD * (h + 1))
        ext = (lane >= 3 * h) & (lane < 3 * h + 3)
    else:
        feat = (lane >= HD * h) & (lane < HD * (h + 1))
        ext = (lane >= GD + 3 * h) & (lane < GD + 3 * h + 3)
    return feat | ext


def feature_mask(rows, h, high):
    lane = lanes(rows) - (64 if high else 0)
    return (lane >= HD * h) & (lane < HD * (h + 1))


def stack_heads(value, high):
    rows = value.shape[0]
    zero = jnp.zeros_like(value)
    return jnp.concatenate(
        [jnp.where(head_mask(rows, h, high), value, zero) for h in range(NH)], axis=0
    )


def merge_heads(stacked, high):
    rows = stacked.shape[0] // NH
    out = jnp.zeros((rows, EXT), F32)
    for h in range(NH):
        out = out + jnp.where(feature_mask(rows, h, high), stacked[h * rows : (h + 1) * rows], 0.0)
    return out


def pieces(value):
    first = value.astype(BF).astype(F32)
    second = (value - first).astype(BF).astype(F32)
    third = (value - first - second).astype(BF).astype(F32)
    return (first, second, third)


def add_extras(base, columns, high):
    rows = base.shape[0]
    lane = lanes(rows)
    start = 0 if high else GD
    for h in range(NH):
        for i, piece in enumerate(pieces(columns[h])):
            base = jnp.where(lane == start + 3 * h + i, piece, base)
    return base


def key_form(kv):
    lane = lanes(kv.shape[0])
    one = jnp.ones((kv.shape[0], EXT), BF)
    zero = jnp.zeros((kv.shape[0], EXT), BF)
    low = jnp.where(lane < GD, kv[:, :EXT], jnp.where(lane < GD + 9, one, zero))
    high = jnp.where(lane >= 64, kv[:, 128:384], jnp.where(lane < 9, one, zero))
    return (low, high)


def block_rows(index):
    return pl.ds(pl.multiple_of(index * BLK, BLK), BLK)


def stacked_pos(place_a, place_b):
    row = lax.broadcasted_iota(jnp.int32, (NH * CHUNK, 1), 0)
    place = jnp.where(row % CHUNK < BLK, place_a, place_b)
    return place * BLK + row % BLK


def col_pos(tile):
    return tile * TILE + lax.broadcasted_iota(jnp.int32, (NH * CHUNK, TILE), 1)


def fold(value, op):
    out = value[:, :128]
    for i in range(1, value.shape[1] // 128):
        out = op(out, value[:, i * 128 : (i + 1) * 128])
    return out


def tile_rows(t):
    return pl.ds(pl.multiple_of(t * TILE, TILE), TILE)


def fwd_kernel(
    kplace_ref, own_ref, place_ref, q_ref, *refs
):
    kv_refs, (attn_ref, o_ref, qe_ref, ks_ref, vs_ref, s_scr, m_scr, l_scr, acc_scr) = refs[:8], refs[13:]
    for k in range(8):
        for b in range(8):
            low, high = key_form(kv_refs[k][b * BLK : (b + 1) * BLK, :])
            dst = block_rows(kplace_ref[8 * k + b])
            ks_ref[dst, :] = low
            vs_ref[dst, :] = high

    for c in range(ROWS // CHUNK):
        place_a, place_b = place_ref[2 * c], place_ref[2 * c + 1]
        blocks = (own_ref[2 * c], own_ref[2 * c + 1])
        query = jnp.concatenate([q_ref[block_rows(b), :] for b in blocks], axis=0)
        stacked = stack_heads(query, False)
        qpos = stacked_pos(place_a, place_b)
        tiles = place_a // (TILE // BLK) + 1
        m_scr[...] = jnp.full(m_scr.shape, -1e30, F32)

        def score_step(t, _):
            scores = dot_t(stacked, ks_ref[tile_rows(t), :])
            scores = jnp.where(col_pos(t) <= qpos, scores, -1e30)
            s_scr[t] = scores
            m_scr[...] = jnp.maximum(m_scr[...], fold(scores, jnp.maximum))
            return 0

        lax.fori_loop(0, tiles, score_step, 0)
        peak = jnp.max(m_scr[...], axis=1, keepdims=True)
        l_scr[...] = jnp.zeros(l_scr.shape, F32)
        acc_scr[...] = jnp.zeros(acc_scr.shape, F32)

        def value_step(t, _):
            prob = jnp.exp(s_scr[t] - peak)
            l_scr[...] = l_scr[...] + fold(prob, jnp.add)
            acc_scr[...] = acc_scr[...] + dot(prob.astype(BF), vs_ref[tile_rows(t), :])
            return 0

        lax.fori_loop(0, tiles, value_step, 0)
        total = jnp.sum(l_scr[...], axis=1, keepdims=True)
        log_total = peak + jnp.log(total)
        out = merge_heads(acc_scr[...] / total, True)
        ext = add_extras(
            query.astype(F32),
            [-log_total[h * CHUNK : (h + 1) * CHUNK] for h in range(NH)],
            False,
        ).astype(BF)
        for i, b in enumerate(blocks):
            rows = slice(i * BLK, (i + 1) * BLK)
            o_ref[block_rows(b), :] = out[rows]
            attn_ref[block_rows(b), :] = out[rows].astype(BF)
            qe_ref[block_rows(b), :] = ext[rows]


def dq_kernel(own_ref, place_ref, qe_ref, de_ref, ks_ref, vs_ref, dq_ref, acc_scr):
    for c in range(ROWS // CHUNK):
        place_a, place_b = place_ref[2 * c], place_ref[2 * c + 1]
        blocks = (own_ref[2 * c], own_ref[2 * c + 1])
        query = stack_heads(jnp.concatenate([qe_ref[block_rows(b), :] for b in blocks], axis=0), False)
        d_out = stack_heads(jnp.concatenate([de_ref[block_rows(b), :] for b in blocks], axis=0), True)
        qpos = stacked_pos(place_a, place_b)
        tiles = place_a // (TILE // BLK) + 1
        acc_scr[...] = jnp.zeros(acc_scr.shape, F32)

        def step(t, _):
            keys = ks_ref[tile_rows(t), :]
            prob = jnp.where(col_pos(t) <= qpos, jnp.exp(dot_t(query, keys)), 0.0)
            d_raw = (prob * dot_t(d_out, vs_ref[tile_rows(t), :])).astype(BF)
            acc_scr[...] = acc_scr[...] + dot(d_raw, keys)
            return 0

        lax.fori_loop(0, tiles, step, 0)
        out = (merge_heads(acc_scr[...], False) * 0.125).astype(BF)
        for i, b in enumerate(blocks):
            dq_ref[block_rows(b), :] = out[i * BLK : (i + 1) * BLK]


def dkv_kernel(qplace_ref, kplace_ref, own_ref, place_ref, kv_ref, qe_ref, *refs):
    de_refs, (dkv_ref, qs_scr, ds_scr, dk_scr, dv_scr) = refs[:8], refs[8:]
    for k in range(8):
        for b in range(8):
            qs_scr[block_rows(qplace_ref[8 * k + b]), :] = qe_ref[(8 * k + b) * BLK : (8 * k + b + 1) * BLK, :]
            ds_scr[block_rows(kplace_ref[8 * k + b]), :] = de_refs[k][b * BLK : (b + 1) * BLK, :]

    for c in range(ROWS // CHUNK):
        place_a, place_b = place_ref[2 * c], place_ref[2 * c + 1]
        blocks = (own_ref[2 * c], own_ref[2 * c + 1])
        low, high = key_form(jnp.concatenate([kv_ref[block_rows(b), :] for b in blocks], axis=0))
        keys = stack_heads(low, False)
        values = stack_heads(high, True)
        kpos = stacked_pos(place_a, place_b)
        dk_scr[...] = jnp.zeros(dk_scr.shape, F32)
        dv_scr[...] = jnp.zeros(dv_scr.shape, F32)

        def step(t, _):
            query = qs_scr[tile_rows(t), :]
            d_out = ds_scr[tile_rows(t), :]
            prob = jnp.where(col_pos(t) >= kpos, jnp.exp(dot_t(keys, query)), 0.0)
            d_raw = (prob * dot_t(values, d_out)).astype(BF)
            dv_scr[...] = dv_scr[...] + dot(prob.astype(BF), d_out)
            dk_scr[...] = dk_scr[...] + dot(d_raw, query)
            return 0

        lax.fori_loop(place_b // (TILE // BLK), LEN // TILE, step, 0)
        d_keys = merge_heads(dk_scr[...], False)
        d_values = merge_heads(dv_scr[...], True)
        out = jnp.concatenate(
            [d_keys[:, :128], d_keys[:, 128:] + d_values[:, :128], d_values[:, 128:]], axis=1
        ).astype(BF)
        for i, b in enumerate(blocks):
            dkv_ref[block_rows(b), :] = out[i * BLK : (i + 1) * BLK]


def delta_kernel(d_ref, o_ref, branch_ref, de_ref, same_ref):
    same_ref[...] = branch_ref[...]
    d_out = jnp.concatenate([jnp.zeros((ROWS, 64), F32), d_ref[...].astype(F32)], axis=1)
    product = d_out * o_ref[...]
    sums = [
        -jnp.sum(jnp.where(feature_mask(ROWS, h, True), product, 0.0), axis=1, keepdims=True)
        for h in range(NH)
    ]
    de_ref[...] = add_extras(d_out, sums, True).astype(BF)


SMEM = pl.BlockSpec(memory_space=pltpu.SMEM)
VM = pl.BlockSpec(memory_space=pltpu.VMEM)
ANY = pl.BlockSpec(memory_space=pl.ANY)
PARAMS = pltpu.CompilerParams(vmem_limit_bytes=VMEM_LIMIT)


def shape(*dims, dtype=BF):
    return jax.ShapeDtypeStruct(dims, dtype)


def attention_forward(kplace, own, place, query, kv, early):
    return pl.pallas_call(
        fwd_kernel,
        out_shape=(
            shape(ROWS, EXT), shape(ROWS, EXT, dtype=F32), shape(ROWS, EXT),
            shape(LEN, EXT), shape(LEN, EXT),
        ),
        in_specs=[SMEM] * 3 + [VM] * 9 + [ANY] * 5,
        out_specs=(VM,) * 5,
        scratch_shapes=[
            pltpu.VMEM((LEN // TILE, NH * CHUNK, TILE), F32),
            pltpu.VMEM((NH * CHUNK, 128), F32),
            pltpu.VMEM((NH * CHUNK, 128), F32),
            pltpu.VMEM((NH * CHUNK, EXT), F32),
        ],
        compiler_params=PARAMS,
        cost_estimate=pl.CostEstimate(flops=16 * 10**9, bytes_accessed=10**7, transcendentals=4 * 10**6),
    )(kplace, own, place, query, *kv, *early)


def attention_dq(own, place, qe, de, ks, vs):
    return pl.pallas_call(
        dq_kernel,
        out_shape=shape(ROWS, EXT),
        in_specs=[SMEM] * 2 + [VM] * 4,
        out_specs=VM,
        scratch_shapes=[pltpu.VMEM((NH * CHUNK, EXT), F32)],
        compiler_params=PARAMS,
        cost_estimate=pl.CostEstimate(flops=14 * 10**9, bytes_accessed=10**7, transcendentals=4 * 10**6),
    )(own, place, qe, de, ks, vs)


def attention_dkv(qplace, kplace, own, place, kv, qe, de):
    return pl.pallas_call(
        dkv_kernel,
        out_shape=shape(ROWS, 2 * GD),
        in_specs=[SMEM] * 4 + [VM] * 10,
        out_specs=VM,
        scratch_shapes=[
            pltpu.VMEM((LEN, EXT), BF),
            pltpu.VMEM((LEN, EXT), BF),
            pltpu.VMEM((NH * CHUNK, EXT), F32),
            pltpu.VMEM((NH * CHUNK, EXT), F32),
        ],
        compiler_params=PARAMS,
        cost_estimate=pl.CostEstimate(flops=15 * 10**9, bytes_accessed=10**7, transcendentals=4 * 10**6),
    )(qplace, kplace, own, place, kv, qe, *de)


def delta_rows(d_attn, o, d_branch):
    return pl.pallas_call(
        delta_kernel,
        out_shape=(shape(ROWS, EXT), shape(128, D)),
        in_specs=[VM] * 3,
        out_specs=(VM, VM),
        compiler_params=PARAMS,
        cost_estimate=pl.CostEstimate(flops=10**6, bytes_accessed=10**6, transcendentals=0),
    )(d_attn, o, d_branch)


def prep_kernel(at_ref, w_ref, gain_ref, bias_ref, vb_ref, cols_ref):
    for k in range(4):

        @pl.when(at_ref[0] == k)
        def _():
            for i, part in enumerate((1, 2, 0)):
                start = part * D + k * GD
                cols_ref[:GD, i * GD : (i + 1) * GD] = w_ref[:, start : start + GD]

    small = jnp.concatenate(
        [gain_ref[...].astype(F32), bias_ref[...].astype(F32), vb_ref[...].astype(F32), jnp.zeros((8, GD), F32)],
        axis=0,
    )
    cols_ref[GD:, :] = jnp.concatenate([small, jnp.zeros((16, 2 * GD), F32)], axis=1).astype(BF)


def prepare(at, w, gains, biases, vb):
    return pl.pallas_call(
        prep_kernel,
        out_shape=shape(GD + 16, 3 * GD),
        in_specs=[SMEM] + [VM] * 4,
        out_specs=VM,
        compiler_params=PARAMS,
        cost_estimate=pl.CostEstimate(flops=1000, bytes_accessed=10**6, transcendentals=0),
    )(at, w, gains, biases, vb)


def qkv_kernel(at_ref, *refs):
    toks, ws = refs[:4], refs[4:8]
    kv_ref, q_ref, h1_ref, n1_ref, w_ref, small_ref, w_scr = refs[8:]
    yi, zi = at_ref[0], at_ref[1]
    for s in range(4):
        w_scr[s] = ws[s][...]
    for g in range(4):
        slot = (zi - g + 4) % 4
        w_ref[g * GD : (g + 1) * GD, :] = w_scr[slot, :GD]
        small_ref[:, g * GD : (g + 1) * GD] = w_scr[slot, GD:, :256].astype(F32)[:8, :GD]
    gain, shift = small_ref[0:1, :], small_ref[2:3, :]
    for s in range(4):
        rows = slice(128 * s, 128 * (s + 1))
        normed, _ = normalize(toks[s][...].astype(F32))
        n1_ref[rows, :] = normed
        h1_ref[rows, :] = (normed * gain + shift).astype(BF)
    own = w_scr[(zi - yi + 4) % 4, GD:, :256].astype(F32)[:8, :GD]
    qkv = dot(h1_ref[...], w_ref[...])
    kv_ref[:, :GD] = qkv[:, :GD].astype(BF)
    kv_ref[:, GD:] = (qkv[:, GD : 2 * GD] + own[7:8]).astype(BF)
    query = (qkv[:, 2 * GD :] + own[3:4]).astype(BF).astype(F32) * 0.125
    q_ref[...] = jnp.concatenate([query, jnp.zeros((ROWS, EXT - GD), F32)], axis=1).astype(BF)


def first_rows(at, toks, ws):
    return pl.pallas_call(
        qkv_kernel,
        out_shape=(
            shape(ROWS, 2 * GD), shape(ROWS, EXT), shape(ROWS, D), shape(ROWS, D, dtype=F32),
            shape(D, 3 * GD), shape(8, D, dtype=F32),
        ),
        in_specs=[SMEM] + [VM] * 8,
        out_specs=(VM,) * 6,
        scratch_shapes=[pltpu.VMEM((4, GD + 16, 3 * GD), BF)],
        compiler_params=PARAMS,
        cost_estimate=pl.CostEstimate(flops=5 * 10**8, bytes_accessed=6 * 10**6, transcendentals=0),
    )(at, *toks, *ws)


def mlp_kernel(*refs):
    h2s, cots = refs[:4], refs[4:8]
    up_ref, down_ref, ub_ref, h2_ref, cot_ref, act_ref, dup_ref, dh_ref = refs[8:]
    for s in range(4):
        rows = slice(128 * s, 128 * (s + 1))
        h2, cot = h2s[s][...], cots[s][...]
        h2_ref[rows, :] = h2
        cot_ref[rows, :] = cot
        up = dot(h2, up_ref[...]) + ub_ref[...].astype(F32)
        d_act = dot_t(cot, down_ref[...])
        square = up * up
        th = jnp.tanh(0.7978845608028654 * (up + 0.044715 * (square * up)))
        half = 0.5 * (1.0 + th)
        slope = half + 0.5 * up * (1.0 - th * th) * (
            0.7978845608028654 * (1.0 + 3 * 0.044715 * square)
        )
        act_ref[rows, :] = (up * half).astype(BF)
        d_up = (slope * d_act).astype(BF)
        dup_ref[rows, :] = d_up
        dh_ref[rows, :] = dot_t(d_up, up_ref[...]).astype(BF)


def feed_forward(h2s, cots, w_up, w_down, ub):
    return pl.pallas_call(
        mlp_kernel,
        out_shape=(shape(ROWS, D),) * 5,
        in_specs=[VM] * 11,
        out_specs=(VM,) * 5,
        compiler_params=PARAMS,
        cost_estimate=pl.CostEstimate(flops=4 * 10**9, bytes_accessed=6 * 10**6, transcendentals=4 * 10**5),
    )(*h2s, *cots, w_up, w_down, ub)


def wgrad_kernel(
    at_ref, h2_ref, dup_ref, act_ref, cot_ref, gout_ref, wd_ref, keep_ref, give_ref, down_ref
):
    down_ref[...] = dot(act_ref[...], wd_ref[...]).astype(BF)
    yi, ci = at_ref[0], at_ref[2]
    g_up = t_dot(h2_ref[...], dup_ref[...])
    g_down = t_dot(act_ref[...], cot_ref[...])
    vec = jnp.concatenate(
        [
            jnp.sum(dup_ref[...].astype(F32), axis=0, keepdims=True),
            jnp.sum(cot_ref[...].astype(F32), axis=0, keepdims=True),
            jnp.zeros((6, D), F32),
        ],
        axis=0,
    )
    g_out = gout_ref[...].astype(F32)
    for c in range(2):
        for j in range(4):
            b = 4 * c + j
            block = jnp.concatenate(
                [g_up[GD * z + 24 * b : GD * z + 24 * (b + 1)] for z in range(4)]
                + [g_down[96 * b : 96 * (b + 1)], g_out[24 * b : 24 * (b + 1)], vec],
                axis=0,
            ).astype(BF)
            slot = (j - yi + 4) % 4

            @pl.when(ci == c)
            def _():
                keep_ref[slot] = block

            @pl.when(ci != c)
            def _():
                give_ref[slot] = block


def weight_blocks(at, h2, d_up, act, cot, g_out, w_down):
    return pl.pallas_call(
        wgrad_kernel,
        out_shape=(shape(4, 224, D), shape(4, 224, D), shape(ROWS, D)),
        in_specs=[SMEM] + [VM] * 6,
        out_specs=(VM,) * 3,
        compiler_params=PARAMS,
        cost_estimate=pl.CostEstimate(flops=3 * 10**9, bytes_accessed=6 * 10**6, transcendentals=0),
    )(at, h2, d_up, act, cot, g_out, w_down)


def mid_kernel(at_ref, *refs):
    slots, (up_ref, down_ref, out_ref, vec_ref, scr) = refs[:4], refs[4:]
    yi, zi, ci = at_ref[0], at_ref[1], at_ref[2]
    for s in range(4):
        for c in range(2):
            scr[s, c] = slots[s][c].astype(F32)
    for c in range(2):
        for j in range(4):
            b = 4 * c + j
            ys, cs = (yi - j + 4) % 4, (ci + c) % 2
            for g in range(4):
                zs = (zi - g + 4) % 4
                up_ref[24 * b : 24 * (b + 1), g * D : (g + 1) * D] = scr[
                    ys, cs, pl.ds(pl.multiple_of(24 * zs, 8), 24)
                ]
            down_ref[96 * b : 96 * (b + 1), :] = scr[ys, cs, 96:192]
            out_ref[24 * b : 24 * (b + 1), :] = scr[ys, cs, 192:216]
            if b == 0:
                vec_ref[...] = scr[ys, cs, 216:224]


def mid_rows(at, slots):
    return pl.pallas_call(
        mid_kernel,
        out_shape=(
            shape(GD, 4 * D, dtype=F32), shape(D, D, dtype=F32), shape(GD, D, dtype=F32),
            shape(8, D, dtype=F32),
        ),
        in_specs=[SMEM] + [VM] * 4,
        out_specs=(VM,) * 4,
        scratch_shapes=[pltpu.VMEM((4, 2, 224, D), F32)],
        compiler_params=PARAMS,
        cost_estimate=pl.CostEstimate(flops=10**6, bytes_accessed=8 * 10**6, transcendentals=0),
    )(at, *slots)


def tail_kernel(at_ref, dkv_ref, dq_ref, h1_ref, n1_ref, w_ref, vec_ref, dh_ref, t_ref):
    yi, zi = at_ref[0], at_ref[1]
    d_qkv = jnp.concatenate([dkv_ref[...], dq_ref[...]], axis=1)
    d_h1 = dot_t(d_qkv[:, : 3 * GD], w_ref[...])
    dh_ref[...] = d_h1.astype(BF)
    sums = jnp.sum(d_qkv.astype(F32), axis=0, keepdims=True)
    at_own = lambda v: jnp.concatenate([jnp.where(yi == k, v, 0.0) for k in range(4)], axis=1)
    vectors = jnp.concatenate(
        [
            jnp.sum(d_h1 * n1_ref[...], axis=0, keepdims=True),
            jnp.sum(d_h1, axis=0, keepdims=True),
            at_own(sums[:, 2 * GD : 3 * GD]),
            at_own(sums[:, GD : 2 * GD]),
            vec_ref[4:8, :],
        ],
        axis=0,
    ).astype(BF)
    row = lax.broadcasted_iota(jnp.int32, (8, 128), 0)
    lane = lax.broadcasted_iota(jnp.int32, (8, 128), 1)
    columns = t_dot(vectors, jnp.where(lane == row + 64, 1.0, 0.0).astype(BF))
    grad = t_dot(h1_ref[...], d_qkv)
    for g in range(4):
        rows = slice(g * GD, (g + 1) * GD)
        slot = (g - zi + 4) % 4
        t_ref[slot, :, :512] = grad[rows, :512].astype(BF)
        t_ref[slot, :, 512:] = (grad[rows, 512:] + columns[rows]).astype(BF)


def last_gradients(at, d_kv, d_q, h1, n1, w, vec):
    return pl.pallas_call(
        tail_kernel,
        out_shape=(shape(ROWS, D), shape(4, GD, 640)),
        in_specs=[SMEM] + [VM] * 6,
        out_specs=(VM, VM),
        compiler_params=PARAMS,
        cost_estimate=pl.CostEstimate(flops=3 * 10**9, bytes_accessed=6 * 10**6, transcendentals=0),
    )(at, d_kv, d_q, h1, n1, w, vec)


def final_kernel(at_ref, *refs):
    slots, (grad_ref, vec_ref, scr) = refs[:4], refs[4:]
    for s in range(4):
        for c in range(2):
            scr[s, c] = slots[s][c]
    yi, ci = at_ref[0], at_ref[2]
    for c in range(2):
        rows = slice(96 * c, 96 * (c + 1))
        total = []
        for g in range(4):
            value = scr[(yi - g + 4) % 4, (ci + c) % 2].astype(F32)
            for i, part in enumerate((1, 2, 0)):
                start = part * D + g * GD
                grad_ref[rows, start : start + GD] = value[:, i * GD : (i + 1) * GD]
            total.append(value[:, 512:])
        vec_ref[rows, :] = (total[0] + total[1]) + (total[2] + total[3])


def final_rows(at, slots):
    return pl.pallas_call(
        final_kernel,
        out_shape=(shape(GD, 3 * D, dtype=F32), shape(GD, 128, dtype=F32)),
        in_specs=[SMEM] + [VM] * 4,
        out_specs=(VM, VM),
        scratch_shapes=[pltpu.VMEM((4, 2, 96, 640), BF)],
        compiler_params=PARAMS,
        cost_estimate=pl.CostEstimate(flops=10**6, bytes_accessed=3 * 10**6, transcendentals=0),
    )(at, *slots)


def gather(value, axes, axis=0):
    return lax.all_gather(value, axes, axis=axis, tiled=True)


def swap(value, axes):
    return lax.all_to_all(value, axes, 0, 0)


def send(value, axis, step):
    n = lax.axis_size(axis)
    return lax.ppermute(value, axis, [(i, (i + step) % n) for i in range(n)])


def spread(value, axis):
    return [value] + [send(value, axis, s) for s in range(1, 4)]


def exchange(slots, axis, step):
    return [slots[0]] + [send(slots[s], axis, s * step) for s in range(1, 4)]


def add_slots(slots):
    a, b, c, d = (v.astype(F32) for v in slots)
    return (a + c) + (b + d)


def group_of(value, index, size, axis=0):
    return lax.dynamic_slice_in_dim(value, (index % 4) * size, size, axis)


def local(
    tokens, qkv_w, out_w, up_w, down_w, norm_gains, biases, value_bias, up_bias, cotangent, block_place
):
    xi = lax.axis_index("x")
    yi = lax.axis_index("y")
    ci = lax.axis_index("core")
    zi = lax.axis_index("fsdp")
    tok_own = tokens[0]
    cot_own = cotangent[0]

    at = jnp.stack([yi, zi, ci]).astype(jnp.int32)
    ws = spread(prepare(at, qkv_w, norm_gains, biases, value_bias[None]), "fsdp")
    toks = spread(tok_own, "y")

    ids = jnp.arange(NBLK, dtype=jnp.int32)
    slot_x, slot_c, slot_y, blk = ids // 16, (ids // 8) % 2, (ids // 2) % 4, ids % 2
    pick = lambda at: jnp.sum(jnp.where(at[:, None] == ids[None, :], block_place[None, :], 0), axis=1)
    at_y = (yi - slot_y + 4) % 4
    key_place = pick(at_y * 16 + ((xi - slot_x + 4) % 4) * 4 + ((ci + slot_c) % 2) * 2 + blk)
    query_place = pick(at_y * 16 + slot_x * 4 + slot_c * 2 + blk)
    own_place = key_place[:8]
    rank = jnp.sum((own_place[None, :] > own_place[:, None]).astype(jnp.int32), axis=1)
    order = jnp.arange(8, dtype=jnp.int32)
    hit = rank[None, :] == order[:, None]
    own = jnp.sum(jnp.where(hit, order[None, :], 0), axis=1)
    place = jnp.sum(jnp.where(hit, own_place[None, :], 0), axis=1)

    w_out = gather(out_w, "fsdp")
    w_out = jnp.concatenate([group_of(w_out, yi + s, GD) for s in range(4)], axis=0)
    w_up = swap(up_w.reshape(GD, 4, D).transpose(1, 0, 2), "fsdp").reshape(D, D)
    w_down = down_w
    cots = spread(cot_own, "fsdp")

    kv_own, query, h1, n1y, w_qkv, small = first_rows(at, toks, ws)
    gain1, gain2 = small[0], small[1]
    out_bias, shift2, down_bias = small[4], small[5], small[6]
    kv_all = [p for v in spread(kv_own, "x") for p in (v, send(v, "core", 1))]
    attn, o_exact, qe, ks, vs = attention_forward(key_place, own, place, query, kv_all, cots + [w_up])
    qe_all = gather(qe, XC)

    attn = attn[:, 64:]
    attn_own = exchange([attn[128 * s : 128 * (s + 1)] for s in range(4)], "y", -1)
    attn_own = jnp.concatenate(attn_own, axis=1)
    x2 = tok_own.astype(F32) + (dot(attn_own, w_out) + out_bias)
    n2, s2 = normalize(x2)
    h2_own = (n2 * gain2 + shift2).astype(BF)

    h2, cot_z, act, d_up, d_h2_part = feed_forward(
        spread(h2_own, "fsdp"), cots, w_up, w_down, up_bias[None]
    )
    back = lambda v: add_slots(exchange([v[128 * s : 128 * (s + 1)] for s in range(4)], "fsdp", -1))
    d_h2 = back(d_h2_part)
    cot32 = cot_own.astype(F32)
    d_x2 = cot32 + norm_back(d_h2 * gain2, n2, s2)
    d_branch = d_x2.astype(BF)
    d_attn = dot_t(d_branch, w_out).astype(BF)
    d_attn_own = exchange([d_attn[:, GD * s : GD * (s + 1)] for s in range(4)], "y", 1)
    d_attn_own = jnp.concatenate(d_attn_own, axis=0)
    de, d_branch_late = delta_rows(d_attn_own, o_exact, d_branch)
    de_all = [p for v in spread(de, "x") for p in (v, send(v, "core", 1))]
    d_q = attention_dq(own, place, qe, de, ks, vs)
    d_kv = attention_dkv(query_place, key_place, own, place, kv_own, qe_all, de_all)

    d_branch_y = jnp.concatenate(spread(d_branch_late, "y"), axis=0)
    g_out = t_dot(attn, d_branch_y).astype(BF)
    g_out = lax.ppermute(
        g_out, ("y", "fsdp"), [(a * 4 + b, b * 4 + a) for a in range(4) for b in range(4)]
    )
    keep, give, down = weight_blocks(at, h2, d_up, act, cot_z, g_out, w_down)
    layer_out = (x2 + back(down) + down_bias).astype(BF)
    mid = (keep.astype(F32) + send(give, "core", 1).astype(F32)).astype(BF)
    mid = add_slots(exchange([mid[s] for s in range(4)], "y", 1)).astype(BF)
    mid = add_slots(spread(mid, "x")).astype(BF)
    mid_up = exchange([group_of(mid[:96], zi + s, 24) for s in range(4)], "fsdp", 1)
    mid = jnp.concatenate(mid_up + [mid[96:]], axis=0)
    mid = [jnp.stack([v, send(v, "core", 1)]) for v in spread(mid, "y")]
    grad_up, grad_down, grad_out, vec = mid_rows(at, mid)
    grad_up_bias = vec[0]
    grad_down_bias = lax.dynamic_slice(vec[1], (zi * GD,), (GD,))

    vec = jnp.stack([jnp.sum(d_h2 * n2, axis=0), jnp.sum(d_branch.astype(F32), axis=0), jnp.sum(d_h2, axis=0)])
    vec = jnp.pad(vec, ((4, 1), (0, 0)))
    d_h1_send, tail = last_gradients(at, d_kv, d_q, h1, n1y, w_qkv, vec)
    d_h1 = add_slots(exchange([d_h1_send[128 * s : 128 * (s + 1)] for s in range(4)], "y", -1))
    n1, s1 = normalize(tok_own.astype(F32))
    input_grad = (d_x2 + norm_back(d_h1 * gain1, n1, s1)).astype(BF)

    tail = add_slots(exchange([tail[s] for s in range(4)], "fsdp", 1)).astype(BF)
    kept = lax.dynamic_slice_in_dim(tail, ci * 96, 96, 0)
    given = lax.dynamic_slice_in_dim(tail, (1 - ci) * 96, 96, 0)
    tail = (kept.astype(F32) + send(given, "core", 1).astype(F32)).astype(BF)
    tail = add_slots(spread(tail, "x")).astype(BF)
    tail = [jnp.stack([v, send(v, "core", 1)]) for v in spread(tail, "y")]
    grad_qkv, vectors = final_rows(at, tail)
    vectors = vectors[:, 64:71].T
    grad_gains = jnp.stack([vectors[0], vectors[4]])
    grad_biases = jnp.stack([vectors[1], vectors[2], vectors[5], vectors[6], grad_down_bias])
    grad_value_bias = vectors[3]
    return (
        layer_out[None], input_grad[None], grad_qkv, grad_out, grad_up, grad_down,
        grad_gains, grad_biases, grad_value_bias, grad_up_bias,
    )


def solution(mesh):
    grid = Mesh(mesh.devices.reshape(4, 4, 2, 4), ("y", "x", "core", "fsdp"))
    rows = P("fsdp", CTX, None)
    in_specs = (
        rows, P("fsdp", None), P("fsdp", None), P("fsdp", None), P("fsdp", None),
        P(None, "fsdp"), P(None, "fsdp"), P("fsdp"), P("fsdp"), rows, P(),
    )
    out_specs = (
        rows, rows, P("fsdp", None), P("fsdp", None), P("fsdp", None), P("fsdp", None),
        P(None, "fsdp"), P(None, "fsdp"), P("fsdp"), P("fsdp"),
    )
    return jax.shard_map(local, mesh=grid, in_specs=in_specs, out_specs=out_specs, check_vma=False)
```

```python
import functools

import jax
import jax.numpy as jnp
from jax import lax
from jax.experimental import pallas as pl
from jax.experimental.pallas import tpu as pltpu
from jax.sharding import Mesh
from jax.sharding import PartitionSpec as P

EPS = 1e-05
D = 768
GD = 192
NH = 3
HD = 64
ROWS = 512
LEN = 4096
BLK = 64
NBLK = 64
EXT = 256
TILE = 512
CHUNK = 128
BF = jnp.bfloat16
F32 = jnp.float32
XC = ("x", "core")
CTX = ("y", "x", "core")
VMEM_LIMIT = 48 * 1024 * 1024


def dot(a, b):
    return lax.dot_general(a, b, (((1,), (0,)), ((), ())), preferred_element_type=F32)


def dot_t(a, b):
    return lax.dot_general(a, b, (((1,), (1,)), ((), ())), preferred_element_type=F32)


def t_dot(a, b):
    return lax.dot_general(a, b, (((0,), (0,)), ((), ())), preferred_element_type=F32)


def normalize(value):
    center = value - jnp.mean(value, axis=-1, keepdims=True)
    factor = lax.rsqrt(jnp.mean(center * center, axis=-1, keepdims=True) + EPS)
    return (center * factor, factor)


def norm_back(scaled, normed, factor):
    return factor * (
        scaled
        - jnp.mean(scaled, axis=-1, keepdims=True)
        - normed * jnp.mean(scaled * normed, axis=-1, keepdims=True)
    )


def lanes(rows):
    return lax.broadcasted_iota(jnp.int32, (rows, EXT), 1)


def head_mask(rows, h, high):
    lane = lanes(rows)
    if high:
        feat = (lane >= 64 + HD * h) & (lane < 64 + HD * (h + 1))
        ext = (lane >= 3 * h) & (lane < 3 * h + 3)
    else:
        feat = (lane >= HD * h) & (lane < HD * (h + 1))
        ext = (lane >= GD + 3 * h) & (lane < GD + 3 * h + 3)
    return feat | ext


def feature_mask(rows, h, high):
    lane = lanes(rows) - (64 if high else 0)
    return (lane >= HD * h) & (lane < HD * (h + 1))


def stack_heads(value, high):
    rows = value.shape[0]
    zero = jnp.zeros_like(value)
    return jnp.concatenate(
        [jnp.where(head_mask(rows, h, high), value, zero) for h in range(NH)], axis=0
    )


def merge_heads(stacked, high):
    rows = stacked.shape[0] // NH
    out = jnp.zeros((rows, EXT), F32)
    for h in range(NH):
        out = out + jnp.where(feature_mask(rows, h, high), stacked[h * rows : (h + 1) * rows], 0.0)
    return out


def pieces(value):
    first = value.astype(BF).astype(F32)
    second = (value - first).astype(BF).astype(F32)
    third = (value - first - second).astype(BF).astype(F32)
    return (first, second, third)


def add_extras(base, columns, high):
    rows = base.shape[0]
    lane = lanes(rows)
    start = 0 if high else GD
    for h in range(NH):
        for i, piece in enumerate(pieces(columns[h])):
            base = jnp.where(lane == start + 3 * h + i, piece, base)
    return base


def key_form(kv):
    lane = lanes(kv.shape[0])
    one = jnp.ones((kv.shape[0], EXT), BF)
    zero = jnp.zeros((kv.shape[0], EXT), BF)
    low = jnp.where(lane < GD, kv[:, :EXT], jnp.where(lane < GD + 9, one, zero))
    high = jnp.where(lane >= 64, kv[:, 128:384], jnp.where(lane < 9, one, zero))
    return (low, high)


def block_rows(index):
    return pl.ds(pl.multiple_of(index * BLK, BLK), BLK)


def stacked_pos(place_a, place_b):
    row = lax.broadcasted_iota(jnp.int32, (NH * CHUNK, 1), 0)
    place = jnp.where(row % CHUNK < BLK, place_a, place_b)
    return place * BLK + row % BLK


def col_pos(tile):
    return tile * TILE + lax.broadcasted_iota(jnp.int32, (NH * CHUNK, TILE), 1)


def fold(value, op):
    out = value[:, :128]
    for i in range(1, value.shape[1] // 128):
        out = op(out, value[:, i * 128 : (i + 1) * 128])
    return out


def tile_rows(t):
    return pl.ds(pl.multiple_of(t * TILE, TILE), TILE)


def fwd_kernel(
    kplace_ref, own_ref, place_ref, q_ref, *refs
):
    kv_refs = refs[:8]
    attn_ref, o_ref, qe_ref, ks_ref, vs_ref, s_scr, m_scr, l_scr, acc_scr, land, sems = refs[9:]
    copies = [pltpu.make_async_copy(kv_refs[k], land.at[k], sems.at[k]) for k in range(8)]
    for copy in copies:
        copy.start()
    for k in range(8):
        copies[k].wait()
        for b in range(8):
            low, high = key_form(land[k, b * BLK : (b + 1) * BLK, :])
            dst = block_rows(kplace_ref[8 * k + b])
            ks_ref[dst, :] = low
            vs_ref[dst, :] = high

    for c in range(ROWS // CHUNK):
        place_a, place_b = place_ref[2 * c], place_ref[2 * c + 1]
        blocks = (own_ref[2 * c], own_ref[2 * c + 1])
        query = jnp.concatenate([q_ref[block_rows(b), :] for b in blocks], axis=0)
        stacked = stack_heads(query, False)
        qpos = stacked_pos(place_a, place_b)
        tiles = place_a // (TILE // BLK) + 1
        m_scr[...] = jnp.full(m_scr.shape, -1e30, F32)

        def score_step(t, _):
            scores = dot_t(stacked, ks_ref[tile_rows(t), :])
            scores = jnp.where(col_pos(t) <= qpos, scores, -1e30)
            s_scr[t] = scores
            m_scr[...] = jnp.maximum(m_scr[...], fold(scores, jnp.maximum))
            return 0

        lax.fori_loop(0, tiles, score_step, 0)
        peak = jnp.max(m_scr[...], axis=1, keepdims=True)
        l_scr[...] = jnp.zeros(l_scr.shape, F32)
        acc_scr[...] = jnp.zeros(acc_scr.shape, F32)

        def value_step(t, _):
            prob = jnp.exp(s_scr[t] - peak)
            l_scr[...] = l_scr[...] + fold(prob, jnp.add)
            acc_scr[...] = acc_scr[...] + dot(prob.astype(BF), vs_ref[tile_rows(t), :])
            return 0

        lax.fori_loop(0, tiles, value_step, 0)
        total = jnp.sum(l_scr[...], axis=1, keepdims=True)
        log_total = peak + jnp.log(total)
        out = merge_heads(acc_scr[...] / total, True)
        ext = add_extras(
            query.astype(F32),
            [-log_total[h * CHUNK : (h + 1) * CHUNK] for h in range(NH)],
            False,
        ).astype(BF)
        for i, b in enumerate(blocks):
            rows = slice(i * BLK, (i + 1) * BLK)
            o_ref[block_rows(b), :] = out[rows]
            attn_ref[block_rows(b), :] = out[rows].astype(BF)
            qe_ref[block_rows(b), :] = ext[rows]


def dq_kernel(own_ref, place_ref, qe_ref, de_ref, ks_ref, vs_ref, dq_ref, acc_scr):
    for c in range(ROWS // CHUNK):
        place_a, place_b = place_ref[2 * c], place_ref[2 * c + 1]
        blocks = (own_ref[2 * c], own_ref[2 * c + 1])
        query = stack_heads(jnp.concatenate([qe_ref[block_rows(b), :] for b in blocks], axis=0), False)
        d_out = stack_heads(jnp.concatenate([de_ref[block_rows(b), :] for b in blocks], axis=0), True)
        qpos = stacked_pos(place_a, place_b)
        tiles = place_a // (TILE // BLK) + 1
        acc_scr[...] = jnp.zeros(acc_scr.shape, F32)

        def step(t, _):
            keys = ks_ref[tile_rows(t), :]
            prob = jnp.where(col_pos(t) <= qpos, jnp.exp(dot_t(query, keys)), 0.0)
            d_raw = (prob * dot_t(d_out, vs_ref[tile_rows(t), :])).astype(BF)
            acc_scr[...] = acc_scr[...] + dot(d_raw, keys)
            return 0

        lax.fori_loop(0, tiles, step, 0)
        out = (merge_heads(acc_scr[...], False) * 0.125).astype(BF)
        for i, b in enumerate(blocks):
            dq_ref[block_rows(b), :] = out[i * BLK : (i + 1) * BLK]


def dkv_kernel(qplace_ref, kplace_ref, own_ref, place_ref, kv_ref, qe_ref, *refs):
    de_refs, (dkv_ref, qs_scr, ds_scr, dk_scr, dv_scr, q_land, d_land, sems) = refs[:8], refs[8:]
    q_copy = pltpu.make_async_copy(qe_ref, q_land, sems.at[8])
    q_copy.start()
    copies = [pltpu.make_async_copy(de_refs[k], d_land.at[k], sems.at[k]) for k in range(8)]
    for copy in copies:
        copy.start()
    q_copy.wait()
    for b in range(NBLK):
        qs_scr[block_rows(qplace_ref[b]), :] = q_land[b * BLK : (b + 1) * BLK, :]
    for k in range(8):
        copies[k].wait()
        for b in range(8):
            ds_scr[block_rows(kplace_ref[8 * k + b]), :] = d_land[k, b * BLK : (b + 1) * BLK, :]

    for c in range(ROWS // CHUNK):
        place_a, place_b = place_ref[2 * c], place_ref[2 * c + 1]
        blocks = (own_ref[2 * c], own_ref[2 * c + 1])
        low, high = key_form(jnp.concatenate([kv_ref[block_rows(b), :] for b in blocks], axis=0))
        keys = stack_heads(low, False)
        values = stack_heads(high, True)
        kpos = stacked_pos(place_a, place_b)
        dk_scr[...] = jnp.zeros(dk_scr.shape, F32)
        dv_scr[...] = jnp.zeros(dv_scr.shape, F32)

        def step(t, _):
            query = qs_scr[tile_rows(t), :]
            d_out = ds_scr[tile_rows(t), :]
            prob = jnp.where(col_pos(t) >= kpos, jnp.exp(dot_t(keys, query)), 0.0)
            d_raw = (prob * dot_t(values, d_out)).astype(BF)
            dv_scr[...] = dv_scr[...] + dot(prob.astype(BF), d_out)
            dk_scr[...] = dk_scr[...] + dot(d_raw, query)
            return 0

        lax.fori_loop(place_b // (TILE // BLK), LEN // TILE, step, 0)
        d_keys = merge_heads(dk_scr[...], False)
        d_values = merge_heads(dv_scr[...], True)
        out = jnp.concatenate(
            [d_keys[:, :128], d_keys[:, 128:] + d_values[:, :128], d_values[:, 128:]], axis=1
        ).astype(BF)
        for i, b in enumerate(blocks):
            dkv_ref[block_rows(b), :] = out[i * BLK : (i + 1) * BLK]


def delta_kernel(d_ref, o_ref, early_ref, de_ref):
    d_out = jnp.concatenate([jnp.zeros((ROWS, 64), F32), d_ref[...].astype(F32)], axis=1)
    product = d_out * o_ref[...]
    sums = [
        -jnp.sum(jnp.where(feature_mask(ROWS, h, True), product, 0.0), axis=1, keepdims=True)
        for h in range(NH)
    ]
    de_ref[...] = add_extras(d_out, sums, True).astype(BF)


SMEM = pl.BlockSpec(memory_space=pltpu.SMEM)
VM = pl.BlockSpec(memory_space=pltpu.VMEM)
ANY = pl.BlockSpec(memory_space=pl.ANY)
PARAMS = pltpu.CompilerParams(vmem_limit_bytes=VMEM_LIMIT)


def shape(*dims, dtype=BF):
    return jax.ShapeDtypeStruct(dims, dtype)


def attention_forward(kplace, own, place, query, kv, early):
    return pl.pallas_call(
        fwd_kernel,
        out_shape=(
            shape(ROWS, EXT), shape(ROWS, EXT, dtype=F32), shape(ROWS, EXT),
            shape(LEN, EXT), shape(LEN, EXT),
        ),
        in_specs=[SMEM] * 3 + [VM] + [ANY] * 9,
        out_specs=(VM,) * 5,
        scratch_shapes=[
            pltpu.VMEM((LEN // TILE, NH * CHUNK, TILE), F32),
            pltpu.VMEM((NH * CHUNK, 128), F32),
            pltpu.VMEM((NH * CHUNK, 128), F32),
            pltpu.VMEM((NH * CHUNK, EXT), F32),
            pltpu.VMEM((8, ROWS, 2 * GD), BF),
            pltpu.SemaphoreType.DMA((8,)),
        ],
        compiler_params=PARAMS,
        cost_estimate=pl.CostEstimate(flops=16 * 10**9, bytes_accessed=10**7, transcendentals=4 * 10**6),
    )(kplace, own, place, query, *kv, *early)


def attention_dq(own, place, qe, de, ks, vs):
    return pl.pallas_call(
        dq_kernel,
        out_shape=shape(ROWS, EXT),
        in_specs=[SMEM] * 2 + [VM] * 4,
        out_specs=VM,
        scratch_shapes=[pltpu.VMEM((NH * CHUNK, EXT), F32)],
        compiler_params=PARAMS,
        cost_estimate=pl.CostEstimate(flops=14 * 10**9, bytes_accessed=10**7, transcendentals=4 * 10**6),
    )(own, place, qe, de, ks, vs)


def attention_dkv(qplace, kplace, own, place, kv, qe, de):
    return pl.pallas_call(
        dkv_kernel,
        out_shape=shape(ROWS, 2 * GD),
        in_specs=[SMEM] * 4 + [VM] + [ANY] * 9,
        out_specs=VM,
        scratch_shapes=[
            pltpu.VMEM((LEN, EXT), BF),
            pltpu.VMEM((LEN, EXT), BF),
            pltpu.VMEM((NH * CHUNK, EXT), F32),
            pltpu.VMEM((NH * CHUNK, EXT), F32),
            pltpu.VMEM((LEN, EXT), BF),
            pltpu.VMEM((8, ROWS, EXT), BF),
            pltpu.SemaphoreType.DMA((9,)),
        ],
        compiler_params=PARAMS,
        cost_estimate=pl.CostEstimate(flops=15 * 10**9, bytes_accessed=10**7, transcendentals=4 * 10**6),
    )(qplace, kplace, own, place, kv, qe, *de)


def delta_rows(d_attn, o, early):
    return pl.pallas_call(
        delta_kernel,
        out_shape=shape(ROWS, EXT),
        in_specs=[VM] * 2 + [ANY],
        out_specs=VM,
        compiler_params=PARAMS,
        cost_estimate=pl.CostEstimate(flops=10**6, bytes_accessed=10**6, transcendentals=0),
    )(d_attn, o, early)


def prep_kernel(at_ref, w_ref, gain_ref, bias_ref, vb_ref, cols_ref):
    for k in range(4):

        @pl.when(at_ref[0] == k)
        def _():
            for i, part in enumerate((1, 2, 0)):
                start = part * D + k * GD
                cols_ref[:GD, i * GD : (i + 1) * GD] = w_ref[:, start : start + GD]

    small = jnp.concatenate(
        [gain_ref[...].astype(F32), bias_ref[...].astype(F32), vb_ref[...].astype(F32), jnp.zeros((8, GD), F32)],
        axis=0,
    )
    cols_ref[GD:, :] = jnp.concatenate([small, jnp.zeros((16, 2 * GD), F32)], axis=1).astype(BF)


def prepare(at, w, gains, biases, vb):
    return pl.pallas_call(
        prep_kernel,
        out_shape=shape(GD + 16, 3 * GD),
        in_specs=[SMEM] + [VM] * 4,
        out_specs=VM,
        compiler_params=PARAMS,
        cost_estimate=pl.CostEstimate(flops=1000, bytes_accessed=10**6, transcendentals=0),
    )(at, w, gains, biases, vb)


def qkv_kernel(at_ref, *refs):
    toks, ws = refs[:4], refs[4:8]
    up_ref, kv_ref, q_ref, h1_ref, n1_ref, w_ref, small_ref, upg_ref, w_scr = refs[8:]
    yi, zi = at_ref[0], at_ref[1]
    for s in range(4):
        w_scr[s] = ws[s][...]
    for g in range(4):
        slot = (zi - g + 4) % 4
        w_ref[g * GD : (g + 1) * GD, :] = w_scr[slot, :GD]
        small_ref[:, g * GD : (g + 1) * GD] = w_scr[slot, GD:, :256].astype(F32)[:8, :GD]
    gain, shift = small_ref[0:1, :], small_ref[2:3, :]
    for s in range(4):
        rows = slice(128 * s, 128 * (s + 1))
        normed, _ = normalize(toks[s][...].astype(F32))
        n1_ref[rows, :] = normed
        h1_ref[rows, :] = (normed * gain + shift).astype(BF)
    for g in range(4):
        upg_ref[g] = up_ref[:, g * D : (g + 1) * D]
    own = w_scr[(zi - yi + 4) % 4, GD:, :256].astype(F32)[:8, :GD]
    qkv = dot(h1_ref[...], w_ref[...])
    kv_ref[:, :GD] = qkv[:, :GD].astype(BF)
    kv_ref[:, GD:] = (qkv[:, GD : 2 * GD] + own[7:8]).astype(BF)
    query = (qkv[:, 2 * GD :] + own[3:4]).astype(BF).astype(F32) * 0.125
    q_ref[...] = jnp.concatenate([query, jnp.zeros((ROWS, EXT - GD), F32)], axis=1).astype(BF)


def first_rows(at, toks, ws, up_w):
    return pl.pallas_call(
        qkv_kernel,
        out_shape=(
            shape(ROWS, 2 * GD), shape(ROWS, EXT), shape(ROWS, D), shape(ROWS, D, dtype=F32),
            shape(D, 3 * GD), shape(8, D, dtype=F32), shape(4, GD, D),
        ),
        in_specs=[SMEM] + [VM] * 9,
        out_specs=(VM,) * 7,
        scratch_shapes=[pltpu.VMEM((4, GD + 16, 3 * GD), BF)],
        compiler_params=PARAMS,
        cost_estimate=pl.CostEstimate(flops=5 * 10**8, bytes_accessed=6 * 10**6, transcendentals=0),
    )(at, *toks, *ws, up_w)


def mlp_kernel(at_ref, *refs):
    h2s = refs[:4]
    cots_ref, up_ref, down_ref, ub_ref, h2_ref, cot_ref, act_ref, dup_ref, dh_ref = refs[4:]
    for s in range(4):
        rows = slice(128 * s, 128 * (s + 1))
        h2 = h2s[s][...]
        cot = cots_ref[pl.ds(pl.multiple_of((at_ref[1] - s + 4) % 4 * 128, 128), 128), :]
        h2_ref[rows, :] = h2
        cot_ref[rows, :] = cot
        up = dot(h2, up_ref[...]) + ub_ref[...].astype(F32)
        d_act = dot_t(cot, down_ref[...])
        square = up * up
        th = jnp.tanh(0.7978845608028654 * (up + 0.044715 * (square * up)))
        half = 0.5 * (1.0 + th)
        slope = half + 0.5 * up * (1.0 - th * th) * (
            0.7978845608028654 * (1.0 + 3 * 0.044715 * square)
        )
        act_ref[rows, :] = (up * half).astype(BF)
        d_up = (slope * d_act).astype(BF)
        dup_ref[rows, :] = d_up
        dh_ref[rows, :] = dot_t(d_up, up_ref[...]).astype(BF)


def feed_forward(at, h2s, cots, w_up, w_down, ub):
    return pl.pallas_call(
        mlp_kernel,
        out_shape=(shape(ROWS, D),) * 5,
        in_specs=[SMEM] + [VM] * 8,
        out_specs=(VM,) * 5,
        compiler_params=PARAMS,
        cost_estimate=pl.CostEstimate(flops=4 * 10**9, bytes_accessed=6 * 10**6, transcendentals=4 * 10**5),
    )(at, *h2s, cots, w_up, w_down, ub)


def wgrad_kernel(
    at_ref, h2_ref, dup_ref, act_ref, cot_ref, attn_ref, branch_ref, wd_ref,
    keep_ref, give_ref, down_ref, out_scr,
):
    yi, ci = at_ref[0], at_ref[2]
    down_ref[...] = dot(act_ref[...], wd_ref[...]).astype(BF)
    g_up = t_dot(h2_ref[...], dup_ref[...])
    g_down = t_dot(act_ref[...], cot_ref[...])
    g_out = t_dot(attn_ref[...], branch_ref[...])
    for s in range(4):
        out_scr[s] = g_out[GD * s : GD * (s + 1)]
    vec = jnp.concatenate(
        [
            jnp.sum(dup_ref[...].astype(F32), axis=0, keepdims=True),
            jnp.sum(cot_ref[...].astype(F32), axis=0, keepdims=True),
            jnp.zeros((14, D), F32),
        ],
        axis=0,
    )
    for c in range(2):
        for j in range(4):
            b = 4 * c + j
            parts = []
            for z in range(4):
                parts.append(g_up[GD * z + 24 * b : GD * z + 24 * (b + 1)])
                parts.append(out_scr[(z - yi + 4) % 4, 24 * b : 24 * (b + 1)])
            parts += [g_down[96 * b : 96 * (b + 1)], vec]
            block = jnp.concatenate(parts, axis=0).astype(BF)
            slot = (j - yi + 4) % 4

            @pl.when(ci == c)
            def _():
                keep_ref[slot] = block

            @pl.when(ci != c)
            def _():
                give_ref[slot] = block


def weight_blocks(at, h2, d_up, act, cot, attn, d_branch, w_down):
    return pl.pallas_call(
        wgrad_kernel,
        out_shape=(shape(4, 304, D), shape(4, 304, D), shape(ROWS, D)),
        in_specs=[SMEM] + [VM] * 7,
        out_specs=(VM,) * 3,
        scratch_shapes=[pltpu.VMEM((4, GD, D), F32)],
        compiler_params=PARAMS,
        cost_estimate=pl.CostEstimate(flops=5 * 10**9, bytes_accessed=6 * 10**6, transcendentals=0),
    )(at, h2, d_up, act, cot, attn, d_branch, w_down)


def add_kernel(a_ref, b_ref, early_ref, out_ref):
    for s in range(4):
        out_ref[s] = (a_ref[s].astype(F32) + b_ref[s].astype(F32)).astype(BF)


def add_blocks(a, b, early):
    return pl.pallas_call(
        add_kernel,
        out_shape=shape(*a.shape),
        in_specs=[VM] * 2 + [ANY],
        out_specs=VM,
        compiler_params=PARAMS,
        cost_estimate=pl.CostEstimate(flops=10**6, bytes_accessed=6 * 10**6, transcendentals=0),
    )(a, b, early)


def mid_kernel(at_ref, *refs):
    slots, (up_ref, down_ref, out_ref, vec_ref, scr) = refs[:4], refs[4:]
    yi, zi, ci = at_ref[0], at_ref[1], at_ref[2]
    for s in range(4):
        for c in range(2):
            scr[s, c] = slots[s][c].astype(F32)
    for c in range(2):
        for j in range(4):
            b = 4 * c + j
            ys, cs = (yi - j + 4) % 4, (ci + c) % 2
            for g in range(4):
                zs = (zi - g + 4) % 4
                up_ref[24 * b : 24 * (b + 1), g * D : (g + 1) * D] = scr[
                    ys, cs, pl.ds(pl.multiple_of(24 * zs, 8), 24)
                ]
            down_ref[96 * b : 96 * (b + 1), :] = scr[ys, cs, 96:192]
            out_ref[24 * b : 24 * (b + 1), :] = scr[ys, cs, 192:216]
            if b == 0:
                vec_ref[...] = scr[ys, cs, 216:224]


def mid_rows(at, slots):
    return pl.pallas_call(
        mid_kernel,
        out_shape=(
            shape(GD, 4 * D, dtype=F32), shape(D, D, dtype=F32), shape(GD, D, dtype=F32),
            shape(8, D, dtype=F32),
        ),
        in_specs=[SMEM] + [VM] * 4,
        out_specs=(VM,) * 4,
        scratch_shapes=[pltpu.VMEM((4, 2, 232, D), F32)],
        compiler_params=PARAMS,
        cost_estimate=pl.CostEstimate(flops=10**6, bytes_accessed=8 * 10**6, transcendentals=0),
    )(at, *slots)


def tail_kernel(at_ref, dkv_ref, dq_ref, h1_ref, n1_ref, w_ref, vec_ref, dh_ref, t_ref):
    yi, zi = at_ref[0], at_ref[1]
    d_qkv = jnp.concatenate([dkv_ref[...], dq_ref[...]], axis=1)
    d_h1 = dot_t(d_qkv[:, : 3 * GD], w_ref[...])
    dh_ref[...] = d_h1.astype(BF)
    sums = jnp.sum(d_qkv.astype(F32), axis=0, keepdims=True)
    at_own = lambda v: jnp.concatenate([jnp.where(yi == k, v, 0.0) for k in range(4)], axis=1)
    vectors = jnp.concatenate(
        [
            jnp.sum(d_h1 * n1_ref[...], axis=0, keepdims=True),
            jnp.sum(d_h1, axis=0, keepdims=True),
            at_own(sums[:, 2 * GD : 3 * GD]),
            at_own(sums[:, GD : 2 * GD]),
            vec_ref[4:8, :],
        ],
        axis=0,
    ).astype(BF)
    row = lax.broadcasted_iota(jnp.int32, (8, 128), 0)
    lane = lax.broadcasted_iota(jnp.int32, (8, 128), 1)
    columns = t_dot(vectors, jnp.where(lane == row + 64, 1.0, 0.0).astype(BF))
    grad = t_dot(h1_ref[...], d_qkv)
    for g in range(4):
        rows = slice(g * GD, (g + 1) * GD)
        slot = (g - zi + 4) % 4
        t_ref[slot, :, :512] = grad[rows, :512].astype(BF)
        t_ref[slot, :, 512:] = (grad[rows, 512:] + columns[rows]).astype(BF)


def last_gradients(at, d_kv, d_q, h1, n1, w, vec):
    return pl.pallas_call(
        tail_kernel,
        out_shape=(shape(ROWS, D), shape(4, GD, 640)),
        in_specs=[SMEM] + [VM] * 6,
        out_specs=(VM, VM),
        compiler_params=PARAMS,
        cost_estimate=pl.CostEstimate(flops=3 * 10**9, bytes_accessed=6 * 10**6, transcendentals=0),
    )(at, d_kv, d_q, h1, n1, w, vec)


def sum_kernel(at_ref, t_ref, *refs):
    slots, (dh_ref, kept_ref, given_ref, same_ref) = refs[:3], refs[3:]
    same_ref[...] = dh_ref[...]
    for c in range(2):
        rows = slice(96 * c, 96 * (c + 1))
        a, b, d, e = (v.astype(F32) for v in [t_ref[0, rows]] + [r[rows] for r in slots])
        total = ((a + d) + (b + e)).astype(BF)

        @pl.when(at_ref[2] == c)
        def _():
            kept_ref[...] = total

        @pl.when(at_ref[2] != c)
        def _():
            given_ref[...] = total


def sum_slots(at, own, slots, d_h1):
    return pl.pallas_call(
        sum_kernel,
        out_shape=(shape(96, 640), shape(96, 640), shape(ROWS, D)),
        in_specs=[SMEM] + [VM] * 5,
        out_specs=(VM,) * 3,
        compiler_params=PARAMS,
        cost_estimate=pl.CostEstimate(flops=10**6, bytes_accessed=3 * 10**6, transcendentals=0),
    )(at, own, *slots, d_h1)


def final_kernel(at_ref, *refs):
    slots, (grad_ref, vec_ref, scr) = refs[:4], refs[4:]
    for s in range(4):
        for c in range(2):
            scr[s, c] = slots[s][c]
    yi, ci = at_ref[0], at_ref[2]
    for c in range(2):
        rows = slice(96 * c, 96 * (c + 1))
        total = []
        for g in range(4):
            value = scr[(yi - g + 4) % 4, (ci + c) % 2].astype(F32)
            for i, part in enumerate((1, 2, 0)):
                start = part * D + g * GD
                grad_ref[rows, start : start + GD] = value[:, i * GD : (i + 1) * GD]
            total.append(value[:, 512:])
        vec_ref[rows, :] = (total[0] + total[1]) + (total[2] + total[3])


def final_rows(at, slots):
    return pl.pallas_call(
        final_kernel,
        out_shape=(shape(GD, 3 * D, dtype=F32), shape(GD, 128, dtype=F32)),
        in_specs=[SMEM] + [VM] * 4,
        out_specs=(VM, VM),
        scratch_shapes=[pltpu.VMEM((4, 2, 96, 640), BF)],
        compiler_params=PARAMS,
        cost_estimate=pl.CostEstimate(flops=10**6, bytes_accessed=3 * 10**6, transcendentals=0),
    )(at, *slots)


def gather(value, axes, axis=0):
    return lax.all_gather(value, axes, axis=axis, tiled=True)


def swap(value, axes):
    return lax.all_to_all(value, axes, 0, 0)


def send(value, axis, step):
    n = lax.axis_size(axis)
    return lax.ppermute(value, axis, [(i, (i + step) % n) for i in range(n)])


def spread(value, axis):
    return [value] + [send(value, axis, s) for s in range(1, 4)]


def exchange(slots, axis, step):
    return [slots[0]] + [send(slots[s], axis, s * step) for s in range(1, 4)]


def add_slots(slots):
    a, b, c, d = (v.astype(F32) for v in slots)
    return (a + c) + (b + d)


def group_of(value, index, size, axis=0):
    return lax.dynamic_slice_in_dim(value, (index % 4) * size, size, axis)


def local(
    tokens, qkv_w, out_w, up_w, down_w, norm_gains, biases, value_bias, up_bias, cotangent, block_place
):
    xi = lax.axis_index("x")
    yi = lax.axis_index("y")
    ci = lax.axis_index("core")
    zi = lax.axis_index("fsdp")
    tok_own = tokens[0]
    cot_own = cotangent[0]

    at = jnp.stack([yi, zi, ci]).astype(jnp.int32)
    ws = spread(prepare(at, qkv_w, norm_gains, biases, value_bias[None]), "fsdp")
    toks = spread(tok_own, "y")

    ids = jnp.arange(NBLK, dtype=jnp.int32)
    slot_x, slot_c, slot_y, blk = ids // 16, (ids // 8) % 2, (ids // 2) % 4, ids % 2
    pick = lambda at: jnp.sum(jnp.where(at[:, None] == ids[None, :], block_place[None, :], 0), axis=1)
    at_y = (yi - slot_y + 4) % 4
    key_place = pick(at_y * 16 + ((xi - slot_x + 4) % 4) * 4 + ((ci + slot_c) % 2) * 2 + blk)
    query_place = pick(at_y * 16 + slot_x * 4 + slot_c * 2 + blk)
    own_place = key_place[:8]
    rank = jnp.sum((own_place[None, :] > own_place[:, None]).astype(jnp.int32), axis=1)
    order = jnp.arange(8, dtype=jnp.int32)
    hit = rank[None, :] == order[:, None]
    own = jnp.sum(jnp.where(hit, order[None, :], 0), axis=1)
    place = jnp.sum(jnp.where(hit, own_place[None, :], 0), axis=1)

    w_out = gather(out_w, "fsdp")
    w_out = jnp.concatenate([group_of(w_out, yi + s, GD) for s in range(4)], axis=0)
    w_down = down_w
    cot_all = gather(cot_own, "fsdp")

    kv_own, query, h1, n1y, w_qkv, small, up_groups = first_rows(at, toks, ws, up_w)
    w_up = swap(up_groups, "fsdp").reshape(D, D)
    gain1, gain2 = small[0], small[1]
    out_bias, shift2, down_bias = small[4], small[5], small[6]
    kv_all = [p for v in spread(kv_own, "x") for p in (v, send(v, "core", 1))]
    attn, o_exact, qe, ks, vs = attention_forward(key_place, own, place, query, kv_all, [w_up])
    qe_all = gather(qe, XC)

    attn = attn[:, 64:]
    attn_own = exchange([attn[128 * s : 128 * (s + 1)] for s in range(4)], "y", -1)
    attn_own = jnp.concatenate(attn_own, axis=1)
    x2 = tok_own.astype(F32) + (dot(attn_own, w_out) + out_bias)
    n2, s2 = normalize(x2)
    h2_own = (n2 * gain2 + shift2).astype(BF)

    h2, cot_z, act, d_up, d_h2_part = feed_forward(
        at, spread(h2_own, "fsdp"), cot_all, w_up, w_down, up_bias[None]
    )
    back = lambda v: add_slots(exchange([v[128 * s : 128 * (s + 1)] for s in range(4)], "fsdp", -1))
    d_h2 = back(d_h2_part)
    cot32 = cot_own.astype(F32)
    d_x2 = cot32 + norm_back(d_h2 * gain2, n2, s2)
    d_branch = d_x2.astype(BF)
    d_attn = dot_t(d_branch, w_out).astype(BF)
    d_attn_own = exchange([d_attn[:, GD * s : GD * (s + 1)] for s in range(4)], "y", 1)
    d_attn_own = jnp.concatenate(d_attn_own, axis=0)
    de = delta_rows(d_attn_own, o_exact, qe_all)
    de_all = [p for v in spread(de, "x") for p in (v, send(v, "core", 1))]
    d_q = attention_dq(own, place, qe, de, ks, vs)
    d_kv = attention_dkv(query_place, key_place, own, place, kv_own, qe_all, de_all)

    keep, give, down = weight_blocks(at, h2, d_up, act, cot_z, attn_own, d_branch, w_down)
    layer_out = (x2 + back(down) + down_bias).astype(BF)
    mid = add_blocks(keep, send(give, "core", 1), de)
    mid = add_slots(exchange([mid[s] for s in range(4)], "y", 1)).astype(BF)
    mid = add_slots(spread(mid, "x")).astype(BF)
    parts = exchange([group_of(mid[:192], zi + s, 48) for s in range(4)], "fsdp", 1)
    mid_out = add_slots([v[24:] for v in parts]).astype(BF)
    mid = jnp.concatenate([v[:24] for v in parts] + [mid[192:288], mid_out, mid[288:]], axis=0)
    mid = [jnp.stack([v, send(v, "core", 1)]) for v in spread(mid, "y")]
    grad_up, grad_down, grad_out, vec = mid_rows(at, mid)
    grad_up_bias = vec[0]
    grad_down_bias = lax.dynamic_slice(vec[1], (zi * GD,), (GD,))

    vec = jnp.stack([jnp.sum(d_h2 * n2, axis=0), jnp.sum(d_branch.astype(F32), axis=0), jnp.sum(d_h2, axis=0)])
    vec = jnp.pad(vec, ((4, 1), (0, 0)))
    d_h1_send, tail = last_gradients(at, d_kv, d_q, h1, n1y, w_qkv, vec)
    received = [send(tail[s], "fsdp", s) for s in range(1, 4)]
    kept, given, d_h1_send = sum_slots(at, tail, received, d_h1_send)
    d_h1 = add_slots(exchange([d_h1_send[128 * s : 128 * (s + 1)] for s in range(4)], "y", -1))
    n1, s1 = normalize(tok_own.astype(F32))
    input_grad = (d_x2 + norm_back(d_h1 * gain1, n1, s1)).astype(BF)

    tail = (kept.astype(F32) + send(given, "core", 1).astype(F32)).astype(BF)
    tail = add_slots(spread(tail, "x")).astype(BF)
    tail = [jnp.stack([v, send(v, "core", 1)]) for v in spread(tail, "y")]
    grad_qkv, vectors = final_rows(at, tail)
    vectors = vectors[:, 64:71].T
    grad_gains = jnp.stack([vectors[0], vectors[4]])
    grad_biases = jnp.stack([vectors[1], vectors[2], vectors[5], vectors[6], grad_down_bias])
    grad_value_bias = vectors[3]
    return (
        layer_out[None], input_grad[None], grad_qkv, grad_out, grad_up, grad_down,
        grad_gains, grad_biases, grad_value_bias, grad_up_bias,
    )


def solution(mesh):
    grid = Mesh(mesh.devices.reshape(4, 4, 2, 4), ("y", "x", "core", "fsdp"))
    rows = P("fsdp", CTX, None)
    in_specs = (
        rows, P("fsdp", None), P("fsdp", None), P("fsdp", None), P("fsdp", None),
        P(None, "fsdp"), P(None, "fsdp"), P("fsdp"), P("fsdp"), rows, P(),
    )
    out_specs = (
        rows, rows, P("fsdp", None), P("fsdp", None), P("fsdp", None), P("fsdp", None),
        P(None, "fsdp"), P(None, "fsdp"), P("fsdp"), P("fsdp"),
    )
    return jax.shard_map(local, mesh=grid, in_specs=in_specs, out_specs=out_specs, check_vma=False)
```

```python
import functools

import jax
import jax.numpy as jnp
from jax import lax
from jax.experimental import pallas as pl
from jax.experimental.pallas import tpu as pltpu
from jax.sharding import Mesh
from jax.sharding import PartitionSpec as P

EPS = 1e-05
D = 768
GD = 192
NH = 3
HD = 64
ROWS = 512
LEN = 4096
BLK = 64
NBLK = 64
EXT = 256
TILE = 512
CHUNK = 128
BF = jnp.bfloat16
F32 = jnp.float32
XC = ("x", "core")
CTX = ("y", "x", "core")


def dot(a, b):
    return lax.dot_general(a, b, (((1,), (0,)), ((), ())), preferred_element_type=F32)


def dot_t(a, b):
    return lax.dot_general(a, b, (((1,), (1,)), ((), ())), preferred_element_type=F32)


def t_dot(a, b):
    return lax.dot_general(a, b, (((0,), (0,)), ((), ())), preferred_element_type=F32)


def normalize(value):
    center = value - jnp.mean(value, axis=-1, keepdims=True)
    factor = lax.rsqrt(jnp.mean(center * center, axis=-1, keepdims=True) + EPS)
    return (center * factor, factor)


def norm_back(scaled, normed, factor):
    return factor * (
        scaled
        - jnp.mean(scaled, axis=-1, keepdims=True)
        - normed * jnp.mean(scaled * normed, axis=-1, keepdims=True)
    )


def lanes(rows):
    return lax.broadcasted_iota(jnp.int32, (rows, EXT), 1)


def head_mask(rows, h, high):
    lane = lanes(rows)
    if high:
        feat = (lane >= 64 + HD * h) & (lane < 64 + HD * (h + 1))
        ext = (lane >= 3 * h) & (lane < 3 * h + 3)
    else:
        feat = (lane >= HD * h) & (lane < HD * (h + 1))
        ext = (lane >= GD + 3 * h) & (lane < GD + 3 * h + 3)
    return feat | ext


def feature_mask(rows, h, high):
    lane = lanes(rows) - (64 if high else 0)
    return (lane >= HD * h) & (lane < HD * (h + 1))


def stack_heads(value, high):
    rows = value.shape[0]
    zero = jnp.zeros_like(value)
    return jnp.concatenate(
        [jnp.where(head_mask(rows, h, high), value, zero) for h in range(NH)], axis=0
    )


def merge_heads(stacked, high):
    rows = stacked.shape[0] // NH
    out = jnp.zeros((rows, EXT), F32)
    for h in range(NH):
        out = out + jnp.where(feature_mask(rows, h, high), stacked[h * rows : (h + 1) * rows], 0.0)
    return out


def pieces(value):
    first = value.astype(BF).astype(F32)
    second = (value - first).astype(BF).astype(F32)
    third = (value - first - second).astype(BF).astype(F32)
    return (first, second, third)


def add_extras(base, columns, high):
    rows = base.shape[0]
    lane = lanes(rows)
    start = 0 if high else GD
    for h in range(NH):
        for i, piece in enumerate(pieces(columns[h])):
            base = jnp.where(lane == start + 3 * h + i, piece, base)
    return base


def key_form(kv):
    lane = lanes(kv.shape[0])
    one = jnp.ones((kv.shape[0], EXT), BF)
    zero = jnp.zeros((kv.shape[0], EXT), BF)
    low = jnp.where(lane < GD, kv[:, :EXT], jnp.where(lane < GD + 9, one, zero))
    high = jnp.where(lane >= 64, kv[:, 128:384], jnp.where(lane < 9, one, zero))
    return (low, high)


def block_rows(index):
    return pl.ds(pl.multiple_of(index * BLK, BLK), BLK)


def stacked_pos(place_a, place_b):
    row = lax.broadcasted_iota(jnp.int32, (NH * CHUNK, 1), 0)
    place = jnp.where(row % CHUNK < BLK, place_a, place_b)
    return place * BLK + row % BLK


def col_pos(tile):
    return tile * TILE + lax.broadcasted_iota(jnp.int32, (NH * CHUNK, TILE), 1)


def fold(value, op):
    out = value[:, :128]
    for i in range(1, value.shape[1] // 128):
        out = op(out, value[:, i * 128 : (i + 1) * 128])
    return out


def tile_rows(t):
    return pl.ds(pl.multiple_of(t * TILE, TILE), TILE)


def fwd_kernel(
    kplace_ref, own_ref, place_ref, q_ref, *refs
):
    kv_refs = refs[:8]
    attn_ref, o_ref, qe_ref, ks_ref, vs_ref, s_scr, m_scr, l_scr, acc_scr, land, sems = refs[9:]
    copies = [pltpu.make_async_copy(kv_refs[k], land.at[k], sems.at[k]) for k in range(8)]
    for copy in copies:
        copy.start()
    for k in range(8):
        copies[k].wait()
        for b in range(8):
            low, high = key_form(land[k, b * BLK : (b + 1) * BLK, :])
            dst = block_rows(kplace_ref[8 * k + b])
            ks_ref[dst, :] = low
            vs_ref[dst, :] = high

    for c in range(ROWS // CHUNK):
        place_a, place_b = place_ref[2 * c], place_ref[2 * c + 1]
        blocks = (own_ref[2 * c], own_ref[2 * c + 1])
        query = jnp.concatenate([q_ref[block_rows(b), :] for b in blocks], axis=0)
        stacked = stack_heads(query, False)
        qpos = stacked_pos(place_a, place_b)
        tiles = place_a // (TILE // BLK) + 1
        m_scr[...] = jnp.full(m_scr.shape, -1e30, F32)

        def score_step(t, _):
            scores = dot_t(stacked, ks_ref[tile_rows(t), :])
            scores = jnp.where(col_pos(t) <= qpos, scores, -1e30)
            s_scr[t] = scores
            m_scr[...] = jnp.maximum(m_scr[...], fold(scores, jnp.maximum))
            return 0

        lax.fori_loop(0, tiles, score_step, 0)
        peak = jnp.max(m_scr[...], axis=1, keepdims=True)
        l_scr[...] = jnp.zeros(l_scr.shape, F32)
        acc_scr[...] = jnp.zeros(acc_scr.shape, F32)

        def value_step(t, _):
            prob = jnp.exp(s_scr[t] - peak)
            l_scr[...] = l_scr[...] + fold(prob, jnp.add)
            acc_scr[...] = acc_scr[...] + dot(prob.astype(BF), vs_ref[tile_rows(t), :])
            return 0

        lax.fori_loop(0, tiles, value_step, 0)
        total = jnp.sum(l_scr[...], axis=1, keepdims=True)
        log_total = peak + jnp.log(total)
        out = merge_heads(acc_scr[...] / total, True)
        ext = add_extras(
            query.astype(F32),
            [-log_total[h * CHUNK : (h + 1) * CHUNK] for h in range(NH)],
            False,
        ).astype(BF)
        for i, b in enumerate(blocks):
            rows = slice(i * BLK, (i + 1) * BLK)
            o_ref[block_rows(b), :] = out[rows]
            attn_ref[block_rows(b), :] = out[rows].astype(BF)
            qe_ref[block_rows(b), :] = ext[rows]


def dq_kernel(chunks, own_ref, place_ref, qe_ref, de_ref, ks_ref, vs_ref, *refs):
    *before, dq_ref, acc_scr = refs
    if before:
        dq_ref[...] = before[0][...]
    for c in chunks:
        place_a, place_b = place_ref[2 * c], place_ref[2 * c + 1]
        blocks = (own_ref[2 * c], own_ref[2 * c + 1])
        query = stack_heads(jnp.concatenate([qe_ref[block_rows(b), :] for b in blocks], axis=0), False)
        d_out = stack_heads(jnp.concatenate([de_ref[block_rows(b), :] for b in blocks], axis=0), True)
        qpos = stacked_pos(place_a, place_b)
        tiles = place_a // (TILE // BLK) + 1
        acc_scr[...] = jnp.zeros(acc_scr.shape, F32)

        def step(t, _):
            keys = ks_ref[tile_rows(t), :]
            prob = jnp.where(col_pos(t) <= qpos, jnp.exp(dot_t(query, keys)), 0.0)
            d_raw = (prob * dot_t(d_out, vs_ref[tile_rows(t), :])).astype(BF)
            acc_scr[...] = acc_scr[...] + dot(d_raw, keys)
            return 0

        lax.fori_loop(0, tiles, step, 0)
        out = (merge_heads(acc_scr[...], False) * 0.125).astype(BF)
        for i, b in enumerate(blocks):
            dq_ref[block_rows(b), :] = out[i * BLK : (i + 1) * BLK]


def dkv_kernel(qplace_ref, kplace_ref, own_ref, place_ref, kv_ref, qe_ref, *refs):
    de_refs, (dkv_ref, qs_scr, ds_scr, dk_scr, dv_scr, q_land, d_land, sems) = refs[:8], refs[8:]
    q_copy = pltpu.make_async_copy(qe_ref, q_land, sems.at[8])
    q_copy.start()
    copies = [pltpu.make_async_copy(de_refs[k], d_land.at[k], sems.at[k]) for k in range(8)]
    for copy in copies:
        copy.start()
    q_copy.wait()
    for b in range(NBLK):
        qs_scr[block_rows(qplace_ref[b]), :] = q_land[b * BLK : (b + 1) * BLK, :]
    for k in range(8):
        copies[k].wait()
        for b in range(8):
            ds_scr[block_rows(kplace_ref[8 * k + b]), :] = d_land[k, b * BLK : (b + 1) * BLK, :]

    for c in range(ROWS // CHUNK):
        place_a, place_b = place_ref[2 * c], place_ref[2 * c + 1]
        blocks = (own_ref[2 * c], own_ref[2 * c + 1])
        low, high = key_form(jnp.concatenate([kv_ref[block_rows(b), :] for b in blocks], axis=0))
        keys = stack_heads(low, False)
        values = stack_heads(high, True)
        kpos = stacked_pos(place_a, place_b)
        dk_scr[...] = jnp.zeros(dk_scr.shape, F32)
        dv_scr[...] = jnp.zeros(dv_scr.shape, F32)

        def step(t, _):
            query = qs_scr[tile_rows(t), :]
            d_out = ds_scr[tile_rows(t), :]
            prob = jnp.where(col_pos(t) >= kpos, jnp.exp(dot_t(keys, query)), 0.0)
            d_raw = (prob * dot_t(values, d_out)).astype(BF)
            dv_scr[...] = dv_scr[...] + dot(prob.astype(BF), d_out)
            dk_scr[...] = dk_scr[...] + dot(d_raw, query)
            return 0

        lax.fori_loop(place_b // (TILE // BLK), LEN // TILE, step, 0)
        d_keys = merge_heads(dk_scr[...], False)
        d_values = merge_heads(dv_scr[...], True)
        out = jnp.concatenate(
            [d_keys[:, :128], d_keys[:, 128:] + d_values[:, :128], d_values[:, 128:]], axis=1
        ).astype(BF)
        for i, b in enumerate(blocks):
            dkv_ref[block_rows(b), :] = out[i * BLK : (i + 1) * BLK]


def delta_kernel(d_ref, o_ref, early_ref, de_ref):
    d_out = jnp.concatenate([jnp.zeros((ROWS, 64), F32), d_ref[...].astype(F32)], axis=1)
    product = d_out * o_ref[...]
    sums = [
        -jnp.sum(jnp.where(feature_mask(ROWS, h, True), product, 0.0), axis=1, keepdims=True)
        for h in range(NH)
    ]
    de_ref[...] = add_extras(d_out, sums, True).astype(BF)


SMEM = pl.BlockSpec(memory_space=pltpu.SMEM)
VM = pl.BlockSpec(memory_space=pltpu.VMEM)
ANY = pl.BlockSpec(memory_space=pl.ANY)


def limit(mib):
    return pltpu.CompilerParams(vmem_limit_bytes=mib * 1024 * 1024)


def shape(*dims, dtype=BF):
    return jax.ShapeDtypeStruct(dims, dtype)


def attention_forward(kplace, own, place, query, kv, early):
    return pl.pallas_call(
        fwd_kernel,
        out_shape=(
            shape(ROWS, EXT), shape(ROWS, EXT, dtype=F32), shape(ROWS, EXT),
            shape(LEN, EXT), shape(LEN, EXT),
        ),
        in_specs=[SMEM] * 3 + [VM] + [ANY] * 9,
        out_specs=(VM,) * 5,
        scratch_shapes=[
            pltpu.VMEM((LEN // TILE, NH * CHUNK, TILE), F32),
            pltpu.VMEM((NH * CHUNK, 128), F32),
            pltpu.VMEM((NH * CHUNK, 128), F32),
            pltpu.VMEM((NH * CHUNK, EXT), F32),
            pltpu.VMEM((8, ROWS, 2 * GD), BF),
            pltpu.SemaphoreType.DMA((8,)),
        ],
        compiler_params=limit(34),
        cost_estimate=pl.CostEstimate(flops=16 * 10**9, bytes_accessed=10**7, transcendentals=4 * 10**6),
    )(kplace, own, place, query, *kv, *early)


def attention_dq(chunks, own, place, qe, de, ks, vs, *before):
    return pl.pallas_call(
        functools.partial(dq_kernel, chunks),
        out_shape=shape(ROWS, EXT),
        in_specs=[SMEM] * 2 + [VM] * (4 + len(before)),
        out_specs=VM,
        scratch_shapes=[pltpu.VMEM((NH * CHUNK, EXT), F32)],
        compiler_params=limit(20),
        cost_estimate=pl.CostEstimate(flops=8 * 10**9, bytes_accessed=5 * 10**6, transcendentals=2 * 10**6),
    )(own, place, qe, de, ks, vs, *before)


def attention_dkv(qplace, kplace, own, place, kv, qe, de):
    return pl.pallas_call(
        dkv_kernel,
        out_shape=shape(ROWS, 2 * GD),
        in_specs=[SMEM] * 4 + [VM] + [ANY] * 9,
        out_specs=VM,
        scratch_shapes=[
            pltpu.VMEM((LEN, EXT), BF),
            pltpu.VMEM((LEN, EXT), BF),
            pltpu.VMEM((NH * CHUNK, EXT), F32),
            pltpu.VMEM((NH * CHUNK, EXT), F32),
            pltpu.VMEM((LEN, EXT), BF),
            pltpu.VMEM((8, ROWS, EXT), BF),
            pltpu.SemaphoreType.DMA((9,)),
        ],
        compiler_params=limit(28),
        cost_estimate=pl.CostEstimate(flops=15 * 10**9, bytes_accessed=10**7, transcendentals=4 * 10**6),
    )(qplace, kplace, own, place, kv, qe, *de)


def delta_rows(d_attn, o, early):
    return pl.pallas_call(
        delta_kernel,
        out_shape=shape(ROWS, EXT),
        in_specs=[VM] * 2 + [ANY],
        out_specs=VM,
        compiler_params=limit(8),
        cost_estimate=pl.CostEstimate(flops=10**6, bytes_accessed=10**6, transcendentals=0),
    )(d_attn, o, early)


def prep_kernel(at_ref, w_ref, gain_ref, bias_ref, vb_ref, cols_ref):
    for k in range(4):

        @pl.when(at_ref[0] == k)
        def _():
            for i, part in enumerate((1, 2, 0)):
                start = part * D + k * GD
                cols_ref[:GD, i * GD : (i + 1) * GD] = w_ref[:, start : start + GD]

    small = jnp.concatenate(
        [gain_ref[...].astype(F32), bias_ref[...].astype(F32), vb_ref[...].astype(F32), jnp.zeros((8, GD), F32)],
        axis=0,
    )
    cols_ref[GD:, :] = jnp.concatenate([small, jnp.zeros((16, 2 * GD), F32)], axis=1).astype(BF)


def prepare(at, w, gains, biases, vb):
    return pl.pallas_call(
        prep_kernel,
        out_shape=shape(GD + 16, 3 * GD),
        in_specs=[SMEM] + [VM] * 4,
        out_specs=VM,
        compiler_params=limit(8),
        cost_estimate=pl.CostEstimate(flops=1000, bytes_accessed=10**6, transcendentals=0),
    )(at, w, gains, biases, vb)


def qkv_kernel(at_ref, *refs):
    toks, ws = refs[:4], refs[4:8]
    kv_ref, q_ref, h1_ref, n1_ref, w_ref, small_ref, w_scr = refs[8:]
    yi, zi = at_ref[0], at_ref[1]
    for s in range(4):
        w_scr[s] = ws[s][...]
    for g in range(4):
        slot = (zi - g + 4) % 4
        w_ref[g * GD : (g + 1) * GD, :] = w_scr[slot, :GD]
        small_ref[:, g * GD : (g + 1) * GD] = w_scr[slot, GD:, :256].astype(F32)[:8, :GD]
    gain, shift = small_ref[0:1, :], small_ref[2:3, :]
    for s in range(4):
        rows = slice(128 * s, 128 * (s + 1))
        normed, _ = normalize(toks[s][...].astype(F32))
        n1_ref[rows, :] = normed
        h1_ref[rows, :] = (normed * gain + shift).astype(BF)
    own = w_scr[(zi - yi + 4) % 4, GD:, :256].astype(F32)[:8, :GD]
    qkv = dot(h1_ref[...], w_ref[...])
    kv_ref[:, :GD] = qkv[:, :GD].astype(BF)
    kv_ref[:, GD:] = (qkv[:, GD : 2 * GD] + own[7:8]).astype(BF)
    query = (qkv[:, 2 * GD :] + own[3:4]).astype(BF).astype(F32) * 0.125
    q_ref[...] = jnp.concatenate([query, jnp.zeros((ROWS, EXT - GD), F32)], axis=1).astype(BF)


def regroup_kernel(up_ref, early_ref, out_ref):
    for g in range(4):
        out_ref[g] = up_ref[:, g * D : (g + 1) * D]


def regroup(up_w, early):
    return pl.pallas_call(
        regroup_kernel,
        out_shape=shape(4, GD, D),
        in_specs=[VM, ANY],
        out_specs=VM,
        compiler_params=limit(8),
        cost_estimate=pl.CostEstimate(flops=1000, bytes_accessed=2 * 10**6, transcendentals=0),
    )(up_w, early)


def first_rows(at, toks, ws):
    return pl.pallas_call(
        qkv_kernel,
        out_shape=(
            shape(ROWS, 2 * GD), shape(ROWS, EXT), shape(ROWS, D), shape(ROWS, D, dtype=F32),
            shape(D, 3 * GD), shape(8, D, dtype=F32),
        ),
        in_specs=[SMEM] + [VM] * 8,
        out_specs=(VM,) * 6,
        scratch_shapes=[pltpu.VMEM((4, GD + 16, 3 * GD), BF)],
        compiler_params=limit(20),
        cost_estimate=pl.CostEstimate(flops=5 * 10**8, bytes_accessed=6 * 10**6, transcendentals=0),
    )(at, *toks, *ws)


def mlp_kernel(at_ref, *refs):
    h2s = refs[:4]
    cots_ref, up_ref, down_ref, ub_ref, h2_ref, cot_ref, act_ref, dup_ref, dh_ref = refs[4:]
    for s in range(4):
        rows = slice(128 * s, 128 * (s + 1))
        h2 = h2s[s][...]
        cot = cots_ref[pl.ds(pl.multiple_of((at_ref[1] - s + 4) % 4 * 128, 128), 128), :]
        h2_ref[rows, :] = h2
        cot_ref[rows, :] = cot
        up = dot(h2, up_ref[...]) + ub_ref[...].astype(F32)
        d_act = dot_t(cot, down_ref[...])
        square = up * up
        th = jnp.tanh(0.7978845608028654 * (up + 0.044715 * (square * up)))
        half = 0.5 * (1.0 + th)
        slope = half + 0.5 * up * (1.0 - th * th) * (
            0.7978845608028654 * (1.0 + 3 * 0.044715 * square)
        )
        act_ref[rows, :] = (up * half).astype(BF)
        d_up = (slope * d_act).astype(BF)
        dup_ref[rows, :] = d_up
        dh_ref[rows, :] = dot_t(d_up, up_ref[...]).astype(BF)


def feed_forward(at, h2s, cots, w_up, w_down, ub):
    return pl.pallas_call(
        mlp_kernel,
        out_shape=(shape(ROWS, D),) * 5,
        in_specs=[SMEM] + [VM] * 8,
        out_specs=(VM,) * 5,
        compiler_params=limit(20),
        cost_estimate=pl.CostEstimate(flops=4 * 10**9, bytes_accessed=6 * 10**6, transcendentals=4 * 10**5),
    )(at, *h2s, cots, w_up, w_down, ub)


def wgrad_kernel(
    at_ref, h2_ref, dup_ref, act_ref, cot_ref, attn_ref, branch_ref, wd_ref, early_ref,
    keep_ref, give_ref, down_ref, out_scr,
):
    yi, ci = at_ref[0], at_ref[2]
    down_ref[...] = dot(act_ref[...], wd_ref[...]).astype(BF)
    g_up = t_dot(h2_ref[...], dup_ref[...])
    g_down = t_dot(act_ref[...], cot_ref[...])
    g_out = t_dot(attn_ref[...], branch_ref[...])
    for s in range(4):
        out_scr[s] = g_out[GD * s : GD * (s + 1)]
    vec = jnp.concatenate(
        [
            jnp.sum(dup_ref[...].astype(F32), axis=0, keepdims=True),
            jnp.sum(cot_ref[...].astype(F32), axis=0, keepdims=True),
            jnp.zeros((14, D), F32),
        ],
        axis=0,
    )
    for c in range(2):
        for j in range(4):
            b = 4 * c + j
            parts = []
            for z in range(4):
                parts.append(g_up[GD * z + 24 * b : GD * z + 24 * (b + 1)])
                parts.append(out_scr[(z - yi + 4) % 4, 24 * b : 24 * (b + 1)])
            parts += [g_down[96 * b : 96 * (b + 1)], vec]
            block = jnp.concatenate(parts, axis=0).astype(BF)

            @pl.when(ci == c)
            def _():
                keep_ref[j] = block

            @pl.when(ci != c)
            def _():
                give_ref[j] = block


def weight_blocks(at, h2, d_up, act, cot, attn, d_branch, w_down, early):
    return pl.pallas_call(
        wgrad_kernel,
        out_shape=(shape(4, 304, D), shape(4, 304, D), shape(ROWS, D)),
        in_specs=[SMEM] + [VM] * 7 + [ANY],
        out_specs=(VM,) * 3,
        scratch_shapes=[pltpu.VMEM((4, GD, D), F32)],
        compiler_params=limit(30),
        cost_estimate=pl.CostEstimate(flops=5 * 10**9, bytes_accessed=6 * 10**6, transcendentals=0),
    )(at, h2, d_up, act, cot, attn, d_branch, w_down, early)


def add_kernel(a_ref, b_ref, out_ref):
    for s in range(4):
        out_ref[s] = (a_ref[s].astype(F32) + b_ref[s].astype(F32)).astype(BF)


def add_blocks(a, b):
    return pl.pallas_call(
        add_kernel,
        out_shape=shape(*a.shape),
        in_specs=[VM] * 2,
        out_specs=VM,
        compiler_params=limit(16),
        cost_estimate=pl.CostEstimate(flops=10**6, bytes_accessed=6 * 10**6, transcendentals=0),
    )(a, b)


def mid_kernel(blocks_ref, up_ref, down_ref, out_ref, vec_ref):
    for c in range(2):
        for j in range(4):
            b = 4 * c + j
            block = blocks_ref[2 * j + c].astype(F32)
            for g in range(4):
                up_ref[24 * b : 24 * (b + 1), g * D : (g + 1) * D] = block[24 * g : 24 * (g + 1)]
            down_ref[96 * b : 96 * (b + 1), :] = block[96:192]
            out_ref[24 * b : 24 * (b + 1), :] = block[192:216]
            if b == 0:
                vec_ref[...] = block[216:224]


def mid_rows(blocks):
    return pl.pallas_call(
        mid_kernel,
        out_shape=(
            shape(GD, 4 * D, dtype=F32), shape(D, D, dtype=F32), shape(GD, D, dtype=F32),
            shape(8, D, dtype=F32),
        ),
        in_specs=[VM],
        out_specs=(VM,) * 4,
        compiler_params=limit(20),
        cost_estimate=pl.CostEstimate(flops=10**6, bytes_accessed=8 * 10**6, transcendentals=0),
    )(blocks)


def tail_kernel(at_ref, dkv_ref, dq_ref, h1_ref, n1_ref, w_ref, vec_ref, dh_ref, t_ref):
    yi, zi = at_ref[0], at_ref[1]
    d_qkv = jnp.concatenate([dkv_ref[...], dq_ref[...]], axis=1)
    d_h1 = dot_t(d_qkv[:, : 3 * GD], w_ref[...])
    dh_ref[...] = d_h1.astype(BF)
    sums = jnp.sum(d_qkv.astype(F32), axis=0, keepdims=True)
    at_own = lambda v: jnp.concatenate([jnp.where(yi == k, v, 0.0) for k in range(4)], axis=1)
    vectors = jnp.concatenate(
        [
            jnp.sum(d_h1 * n1_ref[...], axis=0, keepdims=True),
            jnp.sum(d_h1, axis=0, keepdims=True),
            at_own(sums[:, 2 * GD : 3 * GD]),
            at_own(sums[:, GD : 2 * GD]),
            vec_ref[4:8, :],
        ],
        axis=0,
    ).astype(BF)
    row = lax.broadcasted_iota(jnp.int32, (8, 128), 0)
    lane = lax.broadcasted_iota(jnp.int32, (8, 128), 1)
    columns = t_dot(vectors, jnp.where(lane == row + 64, 1.0, 0.0).astype(BF))
    grad = t_dot(h1_ref[...], d_qkv)
    for g in range(4):
        rows = slice(g * GD, (g + 1) * GD)
        slot = (g - zi + 4) % 4
        t_ref[slot, :, :512] = grad[rows, :512].astype(BF)
        t_ref[slot, :, 512:] = (grad[rows, 512:] + columns[rows]).astype(BF)


def last_gradients(at, d_kv, d_q, h1, n1, w, vec):
    return pl.pallas_call(
        tail_kernel,
        out_shape=(shape(ROWS, D), shape(4, GD, 640)),
        in_specs=[SMEM] + [VM] * 6,
        out_specs=(VM, VM),
        compiler_params=limit(20),
        cost_estimate=pl.CostEstimate(flops=3 * 10**9, bytes_accessed=6 * 10**6, transcendentals=0),
    )(at, d_kv, d_q, h1, n1, w, vec)


def sum_kernel(at_ref, t_ref, *refs):
    slots, (dh_ref, kept_ref, given_ref, same_ref) = refs[:3], refs[3:]
    same_ref[...] = dh_ref[...]
    for c in range(2):
        rows = slice(96 * c, 96 * (c + 1))
        a, b, d, e = (v.astype(F32) for v in [t_ref[0, rows]] + [r[rows] for r in slots])
        total = ((a + d) + (b + e)).astype(BF)

        @pl.when(at_ref[2] == c)
        def _():
            kept_ref[...] = total

        @pl.when(at_ref[2] != c)
        def _():
            given_ref[...] = total


def sum_slots(at, own, slots, d_h1):
    return pl.pallas_call(
        sum_kernel,
        out_shape=(shape(96, 640), shape(96, 640), shape(ROWS, D)),
        in_specs=[SMEM] + [VM] * 5,
        out_specs=(VM,) * 3,
        compiler_params=limit(12),
        cost_estimate=pl.CostEstimate(flops=10**6, bytes_accessed=3 * 10**6, transcendentals=0),
    )(at, own, *slots, d_h1)


def final_kernel(at_ref, *refs):
    slots, (grad_ref, vec_ref, scr) = refs[:4], refs[4:]
    for s in range(4):
        for c in range(2):
            scr[s, c] = slots[s][c]
    yi, ci = at_ref[0], at_ref[2]
    for c in range(2):
        rows = slice(96 * c, 96 * (c + 1))
        total = []
        for g in range(4):
            value = scr[(yi - g + 4) % 4, (ci + c) % 2].astype(F32)
            for i, part in enumerate((1, 2, 0)):
                start = part * D + g * GD
                grad_ref[rows, start : start + GD] = value[:, i * GD : (i + 1) * GD]
            total.append(value[:, 512:])
        vec_ref[rows, :] = (total[0] + total[1]) + (total[2] + total[3])


def final_rows(at, slots):
    return pl.pallas_call(
        final_kernel,
        out_shape=(shape(GD, 3 * D, dtype=F32), shape(GD, 128, dtype=F32)),
        in_specs=[SMEM] + [VM] * 4,
        out_specs=(VM, VM),
        scratch_shapes=[pltpu.VMEM((4, 2, 96, 640), BF)],
        compiler_params=limit(12),
        cost_estimate=pl.CostEstimate(flops=10**6, bytes_accessed=3 * 10**6, transcendentals=0),
    )(at, *slots)


def gather(value, axes, axis=0):
    return lax.all_gather(value, axes, axis=axis, tiled=True)


def swap(value, axes):
    return lax.all_to_all(value, axes, 0, 0)


def send(value, axis, step):
    n = lax.axis_size(axis)
    return lax.ppermute(value, axis, [(i, (i + step) % n) for i in range(n)])


def spread(value, axis):
    return [value] + [send(value, axis, s) for s in range(1, 4)]


def exchange(slots, axis, step):
    return [slots[0]] + [send(slots[s], axis, s * step) for s in range(1, 4)]


def add_slots(slots):
    a, b, c, d = (v.astype(F32) for v in slots)
    return (a + c) + (b + d)


def group_of(value, index, size, axis=0):
    return lax.dynamic_slice_in_dim(value, (index % 4) * size, size, axis)


def local(
    tokens, qkv_w, out_w, up_w, down_w, norm_gains, biases, value_bias, up_bias, cotangent, block_place
):
    xi = lax.axis_index("x")
    yi = lax.axis_index("y")
    ci = lax.axis_index("core")
    zi = lax.axis_index("fsdp")
    tok_own = tokens[0]
    cot_own = cotangent[0]

    at = jnp.stack([yi, zi, ci]).astype(jnp.int32)
    ws = spread(prepare(at, qkv_w, norm_gains, biases, value_bias[None]), "fsdp")
    toks = spread(tok_own, "y")

    ids = jnp.arange(NBLK, dtype=jnp.int32)
    slot_x, slot_c, slot_y, blk = ids // 16, (ids // 8) % 2, (ids // 2) % 4, ids % 2
    pick = lambda at: jnp.sum(jnp.where(at[:, None] == ids[None, :], block_place[None, :], 0), axis=1)
    at_y = (yi - slot_y + 4) % 4
    key_place = pick(at_y * 16 + ((xi - slot_x + 4) % 4) * 4 + ((ci + slot_c) % 2) * 2 + blk)
    query_place = pick(at_y * 16 + slot_x * 4 + slot_c * 2 + blk)
    own_place = key_place[:8]
    rank = jnp.sum((own_place[None, :] > own_place[:, None]).astype(jnp.int32), axis=1)
    order = jnp.arange(8, dtype=jnp.int32)
    hit = rank[None, :] == order[:, None]
    own = jnp.sum(jnp.where(hit, order[None, :], 0), axis=1)
    place = jnp.sum(jnp.where(hit, own_place[None, :], 0), axis=1)

    w_out = gather(out_w, "fsdp")
    w_out = jnp.concatenate([group_of(w_out, yi + s, GD) for s in range(4)], axis=0)
    w_down = down_w
    cot_all = gather(cot_own, "fsdp")

    kv_own, query, h1, n1y, w_qkv, small = first_rows(at, toks, ws)
    gain1, gain2 = small[0], small[1]
    out_bias, shift2, down_bias = small[4], small[5], small[6]
    with jax.named_scope("kv"):
        kv_all = [p for v in spread(kv_own, "x") for p in (v, send(v, "core", 1))]
    with jax.named_scope("w_up"):
        w_up = swap(regroup(up_w, kv_all[2]), "fsdp").reshape(D, D)
    attn, o_exact, qe, ks, vs = attention_forward(key_place, own, place, query, kv_all, [cot_all])
    qe_all = gather(qe, XC)

    attn = attn[:, 64:]
    with jax.named_scope("attn_y"):
        attn_own = exchange([attn[128 * s : 128 * (s + 1)] for s in range(4)], "y", -1)
    attn_own = jnp.concatenate(attn_own, axis=1)
    x2 = tok_own.astype(F32) + (dot(attn_own, w_out) + out_bias)
    n2, s2 = normalize(x2)
    h2_own = (n2 * gain2 + shift2).astype(BF)

    with jax.named_scope("h2_z"):
        h2s = spread(h2_own, "fsdp")
    h2, cot_z, act, d_up, d_h2_part = feed_forward(
        at, h2s, cot_all, w_up, w_down, up_bias[None]
    )
    back = lambda v: add_slots(exchange([v[128 * s : 128 * (s + 1)] for s in range(4)], "fsdp", -1))
    with jax.named_scope("d_h2_z"):
        d_h2 = back(d_h2_part)
    cot32 = cot_own.astype(F32)
    d_x2 = cot32 + norm_back(d_h2 * gain2, n2, s2)
    d_branch = d_x2.astype(BF)
    d_attn = dot_t(d_branch, w_out).astype(BF)
    with jax.named_scope("d_attn_y"):
        d_attn_own = exchange([d_attn[:, GD * s : GD * (s + 1)] for s in range(4)], "y", 1)
    d_attn_own = jnp.concatenate(d_attn_own, axis=0)
    de = delta_rows(d_attn_own, o_exact, qe_all)
    with jax.named_scope("de"):
        de_all = [p for v in spread(de, "x") for p in (v, send(v, "core", 1))]
    d_q = attention_dq((0, 3), own, place, qe, de, ks, vs)
    d_q = attention_dq((1, 2), own, place, qe, de, ks, vs, d_q)
    d_kv = attention_dkv(query_place, key_place, own, place, kv_own, qe_all, de_all)

    keep, give, down = weight_blocks(at, h2, d_up, act, cot_z, attn_own, d_branch, w_down, de)
    with jax.named_scope("down"):
        layer_out = (x2 + back(down) + down_bias).astype(BF)
    with jax.named_scope("mid"):
        mid = add_blocks(keep, send(give, "core", 1))
        mid = jnp.sum(swap(mid, "y").astype(F32), axis=0).astype(BF)
        mid = jnp.sum(lax.all_gather(mid, "x", axis=0).astype(F32), axis=0).astype(BF)
        parts = swap(mid[:192].reshape(4, 48, D), "fsdp")
        mid_out = jnp.sum(parts[:, 24:].astype(F32), axis=0).astype(BF)
        mid = jnp.concatenate(
            [parts[:, :24].reshape(96, D), mid[192:288], mid_out, mid[288:]], axis=0
        )
        mid = lax.all_gather(mid, ("y", "core"), axis=0)
    grad_up, grad_down, grad_out, vec = mid_rows(mid)
    grad_up_bias = vec[0]
    grad_down_bias = lax.dynamic_slice(vec[1], (zi * GD,), (GD,))

    vec = jnp.stack([jnp.sum(d_h2 * n2, axis=0), jnp.sum(d_branch.astype(F32), axis=0), jnp.sum(d_h2, axis=0)])
    vec = jnp.pad(vec, ((4, 1), (0, 0)))
    d_h1_send, tail = last_gradients(at, d_kv, d_q, h1, n1y, w_qkv, vec)
    with jax.named_scope("tail_z"):
        received = [send(tail[s], "fsdp", s) for s in range(1, 4)]
    kept, given, d_h1_send = sum_slots(at, tail, received, d_h1_send)
    with jax.named_scope("d_h1_y"):
        d_h1 = add_slots(exchange([d_h1_send[128 * s : 128 * (s + 1)] for s in range(4)], "y", -1))
    n1, s1 = normalize(tok_own.astype(F32))
    input_grad = (d_x2 + norm_back(d_h1 * gain1, n1, s1)).astype(BF)

    with jax.named_scope("tail_core"):
        tail = (kept.astype(F32) + send(given, "core", 1).astype(F32)).astype(BF)
    with jax.named_scope("tail_x"):
        tail = add_slots(spread(tail, "x")).astype(BF)
    with jax.named_scope("tail_y"):
        tail = [jnp.stack([v, send(v, "core", 1)]) for v in spread(tail, "y")]
    grad_qkv, vectors = final_rows(at, tail)
    vectors = vectors[:, 64:71].T
    grad_gains = jnp.stack([vectors[0], vectors[4]])
    grad_biases = jnp.stack([vectors[1], vectors[2], vectors[5], vectors[6], grad_down_bias])
    grad_value_bias = vectors[3]
    return (
        layer_out[None], input_grad[None], grad_qkv, grad_out, grad_up, grad_down,
        grad_gains, grad_biases, grad_value_bias, grad_up_bias,
    )


def solution(mesh):
    grid = Mesh(mesh.devices.reshape(4, 4, 2, 4), ("y", "x", "core", "fsdp"))
    rows = P("fsdp", CTX, None)
    in_specs = (
        rows, P("fsdp", None), P("fsdp", None), P("fsdp", None), P("fsdp", None),
        P(None, "fsdp"), P(None, "fsdp"), P("fsdp"), P("fsdp"), rows, P(),
    )
    out_specs = (
        rows, rows, P("fsdp", None), P("fsdp", None), P("fsdp", None), P("fsdp", None),
        P(None, "fsdp"), P(None, "fsdp"), P("fsdp"), P("fsdp"),
    )
    return jax.shard_map(local, mesh=grid, in_specs=in_specs, out_specs=out_specs, check_vma=False)
```

```python
import functools

import jax
import jax.numpy as jnp
from jax import lax
from jax.experimental import pallas as pl
from jax.experimental.pallas import tpu as pltpu
from jax.sharding import Mesh
from jax.sharding import PartitionSpec as P

EPS = 1e-05
D = 768
GD = 192
NH = 3
HD = 64
ROWS = 512
LEN = 4096
BLK = 64
NBLK = 64
EXT = 256
TILE = 512
CHUNK = 128
BF = jnp.bfloat16
F32 = jnp.float32
XC = ("x", "core")
CTX = ("y", "x", "core")


def dot(a, b):
    return lax.dot_general(a, b, (((1,), (0,)), ((), ())), preferred_element_type=F32)


def dot_t(a, b):
    return lax.dot_general(a, b, (((1,), (1,)), ((), ())), preferred_element_type=F32)


def t_dot(a, b):
    return lax.dot_general(a, b, (((0,), (0,)), ((), ())), preferred_element_type=F32)


def normalize(value):
    center = value - jnp.mean(value, axis=-1, keepdims=True)
    factor = lax.rsqrt(jnp.mean(center * center, axis=-1, keepdims=True) + EPS)
    return (center * factor, factor)


def norm_back(scaled, normed, factor):
    return factor * (
        scaled
        - jnp.mean(scaled, axis=-1, keepdims=True)
        - normed * jnp.mean(scaled * normed, axis=-1, keepdims=True)
    )


def lanes(rows):
    return lax.broadcasted_iota(jnp.int32, (rows, EXT), 1)


def head_mask(rows, h, high):
    lane = lanes(rows)
    if high:
        feat = (lane >= 64 + HD * h) & (lane < 64 + HD * (h + 1))
        ext = (lane >= 3 * h) & (lane < 3 * h + 3)
    else:
        feat = (lane >= HD * h) & (lane < HD * (h + 1))
        ext = (lane >= GD + 3 * h) & (lane < GD + 3 * h + 3)
    return feat | ext


def feature_mask(rows, h, high):
    lane = lanes(rows) - (64 if high else 0)
    return (lane >= HD * h) & (lane < HD * (h + 1))


def stack_heads(value, high):
    rows = value.shape[0]
    zero = jnp.zeros_like(value)
    return jnp.concatenate(
        [jnp.where(head_mask(rows, h, high), value, zero) for h in range(NH)], axis=0
    )


def merge_heads(stacked, high):
    rows = stacked.shape[0] // NH
    out = jnp.zeros((rows, EXT), F32)
    for h in range(NH):
        out = out + jnp.where(feature_mask(rows, h, high), stacked[h * rows : (h + 1) * rows], 0.0)
    return out


def pieces(value):
    first = value.astype(BF).astype(F32)
    second = (value - first).astype(BF).astype(F32)
    third = (value - first - second).astype(BF).astype(F32)
    return (first, second, third)


def add_extras(base, columns, high):
    rows = base.shape[0]
    lane = lanes(rows)
    start = 0 if high else GD
    for h in range(NH):
        for i, piece in enumerate(pieces(columns[h])):
            base = jnp.where(lane == start + 3 * h + i, piece, base)
    return base


def key_form(kv):
    lane = lanes(kv.shape[0])
    one = jnp.ones((kv.shape[0], EXT), BF)
    zero = jnp.zeros((kv.shape[0], EXT), BF)
    low = jnp.where(lane < GD, kv[:, :EXT], jnp.where(lane < GD + 9, one, zero))
    high = jnp.where(lane >= 64, kv[:, 128:384], jnp.where(lane < 9, one, zero))
    return (low, high)


def block_rows(index):
    return pl.ds(pl.multiple_of(index * BLK, BLK), BLK)


def stacked_pos(place_a, place_b):
    row = lax.broadcasted_iota(jnp.int32, (NH * CHUNK, 1), 0)
    place = jnp.where(row % CHUNK < BLK, place_a, place_b)
    return place * BLK + row % BLK


def col_pos(tile):
    return tile * TILE + lax.broadcasted_iota(jnp.int32, (NH * CHUNK, TILE), 1)


def fold(value, op):
    out = value[:, :128]
    for i in range(1, value.shape[1] // 128):
        out = op(out, value[:, i * 128 : (i + 1) * 128])
    return out


def tile_rows(t):
    return pl.ds(pl.multiple_of(t * TILE, TILE), TILE)


def fwd_kernel(
    kplace_ref, own_ref, place_ref, q_ref, *refs
):
    kv_refs = refs[:8]
    attn_ref, o_ref, qe_ref, ks_ref, vs_ref, s_scr, m_scr, l_scr, acc_scr, land, sems = refs[8:]
    copies = [pltpu.make_async_copy(kv_refs[k], land.at[k], sems.at[k]) for k in range(8)]
    for copy in copies:
        copy.start()
    for k in range(8):
        copies[k].wait()
        for b in range(8):
            low, high = key_form(land[k, b * BLK : (b + 1) * BLK, :])
            dst = block_rows(kplace_ref[8 * k + b])
            ks_ref[dst, :] = low
            vs_ref[dst, :] = high

    for c in range(ROWS // CHUNK):
        place_a, place_b = place_ref[2 * c], place_ref[2 * c + 1]
        blocks = (own_ref[2 * c], own_ref[2 * c + 1])
        query = jnp.concatenate([q_ref[block_rows(b), :] for b in blocks], axis=0)
        stacked = stack_heads(query, False)
        qpos = stacked_pos(place_a, place_b)
        tiles = place_a // (TILE // BLK) + 1
        m_scr[...] = jnp.full(m_scr.shape, -1e30, F32)

        def score_step(t, _):
            scores = dot_t(stacked, ks_ref[tile_rows(t), :])
            scores = jnp.where(col_pos(t) <= qpos, scores, -1e30)
            s_scr[t] = scores
            m_scr[...] = jnp.maximum(m_scr[...], fold(scores, jnp.maximum))
            return 0

        lax.fori_loop(0, tiles, score_step, 0)
        peak = jnp.max(m_scr[...], axis=1, keepdims=True)
        l_scr[...] = jnp.zeros(l_scr.shape, F32)
        acc_scr[...] = jnp.zeros(acc_scr.shape, F32)

        def value_step(t, _):
            prob = jnp.exp(s_scr[t] - peak)
            l_scr[...] = l_scr[...] + fold(prob, jnp.add)
            acc_scr[...] = acc_scr[...] + dot(prob.astype(BF), vs_ref[tile_rows(t), :])
            return 0

        lax.fori_loop(0, tiles, value_step, 0)
        total = jnp.sum(l_scr[...], axis=1, keepdims=True)
        log_total = peak + jnp.log(total)
        out = merge_heads(acc_scr[...] / total, True)
        ext = add_extras(
            query.astype(F32),
            [-log_total[h * CHUNK : (h + 1) * CHUNK] for h in range(NH)],
            False,
        ).astype(BF)
        for i, b in enumerate(blocks):
            rows = slice(i * BLK, (i + 1) * BLK)
            o_ref[block_rows(b), :] = out[rows]
            attn_ref[block_rows(b), :] = out[rows].astype(BF)
            qe_ref[block_rows(b), :] = ext[rows]


def dq_kernel(chunks, own_ref, place_ref, qe_ref, de_ref, ks_ref, vs_ref, *refs):
    *before, dq_ref, acc_scr = refs
    if before:
        dq_ref[...] = before[0][...]
    for c in chunks:
        place_a, place_b = place_ref[2 * c], place_ref[2 * c + 1]
        blocks = (own_ref[2 * c], own_ref[2 * c + 1])
        query = stack_heads(jnp.concatenate([qe_ref[block_rows(b), :] for b in blocks], axis=0), False)
        d_out = stack_heads(jnp.concatenate([de_ref[block_rows(b), :] for b in blocks], axis=0), True)
        qpos = stacked_pos(place_a, place_b)
        tiles = place_a // (TILE // BLK) + 1
        acc_scr[...] = jnp.zeros(acc_scr.shape, F32)

        def step(t, _):
            keys = ks_ref[tile_rows(t), :]
            prob = jnp.where(col_pos(t) <= qpos, jnp.exp(dot_t(query, keys)), 0.0)
            d_raw = (prob * dot_t(d_out, vs_ref[tile_rows(t), :])).astype(BF)
            acc_scr[...] = acc_scr[...] + dot(d_raw, keys)
            return 0

        lax.fori_loop(0, tiles, step, 0)
        out = (merge_heads(acc_scr[...], False) * 0.125).astype(BF)
        for i, b in enumerate(blocks):
            dq_ref[block_rows(b), :] = out[i * BLK : (i + 1) * BLK]


def dkv_kernel(qplace_ref, kplace_ref, own_ref, place_ref, kv_ref, qe_ref, *refs):
    de_refs, (dkv_ref, qs_scr, ds_scr, dk_scr, dv_scr, q_land, d_land, sems) = refs[:8], refs[8:]
    q_copy = pltpu.make_async_copy(qe_ref, q_land, sems.at[8])
    q_copy.start()
    copies = [pltpu.make_async_copy(de_refs[k], d_land.at[k], sems.at[k]) for k in range(8)]
    for copy in copies:
        copy.start()
    q_copy.wait()
    for b in range(NBLK):
        qs_scr[block_rows(qplace_ref[b]), :] = q_land[b * BLK : (b + 1) * BLK, :]
    for k in range(8):
        copies[k].wait()
        for b in range(8):
            ds_scr[block_rows(kplace_ref[8 * k + b]), :] = d_land[k, b * BLK : (b + 1) * BLK, :]

    for c in range(ROWS // CHUNK):
        place_a, place_b = place_ref[2 * c], place_ref[2 * c + 1]
        blocks = (own_ref[2 * c], own_ref[2 * c + 1])
        low, high = key_form(jnp.concatenate([kv_ref[block_rows(b), :] for b in blocks], axis=0))
        keys = stack_heads(low, False)
        values = stack_heads(high, True)
        kpos = stacked_pos(place_a, place_b)
        dk_scr[...] = jnp.zeros(dk_scr.shape, F32)
        dv_scr[...] = jnp.zeros(dv_scr.shape, F32)

        def step(t, _):
            query = qs_scr[tile_rows(t), :]
            d_out = ds_scr[tile_rows(t), :]
            prob = jnp.where(col_pos(t) >= kpos, jnp.exp(dot_t(keys, query)), 0.0)
            d_raw = (prob * dot_t(values, d_out)).astype(BF)
            dv_scr[...] = dv_scr[...] + dot(prob.astype(BF), d_out)
            dk_scr[...] = dk_scr[...] + dot(d_raw, query)
            return 0

        lax.fori_loop(place_b // (TILE // BLK), LEN // TILE, step, 0)
        d_keys = merge_heads(dk_scr[...], False)
        d_values = merge_heads(dv_scr[...], True)
        out = jnp.concatenate(
            [d_keys[:, :128], d_keys[:, 128:] + d_values[:, :128], d_values[:, 128:]], axis=1
        ).astype(BF)
        for i, b in enumerate(blocks):
            dkv_ref[block_rows(b), :] = out[i * BLK : (i + 1) * BLK]


def delta_kernel(d_ref, o_ref, early_ref, de_ref):
    d_out = jnp.concatenate([jnp.zeros((ROWS, 64), F32), d_ref[...].astype(F32)], axis=1)
    product = d_out * o_ref[...]
    sums = [
        -jnp.sum(jnp.where(feature_mask(ROWS, h, True), product, 0.0), axis=1, keepdims=True)
        for h in range(NH)
    ]
    de_ref[...] = add_extras(d_out, sums, True).astype(BF)


SMEM = pl.BlockSpec(memory_space=pltpu.SMEM)
VM = pl.BlockSpec(memory_space=pltpu.VMEM)
ANY = pl.BlockSpec(memory_space=pl.ANY)


def limit(mib):
    return pltpu.CompilerParams(vmem_limit_bytes=mib * 1024 * 1024)


def shape(*dims, dtype=BF):
    return jax.ShapeDtypeStruct(dims, dtype)


def attention_forward(kplace, own, place, query, kv):
    return pl.pallas_call(
        fwd_kernel,
        out_shape=(
            shape(ROWS, EXT), shape(ROWS, EXT, dtype=F32), shape(ROWS, EXT),
            shape(LEN, EXT), shape(LEN, EXT),
        ),
        in_specs=[SMEM] * 3 + [VM] + [ANY] * 8,
        out_specs=(VM,) * 5,
        scratch_shapes=[
            pltpu.VMEM((LEN // TILE, NH * CHUNK, TILE), F32),
            pltpu.VMEM((NH * CHUNK, 128), F32),
            pltpu.VMEM((NH * CHUNK, 128), F32),
            pltpu.VMEM((NH * CHUNK, EXT), F32),
            pltpu.VMEM((8, ROWS, 2 * GD), BF),
            pltpu.SemaphoreType.DMA((8,)),
        ],
        compiler_params=limit(34),
        cost_estimate=pl.CostEstimate(flops=16 * 10**9, bytes_accessed=10**7, transcendentals=4 * 10**6),
    )(kplace, own, place, query, *kv)


def attention_dq(chunks, own, place, qe, de, ks, vs, *before):
    return pl.pallas_call(
        functools.partial(dq_kernel, chunks),
        out_shape=shape(ROWS, EXT),
        in_specs=[SMEM] * 2 + [VM] * (4 + len(before)),
        out_specs=VM,
        scratch_shapes=[pltpu.VMEM((NH * CHUNK, EXT), F32)],
        compiler_params=limit(20),
        cost_estimate=pl.CostEstimate(flops=8 * 10**9, bytes_accessed=5 * 10**6, transcendentals=2 * 10**6),
    )(own, place, qe, de, ks, vs, *before)


def attention_dkv(qplace, kplace, own, place, kv, qe, de):
    return pl.pallas_call(
        dkv_kernel,
        out_shape=shape(ROWS, 2 * GD),
        in_specs=[SMEM] * 4 + [VM] + [ANY] * 9,
        out_specs=VM,
        scratch_shapes=[
            pltpu.VMEM((LEN, EXT), BF),
            pltpu.VMEM((LEN, EXT), BF),
            pltpu.VMEM((NH * CHUNK, EXT), F32),
            pltpu.VMEM((NH * CHUNK, EXT), F32),
            pltpu.VMEM((LEN, EXT), BF),
            pltpu.VMEM((8, ROWS, EXT), BF),
            pltpu.SemaphoreType.DMA((9,)),
        ],
        compiler_params=limit(28),
        cost_estimate=pl.CostEstimate(flops=15 * 10**9, bytes_accessed=10**7, transcendentals=4 * 10**6),
    )(qplace, kplace, own, place, kv, qe, *de)


def delta_rows(d_attn, o, early):
    return pl.pallas_call(
        delta_kernel,
        out_shape=shape(ROWS, EXT),
        in_specs=[VM] * 2 + [ANY],
        out_specs=VM,
        compiler_params=limit(8),
        cost_estimate=pl.CostEstimate(flops=10**6, bytes_accessed=10**6, transcendentals=0),
    )(d_attn, o, early)


def prep_kernel(at_ref, w_ref, gain_ref, bias_ref, vb_ref, cols_ref):
    for k in range(4):

        @pl.when(at_ref[0] == k)
        def _():
            for i, part in enumerate((1, 2, 0)):
                start = part * D + k * GD
                cols_ref[:GD, i * GD : (i + 1) * GD] = w_ref[:, start : start + GD]

    small = jnp.concatenate(
        [gain_ref[...].astype(F32), bias_ref[...].astype(F32), vb_ref[...].astype(F32), jnp.zeros((8, GD), F32)],
        axis=0,
    )
    cols_ref[GD:, :] = jnp.concatenate([small, jnp.zeros((16, 2 * GD), F32)], axis=1).astype(BF)


def prepare(at, w, gains, biases, vb):
    return pl.pallas_call(
        prep_kernel,
        out_shape=shape(GD + 16, 3 * GD),
        in_specs=[SMEM] + [VM] * 4,
        out_specs=VM,
        compiler_params=limit(8),
        cost_estimate=pl.CostEstimate(flops=1000, bytes_accessed=10**6, transcendentals=0),
    )(at, w, gains, biases, vb)


def qkv_kernel(at_ref, *refs):
    toks, ws = refs[:4], refs[4:8]
    kv_ref, q_ref, h1_ref, n1_ref, w_ref, small_ref, w_scr = refs[8:]
    yi, zi = at_ref[0], at_ref[1]
    for s in range(4):
        w_scr[s] = ws[s][...]
    for g in range(4):
        slot = (zi - g + 4) % 4
        w_ref[g * GD : (g + 1) * GD, :] = w_scr[slot, :GD]
        small_ref[:, g * GD : (g + 1) * GD] = w_scr[slot, GD:, :256].astype(F32)[:8, :GD]
    gain, shift = small_ref[0:1, :], small_ref[2:3, :]
    for s in range(4):
        rows = slice(128 * s, 128 * (s + 1))
        normed, _ = normalize(toks[s][...].astype(F32))
        n1_ref[rows, :] = normed
        h1_ref[rows, :] = (normed * gain + shift).astype(BF)
    own = w_scr[(zi - yi + 4) % 4, GD:, :256].astype(F32)[:8, :GD]
    qkv = dot(h1_ref[...], w_ref[...])
    kv_ref[:, :GD] = qkv[:, :GD].astype(BF)
    kv_ref[:, GD:] = (qkv[:, GD : 2 * GD] + own[7:8]).astype(BF)
    query = (qkv[:, 2 * GD :] + own[3:4]).astype(BF).astype(F32) * 0.125
    q_ref[...] = jnp.concatenate([query, jnp.zeros((ROWS, EXT - GD), F32)], axis=1).astype(BF)


def first_rows(at, toks, ws):
    return pl.pallas_call(
        qkv_kernel,
        out_shape=(
            shape(ROWS, 2 * GD), shape(ROWS, EXT), shape(ROWS, D), shape(ROWS, D, dtype=F32),
            shape(D, 3 * GD), shape(8, D, dtype=F32),
        ),
        in_specs=[SMEM] + [VM] * 8,
        out_specs=(VM,) * 6,
        scratch_shapes=[pltpu.VMEM((4, GD + 16, 3 * GD), BF)],
        compiler_params=limit(20),
        cost_estimate=pl.CostEstimate(flops=5 * 10**8, bytes_accessed=6 * 10**6, transcendentals=0),
    )(at, *toks, *ws)


def mlp_kernel(at_ref, *refs):
    h2s = refs[:4]
    both_ref, all_ref, down_ref, ub_ref, h2_ref, cot_ref, act_ref, dup_ref, dh_ref, up_ref, cots, sems = refs[4:]
    zi = at_ref[1]
    up_copy = pltpu.make_async_copy(
        all_ref.at[:, pl.ds(pl.multiple_of(zi * D, D), D)], up_ref, sems.at[4]
    )
    up_copy.start()
    copies = [
        pltpu.make_async_copy(both_ref.at[(zi - s + 4) % 4, :128], cots.at[s], sems.at[s])
        for s in range(4)
    ]
    for copy in copies:
        copy.start()
    for copy in copies:
        copy.wait()
    up_copy.wait()
    for s in range(4):
        rows = slice(128 * s, 128 * (s + 1))
        h2 = h2s[s][...]
        cot = cots[s]
        h2_ref[rows, :] = h2
        cot_ref[rows, :] = cot
        up = dot(h2, up_ref[...]) + ub_ref[...].astype(F32)
        d_act = dot_t(cot, down_ref[...])
        square = up * up
        th = jnp.tanh(0.7978845608028654 * (up + 0.044715 * (square * up)))
        half = 0.5 * (1.0 + th)
        slope = half + 0.5 * up * (1.0 - th * th) * (
            0.7978845608028654 * (1.0 + 3 * 0.044715 * square)
        )
        act_ref[rows, :] = (up * half).astype(BF)
        d_up = (slope * d_act).astype(BF)
        dup_ref[rows, :] = d_up
        dh_ref[rows, :] = dot_t(d_up, up_ref[...]).astype(BF)


def feed_forward(at, h2s, cots, w_up, w_down, ub):
    return pl.pallas_call(
        mlp_kernel,
        out_shape=(shape(ROWS, D),) * 5,
        in_specs=[SMEM] + [VM] * 4 + [ANY] * 2 + [VM] * 2,
        out_specs=(VM,) * 5,
        scratch_shapes=[
            pltpu.VMEM((D, D), BF), pltpu.VMEM((4, 128, D), BF), pltpu.SemaphoreType.DMA((5,)),
        ],
        compiler_params=limit(20),
        cost_estimate=pl.CostEstimate(flops=4 * 10**9, bytes_accessed=6 * 10**6, transcendentals=4 * 10**5),
    )(at, *h2s, cots, w_up, w_down, ub)


def wgrad_kernel(
    at_ref, h2_ref, dup_ref, act_ref, cot_ref, attn_ref, branch_ref, wd_ref, early_ref,
    keep_ref, give_ref, down_ref, out_scr,
):
    yi, ci = at_ref[0], at_ref[2]
    down_ref[...] = dot(act_ref[...], wd_ref[...]).astype(BF)
    g_up = t_dot(h2_ref[...], dup_ref[...])
    g_down = t_dot(act_ref[...], cot_ref[...])
    g_out = t_dot(attn_ref[...], branch_ref[...])
    for s in range(4):
        out_scr[s] = g_out[GD * s : GD * (s + 1)]
    vec = jnp.concatenate(
        [
            jnp.sum(dup_ref[...].astype(F32), axis=0, keepdims=True),
            jnp.sum(cot_ref[...].astype(F32), axis=0, keepdims=True),
            jnp.zeros((14, D), F32),
        ],
        axis=0,
    )
    for c in range(2):
        for j in range(4):
            b = 4 * c + j
            parts = []
            for z in range(4):
                parts.append(g_up[GD * z + 24 * b : GD * z + 24 * (b + 1)])
                parts.append(out_scr[(z - yi + 4) % 4, 24 * b : 24 * (b + 1)])
            parts += [g_down[96 * b : 96 * (b + 1)], vec]
            block = jnp.concatenate(parts, axis=0).astype(BF)

            @pl.when(ci == c)
            def _():
                keep_ref[j] = block

            @pl.when(ci != c)
            def _():
                give_ref[j] = block


def weight_blocks(at, h2, d_up, act, cot, attn, d_branch, w_down, early):
    return pl.pallas_call(
        wgrad_kernel,
        out_shape=(shape(4, 304, D), shape(4, 304, D), shape(ROWS, D)),
        in_specs=[SMEM] + [VM] * 7 + [ANY],
        out_specs=(VM,) * 3,
        scratch_shapes=[pltpu.VMEM((4, GD, D), F32)],
        compiler_params=limit(30),
        cost_estimate=pl.CostEstimate(flops=5 * 10**9, bytes_accessed=6 * 10**6, transcendentals=0),
    )(at, h2, d_up, act, cot, attn, d_branch, w_down, early)


def add_kernel(a_ref, b_ref, out_ref):
    for s in range(4):
        out_ref[s] = (a_ref[s].astype(F32) + b_ref[s].astype(F32)).astype(BF)


def add_blocks(a, b):
    return pl.pallas_call(
        add_kernel,
        out_shape=shape(*a.shape),
        in_specs=[VM] * 2,
        out_specs=VM,
        compiler_params=limit(16),
        cost_estimate=pl.CostEstimate(flops=10**6, bytes_accessed=6 * 10**6, transcendentals=0),
    )(a, b)


def pass_kernel(in_ref, early_ref, out_ref):
    out_ref[...] = in_ref[...]


def pass_on(value, early):
    return pl.pallas_call(
        pass_kernel,
        out_shape=shape(*value.shape),
        in_specs=[VM, ANY],
        out_specs=VM,
        compiler_params=limit(8),
        cost_estimate=pl.CostEstimate(flops=1000, bytes_accessed=10**6, transcendentals=0),
    )(value, early)


def part_kernel(at_ref, in_ref, early_ref, rest_ref, *refs):
    parts, scr = refs[:4], refs[4]
    scr[...] = (in_ref[0].astype(F32) + in_ref[1].astype(F32)) + (
        in_ref[2].astype(F32) + in_ref[3].astype(F32)
    )
    rest_ref[...] = scr[192:, :].astype(BF)
    for s in range(4):
        start = pl.multiple_of((at_ref[1] + s) % 4 * 48, 8)
        parts[s][...] = scr[pl.ds(start, 48), :].astype(BF)


def part_blocks(at, value, early):
    return pl.pallas_call(
        part_kernel,
        out_shape=(shape(112, D),) + (shape(48, D),) * 4,
        in_specs=[SMEM, VM, ANY],
        out_specs=(VM,) * 5,
        scratch_shapes=[pltpu.VMEM((304, D), F32)],
        compiler_params=limit(12),
        cost_estimate=pl.CostEstimate(flops=10**6, bytes_accessed=3 * 10**6, transcendentals=0),
    )(at, value, early)


def join_kernel(at_ref, rest_ref, early_ref, *refs):
    slots, (out_ref, scr) = refs[:4], refs[4:]
    for s in range(4):
        scr[s] = slots[s][...].astype(F32)
    up = [scr[(at_ref[1] - g + 4) % 4][:24] for g in range(4)]
    g_out = (scr[0] + scr[2])[24:] + (scr[1] + scr[3])[24:]
    rest = rest_ref[...].astype(F32)
    out_ref[...] = jnp.concatenate(up + [rest[:96], g_out, rest[96:]], axis=0).astype(BF)


def join_blocks(at, rest, slots, early):
    return pl.pallas_call(
        join_kernel,
        out_shape=shape(232, D),
        in_specs=[SMEM, VM, ANY] + [VM] * 4,
        out_specs=VM,
        scratch_shapes=[pltpu.VMEM((4, 48, D), F32)],
        compiler_params=limit(12),
        cost_estimate=pl.CostEstimate(flops=10**6, bytes_accessed=10**6, transcendentals=0),
    )(at, rest, early, *slots)


def mid_kernel(blocks_ref, up_ref, down_ref, out_ref, vec_ref):
    for c in range(2):
        for j in range(4):
            b = 4 * c + j
            block = blocks_ref[2 * j + c].astype(F32)
            for g in range(4):
                up_ref[24 * b : 24 * (b + 1), g * D : (g + 1) * D] = block[24 * g : 24 * (g + 1)]
            down_ref[96 * b : 96 * (b + 1), :] = block[96:192]
            out_ref[24 * b : 24 * (b + 1), :] = block[192:216]
            if b == 0:
                vec_ref[...] = block[216:224]


def mid_rows(blocks):
    return pl.pallas_call(
        mid_kernel,
        out_shape=(
            shape(GD, 4 * D, dtype=F32), shape(D, D, dtype=F32), shape(GD, D, dtype=F32),
            shape(8, D, dtype=F32),
        ),
        in_specs=[VM],
        out_specs=(VM,) * 4,
        compiler_params=limit(20),
        cost_estimate=pl.CostEstimate(flops=10**6, bytes_accessed=8 * 10**6, transcendentals=0),
    )(blocks)


def tail_kernel(at_ref, dkv_ref, dq_ref, h1_ref, n1_ref, w_ref, vec_ref, dh_ref, t_ref):
    yi, zi = at_ref[0], at_ref[1]
    d_qkv = jnp.concatenate([dkv_ref[...], dq_ref[...]], axis=1)
    d_h1 = dot_t(d_qkv[:, : 3 * GD], w_ref[...])
    dh_ref[...] = d_h1.astype(BF)
    sums = jnp.sum(d_qkv.astype(F32), axis=0, keepdims=True)
    at_own = lambda v: jnp.concatenate([jnp.where(yi == k, v, 0.0) for k in range(4)], axis=1)
    vectors = jnp.concatenate(
        [
            jnp.sum(d_h1 * n1_ref[...], axis=0, keepdims=True),
            jnp.sum(d_h1, axis=0, keepdims=True),
            at_own(sums[:, 2 * GD : 3 * GD]),
            at_own(sums[:, GD : 2 * GD]),
            vec_ref[4:8, :],
        ],
        axis=0,
    ).astype(BF)
    row = lax.broadcasted_iota(jnp.int32, (8, 128), 0)
    lane = lax.broadcasted_iota(jnp.int32, (8, 128), 1)
    columns = t_dot(vectors, jnp.where(lane == row + 64, 1.0, 0.0).astype(BF))
    grad = t_dot(h1_ref[...], d_qkv)
    for g in range(4):
        rows = slice(g * GD, (g + 1) * GD)
        slot = (g - zi + 4) % 4
        t_ref[slot, :, :512] = grad[rows, :512].astype(BF)
        t_ref[slot, :, 512:] = (grad[rows, 512:] + columns[rows]).astype(BF)


def last_gradients(at, d_kv, d_q, h1, n1, w, vec):
    return pl.pallas_call(
        tail_kernel,
        out_shape=(shape(ROWS, D), shape(4, GD, 640)),
        in_specs=[SMEM] + [VM] * 6,
        out_specs=(VM, VM),
        compiler_params=limit(20),
        cost_estimate=pl.CostEstimate(flops=3 * 10**9, bytes_accessed=6 * 10**6, transcendentals=0),
    )(at, d_kv, d_q, h1, n1, w, vec)


def sum_kernel(at_ref, t_ref, *refs):
    slots, (dh_ref, kept_ref, given_ref, same_ref) = refs[:3], refs[3:]
    same_ref[...] = dh_ref[...]
    for c in range(2):
        rows = slice(96 * c, 96 * (c + 1))
        a, b, d, e = (v.astype(F32) for v in [t_ref[0, rows]] + [r[rows] for r in slots])
        total = ((a + d) + (b + e)).astype(BF)

        @pl.when(at_ref[2] == c)
        def _():
            kept_ref[...] = total

        @pl.when(at_ref[2] != c)
        def _():
            given_ref[...] = total


def sum_slots(at, own, slots, d_h1):
    return pl.pallas_call(
        sum_kernel,
        out_shape=(shape(96, 640), shape(96, 640), shape(ROWS, D)),
        in_specs=[SMEM] + [VM] * 5,
        out_specs=(VM,) * 3,
        compiler_params=limit(12),
        cost_estimate=pl.CostEstimate(flops=10**6, bytes_accessed=3 * 10**6, transcendentals=0),
    )(at, own, *slots, d_h1)


def final_kernel(at_ref, *refs):
    slots, (grad_ref, vec_ref, scr) = refs[:4], refs[4:]
    for s in range(4):
        for c in range(2):
            scr[s, c] = slots[s][c]
    yi, ci = at_ref[0], at_ref[2]
    for c in range(2):
        rows = slice(96 * c, 96 * (c + 1))
        total = []
        for g in range(4):
            value = scr[(yi - g + 4) % 4, (ci + c) % 2].astype(F32)
            for i, part in enumerate((1, 2, 0)):
                start = part * D + g * GD
                grad_ref[rows, start : start + GD] = value[:, i * GD : (i + 1) * GD]
            total.append(value[:, 512:])
        vec_ref[rows, :] = (total[0] + total[1]) + (total[2] + total[3])


def final_rows(at, slots):
    return pl.pallas_call(
        final_kernel,
        out_shape=(shape(GD, 3 * D, dtype=F32), shape(GD, 128, dtype=F32)),
        in_specs=[SMEM] + [VM] * 4,
        out_specs=(VM, VM),
        scratch_shapes=[pltpu.VMEM((4, 2, 96, 640), BF)],
        compiler_params=limit(12),
        cost_estimate=pl.CostEstimate(flops=10**6, bytes_accessed=3 * 10**6, transcendentals=0),
    )(at, *slots)


def gather(value, axes, axis=0):
    return lax.all_gather(value, axes, axis=axis, tiled=True)


def swap(value, axes):
    return lax.all_to_all(value, axes, 0, 0)


def send(value, axis, step):
    n = lax.axis_size(axis)
    return lax.ppermute(value, axis, [(i, (i + step) % n) for i in range(n)])


def spread(value, axis):
    return [value] + [send(value, axis, s) for s in range(1, 4)]


def exchange(slots, axis, step):
    return [slots[0]] + [send(slots[s], axis, s * step) for s in range(1, 4)]


def add_slots(slots):
    a, b, c, d = (v.astype(F32) for v in slots)
    return (a + c) + (b + d)


def group_of(value, index, size, axis=0):
    return lax.dynamic_slice_in_dim(value, (index % 4) * size, size, axis)


def local(
    tokens, qkv_w, out_w, up_w, down_w, norm_gains, biases, value_bias, up_bias, cotangent, block_place
):
    xi = lax.axis_index("x")
    yi = lax.axis_index("y")
    ci = lax.axis_index("core")
    zi = lax.axis_index("fsdp")
    tok_own = tokens[0]
    cot_own = cotangent[0]

    at = jnp.stack([yi, zi, ci]).astype(jnp.int32)
    ws = spread(prepare(at, qkv_w, norm_gains, biases, value_bias[None]), "fsdp")
    toks = spread(tok_own, "y")

    ids = jnp.arange(NBLK, dtype=jnp.int32)
    slot_x, slot_c, slot_y, blk = ids // 16, (ids // 8) % 2, (ids // 2) % 4, ids % 2
    pick = lambda at: jnp.sum(jnp.where(at[:, None] == ids[None, :], block_place[None, :], 0), axis=1)
    at_y = (yi - slot_y + 4) % 4
    key_place = pick(at_y * 16 + ((xi - slot_x + 4) % 4) * 4 + ((ci + slot_c) % 2) * 2 + blk)
    query_place = pick(at_y * 16 + slot_x * 4 + slot_c * 2 + blk)
    own_place = key_place[:8]
    rank = jnp.sum((own_place[None, :] > own_place[:, None]).astype(jnp.int32), axis=1)
    order = jnp.arange(8, dtype=jnp.int32)
    hit = rank[None, :] == order[:, None]
    own = jnp.sum(jnp.where(hit, order[None, :], 0), axis=1)
    place = jnp.sum(jnp.where(hit, own_place[None, :], 0), axis=1)

    both = lax.all_gather(jnp.concatenate([cot_own, out_w], axis=0), "fsdp", axis=0)
    w_out = jnp.concatenate(
        [lax.dynamic_index_in_dim(both, (yi + s) % 4, 0, keepdims=False)[128:] for s in range(4)], axis=0
    )
    w_up = gather(up_w, "fsdp")
    w_down = down_w

    kv_own, query, h1, n1y, w_qkv, small = first_rows(at, toks, ws)
    gain1, gain2 = small[0], small[1]
    out_bias, shift2, down_bias = small[4], small[5], small[6]
    with jax.named_scope("kv"):
        kv_all = [p for v in spread(kv_own, "x") for p in (v, send(v, "core", 1))]
    attn, o_exact, qe, ks, vs = attention_forward(key_place, own, place, query, kv_all)
    qe_all = gather(qe, XC)

    attn = attn[:, 64:]
    with jax.named_scope("attn_y"):
        attn_own = exchange([attn[128 * s : 128 * (s + 1)] for s in range(4)], "y", -1)
    attn_own = jnp.concatenate(attn_own, axis=1)
    x2 = tok_own.astype(F32) + (dot(attn_own, w_out) + out_bias)
    n2, s2 = normalize(x2)
    h2_own = (n2 * gain2 + shift2).astype(BF)

    with jax.named_scope("h2_z"):
        h2s = spread(h2_own, "fsdp")
    h2, cot_z, act, d_up, d_h2_part = feed_forward(
        at, h2s, both, w_up, w_down, up_bias[None]
    )
    back = lambda v: add_slots(exchange([v[128 * s : 128 * (s + 1)] for s in range(4)], "fsdp", -1))
    with jax.named_scope("d_h2_z"):
        d_h2 = back(d_h2_part)
    cot32 = cot_own.astype(F32)
    d_x2 = cot32 + norm_back(d_h2 * gain2, n2, s2)
    d_branch = d_x2.astype(BF)
    d_attn = dot_t(d_branch, w_out).astype(BF)
    with jax.named_scope("d_attn_y"):
        d_attn_own = exchange([d_attn[:, GD * s : GD * (s + 1)] for s in range(4)], "y", 1)
    d_attn_own = jnp.concatenate(d_attn_own, axis=0)
    de = delta_rows(d_attn_own, o_exact, qe_all)
    with jax.named_scope("de"):
        de_all = [p for v in spread(de, "x") for p in (v, send(v, "core", 1))]
    d_q = attention_dq((0, 3), own, place, qe, de, ks, vs)
    d_q = attention_dq((1, 2), own, place, qe, de, ks, vs, d_q)
    d_kv = attention_dkv(query_place, key_place, own, place, kv_own, qe_all, de_all)

    keep, give, down = weight_blocks(at, h2, d_up, act, cot_z, attn_own, d_branch, w_down, de)
    with jax.named_scope("down"):
        layer_out = (x2 + back(down) + down_bias).astype(BF)
    with jax.named_scope("mid"):
        mid = add_blocks(keep, send(give, "core", 1))
        mid = lax.psum_scatter(mid.reshape(1216, D), "y", scatter_dimension=0, tiled=True)
        mid = lax.all_gather(pass_on(mid, d_q), "x", axis=0)
        rest, *parts = part_blocks(at, mid, d_kv)
        parts = exchange(parts, "fsdp", 1)

    vec = jnp.stack([jnp.sum(d_h2 * n2, axis=0), jnp.sum(d_branch.astype(F32), axis=0), jnp.sum(d_h2, axis=0)])
    vec = jnp.pad(vec, ((4, 1), (0, 0)))
    d_h1_send, tail = last_gradients(at, d_kv, d_q, h1, n1y, w_qkv, vec)
    with jax.named_scope("mid"):
        mid = lax.all_gather(join_blocks(at, rest, parts, tail), ("y", "core"), axis=0)
    grad_up, grad_down, grad_out, out_vec = mid_rows(mid)
    grad_up_bias = out_vec[0]
    grad_down_bias = lax.dynamic_slice(out_vec[1], (zi * GD,), (GD,))
    with jax.named_scope("tail_z"):
        received = [send(tail[s], "fsdp", s) for s in range(1, 4)]
    kept, given, d_h1_send = sum_slots(at, tail, received, d_h1_send)
    with jax.named_scope("d_h1_y"):
        d_h1 = add_slots(exchange([d_h1_send[128 * s : 128 * (s + 1)] for s in range(4)], "y", -1))
    n1, s1 = normalize(tok_own.astype(F32))
    input_grad = (d_x2 + norm_back(d_h1 * gain1, n1, s1)).astype(BF)

    with jax.named_scope("tail_core"):
        tail = (kept.astype(F32) + send(given, "core", 1).astype(F32)).astype(BF)
    with jax.named_scope("tail_x"):
        tail = add_slots(spread(tail, "x")).astype(BF)
    with jax.named_scope("tail_y"):
        tail = [jnp.stack([v, send(v, "core", 1)]) for v in spread(tail, "y")]
    grad_qkv, vectors = final_rows(at, tail)
    vectors = vectors[:, 64:71].T
    grad_gains = jnp.stack([vectors[0], vectors[4]])
    grad_biases = jnp.stack([vectors[1], vectors[2], vectors[5], vectors[6], grad_down_bias])
    grad_value_bias = vectors[3]
    return (
        layer_out[None], input_grad[None], grad_qkv, grad_out, grad_up, grad_down,
        grad_gains, grad_biases, grad_value_bias, grad_up_bias,
    )


def solution(mesh):
    grid = Mesh(mesh.devices.reshape(4, 4, 2, 4), ("y", "x", "core", "fsdp"))
    rows = P("fsdp", CTX, None)
    in_specs = (
        rows, P("fsdp", None), P("fsdp", None), P("fsdp", None), P("fsdp", None),
        P(None, "fsdp"), P(None, "fsdp"), P("fsdp"), P("fsdp"), rows, P(),
    )
    out_specs = (
        rows, rows, P("fsdp", None), P("fsdp", None), P("fsdp", None), P("fsdp", None),
        P(None, "fsdp"), P(None, "fsdp"), P("fsdp"), P("fsdp"),
    )
    return jax.shard_map(local, mesh=grid, in_specs=in_specs, out_specs=out_specs, check_vma=False)
```

```python
import functools

import jax
import jax.numpy as jnp
from jax import lax
from jax.experimental import pallas as pl
from jax.experimental.pallas import tpu as pltpu
from jax.sharding import Mesh
from jax.sharding import PartitionSpec as P

EPS = 1e-05
D = 768
GD = 192
NH = 3
HD = 64
ROWS = 512
LEN = 4096
BLK = 64
NBLK = 64
EXT = 256
TILE = 1024
CHUNK = 128
BF = jnp.bfloat16
F32 = jnp.float32
XC = ("x", "core")
CTX = ("y", "x", "core")


def dot(a, b):
    return lax.dot_general(a, b, (((1,), (0,)), ((), ())), preferred_element_type=F32)


def dot_t(a, b):
    return lax.dot_general(a, b, (((1,), (1,)), ((), ())), preferred_element_type=F32)


def t_dot(a, b):
    return lax.dot_general(a, b, (((0,), (0,)), ((), ())), preferred_element_type=F32)


def normalize(value):
    center = value - jnp.mean(value, axis=-1, keepdims=True)
    factor = lax.rsqrt(jnp.mean(center * center, axis=-1, keepdims=True) + EPS)
    return (center * factor, factor)


def norm_back(scaled, normed, factor):
    return factor * (
        scaled
        - jnp.mean(scaled, axis=-1, keepdims=True)
        - normed * jnp.mean(scaled * normed, axis=-1, keepdims=True)
    )


def lanes(rows):
    return lax.broadcasted_iota(jnp.int32, (rows, EXT), 1)


def head_mask(rows, h, high):
    lane = lanes(rows)
    if high:
        feat = (lane >= 64 + HD * h) & (lane < 64 + HD * (h + 1))
        ext = (lane >= 3 * h) & (lane < 3 * h + 3)
    else:
        feat = (lane >= HD * h) & (lane < HD * (h + 1))
        ext = (lane >= GD + 3 * h) & (lane < GD + 3 * h + 3)
    return feat | ext


def feature_mask(rows, h, high):
    lane = lanes(rows) - (64 if high else 0)
    return (lane >= HD * h) & (lane < HD * (h + 1))


def stack_heads(value, high):
    rows = value.shape[0]
    zero = jnp.zeros_like(value)
    return jnp.concatenate(
        [jnp.where(head_mask(rows, h, high), value, zero) for h in range(NH)], axis=0
    )


def merge_heads(stacked, high):
    rows = stacked.shape[0] // NH
    out = jnp.zeros((rows, EXT), F32)
    for h in range(NH):
        out = out + jnp.where(feature_mask(rows, h, high), stacked[h * rows : (h + 1) * rows], 0.0)
    return out


def pieces(value):
    first = value.astype(BF).astype(F32)
    second = (value - first).astype(BF).astype(F32)
    third = (value - first - second).astype(BF).astype(F32)
    return (first, second, third)


def add_extras(base, columns, high):
    rows = base.shape[0]
    lane = lanes(rows)
    start = 0 if high else GD
    for h in range(NH):
        for i, piece in enumerate(pieces(columns[h])):
            base = jnp.where(lane == start + 3 * h + i, piece, base)
    return base


def key_form(kv):
    lane = lanes(kv.shape[0])
    one = jnp.ones((kv.shape[0], EXT), BF)
    zero = jnp.zeros((kv.shape[0], EXT), BF)
    low = jnp.where(lane < GD, kv[:, :EXT], jnp.where(lane < GD + 9, one, zero))
    high = jnp.where(lane >= 64, kv[:, 128:384], jnp.where(lane < 9, one, zero))
    return (low, high)


def block_rows(index):
    return pl.ds(pl.multiple_of(index * BLK, BLK), BLK)


def stacked_pos(place_a, place_b):
    row = lax.broadcasted_iota(jnp.int32, (NH * CHUNK, 1), 0)
    place = jnp.where(row % CHUNK < BLK, place_a, place_b)
    return place * BLK + row % BLK


def col_pos(tile):
    return tile * TILE + lax.broadcasted_iota(jnp.int32, (NH * CHUNK, TILE), 1)


def fold(value, op):
    out = value[:, :128]
    for i in range(1, value.shape[1] // 128):
        out = op(out, value[:, i * 128 : (i + 1) * 128])
    return out


def tile_rows(t):
    return pl.ds(pl.multiple_of(t * TILE, TILE), TILE)


def fwd_kernel(
    kplace_ref, own_ref, place_ref, q_ref, *refs
):
    kv_refs = refs[:8]
    attn_ref, o_ref, qe_ref, ks_out, vs_out, ks_ref, vs_ref, s_scr, m_scr, l_scr, acc_scr, land, sems = refs[8:]
    copies = [pltpu.make_async_copy(kv_refs[k], land.at[k], sems.at[k]) for k in range(8)]
    for copy in copies:
        copy.start()
    for k in range(8):
        copies[k].wait()
        for b in range(8):
            low, high = key_form(land[k, b * BLK : (b + 1) * BLK, :])
            dst = block_rows(kplace_ref[8 * k + b])
            ks_ref[dst, :] = low
            vs_ref[dst, :] = high
    copies = [
        pltpu.make_async_copy(ks_ref, ks_out, sems.at[8]),
        pltpu.make_async_copy(vs_ref, vs_out, sems.at[9]),
    ]
    for copy in copies:
        copy.start()

    for c in range(ROWS // CHUNK):
        place_a, place_b = place_ref[2 * c], place_ref[2 * c + 1]
        blocks = (own_ref[2 * c], own_ref[2 * c + 1])
        query = jnp.concatenate([q_ref[block_rows(b), :] for b in blocks], axis=0)
        stacked = stack_heads(query, False)
        qpos = stacked_pos(place_a, place_b)
        tiles = place_a // (TILE // BLK) + 1
        m_scr[...] = jnp.full(m_scr.shape, -1e30, F32)

        def score_step(t, _):
            scores = dot_t(stacked, ks_ref[tile_rows(t), :])
            scores = jnp.where(col_pos(t) <= qpos, scores, -1e30)
            s_scr[t] = scores
            m_scr[...] = jnp.maximum(m_scr[...], fold(scores, jnp.maximum))
            return 0

        lax.fori_loop(0, tiles, score_step, 0)
        peak = jnp.max(m_scr[...], axis=1, keepdims=True)
        l_scr[...] = jnp.zeros(l_scr.shape, F32)
        acc_scr[...] = jnp.zeros(acc_scr.shape, F32)

        def value_step(t, _):
            prob = jnp.exp(s_scr[t] - peak)
            l_scr[...] = l_scr[...] + fold(prob, jnp.add)
            acc_scr[...] = acc_scr[...] + dot(prob.astype(BF), vs_ref[tile_rows(t), :])
            return 0

        lax.fori_loop(0, tiles, value_step, 0)
        total = jnp.sum(l_scr[...], axis=1, keepdims=True)
        log_total = peak + jnp.log(total)
        out = merge_heads(acc_scr[...] / total, True)
        ext = add_extras(
            query.astype(F32),
            [-log_total[h * CHUNK : (h + 1) * CHUNK] for h in range(NH)],
            False,
        ).astype(BF)
        for i, b in enumerate(blocks):
            rows = slice(i * BLK, (i + 1) * BLK)
            o_ref[block_rows(b), :] = out[rows]
            attn_ref[block_rows(b), :] = out[rows].astype(BF)
            qe_ref[block_rows(b), :] = ext[rows]
    for copy in copies:
        copy.wait()


def dq_kernel(chunks, own_ref, place_ref, qe_ref, de_ref, ks_ref, vs_ref, *refs):
    *before, dq_ref, acc_scr = refs
    if before:
        dq_ref[...] = before[0][...]
    for c in chunks:
        place_a, place_b = place_ref[2 * c], place_ref[2 * c + 1]
        blocks = (own_ref[2 * c], own_ref[2 * c + 1])
        query = stack_heads(jnp.concatenate([qe_ref[block_rows(b), :] for b in blocks], axis=0), False)
        d_out = stack_heads(jnp.concatenate([de_ref[block_rows(b), :] for b in blocks], axis=0), True)
        qpos = stacked_pos(place_a, place_b)
        tiles = place_a // (TILE // BLK) + 1
        acc_scr[...] = jnp.zeros(acc_scr.shape, F32)

        def step(t, _):
            keys = ks_ref[tile_rows(t), :]
            prob = jnp.where(col_pos(t) <= qpos, jnp.exp(dot_t(query, keys)), 0.0)
            d_raw = (prob * dot_t(d_out, vs_ref[tile_rows(t), :])).astype(BF)
            acc_scr[...] = acc_scr[...] + dot(d_raw, keys)
            return 0

        lax.fori_loop(0, tiles, step, 0)
        out = (merge_heads(acc_scr[...], False) * 0.125).astype(BF)
        for i, b in enumerate(blocks):
            dq_ref[block_rows(b), :] = out[i * BLK : (i + 1) * BLK]


def dkv_kernel(qplace_ref, kplace_ref, own_ref, place_ref, kv_ref, qe_ref, *refs):
    de_refs, (dkv_ref, qs_scr, ds_scr, dk_scr, dv_scr, q_land, d_land, sems) = refs[:8], refs[9:]
    q_copy = pltpu.make_async_copy(qe_ref, q_land, sems.at[8])
    q_copy.start()
    copies = [pltpu.make_async_copy(de_refs[k], d_land.at[k], sems.at[k]) for k in range(8)]
    for copy in copies:
        copy.start()
    q_copy.wait()
    for b in range(NBLK):
        qs_scr[block_rows(qplace_ref[b]), :] = q_land[b * BLK : (b + 1) * BLK, :]
    for k in range(8):
        copies[k].wait()
        for b in range(8):
            ds_scr[block_rows(kplace_ref[8 * k + b]), :] = d_land[k, b * BLK : (b + 1) * BLK, :]

    for c in range(ROWS // CHUNK):
        place_a, place_b = place_ref[2 * c], place_ref[2 * c + 1]
        blocks = (own_ref[2 * c], own_ref[2 * c + 1])
        low, high = key_form(jnp.concatenate([kv_ref[block_rows(b), :] for b in blocks], axis=0))
        keys = stack_heads(low, False)
        values = stack_heads(high, True)
        kpos = stacked_pos(place_a, place_b)
        dk_scr[...] = jnp.zeros(dk_scr.shape, F32)
        dv_scr[...] = jnp.zeros(dv_scr.shape, F32)

        def step(t, _):
            query = qs_scr[tile_rows(t), :]
            d_out = ds_scr[tile_rows(t), :]
            prob = jnp.where(col_pos(t) >= kpos, jnp.exp(dot_t(keys, query)), 0.0)
            d_raw = (prob * dot_t(values, d_out)).astype(BF)
            dv_scr[...] = dv_scr[...] + dot(prob.astype(BF), d_out)
            dk_scr[...] = dk_scr[...] + dot(d_raw, query)
            return 0

        lax.fori_loop(place_b // (TILE // BLK), LEN // TILE, step, 0)
        d_keys = merge_heads(dk_scr[...], False)
        d_values = merge_heads(dv_scr[...], True)
        out = jnp.concatenate(
            [d_keys[:, :128], d_keys[:, 128:] + d_values[:, :128], d_values[:, 128:]], axis=1
        ).astype(BF)
        for i, b in enumerate(blocks):
            dkv_ref[block_rows(b), :] = out[i * BLK : (i + 1) * BLK]


def delta_kernel(d_ref, o_ref, early_ref, de_ref):
    d_out = jnp.concatenate([jnp.zeros((ROWS, 64), F32), d_ref[...].astype(F32)], axis=1)
    product = d_out * o_ref[...]
    sums = [
        -jnp.sum(jnp.where(feature_mask(ROWS, h, True), product, 0.0), axis=1, keepdims=True)
        for h in range(NH)
    ]
    de_ref[...] = add_extras(d_out, sums, True).astype(BF)


SMEM = pl.BlockSpec(memory_space=pltpu.SMEM)
VM = pl.BlockSpec(memory_space=pltpu.VMEM)
ANY = pl.BlockSpec(memory_space=pl.ANY)
HBM = pl.BlockSpec(memory_space=pltpu.HBM)


def limit(mib):
    return pltpu.CompilerParams(vmem_limit_bytes=mib * 1024 * 1024)


def staged_kernel(body, counts, *refs):
    n_smem, n_in, n_early, n_out = counts
    cut = lambda n: (refs[:n], refs[n:])
    smem, refs = cut(n_smem)
    ins, refs = cut(n_in)
    _, refs = cut(n_early)
    outs, refs = cut(n_out)
    in_bufs, refs = cut(n_in)
    out_bufs, refs = cut(n_out)
    *scratch, sems = refs
    copies = [pltpu.make_async_copy(a, b, sems.at[i]) for i, (a, b) in enumerate(zip(ins, in_bufs))]
    for copy in copies:
        copy.start()
    for copy in copies:
        copy.wait()
    body(*smem, *in_bufs, *out_bufs, *scratch)
    copies = [pltpu.make_async_copy(a, b, sems.at[i]) for i, (a, b) in enumerate(zip(out_bufs, outs))]
    for copy in copies:
        copy.start()
    for copy in copies:
        copy.wait()


def staged(body, outs, smem, ins, early=(), scratch=(), mib=20, flops=10**6, moved=5 * 10**6):
    buffers = [pltpu.VMEM(v.shape, v.dtype) for v in (*ins, *outs)]
    counts = (len(smem), len(ins), len(early), len(outs))
    return pl.pallas_call(
        functools.partial(staged_kernel, body, counts),
        out_shape=tuple(outs),
        in_specs=[SMEM] * len(smem) + [HBM] * (len(ins) + len(early)),
        out_specs=(HBM,) * len(outs),
        scratch_shapes=buffers + list(scratch) + [pltpu.SemaphoreType.DMA((max(len(ins), len(outs)),))],
        compiler_params=limit(mib),
        cost_estimate=pl.CostEstimate(flops=flops, bytes_accessed=moved, transcendentals=0),
    )(*smem, *ins, *early)


def shape(*dims, dtype=BF):
    return jax.ShapeDtypeStruct(dims, dtype)


def attention_forward(kplace, own, place, query, kv):
    return pl.pallas_call(
        fwd_kernel,
        out_shape=(
            shape(ROWS, EXT), shape(ROWS, EXT, dtype=F32), shape(ROWS, EXT),
            shape(LEN, EXT), shape(LEN, EXT),
        ),
        in_specs=[SMEM] * 3 + [VM] + [HBM] * 8,
        out_specs=(VM,) * 3 + (HBM,) * 2,
        scratch_shapes=[
            pltpu.VMEM((LEN, EXT), BF),
            pltpu.VMEM((LEN, EXT), BF),
            pltpu.VMEM((LEN // TILE, NH * CHUNK, TILE), F32),
            pltpu.VMEM((NH * CHUNK, 128), F32),
            pltpu.VMEM((NH * CHUNK, 128), F32),
            pltpu.VMEM((NH * CHUNK, EXT), F32),
            pltpu.VMEM((8, ROWS, 2 * GD), BF),
            pltpu.SemaphoreType.DMA((10,)),
        ],
        compiler_params=limit(34),
        cost_estimate=pl.CostEstimate(flops=16 * 10**9, bytes_accessed=10**7, transcendentals=4 * 10**6),
    )(kplace, own, place, query, *kv)


def attention_dq(chunks, own, place, qe, de, ks, vs, before=(), early=()):
    return staged(
        functools.partial(dq_kernel, chunks),
        (shape(ROWS, EXT),),
        (own, place), (qe, de, ks, vs, *before), early,
        scratch=[pltpu.VMEM((NH * CHUNK, EXT), F32)],
        mib=24,
        flops=8 * 10**9,
    )[0]


def attention_dkv(qplace, kplace, own, place, kv, qe, de, early):
    return pl.pallas_call(
        dkv_kernel,
        out_shape=shape(ROWS, 2 * GD),
        in_specs=[SMEM] * 4 + [VM] + [HBM] * 10,
        out_specs=VM,
        scratch_shapes=[
            pltpu.VMEM((LEN, EXT), BF),
            pltpu.VMEM((LEN, EXT), BF),
            pltpu.VMEM((NH * CHUNK, EXT), F32),
            pltpu.VMEM((NH * CHUNK, EXT), F32),
            pltpu.VMEM((LEN, EXT), BF),
            pltpu.VMEM((8, ROWS, EXT), BF),
            pltpu.SemaphoreType.DMA((9,)),
        ],
        compiler_params=limit(28),
        cost_estimate=pl.CostEstimate(flops=15 * 10**9, bytes_accessed=10**7, transcendentals=4 * 10**6),
    )(qplace, kplace, own, place, kv, qe, *de, early)


def delta_rows(d_attn, o, early):
    return pl.pallas_call(
        delta_kernel,
        out_shape=shape(ROWS, EXT),
        in_specs=[VM] * 2 + [ANY],
        out_specs=VM,
        compiler_params=limit(8),
        cost_estimate=pl.CostEstimate(flops=10**6, bytes_accessed=10**6, transcendentals=0),
    )(d_attn, o, early)


def prep_kernel(at_ref, w_ref, gain_ref, bias_ref, vb_ref, cols_ref):
    for k in range(4):

        @pl.when(at_ref[0] == k)
        def _():
            for i, part in enumerate((1, 2, 0)):
                start = part * D + k * GD
                cols_ref[:GD, i * GD : (i + 1) * GD] = w_ref[:, start : start + GD]

    small = jnp.concatenate(
        [gain_ref[...].astype(F32), bias_ref[...].astype(F32), vb_ref[...].astype(F32), jnp.zeros((8, GD), F32)],
        axis=0,
    )
    cols_ref[GD:, :] = jnp.concatenate([small, jnp.zeros((16, 2 * GD), F32)], axis=1).astype(BF)


def prepare(at, w, gains, biases, vb):
    return pl.pallas_call(
        prep_kernel,
        out_shape=shape(GD + 16, 3 * GD),
        in_specs=[SMEM] + [VM] * 4,
        out_specs=VM,
        compiler_params=limit(8),
        cost_estimate=pl.CostEstimate(flops=1000, bytes_accessed=10**6, transcendentals=0),
    )(at, w, gains, biases, vb)


def qkv_kernel(at_ref, *refs):
    toks, ws = refs[:4], refs[4:8]
    kv_ref, q_ref, h1_ref, n1_ref, w_ref, small_ref, w_scr = refs[8:]
    yi, zi = at_ref[0], at_ref[1]
    for s in range(4):
        w_scr[s] = ws[s][...]
    for g in range(4):
        slot = (zi - g + 4) % 4
        w_ref[g * GD : (g + 1) * GD, :] = w_scr[slot, :GD]
        small_ref[:, g * GD : (g + 1) * GD] = w_scr[slot, GD:, :256].astype(F32)[:8, :GD]
    gain, shift = small_ref[0:1, :], small_ref[2:3, :]
    for s in range(4):
        rows = slice(128 * s, 128 * (s + 1))
        normed, _ = normalize(toks[s][...].astype(F32))
        n1_ref[rows, :] = normed
        h1_ref[rows, :] = (normed * gain + shift).astype(BF)
    own = w_scr[(zi - yi + 4) % 4, GD:, :256].astype(F32)[:8, :GD]
    qkv = dot(h1_ref[...], w_ref[...])
    kv_ref[:, :GD] = qkv[:, :GD].astype(BF)
    kv_ref[:, GD:] = (qkv[:, GD : 2 * GD] + own[7:8]).astype(BF)
    query = (qkv[:, 2 * GD :] + own[3:4]).astype(BF).astype(F32) * 0.125
    q_ref[...] = jnp.concatenate([query, jnp.zeros((ROWS, EXT - GD), F32)], axis=1).astype(BF)


def first_rows(at, toks, ws):
    return staged(
        qkv_kernel,
        (
            shape(ROWS, 2 * GD), shape(ROWS, EXT), shape(ROWS, D), shape(ROWS, D, dtype=F32),
            shape(D, 3 * GD), shape(8, D, dtype=F32),
        ),
        (at,), (*toks, *ws),
        scratch=[pltpu.VMEM((4, GD + 16, 3 * GD), BF)],
        flops=10**9,
    )


def mlp_kernel(at_ref, both_ref, all_ref, *refs):
    pieces_in, (wd_in, ub_ref) = refs[:4], refs[4:6]
    results, dh_ref = refs[6:10], refs[10]
    h2_ref, cot_ref, act_ref, dup_ref, up_ref, down_ref, sems, out_sems = refs[11:]
    zi = at_ref[1]
    copies = [pltpu.make_async_copy(pieces_in[s], h2_ref.at[128 * s : 128 * (s + 1)], sems.at[s]) for s in range(4)]
    copies += [
        pltpu.make_async_copy(
            both_ref.at[(zi - s + 4) % 4, :128], cot_ref.at[128 * s : 128 * (s + 1)], sems.at[4 + s]
        )
        for s in range(4)
    ]
    copies.append(
        pltpu.make_async_copy(all_ref.at[:, pl.ds(pl.multiple_of(zi * D, D), D)], up_ref, sems.at[8])
    )
    copies.append(pltpu.make_async_copy(wd_in, down_ref, sems.at[9]))
    for copy in copies:
        copy.start()
    for copy in copies:
        copy.wait()
    for s in range(4):
        rows = slice(128 * s, 128 * (s + 1))
        up = dot(h2_ref[rows, :], up_ref[...]) + ub_ref[...].astype(F32)
        d_act = dot_t(cot_ref[rows, :], down_ref[...])
        square = up * up
        th = jnp.tanh(0.7978845608028654 * (up + 0.044715 * (square * up)))
        half = 0.5 * (1.0 + th)
        slope = half + 0.5 * up * (1.0 - th * th) * (
            0.7978845608028654 * (1.0 + 3 * 0.044715 * square)
        )
        act_ref[rows, :] = (up * half).astype(BF)
        d_up = (slope * d_act).astype(BF)
        dup_ref[rows, :] = d_up
        dh_ref[rows, :] = dot_t(d_up, up_ref[...]).astype(BF)
    copies = [
        pltpu.make_async_copy(a, b, out_sems.at[i])
        for i, (a, b) in enumerate(zip((h2_ref, cot_ref, act_ref, dup_ref), results))
    ]
    for copy in copies:
        copy.start()
    for copy in copies:
        copy.wait()


def feed_forward(at, h2s, both, w_up, w_down, ub):
    return pl.pallas_call(
        mlp_kernel,
        out_shape=(shape(ROWS, D),) * 5,
        in_specs=[SMEM] + [HBM] * 7 + [VM],
        out_specs=(HBM,) * 4 + (VM,),
        scratch_shapes=[pltpu.VMEM((ROWS, D), BF)] * 4 + [pltpu.VMEM((D, D), BF)] * 2
        + [pltpu.SemaphoreType.DMA((10,)), pltpu.SemaphoreType.DMA((4,))],
        compiler_params=limit(20),
        cost_estimate=pl.CostEstimate(flops=4 * 10**9, bytes_accessed=6 * 10**6, transcendentals=4 * 10**5),
    )(at, both, w_up, *h2s, w_down, ub)


def wgrad_kernel(
    at_ref, h2_ref, dup_ref, act_ref, cot_ref, attn_ref, branch_ref, wd_ref,
    keep_ref, give_ref, down_ref, out_scr,
):
    yi, ci = at_ref[0], at_ref[2]
    down_ref[...] = dot(act_ref[...], wd_ref[...]).astype(BF)
    g_up = t_dot(h2_ref[...], dup_ref[...])
    g_down = t_dot(act_ref[...], cot_ref[...])
    g_out = t_dot(attn_ref[...], branch_ref[...])
    for s in range(4):
        out_scr[s] = g_out[GD * s : GD * (s + 1)]
    vec = jnp.concatenate(
        [
            jnp.sum(dup_ref[...].astype(F32), axis=0, keepdims=True),
            jnp.sum(cot_ref[...].astype(F32), axis=0, keepdims=True),
            jnp.zeros((14, D), F32),
        ],
        axis=0,
    )
    for c in range(2):
        for j in range(4):
            b = 4 * c + j
            parts = []
            for z in range(4):
                parts.append(g_up[GD * z + 24 * b : GD * z + 24 * (b + 1)])
                parts.append(out_scr[(z - yi + 4) % 4, 24 * b : 24 * (b + 1)])
            parts += [g_down[96 * b : 96 * (b + 1)], vec]
            block = jnp.concatenate(parts, axis=0).astype(BF)

            @pl.when(ci == c)
            def _():
                keep_ref[j] = block

            @pl.when(ci != c)
            def _():
                give_ref[j] = block


def weight_blocks(at, h2, d_up, act, cot, attn, d_branch, w_down, early):
    return staged(
        wgrad_kernel,
        (shape(4, 304, D), shape(4, 304, D), shape(ROWS, D)),
        (at,), (h2, d_up, act, cot, attn, d_branch, w_down), (early,),
        scratch=[pltpu.VMEM((4, GD, D), F32)],
        mib=32,
        flops=5 * 10**9,
    )


def add_kernel(a_ref, b_ref, out_ref):
    for s in range(4):
        out_ref[s] = (a_ref[s].astype(F32) + b_ref[s].astype(F32)).astype(BF)


def add_blocks(a, b):
    return pl.pallas_call(
        add_kernel,
        out_shape=shape(*a.shape),
        in_specs=[VM] * 2,
        out_specs=VM,
        compiler_params=limit(16),
        cost_estimate=pl.CostEstimate(flops=10**6, bytes_accessed=6 * 10**6, transcendentals=0),
    )(a, b)


def mid_kernel(blocks_ref, up_ref, down_ref, out_ref, vec_ref):
    for c in range(2):
        for j in range(4):
            b = 4 * c + j
            block = blocks_ref[2 * j + c].astype(F32)
            for g in range(4):
                up_ref[24 * b : 24 * (b + 1), g * D : (g + 1) * D] = block[24 * g : 24 * (g + 1)]
            down_ref[96 * b : 96 * (b + 1), :] = block[96:192]
            out_ref[24 * b : 24 * (b + 1), :] = block[192:216]
            if b == 0:
                vec_ref[...] = block[216:224]


def mid_rows(blocks):
    return pl.pallas_call(
        mid_kernel,
        out_shape=(
            shape(GD, 4 * D, dtype=F32), shape(D, D, dtype=F32), shape(GD, D, dtype=F32),
            shape(8, D, dtype=F32),
        ),
        in_specs=[VM],
        out_specs=(VM,) * 4,
        compiler_params=limit(20),
        cost_estimate=pl.CostEstimate(flops=10**6, bytes_accessed=8 * 10**6, transcendentals=0),
    )(blocks)


def tail_kernel(
    at_ref, dkv_ref, dq_ref, h1_ref, n1_ref, w_ref, vec_ref, mid_ref, dh_ref, t_ref, rest_ref, scr
):
    yi, zi = at_ref[0], at_ref[1]
    scr[...] = (mid_ref[0].astype(F32) + mid_ref[1].astype(F32)) + (
        mid_ref[2].astype(F32) + mid_ref[3].astype(F32)
    )
    rest_ref[...] = scr[192:, :].astype(BF)
    for s in range(4):
        part = scr[pl.ds(pl.multiple_of((zi + s) % 4 * 48, 8), 48), :]
        t_ref[s, 192:240] = part[:, :640].astype(BF)
        t_ref[s, 240:, :128] = part[:, 640:].astype(BF)
        t_ref[s, 240:, 128:] = jnp.zeros((48, 512), BF)
    d_qkv = jnp.concatenate([dkv_ref[...], dq_ref[...]], axis=1)
    d_h1 = dot_t(d_qkv[:, : 3 * GD], w_ref[...])
    dh_ref[...] = d_h1.astype(BF)
    sums = jnp.sum(d_qkv.astype(F32), axis=0, keepdims=True)
    at_own = lambda v: jnp.concatenate([jnp.where(yi == k, v, 0.0) for k in range(4)], axis=1)
    vectors = jnp.concatenate(
        [
            jnp.sum(d_h1 * n1_ref[...], axis=0, keepdims=True),
            jnp.sum(d_h1, axis=0, keepdims=True),
            at_own(sums[:, 2 * GD : 3 * GD]),
            at_own(sums[:, GD : 2 * GD]),
            vec_ref[4:8, :],
        ],
        axis=0,
    ).astype(BF)
    row = lax.broadcasted_iota(jnp.int32, (8, 128), 0)
    lane = lax.broadcasted_iota(jnp.int32, (8, 128), 1)
    columns = t_dot(vectors, jnp.where(lane == row + 64, 1.0, 0.0).astype(BF))
    grad = t_dot(h1_ref[...], d_qkv)
    for g in range(4):
        rows = slice(g * GD, (g + 1) * GD)
        slot = (g - zi + 4) % 4
        t_ref[slot, :GD, :512] = grad[rows, :512].astype(BF)
        t_ref[slot, :GD, 512:] = (grad[rows, 512:] + columns[rows]).astype(BF)


def last_gradients(at, d_kv, d_q, h1, n1, w, vec, mid):
    return staged(
        tail_kernel,
        (shape(ROWS, D), shape(4, 288, 640), shape(112, D)),
        (at,), (d_kv, d_q, h1, n1, w, vec, mid),
        scratch=[pltpu.VMEM((304, D), F32)],
        mib=24,
        flops=3 * 10**9,
    )


def sum_kernel(at_ref, t_ref, r1, r2, r3, dh_ref, rest_ref, kept_ref, given_ref, same_ref, block_ref, scr):
    same_ref[...] = dh_ref[...]
    slots = (r1, r2, r3)
    for c in range(2):
        rows = slice(96 * c, 96 * (c + 1))
        a, b, d, e = (v.astype(F32) for v in [t_ref[0, rows]] + [r[rows] for r in slots])
        total = ((a + d) + (b + e)).astype(BF)

        @pl.when(at_ref[2] == c)
        def _():
            kept_ref[...] = total

        @pl.when(at_ref[2] != c)
        def _():
            given_ref[...] = total

    for s in range(4):
        part = (t_ref[0, GD:] if s == 0 else slots[s - 1][GD:]).astype(F32)
        scr[s, :, :640] = part[:48]
        scr[s, :, 640:] = part[48:, :128]
    up = [scr[(at_ref[1] - g + 4) % 4][:24] for g in range(4)]
    g_out = (scr[0] + scr[2])[24:] + (scr[1] + scr[3])[24:]
    rest = rest_ref[...].astype(F32)
    block_ref[...] = jnp.concatenate(up + [rest[:96], g_out, rest[96:]], axis=0).astype(BF)


def sum_slots(at, own, slots, d_h1, rest):
    return pl.pallas_call(
        sum_kernel,
        out_shape=(shape(96, 640), shape(96, 640), shape(ROWS, D), shape(232, D)),
        in_specs=[SMEM] + [VM] * 6,
        out_specs=(VM,) * 4,
        scratch_shapes=[pltpu.VMEM((4, 48, D), F32)],
        compiler_params=limit(14),
        cost_estimate=pl.CostEstimate(flops=10**6, bytes_accessed=3 * 10**6, transcendentals=0),
    )(at, own, *slots, d_h1, rest)


def final_kernel(at_ref, *refs):
    slots, (grad_ref, vec_ref, scr) = refs[:4], refs[4:]
    for s in range(4):
        for c in range(2):
            scr[s, c] = slots[s][c]
    yi, ci = at_ref[0], at_ref[2]
    for c in range(2):
        rows = slice(96 * c, 96 * (c + 1))
        total = []
        for g in range(4):
            value = scr[(yi - g + 4) % 4, (ci + c) % 2].astype(F32)
            for i, part in enumerate((1, 2, 0)):
                start = part * D + g * GD
                grad_ref[rows, start : start + GD] = value[:, i * GD : (i + 1) * GD]
            total.append(value[:, 512:])
        vec_ref[rows, :] = (total[0] + total[1]) + (total[2] + total[3])


def final_rows(at, slots):
    return pl.pallas_call(
        final_kernel,
        out_shape=(shape(GD, 3 * D, dtype=F32), shape(GD, 128, dtype=F32)),
        in_specs=[SMEM] + [VM] * 4,
        out_specs=(VM, VM),
        scratch_shapes=[pltpu.VMEM((4, 2, 96, 640), BF)],
        compiler_params=limit(12),
        cost_estimate=pl.CostEstimate(flops=10**6, bytes_accessed=3 * 10**6, transcendentals=0),
    )(at, *slots)


def gather(value, axes, axis=0):
    return lax.all_gather(value, axes, axis=axis, tiled=True)


def swap(value, axes):
    return lax.all_to_all(value, axes, 0, 0)


def send(value, axis, step):
    n = lax.axis_size(axis)
    return lax.ppermute(value, axis, [(i, (i + step) % n) for i in range(n)])


def spread(value, axis):
    return [value] + [send(value, axis, s) for s in range(1, 4)]


def exchange(slots, axis, step):
    return [slots[0]] + [send(slots[s], axis, s * step) for s in range(1, 4)]


def add_slots(slots):
    a, b, c, d = (v.astype(F32) for v in slots)
    return (a + c) + (b + d)


def group_of(value, index, size, axis=0):
    return lax.dynamic_slice_in_dim(value, (index % 4) * size, size, axis)


def local(
    tokens, qkv_w, out_w, up_w, down_w, norm_gains, biases, value_bias, up_bias, cotangent, block_place
):
    xi = lax.axis_index("x")
    yi = lax.axis_index("y")
    ci = lax.axis_index("core")
    zi = lax.axis_index("fsdp")
    tok_own = tokens[0]
    cot_own = cotangent[0]

    at = jnp.stack([yi, zi, ci]).astype(jnp.int32)
    ws = spread(prepare(at, qkv_w, norm_gains, biases, value_bias[None]), "fsdp")
    toks = spread(tok_own, "y")

    ids = jnp.arange(NBLK, dtype=jnp.int32)
    slot_x, slot_c, slot_y, blk = ids // 16, (ids // 8) % 2, (ids // 2) % 4, ids % 2
    pick = lambda at: jnp.sum(jnp.where(at[:, None] == ids[None, :], block_place[None, :], 0), axis=1)
    at_y = (yi - slot_y + 4) % 4
    key_place = pick(at_y * 16 + ((xi - slot_x + 4) % 4) * 4 + ((ci + slot_c) % 2) * 2 + blk)
    query_place = pick(at_y * 16 + slot_x * 4 + slot_c * 2 + blk)
    own_place = key_place[:8]
    rank = jnp.sum((own_place[None, :] > own_place[:, None]).astype(jnp.int32), axis=1)
    order = jnp.arange(8, dtype=jnp.int32)
    hit = rank[None, :] == order[:, None]
    own = jnp.sum(jnp.where(hit, order[None, :], 0), axis=1)
    place = jnp.sum(jnp.where(hit, own_place[None, :], 0), axis=1)

    both = lax.all_gather(jnp.concatenate([cot_own, out_w], axis=0), "fsdp", axis=0)
    w_out = jnp.concatenate(
        [lax.dynamic_index_in_dim(both, (yi + s) % 4, 0, keepdims=False)[128:] for s in range(4)], axis=0
    )
    w_up = gather(up_w, "fsdp")
    w_down = down_w

    kv_own, query, h1, n1y, w_qkv, small = first_rows(at, toks, ws)
    gain1, gain2 = small[0], small[1]
    out_bias, shift2, down_bias = small[4], small[5], small[6]
    with jax.named_scope("kv"):
        kv_all = [p for v in spread(kv_own, "x") for p in (v, send(v, "core", 1))]
    attn, o_exact, qe, ks, vs = attention_forward(key_place, own, place, query, kv_all)
    qe_all = gather(qe, XC)

    attn = attn[:, 64:]
    with jax.named_scope("attn_y"):
        attn_own = exchange([attn[128 * s : 128 * (s + 1)] for s in range(4)], "y", -1)
    attn_own = jnp.concatenate(attn_own, axis=1)
    x2 = tok_own.astype(F32) + (dot(attn_own, w_out) + out_bias)
    n2, s2 = normalize(x2)
    h2_own = (n2 * gain2 + shift2).astype(BF)

    with jax.named_scope("h2_z"):
        h2s = spread(h2_own, "fsdp")
    h2, cot_z, act, d_up, d_h2_part = feed_forward(
        at, h2s, both, w_up, w_down, up_bias[None]
    )
    back = lambda v: add_slots(exchange([v[128 * s : 128 * (s + 1)] for s in range(4)], "fsdp", -1))
    with jax.named_scope("d_h2_z"):
        d_h2 = back(d_h2_part)
    cot32 = cot_own.astype(F32)
    d_x2 = cot32 + norm_back(d_h2 * gain2, n2, s2)
    d_branch = d_x2.astype(BF)
    d_attn = dot_t(d_branch, w_out).astype(BF)
    with jax.named_scope("d_attn_y"):
        d_attn_own = exchange([d_attn[:, GD * s : GD * (s + 1)] for s in range(4)], "y", 1)
    d_attn_own = jnp.concatenate(d_attn_own, axis=0)
    de = delta_rows(d_attn_own, o_exact, qe_all)
    with jax.named_scope("de"):
        de_all = [p for v in spread(de, "x") for p in (v, send(v, "core", 1))]
    d_q = attention_dq((0, 3), own, place, qe, de, ks, vs)
    d_q = attention_dq((1, 2), own, place, qe, de, ks, vs, (d_q,), (de_all[2], de_all[4], de_all[6]))

    keep, give, down = weight_blocks(at, h2, d_up, act, cot_z, attn_own, d_branch, w_down, de)
    with jax.named_scope("down"):
        layer_out = (x2 + back(down) + down_bias).astype(BF)
    with jax.named_scope("mid"):
        mid = add_blocks(keep, send(give, "core", 1))
        mid = lax.psum_scatter(mid.reshape(1216, D), "y", scatter_dimension=0, tiled=True)
        mid = lax.all_gather(mid, "x", axis=0)
    d_kv = attention_dkv(query_place, key_place, own, place, kv_own, qe_all, de_all, layer_out)

    vec = jnp.stack([jnp.sum(d_h2 * n2, axis=0), jnp.sum(d_branch.astype(F32), axis=0), jnp.sum(d_h2, axis=0)])
    vec = jnp.pad(vec, ((4, 1), (0, 0)))
    d_h1_send, tail, rest = last_gradients(at, d_kv, d_q, h1, n1y, w_qkv, vec, mid)
    with jax.named_scope("tail_z"):
        received = [send(tail[s], "fsdp", s) for s in range(1, 4)]
    kept, given, d_h1_send, mid = sum_slots(at, tail, received, d_h1_send, rest)
    with jax.named_scope("mid"):
        mid = lax.all_gather(mid, ("y", "core"), axis=0)
    grad_up, grad_down, grad_out, out_vec = mid_rows(mid)
    grad_up_bias = out_vec[0]
    grad_down_bias = lax.dynamic_slice(out_vec[1], (zi * GD,), (GD,))
    with jax.named_scope("d_h1_y"):
        d_h1 = add_slots(exchange([d_h1_send[128 * s : 128 * (s + 1)] for s in range(4)], "y", -1))
    n1, s1 = normalize(tok_own.astype(F32))
    input_grad = (d_x2 + norm_back(d_h1 * gain1, n1, s1)).astype(BF)

    with jax.named_scope("tail_core"):
        tail = (kept.astype(F32) + send(given, "core", 1).astype(F32)).astype(BF)
    with jax.named_scope("tail_x"):
        tail = add_slots(spread(tail, "x")).astype(BF)
    with jax.named_scope("tail_y"):
        tail = [jnp.stack([v, send(v, "core", 1)]) for v in spread(tail, "y")]
    grad_qkv, vectors = final_rows(at, tail)
    vectors = vectors[:, 64:71].T
    grad_gains = jnp.stack([vectors[0], vectors[4]])
    grad_biases = jnp.stack([vectors[1], vectors[2], vectors[5], vectors[6], grad_down_bias])
    grad_value_bias = vectors[3]
    return (
        layer_out[None], input_grad[None], grad_qkv, grad_out, grad_up, grad_down,
        grad_gains, grad_biases, grad_value_bias, grad_up_bias,
    )


def solution(mesh):
    grid = Mesh(mesh.devices.reshape(4, 4, 2, 4), ("y", "x", "core", "fsdp"))
    rows = P("fsdp", CTX, None)
    in_specs = (
        rows, P("fsdp", None), P("fsdp", None), P("fsdp", None), P("fsdp", None),
        P(None, "fsdp"), P(None, "fsdp"), P("fsdp"), P("fsdp"), rows, P(),
    )
    out_specs = (
        rows, rows, P("fsdp", None), P("fsdp", None), P("fsdp", None), P("fsdp", None),
        P(None, "fsdp"), P(None, "fsdp"), P("fsdp"), P("fsdp"),
    )
    return jax.shard_map(local, mesh=grid, in_specs=in_specs, out_specs=out_specs, check_vma=False)
```

```python
import functools

import jax
import jax.numpy as jnp
from jax import lax
from jax.experimental import pallas as pl
from jax.experimental.pallas import tpu as pltpu
from jax.sharding import Mesh
from jax.sharding import PartitionSpec as P

EPS = 1e-05
D = 768
GD = 192
NH = 3
HD = 64
ROWS = 512
LEN = 4096
BLK = 64
NBLK = 64
EXT = 256
TILE = 1024
CHUNK = 128
BF = jnp.bfloat16
F32 = jnp.float32
XC = ("x", "core")
CTX = ("y", "x", "core")


def dot(a, b):
    return lax.dot_general(a, b, (((1,), (0,)), ((), ())), preferred_element_type=F32)


def dot_t(a, b):
    return lax.dot_general(a, b, (((1,), (1,)), ((), ())), preferred_element_type=F32)


def t_dot(a, b):
    return lax.dot_general(a, b, (((0,), (0,)), ((), ())), preferred_element_type=F32)


def normalize(value):
    center = value - jnp.mean(value, axis=-1, keepdims=True)
    factor = lax.rsqrt(jnp.mean(center * center, axis=-1, keepdims=True) + EPS)
    return (center * factor, factor)


def norm_back(scaled, normed, factor):
    return factor * (
        scaled
        - jnp.mean(scaled, axis=-1, keepdims=True)
        - normed * jnp.mean(scaled * normed, axis=-1, keepdims=True)
    )


def lanes(rows):
    return lax.broadcasted_iota(jnp.int32, (rows, EXT), 1)


def head_mask(rows, h, high):
    lane = lanes(rows)
    if high:
        feat = (lane >= 64 + HD * h) & (lane < 64 + HD * (h + 1))
        ext = (lane >= 3 * h) & (lane < 3 * h + 3)
    else:
        feat = (lane >= HD * h) & (lane < HD * (h + 1))
        ext = (lane >= GD + 3 * h) & (lane < GD + 3 * h + 3)
    return feat | ext


def feature_mask(rows, h, high):
    lane = lanes(rows) - (64 if high else 0)
    return (lane >= HD * h) & (lane < HD * (h + 1))


def stack_heads(value, high):
    rows = value.shape[0]
    zero = jnp.zeros_like(value)
    return jnp.concatenate(
        [jnp.where(head_mask(rows, h, high), value, zero) for h in range(NH)], axis=0
    )


def merge_heads(stacked, high):
    rows = stacked.shape[0] // NH
    out = jnp.zeros((rows, EXT), F32)
    for h in range(NH):
        out = out + jnp.where(feature_mask(rows, h, high), stacked[h * rows : (h + 1) * rows], 0.0)
    return out


def pieces(value):
    first = value.astype(BF).astype(F32)
    second = (value - first).astype(BF).astype(F32)
    third = (value - first - second).astype(BF).astype(F32)
    return (first, second, third)


def add_extras(base, columns, high):
    rows = base.shape[0]
    lane = lanes(rows)
    start = 0 if high else GD
    for h in range(NH):
        for i, piece in enumerate(pieces(columns[h])):
            base = jnp.where(lane == start + 3 * h + i, piece, base)
    return base


def key_form(kv):
    lane = lanes(kv.shape[0])
    one = jnp.ones((kv.shape[0], EXT), BF)
    zero = jnp.zeros((kv.shape[0], EXT), BF)
    low = jnp.where(lane < GD, kv[:, :EXT], jnp.where(lane < GD + 9, one, zero))
    high = jnp.where(lane >= 64, kv[:, 128:384], jnp.where(lane < 9, one, zero))
    return (low, high)


def block_rows(index):
    return pl.ds(pl.multiple_of(index * BLK, BLK), BLK)


def stacked_pos(place_a, place_b):
    row = lax.broadcasted_iota(jnp.int32, (NH * CHUNK, 1), 0)
    place = jnp.where(row % CHUNK < BLK, place_a, place_b)
    return place * BLK + row % BLK


def col_pos(tile):
    return tile * TILE + lax.broadcasted_iota(jnp.int32, (NH * CHUNK, TILE), 1)


def fold(value, op):
    out = value[:, :128]
    for i in range(1, value.shape[1] // 128):
        out = op(out, value[:, i * 128 : (i + 1) * 128])
    return out


def tile_rows(t):
    return pl.ds(pl.multiple_of(t * TILE, TILE), TILE)


def fwd_kernel(
    kplace_ref, own_ref, place_ref, q_ref, *refs
):
    kv_refs = refs[:8]
    attn_ref, o_ref, qe_ref, ks_out, vs_out, ks_ref, vs_ref, s_scr, m_scr, l_scr, acc_scr, land, sems = refs[8:]
    copies = [pltpu.make_async_copy(kv_refs[k], land.at[k], sems.at[k]) for k in range(8)]
    for copy in copies:
        copy.start()
    for k in range(8):
        copies[k].wait()
        for b in range(8):
            low, high = key_form(land[k, b * BLK : (b + 1) * BLK, :])
            dst = block_rows(kplace_ref[8 * k + b])
            ks_ref[dst, :] = low
            vs_ref[dst, :] = high
    copies = [
        pltpu.make_async_copy(ks_ref, ks_out, sems.at[8]),
        pltpu.make_async_copy(vs_ref, vs_out, sems.at[9]),
    ]
    for copy in copies:
        copy.start()

    for c in range(ROWS // CHUNK):
        place_a, place_b = place_ref[2 * c], place_ref[2 * c + 1]
        blocks = (own_ref[2 * c], own_ref[2 * c + 1])
        query = jnp.concatenate([q_ref[block_rows(b), :] for b in blocks], axis=0)
        stacked = stack_heads(query, False)
        qpos = stacked_pos(place_a, place_b)
        tiles = place_a // (TILE // BLK) + 1
        m_scr[...] = jnp.full(m_scr.shape, -1e30, F32)

        def score_step(t, _):
            scores = dot_t(stacked, ks_ref[tile_rows(t), :])
            scores = jnp.where(col_pos(t) <= qpos, scores, -1e30)
            s_scr[t] = scores
            m_scr[...] = jnp.maximum(m_scr[...], fold(scores, jnp.maximum))
            return 0

        lax.fori_loop(0, tiles, score_step, 0)
        peak = jnp.max(m_scr[...], axis=1, keepdims=True)
        l_scr[...] = jnp.zeros(l_scr.shape, F32)
        acc_scr[...] = jnp.zeros(acc_scr.shape, F32)

        def value_step(t, _):
            prob = jnp.exp(s_scr[t] - peak)
            l_scr[...] = l_scr[...] + fold(prob, jnp.add)
            acc_scr[...] = acc_scr[...] + dot(prob.astype(BF), vs_ref[tile_rows(t), :])
            return 0

        lax.fori_loop(0, tiles, value_step, 0)
        total = jnp.sum(l_scr[...], axis=1, keepdims=True)
        log_total = peak + jnp.log(total)
        out = merge_heads(acc_scr[...] / total, True)
        ext = add_extras(
            query.astype(F32),
            [-log_total[h * CHUNK : (h + 1) * CHUNK] for h in range(NH)],
            False,
        ).astype(BF)
        for i, b in enumerate(blocks):
            rows = slice(i * BLK, (i + 1) * BLK)
            o_ref[block_rows(b), :] = out[rows]
            attn_ref[block_rows(b), :] = out[rows].astype(BF)
            qe_ref[block_rows(b), :] = ext[rows]
    for copy in copies:
        copy.wait()


def dq_kernel(chunks, own_ref, place_ref, qe_ref, de_ref, ks_ref, vs_ref, *refs):
    *before, dq_ref, acc_scr = refs
    if before:
        dq_ref[...] = before[0][...]
    for c in chunks:
        place_a, place_b = place_ref[2 * c], place_ref[2 * c + 1]
        blocks = (own_ref[2 * c], own_ref[2 * c + 1])
        query = stack_heads(jnp.concatenate([qe_ref[block_rows(b), :] for b in blocks], axis=0), False)
        d_out = stack_heads(jnp.concatenate([de_ref[block_rows(b), :] for b in blocks], axis=0), True)
        qpos = stacked_pos(place_a, place_b)
        tiles = place_a // (TILE // BLK) + 1
        acc_scr[...] = jnp.zeros(acc_scr.shape, F32)

        def step(t, _):
            keys = ks_ref[tile_rows(t), :]
            prob = jnp.where(col_pos(t) <= qpos, jnp.exp(dot_t(query, keys)), 0.0)
            d_raw = (prob * dot_t(d_out, vs_ref[tile_rows(t), :])).astype(BF)
            acc_scr[...] = acc_scr[...] + dot(d_raw, keys)
            return 0

        lax.fori_loop(0, tiles, step, 0)
        out = (merge_heads(acc_scr[...], False) * 0.125).astype(BF)
        for i, b in enumerate(blocks):
            dq_ref[block_rows(b), :] = out[i * BLK : (i + 1) * BLK]


def dkv_kernel(qplace_ref, kplace_ref, own_ref, place_ref, kv_ref, qe_ref, *refs):
    de_refs, (dkv_ref, qs_scr, ds_scr, dk_scr, dv_scr, q_land, d_land, sems) = refs[:8], refs[9:]
    q_copy = pltpu.make_async_copy(qe_ref, q_land, sems.at[8])
    q_copy.start()
    copies = [pltpu.make_async_copy(de_refs[k], d_land.at[k], sems.at[k]) for k in range(8)]
    for copy in copies:
        copy.start()
    q_copy.wait()
    for b in range(NBLK):
        qs_scr[block_rows(qplace_ref[b]), :] = q_land[b * BLK : (b + 1) * BLK, :]
    for k in range(8):
        copies[k].wait()
        for b in range(8):
            ds_scr[block_rows(kplace_ref[8 * k + b]), :] = d_land[k, b * BLK : (b + 1) * BLK, :]

    for c in range(ROWS // CHUNK):
        place_a, place_b = place_ref[2 * c], place_ref[2 * c + 1]
        blocks = (own_ref[2 * c], own_ref[2 * c + 1])
        low, high = key_form(jnp.concatenate([kv_ref[block_rows(b), :] for b in blocks], axis=0))
        keys = stack_heads(low, False)
        values = stack_heads(high, True)
        kpos = stacked_pos(place_a, place_b)
        dk_scr[...] = jnp.zeros(dk_scr.shape, F32)
        dv_scr[...] = jnp.zeros(dv_scr.shape, F32)

        def step(t, _):
            query = qs_scr[tile_rows(t), :]
            d_out = ds_scr[tile_rows(t), :]
            prob = jnp.where(col_pos(t) >= kpos, jnp.exp(dot_t(keys, query)), 0.0)
            d_raw = (prob * dot_t(values, d_out)).astype(BF)
            dv_scr[...] = dv_scr[...] + dot(prob.astype(BF), d_out)
            dk_scr[...] = dk_scr[...] + dot(d_raw, query)
            return 0

        lax.fori_loop(place_b // (TILE // BLK), LEN // TILE, step, 0)
        d_keys = merge_heads(dk_scr[...], False)
        d_values = merge_heads(dv_scr[...], True)
        out = jnp.concatenate(
            [d_keys[:, :128], d_keys[:, 128:] + d_values[:, :128], d_values[:, 128:]], axis=1
        ).astype(BF)
        for i, b in enumerate(blocks):
            dkv_ref[block_rows(b), :] = out[i * BLK : (i + 1) * BLK]


def delta_kernel(d_ref, o_ref, early_ref, de_ref):
    d_out = jnp.concatenate([jnp.zeros((ROWS, 64), F32), d_ref[...].astype(F32)], axis=1)
    product = d_out * o_ref[...]
    sums = [
        -jnp.sum(jnp.where(feature_mask(ROWS, h, True), product, 0.0), axis=1, keepdims=True)
        for h in range(NH)
    ]
    de_ref[...] = add_extras(d_out, sums, True).astype(BF)


SMEM = pl.BlockSpec(memory_space=pltpu.SMEM)
VM = pl.BlockSpec(memory_space=pltpu.VMEM)
ANY = pl.BlockSpec(memory_space=pl.ANY)
HBM = pl.BlockSpec(memory_space=pltpu.HBM)
PARAMS = pltpu.CompilerParams(vmem_limit_bytes=60 * 1024 * 1024)


def staged_kernel(body, counts, *refs):
    n_smem, n_in, n_early, n_out = counts
    cut = lambda n: (refs[:n], refs[n:])
    smem, refs = cut(n_smem)
    ins, refs = cut(n_in)
    _, refs = cut(n_early)
    outs, refs = cut(n_out)
    in_bufs, refs = cut(n_in)
    out_bufs, refs = cut(n_out)
    *scratch, sems = refs
    copies = [pltpu.make_async_copy(a, b, sems.at[i]) for i, (a, b) in enumerate(zip(ins, in_bufs))]
    for copy in copies:
        copy.start()
    for copy in copies:
        copy.wait()
    body(*smem, *in_bufs, *out_bufs, *scratch)
    copies = [pltpu.make_async_copy(a, b, sems.at[i]) for i, (a, b) in enumerate(zip(out_bufs, outs))]
    for copy in copies:
        copy.start()
    for copy in copies:
        copy.wait()


def staged(body, outs, smem, ins, early=(), scratch=(), flops=10**6, moved=5 * 10**6):
    buffers = [pltpu.VMEM(v.shape, v.dtype) for v in (*ins, *outs)]
    counts = (len(smem), len(ins), len(early), len(outs))
    return pl.pallas_call(
        functools.partial(staged_kernel, body, counts),
        out_shape=tuple(outs),
        in_specs=[SMEM] * len(smem) + [HBM] * (len(ins) + len(early)),
        out_specs=(HBM,) * len(outs),
        scratch_shapes=buffers + list(scratch) + [pltpu.SemaphoreType.DMA((max(len(ins), len(outs)),))],
        compiler_params=PARAMS,
        cost_estimate=pl.CostEstimate(flops=flops, bytes_accessed=moved, transcendentals=0),
    )(*smem, *ins, *early)


def shape(*dims, dtype=BF):
    return jax.ShapeDtypeStruct(dims, dtype)


def attention_forward(kplace, own, place, query, kv):
    return pl.pallas_call(
        fwd_kernel,
        out_shape=(
            shape(ROWS, EXT), shape(ROWS, EXT, dtype=F32), shape(ROWS, EXT),
            shape(LEN, EXT), shape(LEN, EXT),
        ),
        in_specs=[SMEM] * 3 + [VM] + [HBM] * 8,
        out_specs=(VM,) * 3 + (HBM,) * 2,
        scratch_shapes=[
            pltpu.VMEM((LEN, EXT), BF),
            pltpu.VMEM((LEN, EXT), BF),
            pltpu.VMEM((LEN // TILE, NH * CHUNK, TILE), F32),
            pltpu.VMEM((NH * CHUNK, 128), F32),
            pltpu.VMEM((NH * CHUNK, 128), F32),
            pltpu.VMEM((NH * CHUNK, EXT), F32),
            pltpu.VMEM((8, ROWS, 2 * GD), BF),
            pltpu.SemaphoreType.DMA((10,)),
        ],
        compiler_params=PARAMS,
        cost_estimate=pl.CostEstimate(flops=16 * 10**9, bytes_accessed=10**7, transcendentals=4 * 10**6),
    )(kplace, own, place, query, *kv)


def attention_dq(chunks, own, place, qe, de, ks, vs, before=(), early=()):
    return staged(
        functools.partial(dq_kernel, chunks),
        (shape(ROWS, EXT),),
        (own, place), (qe, de, ks, vs, *before), early,
        scratch=[pltpu.VMEM((NH * CHUNK, EXT), F32)],
        flops=8 * 10**9,
    )[0]


def attention_dkv(qplace, kplace, own, place, kv, qe, de, early):
    return pl.pallas_call(
        dkv_kernel,
        out_shape=shape(ROWS, 2 * GD),
        in_specs=[SMEM] * 4 + [VM] + [HBM] * 10,
        out_specs=VM,
        scratch_shapes=[
            pltpu.VMEM((LEN, EXT), BF),
            pltpu.VMEM((LEN, EXT), BF),
            pltpu.VMEM((NH * CHUNK, EXT), F32),
            pltpu.VMEM((NH * CHUNK, EXT), F32),
            pltpu.VMEM((LEN, EXT), BF),
            pltpu.VMEM((8, ROWS, EXT), BF),
            pltpu.SemaphoreType.DMA((9,)),
        ],
        compiler_params=PARAMS,
        cost_estimate=pl.CostEstimate(flops=15 * 10**9, bytes_accessed=10**7, transcendentals=4 * 10**6),
    )(qplace, kplace, own, place, kv, qe, *de, early)


def delta_rows(d_attn, o, early):
    return pl.pallas_call(
        delta_kernel,
        out_shape=shape(ROWS, EXT),
        in_specs=[VM] * 2 + [ANY],
        out_specs=VM,
        compiler_params=PARAMS,
        cost_estimate=pl.CostEstimate(flops=10**6, bytes_accessed=10**6, transcendentals=0),
    )(d_attn, o, early)


def prep_kernel(at_ref, w_ref, gain_ref, bias_ref, vb_ref, cot_ref, out_ref, cols_ref, both_ref, sems):
    copies = [
        pltpu.make_async_copy(cot_ref, both_ref.at[:128], sems.at[0]),
        pltpu.make_async_copy(out_ref, both_ref.at[128:], sems.at[1]),
    ]
    for copy in copies:
        copy.start()
    for k in range(4):

        @pl.when(at_ref[0] == k)
        def _():
            for i, part in enumerate((1, 2, 0)):
                start = part * D + k * GD
                cols_ref[:GD, i * GD : (i + 1) * GD] = w_ref[:, start : start + GD]

    small = jnp.concatenate(
        [gain_ref[...].astype(F32), bias_ref[...].astype(F32), vb_ref[...].astype(F32), jnp.zeros((8, GD), F32)],
        axis=0,
    )
    cols_ref[GD:, :] = jnp.concatenate([small, jnp.zeros((16, 2 * GD), F32)], axis=1).astype(BF)
    for copy in copies:
        copy.wait()


def prepare(at, w, gains, biases, vb, cot, out_w):
    return pl.pallas_call(
        prep_kernel,
        out_shape=(shape(GD + 16, 3 * GD), shape(320, D)),
        in_specs=[SMEM] + [VM] * 4 + [HBM] * 2,
        out_specs=(VM, HBM),
        scratch_shapes=[pltpu.SemaphoreType.DMA((2,))],
        compiler_params=PARAMS,
        cost_estimate=pl.CostEstimate(flops=1000, bytes_accessed=10**6, transcendentals=0),
    )(at, w, gains, biases, vb, cot, out_w)


def qkv_kernel(at_ref, *refs):
    toks, ws = refs[:4], refs[4:8]
    kv_ref, q_ref, h1_ref, n1_ref, w_ref, small_ref, w_scr = refs[8:]
    yi, zi = at_ref[0], at_ref[1]
    for s in range(4):
        w_scr[s] = ws[s][...]
    for g in range(4):
        slot = (zi - g + 4) % 4
        w_ref[g * GD : (g + 1) * GD, :] = w_scr[slot, :GD]
        small_ref[:, g * GD : (g + 1) * GD] = w_scr[slot, GD:, :256].astype(F32)[:8, :GD]
    gain, shift = small_ref[0:1, :], small_ref[2:3, :]
    for s in range(4):
        rows = slice(128 * s, 128 * (s + 1))
        normed, _ = normalize(toks[s][...].astype(F32))
        n1_ref[rows, :] = normed
        h1_ref[rows, :] = (normed * gain + shift).astype(BF)
    own = w_scr[(zi - yi + 4) % 4, GD:, :256].astype(F32)[:8, :GD]
    qkv = dot(h1_ref[...], w_ref[...])
    kv_ref[:, :GD] = qkv[:, :GD].astype(BF)
    kv_ref[:, GD:] = (qkv[:, GD : 2 * GD] + own[7:8]).astype(BF)
    query = (qkv[:, 2 * GD :] + own[3:4]).astype(BF).astype(F32) * 0.125
    q_ref[...] = jnp.concatenate([query, jnp.zeros((ROWS, EXT - GD), F32)], axis=1).astype(BF)


def first_rows(at, toks, ws):
    return staged(
        qkv_kernel,
        (
            shape(ROWS, 2 * GD), shape(ROWS, EXT), shape(ROWS, D), shape(ROWS, D, dtype=F32),
            shape(D, 3 * GD), shape(8, D, dtype=F32),
        ),
        (at,), (*toks, *ws),
        scratch=[pltpu.VMEM((4, GD + 16, 3 * GD), BF)],
        flops=10**9,
    )


def mlp_kernel(at_ref, both_ref, all_ref, *refs):
    pieces_in, (wd_in, ub_ref) = refs[:4], refs[4:6]
    results, dh_ref = refs[6:10], refs[10]
    h2_ref, cot_ref, act_ref, dup_ref, up_ref, down_ref, sems, out_sems = refs[11:]
    zi = at_ref[1]
    copies = [pltpu.make_async_copy(pieces_in[s], h2_ref.at[128 * s : 128 * (s + 1)], sems.at[s]) for s in range(4)]
    copies += [
        pltpu.make_async_copy(
            both_ref.at[(zi - s + 4) % 4, :128], cot_ref.at[128 * s : 128 * (s + 1)], sems.at[4 + s]
        )
        for s in range(4)
    ]
    copies.append(
        pltpu.make_async_copy(all_ref.at[:, pl.ds(pl.multiple_of(zi * D, D), D)], up_ref, sems.at[8])
    )
    copies.append(pltpu.make_async_copy(wd_in, down_ref, sems.at[9]))
    for copy in copies:
        copy.start()
    for copy in copies:
        copy.wait()
    for s in range(4):
        rows = slice(128 * s, 128 * (s + 1))
        up = dot(h2_ref[rows, :], up_ref[...]) + ub_ref[...].astype(F32)
        d_act = dot_t(cot_ref[rows, :], down_ref[...])
        square = up * up
        th = jnp.tanh(0.7978845608028654 * (up + 0.044715 * (square * up)))
        half = 0.5 * (1.0 + th)
        slope = half + 0.5 * up * (1.0 - th * th) * (
            0.7978845608028654 * (1.0 + 3 * 0.044715 * square)
        )
        act_ref[rows, :] = (up * half).astype(BF)
        d_up = (slope * d_act).astype(BF)
        dup_ref[rows, :] = d_up
        dh_ref[rows, :] = dot_t(d_up, up_ref[...]).astype(BF)
    copies = [
        pltpu.make_async_copy(a, b, out_sems.at[i])
        for i, (a, b) in enumerate(zip((h2_ref, cot_ref, act_ref, dup_ref), results))
    ]
    for copy in copies:
        copy.start()
    for copy in copies:
        copy.wait()


def feed_forward(at, h2s, both, w_up, w_down, ub):
    return pl.pallas_call(
        mlp_kernel,
        out_shape=(shape(ROWS, D),) * 5,
        in_specs=[SMEM] + [HBM] * 7 + [VM],
        out_specs=(HBM,) * 4 + (VM,),
        scratch_shapes=[pltpu.VMEM((ROWS, D), BF)] * 4 + [pltpu.VMEM((D, D), BF)] * 2
        + [pltpu.SemaphoreType.DMA((10,)), pltpu.SemaphoreType.DMA((4,))],
        compiler_params=PARAMS,
        cost_estimate=pl.CostEstimate(flops=4 * 10**9, bytes_accessed=6 * 10**6, transcendentals=4 * 10**5),
    )(at, both, w_up, *h2s, w_down, ub)


def wgrad_kernel(
    at_ref, h2_ref, dup_ref, act_ref, cot_ref, wd_ref, keep_ref, give_ref, down_ref
):
    ci = at_ref[2]
    g_up = t_dot(h2_ref[...], dup_ref[...])
    g_down = t_dot(act_ref[...], cot_ref[...])
    vec = jnp.concatenate(
        [
            jnp.sum(dup_ref[...].astype(F32), axis=0, keepdims=True),
            jnp.sum(cot_ref[...].astype(F32), axis=0, keepdims=True),
            jnp.zeros((14, D), F32),
        ],
        axis=0,
    )
    for c in range(2):
        for j in range(4):
            b = 4 * c + j
            parts = [g_up[GD * z + 24 * b : GD * z + 24 * (b + 1)] for z in range(4)]
            parts += [g_down[96 * b : 96 * (b + 1)], vec]
            block = jnp.concatenate(parts, axis=0).astype(BF)

            @pl.when(ci == c)
            def _():
                keep_ref[j] = block

            @pl.when(ci != c)
            def _():
                give_ref[j] = block
    down_ref[...] = dot(act_ref[...], wd_ref[...]).astype(BF)


def weight_blocks(at, h2, d_up, act, cot, w_down):
    return staged(
        wgrad_kernel,
        (shape(4, 208, D), shape(4, 208, D), shape(ROWS, D)),
        (at,), (h2, d_up, act, cot, w_down),
        flops=5 * 10**9,
    )


def ograd_kernel(at_ref, attn_ref, branch_ref, keep_ref, give_ref, out_scr):
    yi, ci = at_ref[0], at_ref[2]
    g_out = t_dot(attn_ref[...], branch_ref[...])
    for s in range(4):
        out_scr[s] = g_out[GD * s : GD * (s + 1)]
    for c in range(2):
        for j in range(4):
            b = 4 * c + j
            block = jnp.concatenate(
                [out_scr[(z - yi + 4) % 4, 24 * b : 24 * (b + 1)] for z in range(4)], axis=0
            ).astype(BF)

            @pl.when(ci == c)
            def _():
                keep_ref[j] = block

            @pl.when(ci != c)
            def _():
                give_ref[j] = block


def output_blocks(at, attn, d_branch, early):
    return staged(
        ograd_kernel,
        (shape(4, 96, D), shape(4, 96, D)),
        (at,), (attn, d_branch), (early,),
        scratch=[pltpu.VMEM((4, GD, D), F32)],
        flops=10**9,
    )


def join_kernel(a_ref, b_ref, out_ref):
    out_ref[:208, :] = a_ref[...]
    out_ref[208:, :] = b_ref[...]


def join_blocks(a, b, early):
    return staged(join_kernel, (shape(304, D),), (), (a, b), (early,))[0]


def add_kernel(a_ref, b_ref, out_ref):
    for s in range(4):
        out_ref[s] = (a_ref[s].astype(F32) + b_ref[s].astype(F32)).astype(BF)


def add_blocks(a, b):
    return pl.pallas_call(
        add_kernel,
        out_shape=shape(*a.shape),
        in_specs=[VM] * 2,
        out_specs=VM,
        compiler_params=PARAMS,
        cost_estimate=pl.CostEstimate(flops=10**6, bytes_accessed=6 * 10**6, transcendentals=0),
    )(a, b)


def mid_kernel(blocks_ref, up_ref, down_ref, out_ref, vec_ref):
    for c in range(2):
        for j in range(4):
            b = 4 * c + j
            block = blocks_ref[2 * j + c].astype(F32)
            for g in range(4):
                up_ref[24 * b : 24 * (b + 1), g * D : (g + 1) * D] = block[24 * g : 24 * (g + 1)]
            down_ref[96 * b : 96 * (b + 1), :] = block[96:192]
            out_ref[24 * b : 24 * (b + 1), :] = block[192:216]
            if b == 0:
                vec_ref[...] = block[216:224]


def mid_rows(blocks):
    return pl.pallas_call(
        mid_kernel,
        out_shape=(
            shape(GD, 4 * D, dtype=F32), shape(D, D, dtype=F32), shape(GD, D, dtype=F32),
            shape(8, D, dtype=F32),
        ),
        in_specs=[VM],
        out_specs=(VM,) * 4,
        compiler_params=PARAMS,
        cost_estimate=pl.CostEstimate(flops=10**6, bytes_accessed=8 * 10**6, transcendentals=0),
    )(blocks)


def tail_kernel(
    at_ref, dkv_ref, dq_ref, h1_ref, n1_ref, w_ref, vec_ref, mid_ref, dh_ref, t_ref, rest_ref, scr
):
    yi, zi = at_ref[0], at_ref[1]
    scr[...] = (mid_ref[0].astype(F32) + mid_ref[1].astype(F32)) + (
        mid_ref[2].astype(F32) + mid_ref[3].astype(F32)
    )
    rest_ref[...] = scr[96:208, :].astype(BF)
    for s in range(4):
        start = (zi + s) % 4 * 24
        part = jnp.concatenate(
            [
                scr[pl.ds(pl.multiple_of(start, 8), 24), :],
                scr[pl.ds(pl.multiple_of(208 + start, 8), 24), :],
            ],
            axis=0,
        )
        t_ref[s, 192:240] = part[:, :640].astype(BF)
        t_ref[s, 240:, :128] = part[:, 640:].astype(BF)
        t_ref[s, 240:, 128:] = jnp.zeros((48, 512), BF)
    d_qkv = jnp.concatenate([dkv_ref[...], dq_ref[...]], axis=1)
    d_h1 = dot_t(d_qkv[:, : 3 * GD], w_ref[...])
    dh_ref[...] = d_h1.astype(BF)
    sums = jnp.sum(d_qkv.astype(F32), axis=0, keepdims=True)
    at_own = lambda v: jnp.concatenate([jnp.where(yi == k, v, 0.0) for k in range(4)], axis=1)
    vectors = jnp.concatenate(
        [
            jnp.sum(d_h1 * n1_ref[...], axis=0, keepdims=True),
            jnp.sum(d_h1, axis=0, keepdims=True),
            at_own(sums[:, 2 * GD : 3 * GD]),
            at_own(sums[:, GD : 2 * GD]),
            vec_ref[4:8, :],
        ],
        axis=0,
    ).astype(BF)
    row = lax.broadcasted_iota(jnp.int32, (8, 128), 0)
    lane = lax.broadcasted_iota(jnp.int32, (8, 128), 1)
    columns = t_dot(vectors, jnp.where(lane == row + 64, 1.0, 0.0).astype(BF))
    grad = t_dot(h1_ref[...], d_qkv)
    for g in range(4):
        rows = slice(g * GD, (g + 1) * GD)
        slot = (g - zi + 4) % 4
        t_ref[slot, :GD, :512] = grad[rows, :512].astype(BF)
        t_ref[slot, :GD, 512:] = (grad[rows, 512:] + columns[rows]).astype(BF)


def last_gradients(at, d_kv, d_q, h1, n1, w, vec, mid):
    return staged(
        tail_kernel,
        (shape(ROWS, D), shape(4, 288, 640), shape(112, D)),
        (at,), (d_kv, d_q, h1, n1, w, vec, mid),
        scratch=[pltpu.VMEM((304, D), F32)],
        flops=3 * 10**9,
    )


def sum_kernel(at_ref, t_ref, r1, r2, r3, dh_ref, rest_ref, kept_ref, given_ref, same_ref, block_ref, scr):
    same_ref[...] = dh_ref[...]
    slots = (r1, r2, r3)
    for c in range(2):
        rows = slice(96 * c, 96 * (c + 1))
        a, b, d, e = (v.astype(F32) for v in [t_ref[0, rows]] + [r[rows] for r in slots])
        total = ((a + d) + (b + e)).astype(BF)

        @pl.when(at_ref[2] == c)
        def _():
            kept_ref[...] = total

        @pl.when(at_ref[2] != c)
        def _():
            given_ref[...] = total

    for s in range(4):
        part = (t_ref[0, GD:] if s == 0 else slots[s - 1][GD:]).astype(F32)
        scr[s, :, :640] = part[:48]
        scr[s, :, 640:] = part[48:, :128]
    up = [scr[(at_ref[1] - g + 4) % 4][:24] for g in range(4)]
    g_out = (scr[0] + scr[2])[24:] + (scr[1] + scr[3])[24:]
    rest = rest_ref[...].astype(F32)
    block_ref[...] = jnp.concatenate(up + [rest[:96], g_out, rest[96:]], axis=0).astype(BF)


def sum_slots(at, own, slots, d_h1, rest):
    return pl.pallas_call(
        sum_kernel,
        out_shape=(shape(96, 640), shape(96, 640), shape(ROWS, D), shape(232, D)),
        in_specs=[SMEM] + [VM] * 6,
        out_specs=(VM,) * 4,
        scratch_shapes=[pltpu.VMEM((4, 48, D), F32)],
        compiler_params=PARAMS,
        cost_estimate=pl.CostEstimate(flops=10**6, bytes_accessed=3 * 10**6, transcendentals=0),
    )(at, own, *slots, d_h1, rest)


def final_kernel(at_ref, *refs):
    slots, (grad_ref, vec_ref, scr) = refs[:4], refs[4:]
    for s in range(4):
        for c in range(2):
            scr[s, c] = slots[s][c]
    yi, ci = at_ref[0], at_ref[2]
    for c in range(2):
        rows = slice(96 * c, 96 * (c + 1))
        total = []
        for g in range(4):
            value = scr[(yi - g + 4) % 4, (ci + c) % 2].astype(F32)
            for i, part in enumerate((1, 2, 0)):
                start = part * D + g * GD
                grad_ref[rows, start : start + GD] = value[:, i * GD : (i + 1) * GD]
            total.append(value[:, 512:])
        vec_ref[rows, :] = (total[0] + total[1]) + (total[2] + total[3])


def final_rows(at, slots):
    return pl.pallas_call(
        final_kernel,
        out_shape=(shape(GD, 3 * D, dtype=F32), shape(GD, 128, dtype=F32)),
        in_specs=[SMEM] + [VM] * 4,
        out_specs=(VM, VM),
        scratch_shapes=[pltpu.VMEM((4, 2, 96, 640), BF)],
        compiler_params=PARAMS,
        cost_estimate=pl.CostEstimate(flops=10**6, bytes_accessed=3 * 10**6, transcendentals=0),
    )(at, *slots)


def gather(value, axes, axis=0):
    return lax.all_gather(value, axes, axis=axis, tiled=True)


def swap(value, axes):
    return lax.all_to_all(value, axes, 0, 0)


def send(value, axis, step):
    n = lax.axis_size(axis)
    return lax.ppermute(value, axis, [(i, (i + step) % n) for i in range(n)])


def spread(value, axis):
    return [value] + [send(value, axis, s) for s in range(1, 4)]


def exchange(slots, axis, step):
    return [slots[0]] + [send(slots[s], axis, s * step) for s in range(1, 4)]


def add_slots(slots):
    a, b, c, d = (v.astype(F32) for v in slots)
    return (a + c) + (b + d)


def group_of(value, index, size, axis=0):
    return lax.dynamic_slice_in_dim(value, (index % 4) * size, size, axis)


def local(
    tokens, qkv_w, out_w, up_w, down_w, norm_gains, biases, value_bias, up_bias, cotangent, block_place
):
    xi = lax.axis_index("x")
    yi = lax.axis_index("y")
    ci = lax.axis_index("core")
    zi = lax.axis_index("fsdp")
    tok_own = tokens[0]
    cot_own = cotangent[0]

    at = jnp.stack([yi, zi, ci]).astype(jnp.int32)
    own_cols, both = prepare(at, qkv_w, norm_gains, biases, value_bias[None], cot_own, out_w)
    ws = spread(own_cols, "fsdp")
    toks = spread(tok_own, "y")

    ids = jnp.arange(NBLK, dtype=jnp.int32)
    slot_x, slot_c, slot_y, blk = ids // 16, (ids // 8) % 2, (ids // 2) % 4, ids % 2
    pick = lambda at: jnp.sum(jnp.where(at[:, None] == ids[None, :], block_place[None, :], 0), axis=1)
    at_y = (yi - slot_y + 4) % 4
    key_place = pick(at_y * 16 + ((xi - slot_x + 4) % 4) * 4 + ((ci + slot_c) % 2) * 2 + blk)
    query_place = pick(at_y * 16 + slot_x * 4 + slot_c * 2 + blk)
    own_place = key_place[:8]
    rank = jnp.sum((own_place[None, :] > own_place[:, None]).astype(jnp.int32), axis=1)
    order = jnp.arange(8, dtype=jnp.int32)
    hit = rank[None, :] == order[:, None]
    own = jnp.sum(jnp.where(hit, order[None, :], 0), axis=1)
    place = jnp.sum(jnp.where(hit, own_place[None, :], 0), axis=1)

    both = lax.all_gather(both, "fsdp", axis=0)
    w_out = jnp.concatenate(
        [lax.dynamic_index_in_dim(both, (yi + s) % 4, 0, keepdims=False)[128:] for s in range(4)], axis=0
    )
    w_up = gather(up_w, "fsdp")
    w_down = down_w

    kv_own, query, h1, n1y, w_qkv, small = first_rows(at, toks, ws)
    gain1, gain2 = small[0], small[1]
    out_bias, shift2, down_bias = small[4], small[5], small[6]
    with jax.named_scope("kv"):
        kv_all = [p for v in spread(kv_own, "x") for p in (v, send(v, "core", 1))]
    attn, o_exact, qe, ks, vs = attention_forward(key_place, own, place, query, kv_all)
    qe_all = gather(qe, XC)

    attn = attn[:, 64:]
    with jax.named_scope("attn_y"):
        attn_own = exchange([attn[128 * s : 128 * (s + 1)] for s in range(4)], "y", -1)
    attn_own = jnp.concatenate(attn_own, axis=1)
    x2 = tok_own.astype(F32) + (dot(attn_own, w_out) + out_bias)
    n2, s2 = normalize(x2)
    h2_own = (n2 * gain2 + shift2).astype(BF)

    with jax.named_scope("h2_z"):
        h2s = spread(h2_own, "fsdp")
    h2, cot_z, act, d_up, d_h2_part = feed_forward(
        at, h2s, both, w_up, w_down, up_bias[None]
    )
    keep, give, down = weight_blocks(at, h2, d_up, act, cot_z, w_down)
    with jax.named_scope("mid"):
        mid = add_blocks(keep, send(give, "core", 1)).reshape(832, D)
        mid = lax.psum_scatter(mid, "y", scatter_dimension=0, tiled=True)
    back = lambda v: add_slots(exchange([v[128 * s : 128 * (s + 1)] for s in range(4)], "fsdp", -1))
    with jax.named_scope("d_h2_z"):
        d_h2 = back(d_h2_part)
    cot32 = cot_own.astype(F32)
    d_x2 = cot32 + norm_back(d_h2 * gain2, n2, s2)
    d_branch = d_x2.astype(BF)
    d_attn = dot_t(d_branch, w_out).astype(BF)
    with jax.named_scope("d_attn_y"):
        d_attn_own = exchange([d_attn[:, GD * s : GD * (s + 1)] for s in range(4)], "y", 1)
    d_attn_own = jnp.concatenate(d_attn_own, axis=0)
    de = delta_rows(d_attn_own, o_exact, qe_all)
    with jax.named_scope("de"):
        de_all = [p for v in spread(de, "x") for p in (v, send(v, "core", 1))]
    d_q_half = attention_dq((0, 3), own, place, qe, de, ks, vs)
    d_q = attention_dq((1, 2), own, place, qe, de, ks, vs, (d_q_half,), (de_all[2], de_all[4], de_all[6]))

    with jax.named_scope("down"):
        layer_out = (x2 + back(down) + down_bias).astype(BF)
    keep, give = output_blocks(at, attn_own, d_branch, de)
    with jax.named_scope("mid_out"):
        mid_out = add_blocks(keep, send(give, "core", 1)).reshape(384, D)
        mid_out = lax.psum_scatter(mid_out, "y", scatter_dimension=0, tiled=True)
    with jax.named_scope("mid"):
        mid = lax.all_gather(join_blocks(mid, mid_out, d_q_half), "x", axis=0)
    d_kv = attention_dkv(query_place, key_place, own, place, kv_own, qe_all, de_all, layer_out)

    vec = jnp.stack([jnp.sum(d_h2 * n2, axis=0), jnp.sum(d_branch.astype(F32), axis=0), jnp.sum(d_h2, axis=0)])
    vec = jnp.pad(vec, ((4, 1), (0, 0)))
    d_h1_send, tail, rest = last_gradients(at, d_kv, d_q, h1, n1y, w_qkv, vec, mid)
    with jax.named_scope("tail_z"):
        received = [send(tail[s], "fsdp", s) for s in range(1, 4)]
    kept, given, d_h1_send, mid = sum_slots(at, tail, received, d_h1_send, rest)
    with jax.named_scope("mid"):
        mid = lax.all_gather(mid, ("y", "core"), axis=0)
    grad_up, grad_down, grad_out, out_vec = mid_rows(mid)
    grad_up_bias = out_vec[0]
    grad_down_bias = lax.dynamic_slice(out_vec[1], (zi * GD,), (GD,))
    with jax.named_scope("d_h1_y"):
        d_h1 = add_slots(exchange([d_h1_send[128 * s : 128 * (s + 1)] for s in range(4)], "y", -1))
    n1, s1 = normalize(tok_own.astype(F32))
    input_grad = (d_x2 + norm_back(d_h1 * gain1, n1, s1)).astype(BF)

    with jax.named_scope("tail_core"):
        tail = (kept.astype(F32) + send(given, "core", 1).astype(F32)).astype(BF)
    with jax.named_scope("tail_x"):
        tail = add_slots(spread(tail, "x")).astype(BF)
    with jax.named_scope("tail_y"):
        tail = [jnp.stack([v, send(v, "core", 1)]) for v in spread(tail, "y")]
    grad_qkv, vectors = final_rows(at, tail)
    vectors = vectors[:, 64:71].T
    grad_gains = jnp.stack([vectors[0], vectors[4]])
    grad_biases = jnp.stack([vectors[1], vectors[2], vectors[5], vectors[6], grad_down_bias])
    grad_value_bias = vectors[3]
    return (
        layer_out[None], input_grad[None], grad_qkv, grad_out, grad_up, grad_down,
        grad_gains, grad_biases, grad_value_bias, grad_up_bias,
    )


def solution(mesh):
    grid = Mesh(mesh.devices.reshape(4, 4, 2, 4), ("y", "x", "core", "fsdp"))
    rows = P("fsdp", CTX, None)
    in_specs = (
        rows, P("fsdp", None), P("fsdp", None), P("fsdp", None), P("fsdp", None),
        P(None, "fsdp"), P(None, "fsdp"), P("fsdp"), P("fsdp"), rows, P(),
    )
    out_specs = (
        rows, rows, P("fsdp", None), P("fsdp", None), P("fsdp", None), P("fsdp", None),
        P(None, "fsdp"), P(None, "fsdp"), P("fsdp"), P("fsdp"),
    )
    return jax.shard_map(local, mesh=grid, in_specs=in_specs, out_specs=out_specs, check_vma=False)
```

```python
import functools

import jax
import jax.numpy as jnp
from jax import lax
from jax.experimental import pallas as pl
from jax.experimental.pallas import tpu as pltpu
from jax.sharding import Mesh
from jax.sharding import PartitionSpec as P

EPS = 1e-05
D = 768
GD = 192
NH = 3
HD = 64
ROWS = 512
LEN = 4096
BLK = 64
NBLK = 64
EXT = 256
TILE = 1024
CHUNK = 128
BF = jnp.bfloat16
F32 = jnp.float32
XC = ("x", "core")
CTX = ("y", "x", "core")


def dot(a, b):
    return lax.dot_general(a, b, (((1,), (0,)), ((), ())), preferred_element_type=F32)


def dot_t(a, b):
    return lax.dot_general(a, b, (((1,), (1,)), ((), ())), preferred_element_type=F32)


def t_dot(a, b):
    return lax.dot_general(a, b, (((0,), (0,)), ((), ())), preferred_element_type=F32)


def normalize(value):
    center = value - jnp.mean(value, axis=-1, keepdims=True)
    factor = lax.rsqrt(jnp.mean(center * center, axis=-1, keepdims=True) + EPS)
    return (center * factor, factor)


def norm_back(scaled, normed, factor):
    return factor * (
        scaled
        - jnp.mean(scaled, axis=-1, keepdims=True)
        - normed * jnp.mean(scaled * normed, axis=-1, keepdims=True)
    )


def lanes(rows):
    return lax.broadcasted_iota(jnp.int32, (rows, EXT), 1)


def head_mask(rows, h, high):
    lane = lanes(rows)
    if high:
        feat = (lane >= 64 + HD * h) & (lane < 64 + HD * (h + 1))
        ext = (lane >= 3 * h) & (lane < 3 * h + 3)
    else:
        feat = (lane >= HD * h) & (lane < HD * (h + 1))
        ext = (lane >= GD + 3 * h) & (lane < GD + 3 * h + 3)
    return feat | ext


def feature_mask(rows, h, high):
    lane = lanes(rows) - (64 if high else 0)
    return (lane >= HD * h) & (lane < HD * (h + 1))


def stack_heads(value, high):
    rows = value.shape[0]
    zero = jnp.zeros_like(value)
    return jnp.concatenate(
        [jnp.where(head_mask(rows, h, high), value, zero) for h in range(NH)], axis=0
    )


def merge_heads(stacked, high):
    rows = stacked.shape[0] // NH
    out = jnp.zeros((rows, EXT), F32)
    for h in range(NH):
        out = out + jnp.where(feature_mask(rows, h, high), stacked[h * rows : (h + 1) * rows], 0.0)
    return out


def pieces(value):
    first = value.astype(BF).astype(F32)
    second = (value - first).astype(BF).astype(F32)
    third = (value - first - second).astype(BF).astype(F32)
    return (first, second, third)


def add_extras(base, columns, high):
    rows = base.shape[0]
    lane = lanes(rows)
    start = 0 if high else GD
    for h in range(NH):
        for i, piece in enumerate(pieces(columns[h])):
            base = jnp.where(lane == start + 3 * h + i, piece, base)
    return base


def key_form(kv):
    lane = lanes(kv.shape[0])
    one = jnp.ones((kv.shape[0], EXT), BF)
    zero = jnp.zeros((kv.shape[0], EXT), BF)
    low = jnp.where(lane < GD, kv[:, :EXT], jnp.where(lane < GD + 9, one, zero))
    high = jnp.where(lane >= 64, kv[:, 128:384], jnp.where(lane < 9, one, zero))
    return (low, high)


def block_rows(index):
    return pl.ds(pl.multiple_of(index * BLK, BLK), BLK)


def stacked_pos(place_a, place_b):
    row = lax.broadcasted_iota(jnp.int32, (NH * CHUNK, 1), 0)
    place = jnp.where(row % CHUNK < BLK, place_a, place_b)
    return place * BLK + row % BLK


def col_pos(tile):
    return tile * TILE + lax.broadcasted_iota(jnp.int32, (NH * CHUNK, TILE), 1)


def fold(value, op):
    out = value[:, :128]
    for i in range(1, value.shape[1] // 128):
        out = op(out, value[:, i * 128 : (i + 1) * 128])
    return out


def tile_rows(t):
    return pl.ds(pl.multiple_of(t * TILE, TILE), TILE)


def fwd_kernel(
    kplace_ref, own_ref, place_ref, q_ref, *refs
):
    kv_refs = refs[:8]
    attn_ref, o_ref, qe_ref, ks_ref, vs_ref, s_scr, m_scr, l_scr, acc_scr, land, sems = refs[8:]
    copies = [pltpu.make_async_copy(kv_refs[k], land.at[k], sems.at[k]) for k in range(8)]
    for copy in copies:
        copy.start()
    for k in range(8):
        copies[k].wait()
        for b in range(8):
            low, high = key_form(land[k, b * BLK : (b + 1) * BLK, :])
            dst = block_rows(kplace_ref[8 * k + b])
            ks_ref[dst, :] = low
            vs_ref[dst, :] = high

    for c in range(ROWS // CHUNK):
        place_a, place_b = place_ref[2 * c], place_ref[2 * c + 1]
        blocks = (own_ref[2 * c], own_ref[2 * c + 1])
        query = jnp.concatenate([q_ref[block_rows(b), :] for b in blocks], axis=0)
        stacked = stack_heads(query, False)
        qpos = stacked_pos(place_a, place_b)
        tiles = place_a // (TILE // BLK) + 1
        m_scr[...] = jnp.full(m_scr.shape, -1e30, F32)

        def score_step(t, _):
            scores = dot_t(stacked, ks_ref[tile_rows(t), :])
            scores = jnp.where(col_pos(t) <= qpos, scores, -1e30)
            s_scr[t] = scores
            m_scr[...] = jnp.maximum(m_scr[...], fold(scores, jnp.maximum))
            return 0

        lax.fori_loop(0, tiles, score_step, 0)
        peak = jnp.max(m_scr[...], axis=1, keepdims=True)
        l_scr[...] = jnp.zeros(l_scr.shape, F32)
        acc_scr[...] = jnp.zeros(acc_scr.shape, F32)

        def value_step(t, _):
            prob = jnp.exp(s_scr[t] - peak)
            l_scr[...] = l_scr[...] + fold(prob, jnp.add)
            acc_scr[...] = acc_scr[...] + dot(prob.astype(BF), vs_ref[tile_rows(t), :])
            return 0

        lax.fori_loop(0, tiles, value_step, 0)
        total = jnp.sum(l_scr[...], axis=1, keepdims=True)
        log_total = peak + jnp.log(total)
        out = merge_heads(acc_scr[...] / total, True)
        ext = add_extras(
            query.astype(F32),
            [-log_total[h * CHUNK : (h + 1) * CHUNK] for h in range(NH)],
            False,
        ).astype(BF)
        for i, b in enumerate(blocks):
            rows = slice(i * BLK, (i + 1) * BLK)
            o_ref[block_rows(b), :] = out[rows]
            attn_ref[block_rows(b), :] = out[rows].astype(BF)
            qe_ref[block_rows(b), :] = ext[rows]


def dq_kernel(chunks, n_before, own_ref, place_ref, qe_ref, de_ref, ks_ref, vs_ref, *refs):
    *before, dq_ref, acc_scr = refs
    if n_before:
        dq_ref[...] = before[0][...]
    for c in chunks:
        place_a, place_b = place_ref[2 * c], place_ref[2 * c + 1]
        blocks = (own_ref[2 * c], own_ref[2 * c + 1])
        query = stack_heads(jnp.concatenate([qe_ref[block_rows(b), :] for b in blocks], axis=0), False)
        d_out = stack_heads(jnp.concatenate([de_ref[block_rows(b), :] for b in blocks], axis=0), True)
        qpos = stacked_pos(place_a, place_b)
        tiles = place_a // (TILE // BLK) + 1
        acc_scr[...] = jnp.zeros(acc_scr.shape, F32)

        def step(t, _):
            keys = ks_ref[tile_rows(t), :]
            prob = jnp.where(col_pos(t) <= qpos, jnp.exp(dot_t(query, keys)), 0.0)
            d_raw = (prob * dot_t(d_out, vs_ref[tile_rows(t), :])).astype(BF)
            acc_scr[...] = acc_scr[...] + dot(d_raw, keys)
            return 0

        lax.fori_loop(0, tiles, step, 0)
        out = (merge_heads(acc_scr[...], False) * 0.125).astype(BF)
        for i, b in enumerate(blocks):
            dq_ref[block_rows(b), :] = out[i * BLK : (i + 1) * BLK]


def dkv_kernel(qplace_ref, kplace_ref, own_ref, place_ref, kv_ref, qe_ref, *refs):
    de_refs, (dkv_ref, qs_scr, ds_scr, dk_scr, dv_scr, q_land, d_land, sems) = refs[:8], refs[10:]
    q_copy = pltpu.make_async_copy(qe_ref, q_land, sems.at[8])
    q_copy.start()
    copies = [pltpu.make_async_copy(de_refs[k], d_land.at[k], sems.at[k]) for k in range(8)]
    for copy in copies:
        copy.start()
    q_copy.wait()
    for b in range(NBLK):
        qs_scr[block_rows(qplace_ref[b]), :] = q_land[b * BLK : (b + 1) * BLK, :]
    for k in range(8):
        copies[k].wait()
        for b in range(8):
            ds_scr[block_rows(kplace_ref[8 * k + b]), :] = d_land[k, b * BLK : (b + 1) * BLK, :]

    for c in range(ROWS // CHUNK):
        place_a, place_b = place_ref[2 * c], place_ref[2 * c + 1]
        blocks = (own_ref[2 * c], own_ref[2 * c + 1])
        low, high = key_form(jnp.concatenate([kv_ref[block_rows(b), :] for b in blocks], axis=0))
        keys = stack_heads(low, False)
        values = stack_heads(high, True)
        kpos = stacked_pos(place_a, place_b)
        dk_scr[...] = jnp.zeros(dk_scr.shape, F32)
        dv_scr[...] = jnp.zeros(dv_scr.shape, F32)

        def step(t, _):
            query = qs_scr[tile_rows(t), :]
            d_out = ds_scr[tile_rows(t), :]
            prob = jnp.where(col_pos(t) >= kpos, jnp.exp(dot_t(keys, query)), 0.0)
            d_raw = (prob * dot_t(values, d_out)).astype(BF)
            dv_scr[...] = dv_scr[...] + dot(prob.astype(BF), d_out)
            dk_scr[...] = dk_scr[...] + dot(d_raw, query)
            return 0

        lax.fori_loop(place_b // (TILE // BLK), LEN // TILE, step, 0)
        d_keys = merge_heads(dk_scr[...], False)
        d_values = merge_heads(dv_scr[...], True)
        out = jnp.concatenate(
            [d_keys[:, :128], d_keys[:, 128:] + d_values[:, :128], d_values[:, 128:]], axis=1
        ).astype(BF)
        for i, b in enumerate(blocks):
            dkv_ref[block_rows(b), :] = out[i * BLK : (i + 1) * BLK]


def delta_kernel(d_ref, o_ref, early_a, early_b, de_ref):
    d_out = jnp.concatenate([jnp.zeros((ROWS, 64), F32), d_ref[...].astype(F32)], axis=1)
    product = d_out * o_ref[...]
    sums = [
        -jnp.sum(jnp.where(feature_mask(ROWS, h, True), product, 0.0), axis=1, keepdims=True)
        for h in range(NH)
    ]
    de_ref[...] = add_extras(d_out, sums, True).astype(BF)


SMEM = pl.BlockSpec(memory_space=pltpu.SMEM)
VM = pl.BlockSpec(memory_space=pltpu.VMEM)
ANY = pl.BlockSpec(memory_space=pl.ANY)
PARAMS = pltpu.CompilerParams(vmem_limit_bytes=48 * 1024 * 1024)


def shape(*dims, dtype=BF):
    return jax.ShapeDtypeStruct(dims, dtype)


def attention_forward(kplace, own, place, query, kv):
    return pl.pallas_call(
        fwd_kernel,
        out_shape=(
            shape(ROWS, EXT), shape(ROWS, EXT, dtype=F32), shape(ROWS, EXT),
            shape(LEN, EXT), shape(LEN, EXT),
        ),
        in_specs=[SMEM] * 3 + [VM] + [ANY] * 8,
        out_specs=(VM,) * 5,
        scratch_shapes=[
            pltpu.VMEM((LEN // TILE, NH * CHUNK, TILE), F32),
            pltpu.VMEM((NH * CHUNK, 128), F32),
            pltpu.VMEM((NH * CHUNK, 128), F32),
            pltpu.VMEM((NH * CHUNK, EXT), F32),
            pltpu.VMEM((8, ROWS, 2 * GD), BF),
            pltpu.SemaphoreType.DMA((8,)),
        ],
        compiler_params=PARAMS,
        cost_estimate=pl.CostEstimate(flops=16 * 10**9, bytes_accessed=10**7, transcendentals=4 * 10**6),
    )(kplace, own, place, query, *kv)


def attention_dq(chunks, own, place, qe, de, ks, vs, before=(), early=()):
    return pl.pallas_call(
        functools.partial(dq_kernel, chunks, len(before)),
        out_shape=shape(ROWS, EXT),
        in_specs=[SMEM] * 2 + [VM] * (4 + len(before)) + [ANY] * len(early),
        out_specs=VM,
        scratch_shapes=[pltpu.VMEM((NH * CHUNK, EXT), F32)],
        compiler_params=PARAMS,
        cost_estimate=pl.CostEstimate(flops=8 * 10**9, bytes_accessed=5 * 10**6, transcendentals=2 * 10**6),
    )(own, place, qe, de, ks, vs, *before, *early)


def attention_dkv(qplace, kplace, own, place, kv, qe, de, early):
    return pl.pallas_call(
        dkv_kernel,
        out_shape=shape(ROWS, 2 * GD),
        in_specs=[SMEM] * 4 + [VM] + [ANY] * 11,
        out_specs=VM,
        scratch_shapes=[
            pltpu.VMEM((LEN, EXT), BF),
            pltpu.VMEM((LEN, EXT), BF),
            pltpu.VMEM((NH * CHUNK, EXT), F32),
            pltpu.VMEM((NH * CHUNK, EXT), F32),
            pltpu.VMEM((LEN, EXT), BF),
            pltpu.VMEM((8, ROWS, EXT), BF),
            pltpu.SemaphoreType.DMA((9,)),
        ],
        compiler_params=PARAMS,
        cost_estimate=pl.CostEstimate(flops=15 * 10**9, bytes_accessed=10**7, transcendentals=4 * 10**6),
    )(qplace, kplace, own, place, kv, qe, *de, *early)


def delta_rows(d_attn, o, early):
    return pl.pallas_call(
        delta_kernel,
        out_shape=shape(ROWS, EXT),
        in_specs=[VM] * 2 + [ANY] * 2,
        out_specs=VM,
        compiler_params=PARAMS,
        cost_estimate=pl.CostEstimate(flops=10**6, bytes_accessed=10**6, transcendentals=0),
    )(d_attn, o, *early)


def prep_kernel(at_ref, w_ref, gain_ref, bias_ref, vb_ref, cols_ref):
    for k in range(4):

        @pl.when(at_ref[0] == k)
        def _():
            for i, part in enumerate((1, 2, 0)):
                start = part * D + k * GD
                cols_ref[:GD, i * GD : (i + 1) * GD] = w_ref[:, start : start + GD]

    small = jnp.concatenate(
        [gain_ref[...].astype(F32), bias_ref[...].astype(F32), vb_ref[...].astype(F32), jnp.zeros((8, GD), F32)],
        axis=0,
    )
    cols_ref[GD:, :] = jnp.concatenate([small, jnp.zeros((16, 2 * GD), F32)], axis=1).astype(BF)


def prepare(at, w, gains, biases, vb):
    return pl.pallas_call(
        prep_kernel,
        out_shape=shape(GD + 16, 3 * GD),
        in_specs=[SMEM] + [VM] * 4,
        out_specs=VM,
        compiler_params=PARAMS,
        cost_estimate=pl.CostEstimate(flops=1000, bytes_accessed=10**6, transcendentals=0),
    )(at, w, gains, biases, vb)


def qkv_kernel(at_ref, *refs):
    toks, ws = refs[:4], refs[4:8]
    kv_ref, q_ref, h1_ref, n1_ref, w_ref, small_ref, w_scr = refs[8:]
    yi, zi = at_ref[0], at_ref[1]
    for s in range(4):
        w_scr[s] = ws[s][...]
    for g in range(4):
        slot = (zi - g + 4) % 4
        w_ref[g * GD : (g + 1) * GD, :] = w_scr[slot, :GD]
        small_ref[:, g * GD : (g + 1) * GD] = w_scr[slot, GD:, :256].astype(F32)[:8, :GD]
    gain, shift = small_ref[0:1, :], small_ref[2:3, :]
    for s in range(4):
        rows = slice(128 * s, 128 * (s + 1))
        normed, _ = normalize(toks[s][...].astype(F32))
        n1_ref[rows, :] = normed
        h1_ref[rows, :] = (normed * gain + shift).astype(BF)
    own = w_scr[(zi - yi + 4) % 4, GD:, :256].astype(F32)[:8, :GD]
    qkv = dot(h1_ref[...], w_ref[...])
    kv_ref[:, :GD] = qkv[:, :GD].astype(BF)
    kv_ref[:, GD:] = (qkv[:, GD : 2 * GD] + own[7:8]).astype(BF)
    query = (qkv[:, 2 * GD :] + own[3:4]).astype(BF).astype(F32) * 0.125
    q_ref[...] = jnp.concatenate([query, jnp.zeros((ROWS, EXT - GD), F32)], axis=1).astype(BF)


def first_rows(at, toks, ws):
    return pl.pallas_call(
        qkv_kernel,
        out_shape=(
            shape(ROWS, 2 * GD), shape(ROWS, EXT), shape(ROWS, D), shape(ROWS, D, dtype=F32),
            shape(D, 3 * GD), shape(8, D, dtype=F32),
        ),
        in_specs=[SMEM] + [VM] * 8,
        out_specs=(VM,) * 6,
        scratch_shapes=[pltpu.VMEM((4, GD + 16, 3 * GD), BF)],
        compiler_params=PARAMS,
        cost_estimate=pl.CostEstimate(flops=5 * 10**8, bytes_accessed=6 * 10**6, transcendentals=0),
    )(at, *toks, *ws)


def mlp_kernel(at_ref, *refs):
    h2s = refs[:4]
    both_ref, all_ref, down_ref, ub_ref, h2_ref, cot_ref, act_ref, dup_ref, dh_ref, up_ref, cots, sems = refs[4:]
    zi = at_ref[1]
    up_copy = pltpu.make_async_copy(
        all_ref.at[:, pl.ds(pl.multiple_of(zi * D, D), D)], up_ref, sems.at[4]
    )
    up_copy.start()
    copies = [
        pltpu.make_async_copy(both_ref.at[(zi - s + 4) % 4, :128], cots.at[s], sems.at[s])
        for s in range(4)
    ]
    for copy in copies:
        copy.start()
    for copy in copies:
        copy.wait()
    up_copy.wait()
    for s in range(4):
        rows = slice(128 * s, 128 * (s + 1))
        h2 = h2s[s][...]
        cot = cots[s]
        h2_ref[rows, :] = h2
        cot_ref[rows, :] = cot
        up = dot(h2, up_ref[...]) + ub_ref[...].astype(F32)
        d_act = dot_t(cot, down_ref[...])
        square = up * up
        th = jnp.tanh(0.7978845608028654 * (up + 0.044715 * (square * up)))
        half = 0.5 * (1.0 + th)
        slope = half + 0.5 * up * (1.0 - th * th) * (
            0.7978845608028654 * (1.0 + 3 * 0.044715 * square)
        )
        act_ref[rows, :] = (up * half).astype(BF)
        d_up = (slope * d_act).astype(BF)
        dup_ref[rows, :] = d_up
        dh_ref[rows, :] = dot_t(d_up, up_ref[...]).astype(BF)


def feed_forward(at, h2s, cots, w_up, w_down, ub):
    return pl.pallas_call(
        mlp_kernel,
        out_shape=(shape(ROWS, D),) * 5,
        in_specs=[SMEM] + [VM] * 4 + [ANY] * 2 + [VM] * 2,
        out_specs=(VM,) * 5,
        scratch_shapes=[
            pltpu.VMEM((D, D), BF), pltpu.VMEM((4, 128, D), BF), pltpu.SemaphoreType.DMA((5,)),
        ],
        compiler_params=PARAMS,
        cost_estimate=pl.CostEstimate(flops=4 * 10**9, bytes_accessed=6 * 10**6, transcendentals=4 * 10**5),
    )(at, *h2s, cots, w_up, w_down, ub)


def wgrad_kernel(
    at_ref, h2_ref, dup_ref, act_ref, cot_ref, wd_ref, keep_ref, give_ref, down_ref
):
    ci = at_ref[2]
    g_up = t_dot(h2_ref[...], dup_ref[...])
    g_down = t_dot(act_ref[...], cot_ref[...])
    vec = jnp.concatenate(
        [
            jnp.sum(dup_ref[...].astype(F32), axis=0, keepdims=True),
            jnp.sum(cot_ref[...].astype(F32), axis=0, keepdims=True),
            jnp.zeros((14, D), F32),
        ],
        axis=0,
    )
    for c in range(2):
        for j in range(4):
            b = 4 * c + j
            parts = [g_up[GD * z + 24 * b : GD * z + 24 * (b + 1)] for z in range(4)]
            parts += [g_down[96 * b : 96 * (b + 1)], vec]
            block = jnp.concatenate(parts, axis=0).astype(BF)

            @pl.when(ci == c)
            def _():
                keep_ref[j] = block

            @pl.when(ci != c)
            def _():
                give_ref[j] = block
    down_ref[...] = dot(act_ref[...], wd_ref[...]).astype(BF)


def weight_blocks(at, h2, d_up, act, cot, w_down):
    return pl.pallas_call(
        wgrad_kernel,
        out_shape=(shape(4, 208, D), shape(4, 208, D), shape(ROWS, D)),
        in_specs=[SMEM] + [VM] * 5,
        out_specs=(VM,) * 3,
        compiler_params=PARAMS,
        cost_estimate=pl.CostEstimate(flops=5 * 10**9, bytes_accessed=6 * 10**6, transcendentals=0),
    )(at, h2, d_up, act, cot, w_down)


def ograd_kernel(at_ref, attn_ref, branch_ref, early_ref, keep_ref, give_ref, out_scr):
    yi, ci = at_ref[0], at_ref[2]
    g_out = t_dot(attn_ref[...], branch_ref[...])
    for s in range(4):
        out_scr[s] = g_out[GD * s : GD * (s + 1)]
    for c in range(2):
        for j in range(4):
            b = 4 * c + j
            block = jnp.concatenate(
                [out_scr[(z - yi + 4) % 4, 24 * b : 24 * (b + 1)] for z in range(4)], axis=0
            ).astype(BF)

            @pl.when(ci == c)
            def _():
                keep_ref[j] = block

            @pl.when(ci != c)
            def _():
                give_ref[j] = block


def output_blocks(at, attn, d_branch, early):
    return pl.pallas_call(
        ograd_kernel,
        out_shape=(shape(4, 96, D), shape(4, 96, D)),
        in_specs=[SMEM] + [VM] * 2 + [ANY],
        out_specs=(VM,) * 2,
        scratch_shapes=[pltpu.VMEM((4, GD, D), F32)],
        compiler_params=PARAMS,
        cost_estimate=pl.CostEstimate(flops=10**9, bytes_accessed=2 * 10**6, transcendentals=0),
    )(at, attn, d_branch, early)


def add_kernel(a_ref, b_ref, out_ref):
    for s in range(4):
        out_ref[s] = (a_ref[s].astype(F32) + b_ref[s].astype(F32)).astype(BF)


def add_blocks(a, b):
    return pl.pallas_call(
        add_kernel,
        out_shape=shape(*a.shape),
        in_specs=[VM] * 2,
        out_specs=VM,
        compiler_params=PARAMS,
        cost_estimate=pl.CostEstimate(flops=10**6, bytes_accessed=6 * 10**6, transcendentals=0),
    )(a, b)


def part_kernel(at_ref, in_ref, early_ref, rest_ref, *refs):
    parts, scr = refs[:4], refs[4]
    scr[...] = (in_ref[0].astype(F32) + in_ref[1].astype(F32)) + (
        in_ref[2].astype(F32) + in_ref[3].astype(F32)
    )
    rest_ref[...] = scr[96:208, :].astype(BF)
    for s in range(4):
        start = (at_ref[1] + s) % 4 * 24
        parts[s][...] = jnp.concatenate(
            [
                scr[pl.ds(pl.multiple_of(start, 8), 24), :],
                scr[pl.ds(pl.multiple_of(208 + start, 8), 24), :],
            ],
            axis=0,
        ).astype(BF)


def part_blocks(at, value, early):
    return pl.pallas_call(
        part_kernel,
        out_shape=(shape(112, D),) + (shape(48, D),) * 4,
        in_specs=[SMEM, VM, ANY],
        out_specs=(VM,) * 5,
        scratch_shapes=[pltpu.VMEM((304, D), F32)],
        compiler_params=PARAMS,
        cost_estimate=pl.CostEstimate(flops=10**6, bytes_accessed=3 * 10**6, transcendentals=0),
    )(at, value, early)


def join_kernel(at_ref, rest_ref, *refs):
    slots, (out_ref, scr) = refs[:4], refs[4:]
    for s in range(4):
        scr[s] = slots[s][...].astype(F32)
    up = [scr[(at_ref[1] - g + 4) % 4][:24] for g in range(4)]
    g_out = (scr[0] + scr[2])[24:] + (scr[1] + scr[3])[24:]
    rest = rest_ref[...].astype(F32)
    out_ref[...] = jnp.concatenate(up + [rest[:96], g_out, rest[96:]], axis=0).astype(BF)


def join_blocks(at, rest, slots):
    return pl.pallas_call(
        join_kernel,
        out_shape=shape(232, D),
        in_specs=[SMEM, VM] + [VM] * 4,
        out_specs=VM,
        scratch_shapes=[pltpu.VMEM((4, 48, D), F32)],
        compiler_params=PARAMS,
        cost_estimate=pl.CostEstimate(flops=10**6, bytes_accessed=10**6, transcendentals=0),
    )(at, rest, *slots)


def mid_kernel(blocks_ref, up_ref, down_ref, out_ref, vec_ref):
    for c in range(2):
        for j in range(4):
            b = 4 * c + j
            block = blocks_ref[2 * j + c].astype(F32)
            for g in range(4):
                up_ref[24 * b : 24 * (b + 1), g * D : (g + 1) * D] = block[24 * g : 24 * (g + 1)]
            down_ref[96 * b : 96 * (b + 1), :] = block[96:192]
            out_ref[24 * b : 24 * (b + 1), :] = block[192:216]
            if b == 0:
                vec_ref[...] = block[216:224]


def mid_rows(blocks):
    return pl.pallas_call(
        mid_kernel,
        out_shape=(
            shape(GD, 4 * D, dtype=F32), shape(D, D, dtype=F32), shape(GD, D, dtype=F32),
            shape(8, D, dtype=F32),
        ),
        in_specs=[VM],
        out_specs=(VM,) * 4,
        compiler_params=PARAMS,
        cost_estimate=pl.CostEstimate(flops=10**6, bytes_accessed=8 * 10**6, transcendentals=0),
    )(blocks)


def tail_kernel(at_ref, dkv_ref, dq_ref, h1_ref, n1_ref, w_ref, vec_ref, dh_ref, t_ref):
    yi, zi = at_ref[0], at_ref[1]
    d_qkv = jnp.concatenate([dkv_ref[...], dq_ref[...]], axis=1)
    d_h1 = dot_t(d_qkv[:, : 3 * GD], w_ref[...])
    dh_ref[...] = d_h1.astype(BF)
    sums = jnp.sum(d_qkv.astype(F32), axis=0, keepdims=True)
    at_own = lambda v: jnp.concatenate([jnp.where(yi == k, v, 0.0) for k in range(4)], axis=1)
    vectors = jnp.concatenate(
        [
            jnp.sum(d_h1 * n1_ref[...], axis=0, keepdims=True),
            jnp.sum(d_h1, axis=0, keepdims=True),
            at_own(sums[:, 2 * GD : 3 * GD]),
            at_own(sums[:, GD : 2 * GD]),
            vec_ref[4:8, :],
        ],
        axis=0,
    ).astype(BF)
    row = lax.broadcasted_iota(jnp.int32, (8, 128), 0)
    lane = lax.broadcasted_iota(jnp.int32, (8, 128), 1)
    columns = t_dot(vectors, jnp.where(lane == row + 64, 1.0, 0.0).astype(BF))
    grad = t_dot(h1_ref[...], d_qkv)
    for g in range(4):
        rows = slice(g * GD, (g + 1) * GD)
        slot = (g - zi + 4) % 4
        t_ref[slot, :, :512] = grad[rows, :512].astype(BF)
        t_ref[slot, :, 512:] = (grad[rows, 512:] + columns[rows]).astype(BF)


def last_gradients(at, d_kv, d_q, h1, n1, w, vec):
    return pl.pallas_call(
        tail_kernel,
        out_shape=(shape(ROWS, D), shape(4, GD, 640)),
        in_specs=[SMEM] + [VM] * 6,
        out_specs=(VM, VM),
        compiler_params=PARAMS,
        cost_estimate=pl.CostEstimate(flops=3 * 10**9, bytes_accessed=6 * 10**6, transcendentals=0),
    )(at, d_kv, d_q, h1, n1, w, vec)


def sum_kernel(at_ref, t_ref, *refs):
    slots, (dh_ref, kept_ref, given_ref, same_ref) = refs[:3], refs[3:]
    same_ref[...] = dh_ref[...]
    for c in range(2):
        rows = slice(96 * c, 96 * (c + 1))
        a, b, d, e = (v.astype(F32) for v in [t_ref[0, rows]] + [r[rows] for r in slots])
        total = ((a + d) + (b + e)).astype(BF)

        @pl.when(at_ref[2] == c)
        def _():
            kept_ref[...] = total

        @pl.when(at_ref[2] != c)
        def _():
            given_ref[...] = total


def sum_slots(at, own, slots, d_h1):
    return pl.pallas_call(
        sum_kernel,
        out_shape=(shape(96, 640), shape(96, 640), shape(ROWS, D)),
        in_specs=[SMEM] + [VM] * 5,
        out_specs=(VM,) * 3,
        compiler_params=PARAMS,
        cost_estimate=pl.CostEstimate(flops=10**6, bytes_accessed=3 * 10**6, transcendentals=0),
    )(at, own, *slots, d_h1)


def final_kernel(at_ref, *refs):
    slots, (grad_ref, vec_ref, scr) = refs[:4], refs[4:]
    for s in range(4):
        for c in range(2):
            scr[s, c] = slots[s][c]
    yi, ci = at_ref[0], at_ref[2]
    for c in range(2):
        rows = slice(96 * c, 96 * (c + 1))
        total = []
        for g in range(4):
            value = scr[(yi - g + 4) % 4, (ci + c) % 2].astype(F32)
            for i, part in enumerate((1, 2, 0)):
                start = part * D + g * GD
                grad_ref[rows, start : start + GD] = value[:, i * GD : (i + 1) * GD]
            total.append(value[:, 512:])
        vec_ref[rows, :] = (total[0] + total[1]) + (total[2] + total[3])


def final_rows(at, slots):
    return pl.pallas_call(
        final_kernel,
        out_shape=(shape(GD, 3 * D, dtype=F32), shape(GD, 128, dtype=F32)),
        in_specs=[SMEM] + [VM] * 4,
        out_specs=(VM, VM),
        scratch_shapes=[pltpu.VMEM((4, 2, 96, 640), BF)],
        compiler_params=PARAMS,
        cost_estimate=pl.CostEstimate(flops=10**6, bytes_accessed=3 * 10**6, transcendentals=0),
    )(at, *slots)


def gather(value, axes, axis=0):
    return lax.all_gather(value, axes, axis=axis, tiled=True)


def swap(value, axes):
    return lax.all_to_all(value, axes, 0, 0)


def send(value, axis, step):
    n = lax.axis_size(axis)
    return lax.ppermute(value, axis, [(i, (i + step) % n) for i in range(n)])


def spread(value, axis):
    return [value] + [send(value, axis, s) for s in range(1, 4)]


def exchange(slots, axis, step):
    return [slots[0]] + [send(slots[s], axis, s * step) for s in range(1, 4)]


def add_slots(slots):
    a, b, c, d = (v.astype(F32) for v in slots)
    return (a + c) + (b + d)


def group_of(value, index, size, axis=0):
    return lax.dynamic_slice_in_dim(value, (index % 4) * size, size, axis)


def local(
    tokens, qkv_w, out_w, up_w, down_w, norm_gains, biases, value_bias, up_bias, cotangent, block_place
):
    xi = lax.axis_index("x")
    yi = lax.axis_index("y")
    ci = lax.axis_index("core")
    zi = lax.axis_index("fsdp")
    tok_own = tokens[0]
    cot_own = cotangent[0]

    at = jnp.stack([yi, zi, ci]).astype(jnp.int32)
    ws = spread(prepare(at, qkv_w, norm_gains, biases, value_bias[None]), "fsdp")
    toks = spread(tok_own, "y")

    ids = jnp.arange(NBLK, dtype=jnp.int32)
    slot_x, slot_c, slot_y, blk = ids // 16, (ids // 8) % 2, (ids // 2) % 4, ids % 2
    pick = lambda at: jnp.sum(jnp.where(at[:, None] == ids[None, :], block_place[None, :], 0), axis=1)
    at_y = (yi - slot_y + 4) % 4
    key_place = pick(at_y * 16 + ((xi - slot_x + 4) % 4) * 4 + ((ci + slot_c) % 2) * 2 + blk)
    query_place = pick(at_y * 16 + slot_x * 4 + slot_c * 2 + blk)
    own_place = key_place[:8]
    rank = jnp.sum((own_place[None, :] > own_place[:, None]).astype(jnp.int32), axis=1)
    order = jnp.arange(8, dtype=jnp.int32)
    hit = rank[None, :] == order[:, None]
    own = jnp.sum(jnp.where(hit, order[None, :], 0), axis=1)
    place = jnp.sum(jnp.where(hit, own_place[None, :], 0), axis=1)

    both = lax.all_gather(jnp.concatenate([cot_own, out_w], axis=0), "fsdp", axis=0)
    w_out = jnp.concatenate(
        [lax.dynamic_index_in_dim(both, (yi + s) % 4, 0, keepdims=False)[128:] for s in range(4)], axis=0
    )
    w_up = gather(up_w, "fsdp")
    w_down = down_w

    kv_own, query, h1, n1y, w_qkv, small = first_rows(at, toks, ws)
    gain1, gain2 = small[0], small[1]
    out_bias, shift2, down_bias = small[4], small[5], small[6]
    with jax.named_scope("kv"):
        kv_all = [p for v in spread(kv_own, "x") for p in (v, send(v, "core", 1))]
    attn, o_exact, qe, ks, vs = attention_forward(key_place, own, place, query, kv_all)
    qe_all = gather(qe, XC)

    attn = attn[:, 64:]
    with jax.named_scope("attn_y"):
        attn_own = exchange([attn[128 * s : 128 * (s + 1)] for s in range(4)], "y", -1)
    attn_own = jnp.concatenate(attn_own, axis=1)
    x2 = tok_own.astype(F32) + (dot(attn_own, w_out) + out_bias)
    n2, s2 = normalize(x2)
    h2_own = (n2 * gain2 + shift2).astype(BF)

    with jax.named_scope("h2_z"):
        h2s = spread(h2_own, "fsdp")
    h2, cot_z, act, d_up, d_h2_part = feed_forward(
        at, h2s, both, w_up, w_down, up_bias[None]
    )
    keep, give, down = weight_blocks(at, h2, d_up, act, cot_z, w_down)
    with jax.named_scope("mid"):
        mid_in = add_blocks(keep, send(give, "core", 1))
        mid = lax.psum_scatter(mid_in.reshape(832, D), "y", scatter_dimension=0, tiled=True)
    back = lambda v: add_slots(exchange([v[128 * s : 128 * (s + 1)] for s in range(4)], "fsdp", -1))
    with jax.named_scope("d_h2_z"):
        d_h2 = back(d_h2_part)
    cot32 = cot_own.astype(F32)
    d_x2 = cot32 + norm_back(d_h2 * gain2, n2, s2)
    d_branch = d_x2.astype(BF)
    d_attn = dot_t(d_branch, w_out).astype(BF)
    with jax.named_scope("d_attn_y"):
        d_attn_own = exchange([d_attn[:, GD * s : GD * (s + 1)] for s in range(4)], "y", 1)
    d_attn_own = jnp.concatenate(d_attn_own, axis=0)
    de = delta_rows(d_attn_own, o_exact, (qe_all, mid_in))
    with jax.named_scope("de"):
        de_all = [p for v in spread(de, "x") for p in (v, send(v, "core", 1))]

    with jax.named_scope("down"):
        layer_out = (x2 + back(down) + down_bias).astype(BF)
    keep, give = output_blocks(at, attn_own, d_branch, de)
    with jax.named_scope("mid_out"):
        mid_out = add_blocks(keep, send(give, "core", 1)).reshape(384, D)
        mid_out = lax.psum_scatter(mid_out, "y", scatter_dimension=0, tiled=True)
    d_q = attention_dq((0, 3), own, place, qe, de, ks, vs)
    d_q = attention_dq((1, 2), own, place, qe, de, ks, vs, (d_q,), (de_all[2], de_all[4], de_all[6], mid))
    d_kv = attention_dkv(
        query_place, key_place, own, place, kv_own, qe_all, de_all, (layer_out, mid_out)
    )
    with jax.named_scope("mid"):
        mid = lax.all_gather(jnp.concatenate([mid, mid_out], axis=0), "x", axis=0)

    vec = jnp.stack([jnp.sum(d_h2 * n2, axis=0), jnp.sum(d_branch.astype(F32), axis=0), jnp.sum(d_h2, axis=0)])
    vec = jnp.pad(vec, ((4, 1), (0, 0)))
    d_h1_send, tail = last_gradients(at, d_kv, d_q, h1, n1y, w_qkv, vec)
    with jax.named_scope("tail_z"):
        received = [send(tail[s], "fsdp", s) for s in range(1, 4)]
    kept, given, d_h1_send = sum_slots(at, tail, received, d_h1_send)
    with jax.named_scope("mid"):
        rest, *parts = part_blocks(at, mid, kept)
        parts = exchange(parts, "fsdp", 1)
        mid = lax.all_gather(join_blocks(at, rest, parts), ("y", "core"), axis=0)
    grad_up, grad_down, grad_out, out_vec = mid_rows(mid)
    grad_up_bias = out_vec[0]
    grad_down_bias = lax.dynamic_slice(out_vec[1], (zi * GD,), (GD,))
    with jax.named_scope("d_h1_y"):
        d_h1 = add_slots(exchange([d_h1_send[128 * s : 128 * (s + 1)] for s in range(4)], "y", -1))
    n1, s1 = normalize(tok_own.astype(F32))
    input_grad = (d_x2 + norm_back(d_h1 * gain1, n1, s1)).astype(BF)

    with jax.named_scope("tail_core"):
        tail = (kept.astype(F32) + send(given, "core", 1).astype(F32)).astype(BF)
    with jax.named_scope("tail_x"):
        tail = add_slots(spread(tail, "x")).astype(BF)
    with jax.named_scope("tail_y"):
        tail = [jnp.stack([v, send(v, "core", 1)]) for v in spread(tail, "y")]
    grad_qkv, vectors = final_rows(at, tail)
    vectors = vectors[:, 64:71].T
    grad_gains = jnp.stack([vectors[0], vectors[4]])
    grad_biases = jnp.stack([vectors[1], vectors[2], vectors[5], vectors[6], grad_down_bias])
    grad_value_bias = vectors[3]
    return (
        layer_out[None], input_grad[None], grad_qkv, grad_out, grad_up, grad_down,
        grad_gains, grad_biases, grad_value_bias, grad_up_bias,
    )


def solution(mesh):
    grid = Mesh(mesh.devices.reshape(4, 4, 2, 4), ("y", "x", "core", "fsdp"))
    rows = P("fsdp", CTX, None)
    in_specs = (
        rows, P("fsdp", None), P("fsdp", None), P("fsdp", None), P("fsdp", None),
        P(None, "fsdp"), P(None, "fsdp"), P("fsdp"), P("fsdp"), rows, P(),
    )
    out_specs = (
        rows, rows, P("fsdp", None), P("fsdp", None), P("fsdp", None), P("fsdp", None),
        P(None, "fsdp"), P(None, "fsdp"), P("fsdp"), P("fsdp"),
    )
    return jax.shard_map(local, mesh=grid, in_specs=in_specs, out_specs=out_specs, check_vma=False)
```

```python
import functools

import jax
import jax.numpy as jnp
from jax import lax
from jax.experimental import pallas as pl
from jax.experimental.pallas import tpu as pltpu
from jax.sharding import Mesh
from jax.sharding import PartitionSpec as P

EPS = 1e-05
D = 768
GD = 192
NH = 3
HD = 64
ROWS = 512
LEN = 4096
BLK = 64
NBLK = 64
EXT = 256
TILE = 1024
CHUNK = 128
BF = jnp.bfloat16
F32 = jnp.float32
XC = ("x", "core")
CTX = ("y", "x", "core")


def dot(a, b):
    return lax.dot_general(a, b, (((1,), (0,)), ((), ())), preferred_element_type=F32)


def dot_t(a, b):
    return lax.dot_general(a, b, (((1,), (1,)), ((), ())), preferred_element_type=F32)


def t_dot(a, b):
    return lax.dot_general(a, b, (((0,), (0,)), ((), ())), preferred_element_type=F32)


def normalize(value):
    center = value - jnp.mean(value, axis=-1, keepdims=True)
    factor = lax.rsqrt(jnp.mean(center * center, axis=-1, keepdims=True) + EPS)
    return (center * factor, factor)


def norm_back(scaled, normed, factor):
    return factor * (
        scaled
        - jnp.mean(scaled, axis=-1, keepdims=True)
        - normed * jnp.mean(scaled * normed, axis=-1, keepdims=True)
    )


def lanes(rows):
    return lax.broadcasted_iota(jnp.int32, (rows, EXT), 1)


def head_mask(rows, h, high):
    lane = lanes(rows)
    if high:
        feat = (lane >= 64 + HD * h) & (lane < 64 + HD * (h + 1))
        ext = (lane >= 3 * h) & (lane < 3 * h + 3)
    else:
        feat = (lane >= HD * h) & (lane < HD * (h + 1))
        ext = (lane >= GD + 3 * h) & (lane < GD + 3 * h + 3)
    return feat | ext


def feature_mask(rows, h, high):
    lane = lanes(rows) - (64 if high else 0)
    return (lane >= HD * h) & (lane < HD * (h + 1))


def stack_heads(value, high):
    rows = value.shape[0]
    zero = jnp.zeros_like(value)
    return jnp.concatenate(
        [jnp.where(head_mask(rows, h, high), value, zero) for h in range(NH)], axis=0
    )


def merge_heads(stacked, high):
    rows = stacked.shape[0] // NH
    out = jnp.zeros((rows, EXT), F32)
    for h in range(NH):
        out = out + jnp.where(feature_mask(rows, h, high), stacked[h * rows : (h + 1) * rows], 0.0)
    return out


def pieces(value):
    first = value.astype(BF).astype(F32)
    second = (value - first).astype(BF).astype(F32)
    third = (value - first - second).astype(BF).astype(F32)
    return (first, second, third)


def add_extras(base, columns, high):
    rows = base.shape[0]
    lane = lanes(rows)
    start = 0 if high else GD
    for h in range(NH):
        for i, piece in enumerate(pieces(columns[h])):
            base = jnp.where(lane == start + 3 * h + i, piece, base)
    return base


def key_form(kv):
    lane = lanes(kv.shape[0])
    one = jnp.ones((kv.shape[0], EXT), BF)
    zero = jnp.zeros((kv.shape[0], EXT), BF)
    low = jnp.where(lane < GD, kv[:, :EXT], jnp.where(lane < GD + 9, one, zero))
    high = jnp.where(lane >= 64, kv[:, 128:384], jnp.where(lane < 9, one, zero))
    return (low, high)


def block_rows(index):
    return pl.ds(pl.multiple_of(index * BLK, BLK), BLK)


def stacked_pos(place_a, place_b):
    row = lax.broadcasted_iota(jnp.int32, (NH * CHUNK, 1), 0)
    place = jnp.where(row % CHUNK < BLK, place_a, place_b)
    return place * BLK + row % BLK


def col_pos(tile):
    return tile * TILE + lax.broadcasted_iota(jnp.int32, (NH * CHUNK, TILE), 1)


def fold(value, op):
    out = value[:, :128]
    for i in range(1, value.shape[1] // 128):
        out = op(out, value[:, i * 128 : (i + 1) * 128])
    return out


def tile_rows(t):
    return pl.ds(pl.multiple_of(t * TILE, TILE), TILE)


def fwd_kernel(
    kplace_ref, own_ref, place_ref, q_ref, *refs
):
    kv_refs = refs[:8]
    attn_ref, o_ref, qe_ref, ks_ref, vs_ref, s_scr, m_scr, l_scr, acc_scr, land, sems = refs[9:]
    copies = [pltpu.make_async_copy(kv_refs[k], land.at[k], sems.at[k]) for k in range(8)]
    for copy in copies:
        copy.start()
    for k in range(8):
        copies[k].wait()
        for b in range(8):
            low, high = key_form(land[k, b * BLK : (b + 1) * BLK, :])
            dst = block_rows(kplace_ref[8 * k + b])
            ks_ref[dst, :] = low
            vs_ref[dst, :] = high

    for c in range(ROWS // CHUNK):
        place_a, place_b = place_ref[2 * c], place_ref[2 * c + 1]
        blocks = (own_ref[2 * c], own_ref[2 * c + 1])
        query = jnp.concatenate([q_ref[block_rows(b), :] for b in blocks], axis=0)
        stacked = stack_heads(query, False)
        qpos = stacked_pos(place_a, place_b)
        tiles = place_a // (TILE // BLK) + 1
        m_scr[...] = jnp.full(m_scr.shape, -1e30, F32)

        def score_step(t, _):
            scores = dot_t(stacked, ks_ref[tile_rows(t), :])
            scores = jnp.where(col_pos(t) <= qpos, scores, -1e30)
            s_scr[t] = scores
            m_scr[...] = jnp.maximum(m_scr[...], fold(scores, jnp.maximum))
            return 0

        lax.fori_loop(0, tiles, score_step, 0)
        peak = jnp.max(m_scr[...], axis=1, keepdims=True)
        l_scr[...] = jnp.zeros(l_scr.shape, F32)
        acc_scr[...] = jnp.zeros(acc_scr.shape, F32)

        def value_step(t, _):
            prob = jnp.exp(s_scr[t] - peak)
            l_scr[...] = l_scr[...] + fold(prob, jnp.add)
            acc_scr[...] = acc_scr[...] + dot(prob.astype(BF), vs_ref[tile_rows(t), :])
            return 0

        lax.fori_loop(0, tiles, value_step, 0)
        total = jnp.sum(l_scr[...], axis=1, keepdims=True)
        log_total = peak + jnp.log(total)
        out = merge_heads(acc_scr[...] / total, True)
        ext = add_extras(
            query.astype(F32),
            [-log_total[h * CHUNK : (h + 1) * CHUNK] for h in range(NH)],
            False,
        ).astype(BF)
        for i, b in enumerate(blocks):
            rows = slice(i * BLK, (i + 1) * BLK)
            o_ref[block_rows(b), :] = out[rows]
            attn_ref[block_rows(b), :] = out[rows].astype(BF)
            qe_ref[block_rows(b), :] = ext[rows]


def dq_kernel(chunks, n_before, own_ref, place_ref, qe_ref, de_ref, ks_ref, vs_ref, *refs):
    *before, dq_ref, acc_scr = refs
    if n_before:
        dq_ref[...] = before[0][...]
    for c in chunks:
        place_a, place_b = place_ref[2 * c], place_ref[2 * c + 1]
        blocks = (own_ref[2 * c], own_ref[2 * c + 1])
        query = stack_heads(jnp.concatenate([qe_ref[block_rows(b), :] for b in blocks], axis=0), False)
        d_out = stack_heads(jnp.concatenate([de_ref[block_rows(b), :] for b in blocks], axis=0), True)
        qpos = stacked_pos(place_a, place_b)
        tiles = place_a // (TILE // BLK) + 1
        acc_scr[...] = jnp.zeros(acc_scr.shape, F32)

        def step(t, _):
            keys = ks_ref[tile_rows(t), :]
            prob = jnp.where(col_pos(t) <= qpos, jnp.exp(dot_t(query, keys)), 0.0)
            d_raw = (prob * dot_t(d_out, vs_ref[tile_rows(t), :])).astype(BF)
            acc_scr[...] = acc_scr[...] + dot(d_raw, keys)
            return 0

        lax.fori_loop(0, tiles, step, 0)
        out = (merge_heads(acc_scr[...], False) * 0.125).astype(BF)
        for i, b in enumerate(blocks):
            dq_ref[block_rows(b), :] = out[i * BLK : (i + 1) * BLK]


def dkv_kernel(qplace_ref, kplace_ref, own_ref, place_ref, kv_ref, qe_ref, *refs):
    de_refs, (dkv_ref, qs_scr, ds_scr, dk_scr, dv_scr, q_land, d_land, sems) = refs[:8], refs[10:]
    q_copy = pltpu.make_async_copy(qe_ref, q_land, sems.at[8])
    q_copy.start()
    copies = [pltpu.make_async_copy(de_refs[k], d_land.at[k], sems.at[k]) for k in range(8)]
    for copy in copies:
        copy.start()
    q_copy.wait()
    for b in range(NBLK):
        qs_scr[block_rows(qplace_ref[b]), :] = q_land[b * BLK : (b + 1) * BLK, :]
    for k in range(8):
        copies[k].wait()
        for b in range(8):
            ds_scr[block_rows(kplace_ref[8 * k + b]), :] = d_land[k, b * BLK : (b + 1) * BLK, :]

    for c in range(ROWS // CHUNK):
        place_a, place_b = place_ref[2 * c], place_ref[2 * c + 1]
        blocks = (own_ref[2 * c], own_ref[2 * c + 1])
        low, high = key_form(jnp.concatenate([kv_ref[block_rows(b), :] for b in blocks], axis=0))
        keys = stack_heads(low, False)
        values = stack_heads(high, True)
        kpos = stacked_pos(place_a, place_b)
        dk_scr[...] = jnp.zeros(dk_scr.shape, F32)
        dv_scr[...] = jnp.zeros(dv_scr.shape, F32)

        def step(t, _):
            query = qs_scr[tile_rows(t), :]
            d_out = ds_scr[tile_rows(t), :]
            prob = jnp.where(col_pos(t) >= kpos, jnp.exp(dot_t(keys, query)), 0.0)
            d_raw = (prob * dot_t(values, d_out)).astype(BF)
            dv_scr[...] = dv_scr[...] + dot(prob.astype(BF), d_out)
            dk_scr[...] = dk_scr[...] + dot(d_raw, query)
            return 0

        lax.fori_loop(place_b // (TILE // BLK), LEN // TILE, step, 0)
        d_keys = merge_heads(dk_scr[...], False)
        d_values = merge_heads(dv_scr[...], True)
        out = jnp.concatenate(
            [d_keys[:, :128], d_keys[:, 128:] + d_values[:, :128], d_values[:, 128:]], axis=1
        ).astype(BF)
        for i, b in enumerate(blocks):
            dkv_ref[block_rows(b), :] = out[i * BLK : (i + 1) * BLK]


def delta_kernel(d_ref, o_ref, early_a, early_b, de_ref):
    d_out = jnp.concatenate([jnp.zeros((ROWS, 64), F32), d_ref[...].astype(F32)], axis=1)
    product = d_out * o_ref[...]
    sums = [
        -jnp.sum(jnp.where(feature_mask(ROWS, h, True), product, 0.0), axis=1, keepdims=True)
        for h in range(NH)
    ]
    de_ref[...] = add_extras(d_out, sums, True).astype(BF)


SMEM = pl.BlockSpec(memory_space=pltpu.SMEM)
VM = pl.BlockSpec(memory_space=pltpu.VMEM)
ANY = pl.BlockSpec(memory_space=pl.ANY)
PARAMS = pltpu.CompilerParams(vmem_limit_bytes=48 * 1024 * 1024)


def shape(*dims, dtype=BF):
    return jax.ShapeDtypeStruct(dims, dtype)


def attention_forward(kplace, own, place, query, kv, early):
    return pl.pallas_call(
        fwd_kernel,
        out_shape=(
            shape(ROWS, EXT), shape(ROWS, EXT, dtype=F32), shape(ROWS, EXT),
            shape(LEN, EXT), shape(LEN, EXT),
        ),
        in_specs=[SMEM] * 3 + [VM] + [ANY] * 9,
        out_specs=(VM,) * 5,
        scratch_shapes=[
            pltpu.VMEM((LEN // TILE, NH * CHUNK, TILE), F32),
            pltpu.VMEM((NH * CHUNK, 128), F32),
            pltpu.VMEM((NH * CHUNK, 128), F32),
            pltpu.VMEM((NH * CHUNK, EXT), F32),
            pltpu.VMEM((8, ROWS, 2 * GD), BF),
            pltpu.SemaphoreType.DMA((8,)),
        ],
        compiler_params=PARAMS,
        cost_estimate=pl.CostEstimate(flops=16 * 10**9, bytes_accessed=10**7, transcendentals=4 * 10**6),
    )(kplace, own, place, query, *kv, early)


def attention_dq(chunks, own, place, qe, de, ks, vs, before=(), early=()):
    return pl.pallas_call(
        functools.partial(dq_kernel, chunks, len(before)),
        out_shape=shape(ROWS, EXT),
        in_specs=[SMEM] * 2 + [VM] * (4 + len(before)) + [ANY] * len(early),
        out_specs=VM,
        scratch_shapes=[pltpu.VMEM((NH * CHUNK, EXT), F32)],
        compiler_params=PARAMS,
        cost_estimate=pl.CostEstimate(flops=8 * 10**9, bytes_accessed=5 * 10**6, transcendentals=2 * 10**6),
    )(own, place, qe, de, ks, vs, *before, *early)


def attention_dkv(qplace, kplace, own, place, kv, qe, de, early):
    return pl.pallas_call(
        dkv_kernel,
        out_shape=shape(ROWS, 2 * GD),
        in_specs=[SMEM] * 4 + [VM] + [ANY] * 11,
        out_specs=VM,
        scratch_shapes=[
            pltpu.VMEM((LEN, EXT), BF),
            pltpu.VMEM((LEN, EXT), BF),
            pltpu.VMEM((NH * CHUNK, EXT), F32),
            pltpu.VMEM((NH * CHUNK, EXT), F32),
            pltpu.VMEM((LEN, EXT), BF),
            pltpu.VMEM((8, ROWS, EXT), BF),
            pltpu.SemaphoreType.DMA((9,)),
        ],
        compiler_params=PARAMS,
        cost_estimate=pl.CostEstimate(flops=15 * 10**9, bytes_accessed=10**7, transcendentals=4 * 10**6),
    )(qplace, kplace, own, place, kv, qe, *de, *early)


def delta_rows(d_attn, o, early):
    return pl.pallas_call(
        delta_kernel,
        out_shape=shape(ROWS, EXT),
        in_specs=[VM] * 2 + [ANY] * 2,
        out_specs=VM,
        compiler_params=PARAMS,
        cost_estimate=pl.CostEstimate(flops=10**6, bytes_accessed=10**6, transcendentals=0),
    )(d_attn, o, *early)


def prep_kernel(at_ref, w_ref, gain_ref, bias_ref, vb_ref, cols_ref):
    for k in range(4):

        @pl.when(at_ref[0] == k)
        def _():
            for i, part in enumerate((1, 2, 0)):
                start = part * D + k * GD
                cols_ref[:GD, i * GD : (i + 1) * GD] = w_ref[:, start : start + GD]

    small = jnp.concatenate(
        [gain_ref[...].astype(F32), bias_ref[...].astype(F32), vb_ref[...].astype(F32), jnp.zeros((8, GD), F32)],
        axis=0,
    )
    cols_ref[GD:, :] = jnp.concatenate([small, jnp.zeros((16, 2 * GD), F32)], axis=1).astype(BF)


def prepare(at, w, gains, biases, vb):
    return pl.pallas_call(
        prep_kernel,
        out_shape=shape(GD + 16, 3 * GD),
        in_specs=[SMEM] + [VM] * 4,
        out_specs=VM,
        compiler_params=PARAMS,
        cost_estimate=pl.CostEstimate(flops=1000, bytes_accessed=10**6, transcendentals=0),
    )(at, w, gains, biases, vb)


def qkv_kernel(at_ref, *refs):
    toks, ws = refs[:4], refs[4:8]
    cot_ref, out_ref = refs[8:10]
    kv_ref, q_ref, h1_ref, n1_ref, w_ref, small_ref, both_ref, w_scr = refs[10:]
    both_ref[:128, :] = cot_ref[...]
    both_ref[128:, :] = out_ref[...]
    yi, zi = at_ref[0], at_ref[1]
    for s in range(4):
        w_scr[s] = ws[s][...]
    for g in range(4):
        slot = (zi - g + 4) % 4
        w_ref[g * GD : (g + 1) * GD, :] = w_scr[slot, :GD]
        small_ref[:, g * GD : (g + 1) * GD] = w_scr[slot, GD:, :256].astype(F32)[:8, :GD]
    gain, shift = small_ref[0:1, :], small_ref[2:3, :]
    for s in range(4):
        rows = slice(128 * s, 128 * (s + 1))
        normed, _ = normalize(toks[s][...].astype(F32))
        n1_ref[rows, :] = normed
        h1_ref[rows, :] = (normed * gain + shift).astype(BF)
    own = w_scr[(zi - yi + 4) % 4, GD:, :256].astype(F32)[:8, :GD]
    qkv = dot(h1_ref[...], w_ref[...])
    kv_ref[:, :GD] = qkv[:, :GD].astype(BF)
    kv_ref[:, GD:] = (qkv[:, GD : 2 * GD] + own[7:8]).astype(BF)
    query = (qkv[:, 2 * GD :] + own[3:4]).astype(BF).astype(F32) * 0.125
    q_ref[...] = jnp.concatenate([query, jnp.zeros((ROWS, EXT - GD), F32)], axis=1).astype(BF)


def first_rows(at, toks, ws, cot, out_w):
    return pl.pallas_call(
        qkv_kernel,
        out_shape=(
            shape(ROWS, 2 * GD), shape(ROWS, EXT), shape(ROWS, D), shape(ROWS, D, dtype=F32),
            shape(D, 3 * GD), shape(8, D, dtype=F32), shape(320, D),
        ),
        in_specs=[SMEM] + [VM] * 10,
        out_specs=(VM,) * 7,
        scratch_shapes=[pltpu.VMEM((4, GD + 16, 3 * GD), BF)],
        compiler_params=PARAMS,
        cost_estimate=pl.CostEstimate(flops=5 * 10**8, bytes_accessed=6 * 10**6, transcendentals=0),
    )(at, *toks, *ws, cot, out_w)


def mlp_kernel(at_ref, *refs):
    h2s = refs[:4]
    both_ref, up_ref, down_ref, ub_ref, h2_ref, cot_ref, act_ref, dup_ref, dh_ref, sems = refs[4:]
    zi = at_ref[1]
    copies = [
        pltpu.make_async_copy(
            both_ref.at[(zi - s + 4) % 4, :128], cot_ref.at[128 * s : 128 * (s + 1)], sems.at[s]
        )
        for s in range(4)
    ]
    for copy in copies:
        copy.start()
    for copy in copies:
        copy.wait()
    for s in range(4):
        rows = slice(128 * s, 128 * (s + 1))
        h2 = h2s[s][...]
        h2_ref[rows, :] = h2
        up = dot(h2, up_ref[...]) + ub_ref[...].astype(F32)
        d_act = dot_t(cot_ref[rows, :], down_ref[...])
        square = up * up
        th = jnp.tanh(0.7978845608028654 * (up + 0.044715 * (square * up)))
        half = 0.5 * (1.0 + th)
        slope = half + 0.5 * up * (1.0 - th * th) * (
            0.7978845608028654 * (1.0 + 3 * 0.044715 * square)
        )
        act_ref[rows, :] = (up * half).astype(BF)
        d_up = (slope * d_act).astype(BF)
        dup_ref[rows, :] = d_up
        dh_ref[rows, :] = dot_t(d_up, up_ref[...]).astype(BF)


def feed_forward(at, h2s, both, w_up, w_down, ub):
    return pl.pallas_call(
        mlp_kernel,
        out_shape=(shape(ROWS, D),) * 5,
        in_specs=[SMEM] + [VM] * 4 + [ANY] + [VM] * 3,
        out_specs=(VM,) * 5,
        scratch_shapes=[pltpu.SemaphoreType.DMA((4,))],
        compiler_params=PARAMS,
        cost_estimate=pl.CostEstimate(flops=4 * 10**9, bytes_accessed=6 * 10**6, transcendentals=4 * 10**5),
    )(at, *h2s, both, w_up, w_down, ub)


def down_kernel(act_ref, wd_ref, early_ref, down_ref):
    down_ref[...] = dot(act_ref[...], wd_ref[...]).astype(BF)


def down_rows(act, w_down, early):
    return pl.pallas_call(
        down_kernel,
        out_shape=shape(ROWS, D),
        in_specs=[VM] * 2 + [ANY],
        out_specs=VM,
        compiler_params=PARAMS,
        cost_estimate=pl.CostEstimate(flops=10**9, bytes_accessed=3 * 10**6, transcendentals=0),
    )(act, w_down, early)


def hold_kernel(*refs):
    for s in range(3):
        refs[4 + s][...] = refs[s][...]


def hold_back(values, early):
    return pl.pallas_call(
        hold_kernel,
        out_shape=tuple(shape(*v.shape) for v in values),
        in_specs=[VM] * 3 + [ANY],
        out_specs=(VM,) * 3,
        compiler_params=PARAMS,
        cost_estimate=pl.CostEstimate(flops=1000, bytes_accessed=10**6, transcendentals=0),
    )(*values, early)


def wgrad_kernel(
    at_ref, h2_ref, dup_ref, act_ref, cot_ref, early_ref, keep_ref, give_ref
):
    ci = at_ref[2]
    g_up = t_dot(h2_ref[...], dup_ref[...])
    g_down = t_dot(act_ref[...], cot_ref[...])
    vec = jnp.concatenate(
        [
            jnp.sum(dup_ref[...].astype(F32), axis=0, keepdims=True),
            jnp.sum(cot_ref[...].astype(F32), axis=0, keepdims=True),
            jnp.zeros((14, D), F32),
        ],
        axis=0,
    )
    for c in range(2):
        for j in range(4):
            b = 4 * c + j
            parts = [g_up[GD * z + 24 * b : GD * z + 24 * (b + 1)] for z in range(4)]
            parts += [g_down[96 * b : 96 * (b + 1)], vec]
            block = jnp.concatenate(parts, axis=0).astype(BF)

            @pl.when(ci == c)
            def _():
                keep_ref[j] = block

            @pl.when(ci != c)
            def _():
                give_ref[j] = block


def weight_blocks(at, h2, d_up, act, cot, early):
    return pl.pallas_call(
        wgrad_kernel,
        out_shape=(shape(4, 208, D), shape(4, 208, D)),
        in_specs=[SMEM] + [VM] * 4 + [ANY],
        out_specs=(VM,) * 2,
        compiler_params=PARAMS,
        cost_estimate=pl.CostEstimate(flops=5 * 10**9, bytes_accessed=6 * 10**6, transcendentals=0),
    )(at, h2, d_up, act, cot, early)


def ograd_kernel(at_ref, attn_ref, branch_ref, keep_ref, give_ref, out_scr):
    yi, ci = at_ref[0], at_ref[2]
    g_out = t_dot(attn_ref[...], branch_ref[...])
    for s in range(4):
        out_scr[s] = g_out[GD * s : GD * (s + 1)]
    for c in range(2):
        for j in range(4):
            b = 4 * c + j
            block = jnp.concatenate(
                [out_scr[(z - yi + 4) % 4, 24 * b : 24 * (b + 1)] for z in range(4)], axis=0
            ).astype(BF)

            @pl.when(ci == c)
            def _():
                keep_ref[j] = block

            @pl.when(ci != c)
            def _():
                give_ref[j] = block


def output_blocks(at, attn, d_branch):
    return pl.pallas_call(
        ograd_kernel,
        out_shape=(shape(4, 96, D), shape(4, 96, D)),
        in_specs=[SMEM] + [VM] * 2,
        out_specs=(VM,) * 2,
        scratch_shapes=[pltpu.VMEM((4, GD, D), F32)],
        compiler_params=PARAMS,
        cost_estimate=pl.CostEstimate(flops=10**9, bytes_accessed=2 * 10**6, transcendentals=0),
    )(at, attn, d_branch)


def add_kernel(a_ref, b_ref, out_ref):
    for s in range(4):
        out_ref[s] = (a_ref[s].astype(F32) + b_ref[s].astype(F32)).astype(BF)


def add_blocks(a, b):
    return pl.pallas_call(
        add_kernel,
        out_shape=shape(*a.shape),
        in_specs=[VM] * 2,
        out_specs=VM,
        compiler_params=PARAMS,
        cost_estimate=pl.CostEstimate(flops=10**6, bytes_accessed=6 * 10**6, transcendentals=0),
    )(a, b)


def mid_kernel(blocks_ref, up_ref, down_ref, out_ref, vec_ref):
    for c in range(2):
        for j in range(4):
            b = 4 * c + j
            block = blocks_ref[2 * j + c].astype(F32)
            for g in range(4):
                up_ref[24 * b : 24 * (b + 1), g * D : (g + 1) * D] = block[24 * g : 24 * (g + 1)]
            down_ref[96 * b : 96 * (b + 1), :] = block[96:192]
            out_ref[24 * b : 24 * (b + 1), :] = block[192:216]
            if b == 0:
                vec_ref[...] = block[216:224]


def mid_rows(blocks):
    return pl.pallas_call(
        mid_kernel,
        out_shape=(
            shape(GD, 4 * D, dtype=F32), shape(D, D, dtype=F32), shape(GD, D, dtype=F32),
            shape(8, D, dtype=F32),
        ),
        in_specs=[VM],
        out_specs=(VM,) * 4,
        compiler_params=PARAMS,
        cost_estimate=pl.CostEstimate(flops=10**6, bytes_accessed=8 * 10**6, transcendentals=0),
    )(blocks)


def tail_kernel(
    at_ref, dkv_ref, dq_ref, h1_ref, n1_ref, w_ref, vec_ref, mid_ref, dh_ref, t_ref, rest_ref, scr
):
    yi, zi = at_ref[0], at_ref[1]
    scr[...] = (mid_ref[0].astype(F32) + mid_ref[1].astype(F32)) + (
        mid_ref[2].astype(F32) + mid_ref[3].astype(F32)
    )
    rest_ref[...] = scr[96:208, :].astype(BF)
    for s in range(4):
        start = (zi + s) % 4 * 24
        part = jnp.concatenate(
            [
                scr[pl.ds(pl.multiple_of(start, 8), 24), :],
                scr[pl.ds(pl.multiple_of(208 + start, 8), 24), :],
            ],
            axis=0,
        )
        t_ref[s, 192:240] = part[:, :640].astype(BF)
        t_ref[s, 240:, :128] = part[:, 640:].astype(BF)
        t_ref[s, 240:, 128:] = jnp.zeros((48, 512), BF)
    d_qkv = jnp.concatenate([dkv_ref[...], dq_ref[...]], axis=1)
    d_h1 = dot_t(d_qkv[:, : 3 * GD], w_ref[...])
    dh_ref[...] = d_h1.astype(BF)
    sums = jnp.sum(d_qkv.astype(F32), axis=0, keepdims=True)
    at_own = lambda v: jnp.concatenate([jnp.where(yi == k, v, 0.0) for k in range(4)], axis=1)
    vectors = jnp.concatenate(
        [
            jnp.sum(d_h1 * n1_ref[...], axis=0, keepdims=True),
            jnp.sum(d_h1, axis=0, keepdims=True),
            at_own(sums[:, 2 * GD : 3 * GD]),
            at_own(sums[:, GD : 2 * GD]),
            vec_ref[4:8, :],
        ],
        axis=0,
    ).astype(BF)
    row = lax.broadcasted_iota(jnp.int32, (8, 128), 0)
    lane = lax.broadcasted_iota(jnp.int32, (8, 128), 1)
    columns = t_dot(vectors, jnp.where(lane == row + 64, 1.0, 0.0).astype(BF))
    grad = t_dot(h1_ref[...], d_qkv)
    for g in range(4):
        rows = slice(g * GD, (g + 1) * GD)
        slot = (g - zi + 4) % 4
        t_ref[slot, :GD, :512] = grad[rows, :512].astype(BF)
        t_ref[slot, :GD, 512:] = (grad[rows, 512:] + columns[rows]).astype(BF)


def last_gradients(at, d_kv, d_q, h1, n1, w, vec, mid):
    return pl.pallas_call(
        tail_kernel,
        out_shape=(shape(ROWS, D), shape(4, 288, 640), shape(112, D)),
        in_specs=[SMEM] + [VM] * 7,
        out_specs=(VM,) * 3,
        scratch_shapes=[pltpu.VMEM((304, D), F32)],
        compiler_params=PARAMS,
        cost_estimate=pl.CostEstimate(flops=3 * 10**9, bytes_accessed=6 * 10**6, transcendentals=0),
    )(at, d_kv, d_q, h1, n1, w, vec, mid)


def sum_kernel(at_ref, t_ref, r1, r2, r3, dh_ref, rest_ref, kept_ref, given_ref, same_ref, block_ref, scr):
    same_ref[...] = dh_ref[...]
    slots = (r1, r2, r3)
    for c in range(2):
        rows = slice(96 * c, 96 * (c + 1))
        a, b, d, e = (v.astype(F32) for v in [t_ref[0, rows]] + [r[rows] for r in slots])
        total = ((a + d) + (b + e)).astype(BF)

        @pl.when(at_ref[2] == c)
        def _():
            kept_ref[...] = total

        @pl.when(at_ref[2] != c)
        def _():
            given_ref[...] = total

    for s in range(4):
        part = (t_ref[0, GD:] if s == 0 else slots[s - 1][GD:]).astype(F32)
        scr[s, :, :640] = part[:48]
        scr[s, :, 640:] = part[48:, :128]
    up = [scr[(at_ref[1] - g + 4) % 4][:24] for g in range(4)]
    g_out = (scr[0] + scr[2])[24:] + (scr[1] + scr[3])[24:]
    rest = rest_ref[...].astype(F32)
    block_ref[...] = jnp.concatenate(up + [rest[:96], g_out, rest[96:]], axis=0).astype(BF)


def sum_slots(at, own, slots, d_h1, rest):
    return pl.pallas_call(
        sum_kernel,
        out_shape=(shape(96, 640), shape(96, 640), shape(ROWS, D), shape(232, D)),
        in_specs=[SMEM] + [VM] * 6,
        out_specs=(VM,) * 4,
        scratch_shapes=[pltpu.VMEM((4, 48, D), F32)],
        compiler_params=PARAMS,
        cost_estimate=pl.CostEstimate(flops=10**6, bytes_accessed=3 * 10**6, transcendentals=0),
    )(at, own, *slots, d_h1, rest)


def final_kernel(at_ref, *refs):
    slots, (grad_ref, vec_ref, scr) = refs[:4], refs[4:]
    for s in range(4):
        for c in range(2):
            scr[s, c] = slots[s][c]
    yi, ci = at_ref[0], at_ref[2]
    for c in range(2):
        rows = slice(96 * c, 96 * (c + 1))
        total = []
        for g in range(4):
            value = scr[(yi - g + 4) % 4, (ci + c) % 2].astype(F32)
            for i, part in enumerate((1, 2, 0)):
                start = part * D + g * GD
                grad_ref[rows, start : start + GD] = value[:, i * GD : (i + 1) * GD]
            total.append(value[:, 512:])
        vec_ref[rows, :] = (total[0] + total[1]) + (total[2] + total[3])


def final_rows(at, slots):
    return pl.pallas_call(
        final_kernel,
        out_shape=(shape(GD, 3 * D, dtype=F32), shape(GD, 128, dtype=F32)),
        in_specs=[SMEM] + [VM] * 4,
        out_specs=(VM, VM),
        scratch_shapes=[pltpu.VMEM((4, 2, 96, 640), BF)],
        compiler_params=PARAMS,
        cost_estimate=pl.CostEstimate(flops=10**6, bytes_accessed=3 * 10**6, transcendentals=0),
    )(at, *slots)


def gather(value, axes, axis=0):
    return lax.all_gather(value, axes, axis=axis, tiled=True)


def swap(value, axes):
    return lax.all_to_all(value, axes, 0, 0)


def send(value, axis, step):
    n = lax.axis_size(axis)
    return lax.ppermute(value, axis, [(i, (i + step) % n) for i in range(n)])


def spread(value, axis):
    return [value] + [send(value, axis, s) for s in range(1, 4)]


def exchange(slots, axis, step):
    return [slots[0]] + [send(slots[s], axis, s * step) for s in range(1, 4)]


def add_slots(slots):
    a, b, c, d = (v.astype(F32) for v in slots)
    return (a + c) + (b + d)


def group_of(value, index, size, axis=0):
    return lax.dynamic_slice_in_dim(value, (index % 4) * size, size, axis)


def local(
    tokens, qkv_w, out_w, up_w, down_w, norm_gains, biases, value_bias, up_bias, cotangent, block_place
):
    xi = lax.axis_index("x")
    yi = lax.axis_index("y")
    ci = lax.axis_index("core")
    zi = lax.axis_index("fsdp")
    tok_own = tokens[0]
    cot_own = cotangent[0]

    at = jnp.stack([yi, zi, ci]).astype(jnp.int32)
    ws = spread(prepare(at, qkv_w, norm_gains, biases, value_bias[None]), "fsdp")
    toks = spread(tok_own, "y")

    ids = jnp.arange(NBLK, dtype=jnp.int32)
    slot_x, slot_c, slot_y, blk = ids // 16, (ids // 8) % 2, (ids // 2) % 4, ids % 2
    pick = lambda at: jnp.sum(jnp.where(at[:, None] == ids[None, :], block_place[None, :], 0), axis=1)
    at_y = (yi - slot_y + 4) % 4
    key_place = pick(at_y * 16 + ((xi - slot_x + 4) % 4) * 4 + ((ci + slot_c) % 2) * 2 + blk)
    query_place = pick(at_y * 16 + slot_x * 4 + slot_c * 2 + blk)
    own_place = key_place[:8]
    rank = jnp.sum((own_place[None, :] > own_place[:, None]).astype(jnp.int32), axis=1)
    order = jnp.arange(8, dtype=jnp.int32)
    hit = rank[None, :] == order[:, None]
    own = jnp.sum(jnp.where(hit, order[None, :], 0), axis=1)
    place = jnp.sum(jnp.where(hit, own_place[None, :], 0), axis=1)

    w_up = swap(up_w.reshape(GD, 4, D).transpose(1, 0, 2), "fsdp").reshape(D, D)
    w_down = down_w

    kv_own, query, h1, n1y, w_qkv, small, both = first_rows(at, toks, ws, cot_own, out_w)
    both = lax.all_gather(both, "fsdp", axis=0)
    w_out = jnp.concatenate(
        [lax.dynamic_index_in_dim(both, (yi + s) % 4, 0, keepdims=False)[128:] for s in range(4)], axis=0
    )
    gain1, gain2 = small[0], small[1]
    out_bias, shift2, down_bias = small[4], small[5], small[6]
    with jax.named_scope("kv"):
        kv_all = [p for v in spread(kv_own, "x") for p in (v, send(v, "core", 1))]
    attn, o_exact, qe, ks, vs = attention_forward(key_place, own, place, query, kv_all, w_up)
    qe_all = gather(qe, XC)

    attn = attn[:, 64:]
    with jax.named_scope("attn_y"):
        attn_own = exchange([attn[128 * s : 128 * (s + 1)] for s in range(4)], "y", -1)
    attn_own = jnp.concatenate(attn_own, axis=1)
    x2 = tok_own.astype(F32) + (dot(attn_own, w_out) + out_bias)
    n2, s2 = normalize(x2)
    h2_own = (n2 * gain2 + shift2).astype(BF)

    with jax.named_scope("h2_z"):
        h2s = spread(h2_own, "fsdp")
    h2, cot_z, act, d_up, d_h2_part = feed_forward(
        at, h2s, both, w_up, w_down, up_bias[None]
    )
    keep, give = weight_blocks(at, h2, d_up, act, cot_z, qe_all)
    with jax.named_scope("mid"):
        mid_in = add_blocks(keep, send(give, "core", 1))
        mid = lax.psum_scatter(mid_in.reshape(832, D), "y", scatter_dimension=0, tiled=True)
    back = lambda v: add_slots(exchange([v[128 * s : 128 * (s + 1)] for s in range(4)], "fsdp", -1))
    with jax.named_scope("d_h2_z"):
        d_h2 = back(d_h2_part)
    cot32 = cot_own.astype(F32)
    d_x2 = cot32 + norm_back(d_h2 * gain2, n2, s2)
    d_branch = d_x2.astype(BF)
    d_attn = dot_t(d_branch, w_out).astype(BF)
    with jax.named_scope("d_attn_y"):
        d_attn_own = exchange([d_attn[:, GD * s : GD * (s + 1)] for s in range(4)], "y", 1)
    d_attn_own = jnp.concatenate(d_attn_own, axis=0)
    de = delta_rows(d_attn_own, o_exact, (qe_all, mid))
    keep, give = output_blocks(at, attn_own, d_branch)
    with jax.named_scope("mid_out"):
        mid_out = add_blocks(keep, send(give, "core", 1)).reshape(384, D)
        mid_out = lax.psum_scatter(mid_out, "y", scatter_dimension=0, tiled=True)
    with jax.named_scope("de"):
        arrived = spread(de, "x")[1:]
        d_q = attention_dq((0, 3), own, place, qe, de, ks, vs)
        arrived = hold_back(arrived, d_q)
        de_all = [p for v in (de, *arrived) for p in (v, send(v, "core", 1))]
    with jax.named_scope("down"):
        layer_out = (x2 + back(down_rows(act, w_down, de)) + down_bias).astype(BF)
    d_q = attention_dq((1, 2), own, place, qe, de, ks, vs, (d_q,), arrived)
    d_kv = attention_dkv(
        query_place, key_place, own, place, kv_own, qe_all, de_all, (layer_out, mid_out)
    )
    with jax.named_scope("mid"):
        mid = lax.all_gather(jnp.concatenate([mid, mid_out], axis=0), "x", axis=0)

    vec = jnp.stack([jnp.sum(d_h2 * n2, axis=0), jnp.sum(d_branch.astype(F32), axis=0), jnp.sum(d_h2, axis=0)])
    vec = jnp.pad(vec, ((4, 1), (0, 0)))
    d_h1_send, tail, rest = last_gradients(at, d_kv, d_q, h1, n1y, w_qkv, vec, mid)
    with jax.named_scope("tail_z"):
        received = [send(tail[s], "fsdp", s) for s in range(1, 4)]
    kept, given, d_h1_send, mid = sum_slots(at, tail, received, d_h1_send, rest)
    with jax.named_scope("mid"):
        mid = lax.all_gather(mid, ("y", "core"), axis=0)
    grad_up, grad_down, grad_out, out_vec = mid_rows(mid)
    grad_up_bias = out_vec[0]
    grad_down_bias = lax.dynamic_slice(out_vec[1], (zi * GD,), (GD,))
    with jax.named_scope("d_h1_y"):
        d_h1 = add_slots(exchange([d_h1_send[128 * s : 128 * (s + 1)] for s in range(4)], "y", -1))
    n1, s1 = normalize(tok_own.astype(F32))
    input_grad = (d_x2 + norm_back(d_h1 * gain1, n1, s1)).astype(BF)

    with jax.named_scope("tail_core"):
        tail = (kept.astype(F32) + send(given, "core", 1).astype(F32)).astype(BF)
    with jax.named_scope("tail_x"):
        tail = add_slots(spread(tail, "x")).astype(BF)
    with jax.named_scope("tail_y"):
        tail = [jnp.stack([v, send(v, "core", 1)]) for v in spread(tail, "y")]
    grad_qkv, vectors = final_rows(at, tail)
    vectors = vectors[:, 64:71].T
    grad_gains = jnp.stack([vectors[0], vectors[4]])
    grad_biases = jnp.stack([vectors[1], vectors[2], vectors[5], vectors[6], grad_down_bias])
    grad_value_bias = vectors[3]
    return (
        layer_out[None], input_grad[None], grad_qkv, grad_out, grad_up, grad_down,
        grad_gains, grad_biases, grad_value_bias, grad_up_bias,
    )


def solution(mesh):
    grid = Mesh(mesh.devices.reshape(4, 4, 2, 4), ("y", "x", "core", "fsdp"))
    rows = P("fsdp", CTX, None)
    in_specs = (
        rows, P("fsdp", None), P("fsdp", None), P("fsdp", None), P("fsdp", None),
        P(None, "fsdp"), P(None, "fsdp"), P("fsdp"), P("fsdp"), rows, P(),
    )
    out_specs = (
        rows, rows, P("fsdp", None), P("fsdp", None), P("fsdp", None), P("fsdp", None),
        P(None, "fsdp"), P(None, "fsdp"), P("fsdp"), P("fsdp"),
    )
    return jax.shard_map(local, mesh=grid, in_specs=in_specs, out_specs=out_specs, check_vma=False)
```

```python
import functools

import jax
import jax.numpy as jnp
from jax import lax
from jax.experimental import pallas as pl
from jax.experimental.pallas import tpu as pltpu
from jax.sharding import Mesh
from jax.sharding import PartitionSpec as P

EPS = 1e-05
D = 768
GD = 192
NH = 3
HD = 64
ROWS = 512
LEN = 4096
BLK = 64
NBLK = 64
EXT = 256
TILE = 1024
CHUNK = 128
BF = jnp.bfloat16
F32 = jnp.float32
XC = ("x", "core")
CTX = ("y", "x", "core")


def dot(a, b):
    return lax.dot_general(a, b, (((1,), (0,)), ((), ())), preferred_element_type=F32)


def dot_t(a, b):
    return lax.dot_general(a, b, (((1,), (1,)), ((), ())), preferred_element_type=F32)


def t_dot(a, b):
    return lax.dot_general(a, b, (((0,), (0,)), ((), ())), preferred_element_type=F32)


def normalize(value):
    center = value - jnp.mean(value, axis=-1, keepdims=True)
    factor = lax.rsqrt(jnp.mean(center * center, axis=-1, keepdims=True) + EPS)
    return (center * factor, factor)


def norm_back(scaled, normed, factor):
    return factor * (
        scaled
        - jnp.mean(scaled, axis=-1, keepdims=True)
        - normed * jnp.mean(scaled * normed, axis=-1, keepdims=True)
    )


def lanes(rows):
    return lax.broadcasted_iota(jnp.int32, (rows, EXT), 1)


def head_mask(rows, h, high):
    lane = lanes(rows)
    if high:
        feat = (lane >= 64 + HD * h) & (lane < 64 + HD * (h + 1))
        ext = (lane >= 3 * h) & (lane < 3 * h + 3)
    else:
        feat = (lane >= HD * h) & (lane < HD * (h + 1))
        ext = (lane >= GD + 3 * h) & (lane < GD + 3 * h + 3)
    return feat | ext


def feature_mask(rows, h, high):
    lane = lanes(rows) - (64 if high else 0)
    return (lane >= HD * h) & (lane < HD * (h + 1))


def stack_heads(value, high):
    rows = value.shape[0]
    zero = jnp.zeros_like(value)
    return jnp.concatenate(
        [jnp.where(head_mask(rows, h, high), value, zero) for h in range(NH)], axis=0
    )


def merge_heads(stacked, high):
    rows = stacked.shape[0] // NH
    out = jnp.zeros((rows, EXT), F32)
    for h in range(NH):
        out = out + jnp.where(feature_mask(rows, h, high), stacked[h * rows : (h + 1) * rows], 0.0)
    return out


def pieces(value):
    first = value.astype(BF).astype(F32)
    second = (value - first).astype(BF).astype(F32)
    third = (value - first - second).astype(BF).astype(F32)
    return (first, second, third)


def add_extras(base, columns, high):
    rows = base.shape[0]
    lane = lanes(rows)
    start = 0 if high else GD
    for h in range(NH):
        for i, piece in enumerate(pieces(columns[h])):
            base = jnp.where(lane == start + 3 * h + i, piece, base)
    return base


def key_form(kv):
    lane = lanes(kv.shape[0])
    one = jnp.ones((kv.shape[0], EXT), BF)
    zero = jnp.zeros((kv.shape[0], EXT), BF)
    low = jnp.where(lane < GD, kv[:, :EXT], jnp.where(lane < GD + 9, one, zero))
    high = jnp.where(lane >= 64, kv[:, 128:384], jnp.where(lane < 9, one, zero))
    return (low, high)


def block_rows(index):
    return pl.ds(pl.multiple_of(index * BLK, BLK), BLK)


def stacked_pos(place_a, place_b):
    row = lax.broadcasted_iota(jnp.int32, (NH * CHUNK, 1), 0)
    place = jnp.where(row % CHUNK < BLK, place_a, place_b)
    return place * BLK + row % BLK


def col_pos(tile):
    return tile * TILE + lax.broadcasted_iota(jnp.int32, (NH * CHUNK, TILE), 1)


def fold(value, op):
    out = value[:, :128]
    for i in range(1, value.shape[1] // 128):
        out = op(out, value[:, i * 128 : (i + 1) * 128])
    return out


def tile_rows(t):
    return pl.ds(pl.multiple_of(t * TILE, TILE), TILE)


def fwd_kernel(
    kplace_ref, own_ref, place_ref, q_ref, *refs
):
    kv_refs = refs[:8]
    attn_ref, o_ref, qe_ref, ks_ref, vs_ref, s_scr, m_scr, l_scr, acc_scr, land, sems = refs[9:]
    copies = [pltpu.make_async_copy(kv_refs[k], land.at[k], sems.at[k]) for k in range(8)]
    for copy in copies:
        copy.start()
    for k in range(8):
        copies[k].wait()
        for b in range(8):
            low, high = key_form(land[k, b * BLK : (b + 1) * BLK, :])
            dst = block_rows(kplace_ref[8 * k + b])
            ks_ref[dst, :] = low
            vs_ref[dst, :] = high

    for c in range(ROWS // CHUNK):
        place_a, place_b = place_ref[2 * c], place_ref[2 * c + 1]
        blocks = (own_ref[2 * c], own_ref[2 * c + 1])
        query = jnp.concatenate([q_ref[block_rows(b), :] for b in blocks], axis=0)
        stacked = stack_heads(query, False)
        qpos = stacked_pos(place_a, place_b)
        tiles = place_a // (TILE // BLK) + 1
        m_scr[...] = jnp.full(m_scr.shape, -1e30, F32)

        def score_step(t, _):
            scores = dot_t(stacked, ks_ref[tile_rows(t), :])
            scores = jnp.where(col_pos(t) <= qpos, scores, -1e30)
            s_scr[t] = scores
            m_scr[...] = jnp.maximum(m_scr[...], fold(scores, jnp.maximum))
            return 0

        lax.fori_loop(0, tiles, score_step, 0)
        peak = jnp.max(m_scr[...], axis=1, keepdims=True)
        l_scr[...] = jnp.zeros(l_scr.shape, F32)
        acc_scr[...] = jnp.zeros(acc_scr.shape, F32)

        def value_step(t, _):
            prob = jnp.exp(s_scr[t] - peak)
            l_scr[...] = l_scr[...] + fold(prob, jnp.add)
            acc_scr[...] = acc_scr[...] + dot(prob.astype(BF), vs_ref[tile_rows(t), :])
            return 0

        lax.fori_loop(0, tiles, value_step, 0)
        total = jnp.sum(l_scr[...], axis=1, keepdims=True)
        log_total = peak + jnp.log(total)
        out = merge_heads(acc_scr[...] / total, True)
        ext = add_extras(
            query.astype(F32),
            [-log_total[h * CHUNK : (h + 1) * CHUNK] for h in range(NH)],
            False,
        ).astype(BF)
        for i, b in enumerate(blocks):
            rows = slice(i * BLK, (i + 1) * BLK)
            o_ref[block_rows(b), :] = out[rows]
            attn_ref[block_rows(b), :] = out[rows].astype(BF)
            qe_ref[block_rows(b), :] = ext[rows]


def dq_kernel(chunks, n_before, own_ref, place_ref, qe_ref, de_ref, ks_ref, vs_ref, *refs):
    *before, dq_ref, acc_scr = refs
    if n_before:
        dq_ref[...] = before[0][...]
    for c in chunks:
        place_a, place_b = place_ref[2 * c], place_ref[2 * c + 1]
        blocks = (own_ref[2 * c], own_ref[2 * c + 1])
        query = stack_heads(jnp.concatenate([qe_ref[block_rows(b), :] for b in blocks], axis=0), False)
        d_out = stack_heads(jnp.concatenate([de_ref[block_rows(b), :] for b in blocks], axis=0), True)
        qpos = stacked_pos(place_a, place_b)
        tiles = place_a // (TILE // BLK) + 1
        acc_scr[...] = jnp.zeros(acc_scr.shape, F32)

        def step(t, _):
            keys = ks_ref[tile_rows(t), :]
            prob = jnp.where(col_pos(t) <= qpos, jnp.exp(dot_t(query, keys)), 0.0)
            d_raw = (prob * dot_t(d_out, vs_ref[tile_rows(t), :])).astype(BF)
            acc_scr[...] = acc_scr[...] + dot(d_raw, keys)
            return 0

        lax.fori_loop(0, tiles, step, 0)
        out = (merge_heads(acc_scr[...], False) * 0.125).astype(BF)
        for i, b in enumerate(blocks):
            dq_ref[block_rows(b), :] = out[i * BLK : (i + 1) * BLK]


def dkv_kernel(qplace_ref, kplace_ref, own_ref, place_ref, kv_ref, qe_ref, *refs):
    de_refs, (dkv_ref, qs_scr, ds_scr, dk_scr, dv_scr, q_land, d_land, sems) = refs[:8], refs[10:]
    q_copy = pltpu.make_async_copy(qe_ref, q_land, sems.at[8])
    q_copy.start()
    copies = [pltpu.make_async_copy(de_refs[k], d_land.at[k], sems.at[k]) for k in range(8)]
    for copy in copies:
        copy.start()
    q_copy.wait()
    for b in range(NBLK):
        qs_scr[block_rows(qplace_ref[b]), :] = q_land[b * BLK : (b + 1) * BLK, :]
    for k in range(8):
        copies[k].wait()
        for b in range(8):
            ds_scr[block_rows(kplace_ref[8 * k + b]), :] = d_land[k, b * BLK : (b + 1) * BLK, :]

    for c in range(ROWS // CHUNK):
        place_a, place_b = place_ref[2 * c], place_ref[2 * c + 1]
        blocks = (own_ref[2 * c], own_ref[2 * c + 1])
        low, high = key_form(jnp.concatenate([kv_ref[block_rows(b), :] for b in blocks], axis=0))
        keys = stack_heads(low, False)
        values = stack_heads(high, True)
        kpos = stacked_pos(place_a, place_b)
        dk_scr[...] = jnp.zeros(dk_scr.shape, F32)
        dv_scr[...] = jnp.zeros(dv_scr.shape, F32)

        def step(t, _):
            query = qs_scr[tile_rows(t), :]
            d_out = ds_scr[tile_rows(t), :]
            prob = jnp.where(col_pos(t) >= kpos, jnp.exp(dot_t(keys, query)), 0.0)
            d_raw = (prob * dot_t(values, d_out)).astype(BF)
            dv_scr[...] = dv_scr[...] + dot(prob.astype(BF), d_out)
            dk_scr[...] = dk_scr[...] + dot(d_raw, query)
            return 0

        lax.fori_loop(place_b // (TILE // BLK), LEN // TILE, step, 0)
        d_keys = merge_heads(dk_scr[...], False)
        d_values = merge_heads(dv_scr[...], True)
        out = jnp.concatenate(
            [d_keys[:, :128], d_keys[:, 128:] + d_values[:, :128], d_values[:, 128:]], axis=1
        ).astype(BF)
        for i, b in enumerate(blocks):
            dkv_ref[block_rows(b), :] = out[i * BLK : (i + 1) * BLK]


def delta_kernel(d_ref, o_ref, early_a, early_b, de_ref):
    d_out = jnp.concatenate([jnp.zeros((ROWS, 64), F32), d_ref[...].astype(F32)], axis=1)
    product = d_out * o_ref[...]
    sums = [
        -jnp.sum(jnp.where(feature_mask(ROWS, h, True), product, 0.0), axis=1, keepdims=True)
        for h in range(NH)
    ]
    de_ref[...] = add_extras(d_out, sums, True).astype(BF)


SMEM = pl.BlockSpec(memory_space=pltpu.SMEM)
VM = pl.BlockSpec(memory_space=pltpu.VMEM)
ANY = pl.BlockSpec(memory_space=pl.ANY)
PARAMS = pltpu.CompilerParams(vmem_limit_bytes=48 * 1024 * 1024)


def shape(*dims, dtype=BF):
    return jax.ShapeDtypeStruct(dims, dtype)


def attention_forward(kplace, own, place, query, kv, early):
    return pl.pallas_call(
        fwd_kernel,
        out_shape=(
            shape(ROWS, EXT), shape(ROWS, EXT, dtype=F32), shape(ROWS, EXT),
            shape(LEN, EXT), shape(LEN, EXT),
        ),
        in_specs=[SMEM] * 3 + [VM] + [ANY] * 9,
        out_specs=(VM,) * 5,
        scratch_shapes=[
            pltpu.VMEM((LEN // TILE, NH * CHUNK, TILE), F32),
            pltpu.VMEM((NH * CHUNK, 128), F32),
            pltpu.VMEM((NH * CHUNK, 128), F32),
            pltpu.VMEM((NH * CHUNK, EXT), F32),
            pltpu.VMEM((8, ROWS, 2 * GD), BF),
            pltpu.SemaphoreType.DMA((8,)),
        ],
        compiler_params=PARAMS,
        cost_estimate=pl.CostEstimate(flops=16 * 10**9, bytes_accessed=10**7, transcendentals=4 * 10**6),
    )(kplace, own, place, query, *kv, early)


def attention_dq(chunks, own, place, qe, de, ks, vs, before=(), early=()):
    return pl.pallas_call(
        functools.partial(dq_kernel, chunks, len(before)),
        out_shape=shape(ROWS, EXT),
        in_specs=[SMEM] * 2 + [VM] * (4 + len(before)) + [ANY] * len(early),
        out_specs=VM,
        scratch_shapes=[pltpu.VMEM((NH * CHUNK, EXT), F32)],
        compiler_params=PARAMS,
        cost_estimate=pl.CostEstimate(flops=8 * 10**9, bytes_accessed=5 * 10**6, transcendentals=2 * 10**6),
    )(own, place, qe, de, ks, vs, *before, *early)


def attention_dkv(qplace, kplace, own, place, kv, qe, de, early):
    return pl.pallas_call(
        dkv_kernel,
        out_shape=shape(ROWS, 2 * GD),
        in_specs=[SMEM] * 4 + [VM] + [ANY] * 11,
        out_specs=VM,
        scratch_shapes=[
            pltpu.VMEM((LEN, EXT), BF),
            pltpu.VMEM((LEN, EXT), BF),
            pltpu.VMEM((NH * CHUNK, EXT), F32),
            pltpu.VMEM((NH * CHUNK, EXT), F32),
            pltpu.VMEM((LEN, EXT), BF),
            pltpu.VMEM((8, ROWS, EXT), BF),
            pltpu.SemaphoreType.DMA((9,)),
        ],
        compiler_params=PARAMS,
        cost_estimate=pl.CostEstimate(flops=15 * 10**9, bytes_accessed=10**7, transcendentals=4 * 10**6),
    )(qplace, kplace, own, place, kv, qe, *de, *early)


def delta_rows(d_attn, o, early):
    return pl.pallas_call(
        delta_kernel,
        out_shape=shape(ROWS, EXT),
        in_specs=[VM] * 2 + [ANY] * 2,
        out_specs=VM,
        compiler_params=PARAMS,
        cost_estimate=pl.CostEstimate(flops=10**6, bytes_accessed=10**6, transcendentals=0),
    )(d_attn, o, *early)


def prep_kernel(at_ref, w_ref, gain_ref, bias_ref, vb_ref, cols_ref):
    for k in range(4):

        @pl.when(at_ref[0] == k)
        def _():
            for i, part in enumerate((1, 2, 0)):
                start = part * D + k * GD
                cols_ref[:GD, i * GD : (i + 1) * GD] = w_ref[:, start : start + GD]

    small = jnp.concatenate(
        [gain_ref[...].astype(F32), bias_ref[...].astype(F32), vb_ref[...].astype(F32), jnp.zeros((8, GD), F32)],
        axis=0,
    )
    cols_ref[GD:, :] = jnp.concatenate([small, jnp.zeros((16, 2 * GD), F32)], axis=1).astype(BF)


def prepare(at, w, gains, biases, vb):
    return pl.pallas_call(
        prep_kernel,
        out_shape=shape(GD + 16, 3 * GD),
        in_specs=[SMEM] + [VM] * 4,
        out_specs=VM,
        compiler_params=PARAMS,
        cost_estimate=pl.CostEstimate(flops=1000, bytes_accessed=10**6, transcendentals=0),
    )(at, w, gains, biases, vb)


def qkv_kernel(at_ref, *refs):
    toks, ws = refs[:4], refs[4:8]
    cot_ref, out_ref = refs[8:10]
    kv_ref, q_ref, h1_ref, n1_ref, w_ref, small_ref, both_ref, w_scr = refs[10:]
    both_ref[:128, :] = cot_ref[...]
    both_ref[128:, :] = out_ref[...]
    yi, zi = at_ref[0], at_ref[1]
    for s in range(4):
        w_scr[s] = ws[s][...]
    for g in range(4):
        slot = (zi - g + 4) % 4
        w_ref[g * GD : (g + 1) * GD, :] = w_scr[slot, :GD]
        small_ref[:, g * GD : (g + 1) * GD] = w_scr[slot, GD:, :256].astype(F32)[:8, :GD]
    gain, shift = small_ref[0:1, :], small_ref[2:3, :]
    for s in range(4):
        rows = slice(128 * s, 128 * (s + 1))
        normed, _ = normalize(toks[s][...].astype(F32))
        n1_ref[rows, :] = normed
        h1_ref[rows, :] = (normed * gain + shift).astype(BF)
    own = w_scr[(zi - yi + 4) % 4, GD:, :256].astype(F32)[:8, :GD]
    qkv = dot(h1_ref[...], w_ref[...])
    kv_ref[:, :GD] = qkv[:, :GD].astype(BF)
    kv_ref[:, GD:] = (qkv[:, GD : 2 * GD] + own[7:8]).astype(BF)
    query = (qkv[:, 2 * GD :] + own[3:4]).astype(BF).astype(F32) * 0.125
    q_ref[...] = jnp.concatenate([query, jnp.zeros((ROWS, EXT - GD), F32)], axis=1).astype(BF)


def first_rows(at, toks, ws, cot, out_w):
    return pl.pallas_call(
        qkv_kernel,
        out_shape=(
            shape(ROWS, 2 * GD), shape(ROWS, EXT), shape(ROWS, D), shape(ROWS, D, dtype=F32),
            shape(D, 3 * GD), shape(8, D, dtype=F32), shape(320, D),
        ),
        in_specs=[SMEM] + [VM] * 10,
        out_specs=(VM,) * 7,
        scratch_shapes=[pltpu.VMEM((4, GD + 16, 3 * GD), BF)],
        compiler_params=PARAMS,
        cost_estimate=pl.CostEstimate(flops=5 * 10**8, bytes_accessed=6 * 10**6, transcendentals=0),
    )(at, *toks, *ws, cot, out_w)


def mlp_kernel(at_ref, *refs):
    h2s = refs[:4]
    both_ref, up_ref, down_ref, ub_ref, h2_ref, cot_ref, act_ref, dup_ref, dh_ref, sems = refs[4:]
    zi = at_ref[1]
    copies = [
        pltpu.make_async_copy(
            both_ref.at[(zi - s + 4) % 4, :128], cot_ref.at[128 * s : 128 * (s + 1)], sems.at[s]
        )
        for s in range(4)
    ]
    for copy in copies:
        copy.start()
    for copy in copies:
        copy.wait()
    for s in range(4):
        rows = slice(128 * s, 128 * (s + 1))
        h2 = h2s[s][...]
        h2_ref[rows, :] = h2
        up = dot(h2, up_ref[...]) + ub_ref[...].astype(F32)
        d_act = dot_t(cot_ref[rows, :], down_ref[...])
        square = up * up
        th = jnp.tanh(0.7978845608028654 * (up + 0.044715 * (square * up)))
        half = 0.5 * (1.0 + th)
        slope = half + 0.5 * up * (1.0 - th * th) * (
            0.7978845608028654 * (1.0 + 3 * 0.044715 * square)
        )
        act_ref[rows, :] = (up * half).astype(BF)
        d_up = (slope * d_act).astype(BF)
        dup_ref[rows, :] = d_up
        dh_ref[rows, :] = dot_t(d_up, up_ref[...]).astype(BF)


def feed_forward(at, h2s, both, w_up, w_down, ub):
    return pl.pallas_call(
        mlp_kernel,
        out_shape=(shape(ROWS, D),) * 5,
        in_specs=[SMEM] + [VM] * 4 + [ANY] + [VM] * 3,
        out_specs=(VM,) * 5,
        scratch_shapes=[pltpu.SemaphoreType.DMA((4,))],
        compiler_params=PARAMS,
        cost_estimate=pl.CostEstimate(flops=4 * 10**9, bytes_accessed=6 * 10**6, transcendentals=4 * 10**5),
    )(at, *h2s, both, w_up, w_down, ub)


def down_kernel(act_ref, wd_ref, early_ref, down_ref):
    down_ref[...] = dot(act_ref[...], wd_ref[...]).astype(BF)


def down_rows(act, w_down, early):
    return pl.pallas_call(
        down_kernel,
        out_shape=shape(ROWS, D),
        in_specs=[VM] * 2 + [ANY],
        out_specs=VM,
        compiler_params=PARAMS,
        cost_estimate=pl.CostEstimate(flops=10**9, bytes_accessed=3 * 10**6, transcendentals=0),
    )(act, w_down, early)


def hold_kernel(*refs):
    for s in range(3):
        refs[4 + s][...] = refs[s][...]


def hold_back(values, early):
    return pl.pallas_call(
        hold_kernel,
        out_shape=tuple(shape(*v.shape) for v in values),
        in_specs=[VM] * 3 + [ANY],
        out_specs=(VM,) * 3,
        compiler_params=PARAMS,
        cost_estimate=pl.CostEstimate(flops=1000, bytes_accessed=10**6, transcendentals=0),
    )(*values, early)


def wgrad_kernel(
    at_ref, h2_ref, dup_ref, act_ref, cot_ref, attn_ref, branch_ref, early_ref,
    keep_ref, give_ref, out_scr,
):
    yi, ci = at_ref[0], at_ref[2]
    g_up = t_dot(h2_ref[...], dup_ref[...])
    g_down = t_dot(act_ref[...], cot_ref[...])
    g_out = t_dot(attn_ref[...], branch_ref[...])
    for s in range(4):
        out_scr[s] = g_out[GD * s : GD * (s + 1)]
    vec = jnp.concatenate(
        [
            jnp.sum(dup_ref[...].astype(F32), axis=0, keepdims=True),
            jnp.sum(cot_ref[...].astype(F32), axis=0, keepdims=True),
            jnp.zeros((14, D), F32),
        ],
        axis=0,
    )
    for c in range(2):
        for j in range(4):
            b = 4 * c + j
            parts = []
            for z in range(4):
                parts.append(g_up[GD * z + 24 * b : GD * z + 24 * (b + 1)])
                parts.append(out_scr[(z - yi + 4) % 4, 24 * b : 24 * (b + 1)])
            parts += [g_down[96 * b : 96 * (b + 1)], vec]
            block = jnp.concatenate(parts, axis=0).astype(BF)
            slot = (j - yi + 4) % 4

            @pl.when(ci == c)
            def _():
                keep_ref[slot] = block

            @pl.when(ci != c)
            def _():
                give_ref[slot] = block


def weight_blocks(at, h2, d_up, act, cot, attn, d_branch, early):
    return pl.pallas_call(
        wgrad_kernel,
        out_shape=(shape(4, 304, D), shape(4, 304, D)),
        in_specs=[SMEM] + [VM] * 6 + [ANY],
        out_specs=(VM,) * 2,
        scratch_shapes=[pltpu.VMEM((4, GD, D), F32)],
        compiler_params=PARAMS,
        cost_estimate=pl.CostEstimate(flops=5 * 10**9, bytes_accessed=6 * 10**6, transcendentals=0),
    )(at, h2, d_up, act, cot, attn, d_branch, early)


def add_kernel(a_ref, b_ref, *outs):
    for s in range(4):
        outs[s][...] = (a_ref[s].astype(F32) + b_ref[s].astype(F32)).astype(BF)


def add_blocks(a, b):
    return pl.pallas_call(
        add_kernel,
        out_shape=(shape(*a.shape[1:]),) * 4,
        in_specs=[VM] * 2,
        out_specs=(VM,) * 4,
        compiler_params=PARAMS,
        cost_estimate=pl.CostEstimate(flops=10**6, bytes_accessed=6 * 10**6, transcendentals=0),
    )(a, b)


def mid_kernel(blocks_ref, up_ref, down_ref, out_ref, vec_ref):
    for c in range(2):
        for j in range(4):
            b = 4 * c + j
            block = blocks_ref[2 * j + c].astype(F32)
            for g in range(4):
                up_ref[24 * b : 24 * (b + 1), g * D : (g + 1) * D] = block[24 * g : 24 * (g + 1)]
            down_ref[96 * b : 96 * (b + 1), :] = block[96:192]
            out_ref[24 * b : 24 * (b + 1), :] = block[192:216]
            if b == 0:
                vec_ref[...] = block[216:224]


def mid_rows(blocks):
    return pl.pallas_call(
        mid_kernel,
        out_shape=(
            shape(GD, 4 * D, dtype=F32), shape(D, D, dtype=F32), shape(GD, D, dtype=F32),
            shape(8, D, dtype=F32),
        ),
        in_specs=[VM],
        out_specs=(VM,) * 4,
        compiler_params=PARAMS,
        cost_estimate=pl.CostEstimate(flops=10**6, bytes_accessed=8 * 10**6, transcendentals=0),
    )(blocks)


def tail_kernel(
    at_ref, dkv_ref, dq_ref, h1_ref, n1_ref, w_ref, vec_ref, m0, m1, m2, m3, dh_ref, t_ref, rest_ref, scr
):
    yi, zi = at_ref[0], at_ref[1]
    scr[...] = (m0[...].astype(F32) + m2[...].astype(F32)) + (
        m1[...].astype(F32) + m3[...].astype(F32)
    )
    rest_ref[...] = scr[192:, :].astype(BF)
    for s in range(4):
        part = scr[pl.ds(pl.multiple_of((zi + s) % 4 * 48, 8), 48), :]
        t_ref[s, 192:240] = part[:, :640].astype(BF)
        t_ref[s, 240:, :128] = part[:, 640:].astype(BF)
        t_ref[s, 240:, 128:] = jnp.zeros((48, 512), BF)
    d_qkv = jnp.concatenate([dkv_ref[...], dq_ref[...]], axis=1)
    d_h1 = dot_t(d_qkv[:, : 3 * GD], w_ref[...])
    dh_ref[...] = d_h1.astype(BF)
    sums = jnp.sum(d_qkv.astype(F32), axis=0, keepdims=True)
    at_own = lambda v: jnp.concatenate([jnp.where(yi == k, v, 0.0) for k in range(4)], axis=1)
    vectors = jnp.concatenate(
        [
            jnp.sum(d_h1 * n1_ref[...], axis=0, keepdims=True),
            jnp.sum(d_h1, axis=0, keepdims=True),
            at_own(sums[:, 2 * GD : 3 * GD]),
            at_own(sums[:, GD : 2 * GD]),
            vec_ref[4:8, :],
        ],
        axis=0,
    ).astype(BF)
    row = lax.broadcasted_iota(jnp.int32, (8, 128), 0)
    lane = lax.broadcasted_iota(jnp.int32, (8, 128), 1)
    columns = t_dot(vectors, jnp.where(lane == row + 64, 1.0, 0.0).astype(BF))
    grad = t_dot(h1_ref[...], d_qkv)
    for g in range(4):
        rows = slice(g * GD, (g + 1) * GD)
        slot = (g - zi + 4) % 4
        t_ref[slot, :GD, :512] = grad[rows, :512].astype(BF)
        t_ref[slot, :GD, 512:] = (grad[rows, 512:] + columns[rows]).astype(BF)


def last_gradients(at, d_kv, d_q, h1, n1, w, vec, mid):
    return pl.pallas_call(
        tail_kernel,
        out_shape=(shape(ROWS, D), shape(4, 288, 640), shape(112, D)),
        in_specs=[SMEM] + [VM] * 10,
        out_specs=(VM,) * 3,
        scratch_shapes=[pltpu.VMEM((304, D), F32)],
        compiler_params=PARAMS,
        cost_estimate=pl.CostEstimate(flops=3 * 10**9, bytes_accessed=6 * 10**6, transcendentals=0),
    )(at, d_kv, d_q, h1, n1, w, vec, *mid)


def sum_kernel(at_ref, t_ref, r1, r2, r3, dh_ref, rest_ref, kept_ref, given_ref, same_ref, block_ref, scr):
    same_ref[...] = dh_ref[...]
    slots = (r1, r2, r3)
    for c in range(2):
        rows = slice(96 * c, 96 * (c + 1))
        a, b, d, e = (v.astype(F32) for v in [t_ref[0, rows]] + [r[rows] for r in slots])
        total = ((a + d) + (b + e)).astype(BF)

        @pl.when(at_ref[2] == c)
        def _():
            kept_ref[...] = total

        @pl.when(at_ref[2] != c)
        def _():
            given_ref[...] = total

    for s in range(4):
        part = (t_ref[0, GD:] if s == 0 else slots[s - 1][GD:]).astype(F32)
        scr[s, :, :640] = part[:48]
        scr[s, :, 640:] = part[48:, :128]
    up = [scr[(at_ref[1] - g + 4) % 4][:24] for g in range(4)]
    g_out = (scr[0] + scr[2])[24:] + (scr[1] + scr[3])[24:]
    rest = rest_ref[...].astype(F32)
    block_ref[...] = jnp.concatenate(up + [rest[:96], g_out, rest[96:]], axis=0).astype(BF)


def sum_slots(at, own, slots, d_h1, rest):
    return pl.pallas_call(
        sum_kernel,
        out_shape=(shape(96, 640), shape(96, 640), shape(ROWS, D), shape(232, D)),
        in_specs=[SMEM] + [VM] * 6,
        out_specs=(VM,) * 4,
        scratch_shapes=[pltpu.VMEM((4, 48, D), F32)],
        compiler_params=PARAMS,
        cost_estimate=pl.CostEstimate(flops=10**6, bytes_accessed=3 * 10**6, transcendentals=0),
    )(at, own, *slots, d_h1, rest)


def final_kernel(at_ref, *refs):
    slots, (grad_ref, vec_ref, scr) = refs[:4], refs[4:]
    for s in range(4):
        for c in range(2):
            scr[s, c] = slots[s][c]
    yi, ci = at_ref[0], at_ref[2]
    for c in range(2):
        rows = slice(96 * c, 96 * (c + 1))
        total = []
        for g in range(4):
            value = scr[(yi - g + 4) % 4, (ci + c) % 2].astype(F32)
            for i, part in enumerate((1, 2, 0)):
                start = part * D + g * GD
                grad_ref[rows, start : start + GD] = value[:, i * GD : (i + 1) * GD]
            total.append(value[:, 512:])
        vec_ref[rows, :] = (total[0] + total[1]) + (total[2] + total[3])


def final_rows(at, slots):
    return pl.pallas_call(
        final_kernel,
        out_shape=(shape(GD, 3 * D, dtype=F32), shape(GD, 128, dtype=F32)),
        in_specs=[SMEM] + [VM] * 4,
        out_specs=(VM, VM),
        scratch_shapes=[pltpu.VMEM((4, 2, 96, 640), BF)],
        compiler_params=PARAMS,
        cost_estimate=pl.CostEstimate(flops=10**6, bytes_accessed=3 * 10**6, transcendentals=0),
    )(at, *slots)


def gather(value, axes, axis=0):
    return lax.all_gather(value, axes, axis=axis, tiled=True)


def swap(value, axes):
    return lax.all_to_all(value, axes, 0, 0)


def send(value, axis, step):
    n = lax.axis_size(axis)
    return lax.ppermute(value, axis, [(i, (i + step) % n) for i in range(n)])


def spread(value, axis):
    return [value] + [send(value, axis, s) for s in range(1, 4)]


def exchange(slots, axis, step):
    return [slots[0]] + [send(slots[s], axis, s * step) for s in range(1, 4)]


def add_slots(slots):
    a, b, c, d = (v.astype(F32) for v in slots)
    return (a + c) + (b + d)


def group_of(value, index, size, axis=0):
    return lax.dynamic_slice_in_dim(value, (index % 4) * size, size, axis)


def local(
    tokens, qkv_w, out_w, up_w, down_w, norm_gains, biases, value_bias, up_bias, cotangent, block_place
):
    xi = lax.axis_index("x")
    yi = lax.axis_index("y")
    ci = lax.axis_index("core")
    zi = lax.axis_index("fsdp")
    tok_own = tokens[0]
    cot_own = cotangent[0]

    at = jnp.stack([yi, zi, ci]).astype(jnp.int32)
    ws = spread(prepare(at, qkv_w, norm_gains, biases, value_bias[None]), "fsdp")
    toks = spread(tok_own, "y")

    ids = jnp.arange(NBLK, dtype=jnp.int32)
    slot_x, slot_c, slot_y, blk = ids // 16, (ids // 8) % 2, (ids // 2) % 4, ids % 2
    pick = lambda at: jnp.sum(jnp.where(at[:, None] == ids[None, :], block_place[None, :], 0), axis=1)
    at_y = (yi - slot_y + 4) % 4
    key_place = pick(at_y * 16 + ((xi - slot_x + 4) % 4) * 4 + ((ci + slot_c) % 2) * 2 + blk)
    query_place = pick(at_y * 16 + slot_x * 4 + slot_c * 2 + blk)
    own_place = key_place[:8]
    rank = jnp.sum((own_place[None, :] > own_place[:, None]).astype(jnp.int32), axis=1)
    order = jnp.arange(8, dtype=jnp.int32)
    hit = rank[None, :] == order[:, None]
    own = jnp.sum(jnp.where(hit, order[None, :], 0), axis=1)
    place = jnp.sum(jnp.where(hit, own_place[None, :], 0), axis=1)

    w_up = swap(up_w.reshape(GD, 4, D).transpose(1, 0, 2), "fsdp").reshape(D, D)
    w_down = down_w

    kv_own, query, h1, n1y, w_qkv, small, both = first_rows(at, toks, ws, cot_own, out_w)
    both = lax.all_gather(both, "fsdp", axis=0)
    w_out = jnp.concatenate(
        [lax.dynamic_index_in_dim(both, (yi + s) % 4, 0, keepdims=False)[128:] for s in range(4)], axis=0
    )
    gain1, gain2 = small[0], small[1]
    out_bias, shift2, down_bias = small[4], small[5], small[6]
    with jax.named_scope("kv"):
        kv_all = [p for v in spread(kv_own, "x") for p in (v, send(v, "core", 1))]
    attn, o_exact, qe, ks, vs = attention_forward(key_place, own, place, query, kv_all, w_up)
    qe_all = gather(qe, XC)

    attn = attn[:, 64:]
    with jax.named_scope("attn_y"):
        attn_own = exchange([attn[128 * s : 128 * (s + 1)] for s in range(4)], "y", -1)
    attn_own = jnp.concatenate(attn_own, axis=1)
    x2 = tok_own.astype(F32) + (dot(attn_own, w_out) + out_bias)
    n2, s2 = normalize(x2)
    h2_own = (n2 * gain2 + shift2).astype(BF)

    with jax.named_scope("h2_z"):
        h2s = spread(h2_own, "fsdp")
    h2, cot_z, act, d_up, d_h2_part = feed_forward(
        at, h2s, both, w_up, w_down, up_bias[None]
    )
    back = lambda v: add_slots(exchange([v[128 * s : 128 * (s + 1)] for s in range(4)], "fsdp", -1))
    with jax.named_scope("d_h2_z"):
        d_h2 = back(d_h2_part)
    cot32 = cot_own.astype(F32)
    d_x2 = cot32 + norm_back(d_h2 * gain2, n2, s2)
    d_branch = d_x2.astype(BF)
    d_attn = dot_t(d_branch, w_out).astype(BF)
    with jax.named_scope("d_attn_y"):
        d_attn_own = exchange([d_attn[:, GD * s : GD * (s + 1)] for s in range(4)], "y", 1)
    d_attn_own = jnp.concatenate(d_attn_own, axis=0)
    de = delta_rows(d_attn_own, o_exact, (qe_all, both))
    keep, give = weight_blocks(at, h2, d_up, act, cot_z, attn_own, d_branch, de)
    with jax.named_scope("mid"):
        mid = add_blocks(keep, send(give, "core", 1))
        mid = add_slots(exchange(mid, "y", 1)).astype(BF)
    with jax.named_scope("de"):
        arrived = spread(de, "x")[1:]
        d_q = attention_dq((0, 3), own, place, qe, de, ks, vs)
        arrived = hold_back(arrived, d_q)
        de_all = [p for v in (de, *arrived) for p in (v, send(v, "core", 1))]
    with jax.named_scope("down"):
        layer_out = (x2 + back(down_rows(act, w_down, de)) + down_bias).astype(BF)
    d_q = attention_dq((1, 2), own, place, qe, de, ks, vs, (d_q,), arrived)
    d_kv = attention_dkv(
        query_place, key_place, own, place, kv_own, qe_all, de_all, (layer_out, mid)
    )
    with jax.named_scope("mid"):
        mid = spread(mid, "x")

    vec = jnp.stack([jnp.sum(d_h2 * n2, axis=0), jnp.sum(d_branch.astype(F32), axis=0), jnp.sum(d_h2, axis=0)])
    vec = jnp.pad(vec, ((4, 1), (0, 0)))
    d_h1_send, tail, rest = last_gradients(at, d_kv, d_q, h1, n1y, w_qkv, vec, mid)
    with jax.named_scope("tail_z"):
        received = [send(tail[s], "fsdp", s) for s in range(1, 4)]
    kept, given, d_h1_send, mid = sum_slots(at, tail, received, d_h1_send, rest)
    with jax.named_scope("mid"):
        mid = lax.all_gather(mid, ("y", "core"), axis=0)
    grad_up, grad_down, grad_out, out_vec = mid_rows(mid)
    grad_up_bias = out_vec[0]
    grad_down_bias = lax.dynamic_slice(out_vec[1], (zi * GD,), (GD,))
    with jax.named_scope("d_h1_y"):
        d_h1 = add_slots(exchange([d_h1_send[128 * s : 128 * (s + 1)] for s in range(4)], "y", -1))
    n1, s1 = normalize(tok_own.astype(F32))
    input_grad = (d_x2 + norm_back(d_h1 * gain1, n1, s1)).astype(BF)

    with jax.named_scope("tail_core"):
        tail = (kept.astype(F32) + send(given, "core", 1).astype(F32)).astype(BF)
    with jax.named_scope("tail_x"):
        tail = add_slots(spread(tail, "x")).astype(BF)
    with jax.named_scope("tail_y"):
        tail = [jnp.stack([v, send(v, "core", 1)]) for v in spread(tail, "y")]
    grad_qkv, vectors = final_rows(at, tail)
    vectors = vectors[:, 64:71].T
    grad_gains = jnp.stack([vectors[0], vectors[4]])
    grad_biases = jnp.stack([vectors[1], vectors[2], vectors[5], vectors[6], grad_down_bias])
    grad_value_bias = vectors[3]
    return (
        layer_out[None], input_grad[None], grad_qkv, grad_out, grad_up, grad_down,
        grad_gains, grad_biases, grad_value_bias, grad_up_bias,
    )


def solution(mesh):
    grid = Mesh(mesh.devices.reshape(4, 4, 2, 4), ("y", "x", "core", "fsdp"))
    rows = P("fsdp", CTX, None)
    in_specs = (
        rows, P("fsdp", None), P("fsdp", None), P("fsdp", None), P("fsdp", None),
        P(None, "fsdp"), P(None, "fsdp"), P("fsdp"), P("fsdp"), rows, P(),
    )
    out_specs = (
        rows, rows, P("fsdp", None), P("fsdp", None), P("fsdp", None), P("fsdp", None),
        P(None, "fsdp"), P(None, "fsdp"), P("fsdp"), P("fsdp"),
    )
    return jax.shard_map(local, mesh=grid, in_specs=in_specs, out_specs=out_specs, check_vma=False)
```

```python
import functools

import jax
import jax.numpy as jnp
from jax import lax
from jax.experimental import pallas as pl
from jax.experimental.pallas import tpu as pltpu
from jax.sharding import Mesh
from jax.sharding import PartitionSpec as P

EPS = 1e-05
D = 768
GD = 192
NH = 3
HD = 64
ROWS = 512
LEN = 4096
BLK = 64
NBLK = 64
EXT = 256
TILE = 1024
CHUNK = 128
BF = jnp.bfloat16
F32 = jnp.float32
XC = ("x", "core")
CTX = ("y", "x", "core")


def dot(a, b):
    return lax.dot_general(a, b, (((1,), (0,)), ((), ())), preferred_element_type=F32)


def dot_t(a, b):
    return lax.dot_general(a, b, (((1,), (1,)), ((), ())), preferred_element_type=F32)


def t_dot(a, b):
    return lax.dot_general(a, b, (((0,), (0,)), ((), ())), preferred_element_type=F32)


def normalize(value):
    center = value - jnp.mean(value, axis=-1, keepdims=True)
    factor = lax.rsqrt(jnp.mean(center * center, axis=-1, keepdims=True) + EPS)
    return (center * factor, factor)


def norm_back(scaled, normed, factor):
    return factor * (
        scaled
        - jnp.mean(scaled, axis=-1, keepdims=True)
        - normed * jnp.mean(scaled * normed, axis=-1, keepdims=True)
    )


def lanes(rows):
    return lax.broadcasted_iota(jnp.int32, (rows, EXT), 1)


def head_mask(rows, h, high):
    lane = lanes(rows)
    if high:
        feat = (lane >= 64 + HD * h) & (lane < 64 + HD * (h + 1))
        ext = (lane >= 3 * h) & (lane < 3 * h + 3)
    else:
        feat = (lane >= HD * h) & (lane < HD * (h + 1))
        ext = (lane >= GD + 3 * h) & (lane < GD + 3 * h + 3)
    return feat | ext


def feature_mask(rows, h, high):
    lane = lanes(rows) - (64 if high else 0)
    return (lane >= HD * h) & (lane < HD * (h + 1))


def stack_heads(value, high):
    rows = value.shape[0]
    zero = jnp.zeros_like(value)
    return jnp.concatenate(
        [jnp.where(head_mask(rows, h, high), value, zero) for h in range(NH)], axis=0
    )


def merge_heads(stacked, high):
    rows = stacked.shape[0] // NH
    out = jnp.zeros((rows, EXT), F32)
    for h in range(NH):
        out = out + jnp.where(feature_mask(rows, h, high), stacked[h * rows : (h + 1) * rows], 0.0)
    return out


def pieces(value):
    first = value.astype(BF).astype(F32)
    second = (value - first).astype(BF).astype(F32)
    third = (value - first - second).astype(BF).astype(F32)
    return (first, second, third)


def add_extras(base, columns, high):
    rows = base.shape[0]
    lane = lanes(rows)
    start = 0 if high else GD
    for h in range(NH):
        for i, piece in enumerate(pieces(columns[h])):
            base = jnp.where(lane == start + 3 * h + i, piece, base)
    return base


def key_form(kv):
    lane = lanes(kv.shape[0])
    one = jnp.ones((kv.shape[0], EXT), BF)
    zero = jnp.zeros((kv.shape[0], EXT), BF)
    low = jnp.where(lane < GD, kv[:, :EXT], jnp.where(lane < GD + 9, one, zero))
    high = jnp.where(lane >= 64, kv[:, 128:384], jnp.where(lane < 9, one, zero))
    return (low, high)


def block_rows(index):
    return pl.ds(pl.multiple_of(index * BLK, BLK), BLK)


def stacked_pos(place_a, place_b):
    row = lax.broadcasted_iota(jnp.int32, (NH * CHUNK, 1), 0)
    place = jnp.where(row % CHUNK < BLK, place_a, place_b)
    return place * BLK + row % BLK


def col_pos(tile):
    return tile * TILE + lax.broadcasted_iota(jnp.int32, (NH * CHUNK, TILE), 1)


def fold(value, op):
    out = value[:, :128]
    for i in range(1, value.shape[1] // 128):
        out = op(out, value[:, i * 128 : (i + 1) * 128])
    return out


def tile_rows(t):
    return pl.ds(pl.multiple_of(t * TILE, TILE), TILE)


def fwd_kernel(
    kplace_ref, own_ref, place_ref, q_ref, *refs
):
    kv_refs = refs[:8]
    attn_ref, o_ref, qe_ref, ks_ref, vs_ref, s_scr, m_scr, l_scr, acc_scr, land, sems = refs[9:]
    copies = [pltpu.make_async_copy(kv_refs[k], land.at[k], sems.at[k]) for k in range(8)]
    for copy in copies:
        copy.start()
    for k in range(8):
        copies[k].wait()
        for b in range(8):
            low, high = key_form(land[k, b * BLK : (b + 1) * BLK, :])
            dst = block_rows(kplace_ref[8 * k + b])
            ks_ref[dst, :] = low
            vs_ref[dst, :] = high

    for c in range(ROWS // CHUNK):
        place_a, place_b = place_ref[2 * c], place_ref[2 * c + 1]
        blocks = (own_ref[2 * c], own_ref[2 * c + 1])
        query = jnp.concatenate([q_ref[block_rows(b), :] for b in blocks], axis=0)
        stacked = stack_heads(query, False)
        qpos = stacked_pos(place_a, place_b)
        tiles = place_a // (TILE // BLK) + 1
        m_scr[...] = jnp.full(m_scr.shape, -1e30, F32)

        def score_step(t, _):
            scores = dot_t(stacked, ks_ref[tile_rows(t), :])
            scores = jnp.where(col_pos(t) <= qpos, scores, -1e30)
            s_scr[t] = scores
            m_scr[...] = jnp.maximum(m_scr[...], fold(scores, jnp.maximum))
            return 0

        lax.fori_loop(0, tiles, score_step, 0)
        peak = jnp.max(m_scr[...], axis=1, keepdims=True)
        l_scr[...] = jnp.zeros(l_scr.shape, F32)
        acc_scr[...] = jnp.zeros(acc_scr.shape, F32)

        def value_step(t, _):
            prob = jnp.exp(s_scr[t] - peak)
            l_scr[...] = l_scr[...] + fold(prob, jnp.add)
            acc_scr[...] = acc_scr[...] + dot(prob.astype(BF), vs_ref[tile_rows(t), :])
            return 0

        lax.fori_loop(0, tiles, value_step, 0)
        total = jnp.sum(l_scr[...], axis=1, keepdims=True)
        log_total = peak + jnp.log(total)
        out = merge_heads(acc_scr[...] / total, True)
        ext = add_extras(
            query.astype(F32),
            [-log_total[h * CHUNK : (h + 1) * CHUNK] for h in range(NH)],
            False,
        ).astype(BF)
        for i, b in enumerate(blocks):
            rows = slice(i * BLK, (i + 1) * BLK)
            o_ref[block_rows(b), :] = out[rows]
            attn_ref[block_rows(b), :] = out[rows].astype(BF)
            qe_ref[block_rows(b), :] = ext[rows]


def dq_kernel(chunks, n_before, own_ref, place_ref, qe_ref, de_ref, ks_ref, vs_ref, *refs):
    *before, dq_ref, acc_scr = refs
    if n_before:
        dq_ref[...] = before[0][...]
    for c in chunks:
        place_a, place_b = place_ref[2 * c], place_ref[2 * c + 1]
        blocks = (own_ref[2 * c], own_ref[2 * c + 1])
        query = stack_heads(jnp.concatenate([qe_ref[block_rows(b), :] for b in blocks], axis=0), False)
        d_out = stack_heads(jnp.concatenate([de_ref[block_rows(b), :] for b in blocks], axis=0), True)
        qpos = stacked_pos(place_a, place_b)
        tiles = place_a // (TILE // BLK) + 1
        acc_scr[...] = jnp.zeros(acc_scr.shape, F32)

        def step(t, _):
            keys = ks_ref[tile_rows(t), :]
            prob = jnp.where(col_pos(t) <= qpos, jnp.exp(dot_t(query, keys)), 0.0)
            d_raw = (prob * dot_t(d_out, vs_ref[tile_rows(t), :])).astype(BF)
            acc_scr[...] = acc_scr[...] + dot(d_raw, keys)
            return 0

        lax.fori_loop(0, tiles, step, 0)
        out = (merge_heads(acc_scr[...], False) * 0.125).astype(BF)
        for i, b in enumerate(blocks):
            dq_ref[block_rows(b), :] = out[i * BLK : (i + 1) * BLK]


def dkv_kernel(qplace_ref, kplace_ref, own_ref, place_ref, kv_ref, qe_ref, *refs):
    de_refs, (dkv_ref, qs_scr, ds_scr, dk_scr, dv_scr, q_land, d_land, sems) = refs[:8], refs[10:]
    q_copy = pltpu.make_async_copy(qe_ref, q_land, sems.at[8])
    q_copy.start()
    copies = [pltpu.make_async_copy(de_refs[k], d_land.at[k], sems.at[k]) for k in range(8)]
    for copy in copies:
        copy.start()
    q_copy.wait()
    for b in range(NBLK):
        qs_scr[block_rows(qplace_ref[b]), :] = q_land[b * BLK : (b + 1) * BLK, :]
    for k in range(8):
        copies[k].wait()
        for b in range(8):
            ds_scr[block_rows(kplace_ref[8 * k + b]), :] = d_land[k, b * BLK : (b + 1) * BLK, :]

    for c in range(ROWS // CHUNK):
        place_a, place_b = place_ref[2 * c], place_ref[2 * c + 1]
        blocks = (own_ref[2 * c], own_ref[2 * c + 1])
        low, high = key_form(jnp.concatenate([kv_ref[block_rows(b), :] for b in blocks], axis=0))
        keys = stack_heads(low, False)
        values = stack_heads(high, True)
        kpos = stacked_pos(place_a, place_b)
        dk_scr[...] = jnp.zeros(dk_scr.shape, F32)
        dv_scr[...] = jnp.zeros(dv_scr.shape, F32)

        def step(t, _):
            query = qs_scr[tile_rows(t), :]
            d_out = ds_scr[tile_rows(t), :]
            prob = jnp.where(col_pos(t) >= kpos, jnp.exp(dot_t(keys, query)), 0.0)
            d_raw = (prob * dot_t(values, d_out)).astype(BF)
            dv_scr[...] = dv_scr[...] + dot(prob.astype(BF), d_out)
            dk_scr[...] = dk_scr[...] + dot(d_raw, query)
            return 0

        lax.fori_loop(place_b // (TILE // BLK), LEN // TILE, step, 0)
        d_keys = merge_heads(dk_scr[...], False)
        d_values = merge_heads(dv_scr[...], True)
        out = jnp.concatenate(
            [d_keys[:, :128], d_keys[:, 128:] + d_values[:, :128], d_values[:, 128:]], axis=1
        ).astype(BF)
        for i, b in enumerate(blocks):
            dkv_ref[block_rows(b), :] = out[i * BLK : (i + 1) * BLK]


def delta_kernel(d_ref, o_ref, early_a, early_b, de_ref):
    d_out = jnp.concatenate([jnp.zeros((ROWS, 64), F32), d_ref[...].astype(F32)], axis=1)
    product = d_out * o_ref[...]
    sums = [
        -jnp.sum(jnp.where(feature_mask(ROWS, h, True), product, 0.0), axis=1, keepdims=True)
        for h in range(NH)
    ]
    de_ref[...] = add_extras(d_out, sums, True).astype(BF)


SMEM = pl.BlockSpec(memory_space=pltpu.SMEM)
VM = pl.BlockSpec(memory_space=pltpu.VMEM)
ANY = pl.BlockSpec(memory_space=pl.ANY)
PARAMS = pltpu.CompilerParams(vmem_limit_bytes=48 * 1024 * 1024)


def shape(*dims, dtype=BF):
    return jax.ShapeDtypeStruct(dims, dtype)


def attention_forward(kplace, own, place, query, kv, early):
    return pl.pallas_call(
        fwd_kernel,
        out_shape=(
            shape(ROWS, EXT), shape(ROWS, EXT, dtype=F32), shape(ROWS, EXT),
            shape(LEN, EXT), shape(LEN, EXT),
        ),
        in_specs=[SMEM] * 3 + [VM] + [ANY] * 9,
        out_specs=(VM,) * 5,
        scratch_shapes=[
            pltpu.VMEM((LEN // TILE, NH * CHUNK, TILE), F32),
            pltpu.VMEM((NH * CHUNK, 128), F32),
            pltpu.VMEM((NH * CHUNK, 128), F32),
            pltpu.VMEM((NH * CHUNK, EXT), F32),
            pltpu.VMEM((8, ROWS, 2 * GD), BF),
            pltpu.SemaphoreType.DMA((8,)),
        ],
        compiler_params=PARAMS,
        cost_estimate=pl.CostEstimate(flops=16 * 10**9, bytes_accessed=10**7, transcendentals=4 * 10**6),
    )(kplace, own, place, query, *kv, early)


def attention_dq(chunks, own, place, qe, de, ks, vs, before=(), early=()):
    return pl.pallas_call(
        functools.partial(dq_kernel, chunks, len(before)),
        out_shape=shape(ROWS, EXT),
        in_specs=[SMEM] * 2 + [VM] * (4 + len(before)) + [ANY] * len(early),
        out_specs=VM,
        scratch_shapes=[pltpu.VMEM((NH * CHUNK, EXT), F32)],
        compiler_params=PARAMS,
        cost_estimate=pl.CostEstimate(flops=8 * 10**9, bytes_accessed=5 * 10**6, transcendentals=2 * 10**6),
    )(own, place, qe, de, ks, vs, *before, *early)


def attention_dkv(qplace, kplace, own, place, kv, qe, de, early):
    return pl.pallas_call(
        dkv_kernel,
        out_shape=shape(ROWS, 2 * GD),
        in_specs=[SMEM] * 4 + [VM] + [ANY] * 11,
        out_specs=VM,
        scratch_shapes=[
            pltpu.VMEM((LEN, EXT), BF),
            pltpu.VMEM((LEN, EXT), BF),
            pltpu.VMEM((NH * CHUNK, EXT), F32),
            pltpu.VMEM((NH * CHUNK, EXT), F32),
            pltpu.VMEM((LEN, EXT), BF),
            pltpu.VMEM((8, ROWS, EXT), BF),
            pltpu.SemaphoreType.DMA((9,)),
        ],
        compiler_params=PARAMS,
        cost_estimate=pl.CostEstimate(flops=15 * 10**9, bytes_accessed=10**7, transcendentals=4 * 10**6),
    )(qplace, kplace, own, place, kv, qe, *de, *early)


def delta_rows(d_attn, o, early):
    return pl.pallas_call(
        delta_kernel,
        out_shape=shape(ROWS, EXT),
        in_specs=[VM] * 2 + [ANY] * 2,
        out_specs=VM,
        compiler_params=PARAMS,
        cost_estimate=pl.CostEstimate(flops=10**6, bytes_accessed=10**6, transcendentals=0),
    )(d_attn, o, *early)


def prep_kernel(at_ref, w_ref, gain_ref, bias_ref, vb_ref, cols_ref):
    for k in range(4):

        @pl.when(at_ref[0] == k)
        def _():
            for i, part in enumerate((1, 2, 0)):
                start = part * D + k * GD
                cols_ref[:GD, i * GD : (i + 1) * GD] = w_ref[:, start : start + GD]

    small = jnp.concatenate(
        [gain_ref[...].astype(F32), bias_ref[...].astype(F32), vb_ref[...].astype(F32), jnp.zeros((8, GD), F32)],
        axis=0,
    )
    cols_ref[GD:, :] = jnp.concatenate([small, jnp.zeros((16, 2 * GD), F32)], axis=1).astype(BF)


def prepare(at, w, gains, biases, vb):
    return pl.pallas_call(
        prep_kernel,
        out_shape=shape(GD + 16, 3 * GD),
        in_specs=[SMEM] + [VM] * 4,
        out_specs=VM,
        compiler_params=PARAMS,
        cost_estimate=pl.CostEstimate(flops=1000, bytes_accessed=10**6, transcendentals=0),
    )(at, w, gains, biases, vb)


def qkv_kernel(at_ref, *refs):
    toks, ws = refs[:4], refs[4:8]
    cot_ref, out_ref = refs[8:10]
    kv_ref, q_ref, h1_ref, n1_ref, w_ref, small_ref, both_ref, w_scr = refs[10:]
    both_ref[:128, :] = cot_ref[...]
    both_ref[128:, :] = out_ref[...]
    yi, zi = at_ref[0], at_ref[1]
    for s in range(4):
        w_scr[s] = ws[s][...]
    for g in range(4):
        slot = (zi - g + 4) % 4
        w_ref[g * GD : (g + 1) * GD, :] = w_scr[slot, :GD]
        small_ref[:, g * GD : (g + 1) * GD] = w_scr[slot, GD:, :256].astype(F32)[:8, :GD]
    gain, shift = small_ref[0:1, :], small_ref[2:3, :]
    for s in range(4):
        rows = slice(128 * s, 128 * (s + 1))
        normed, _ = normalize(toks[s][...].astype(F32))
        n1_ref[rows, :] = normed
        h1_ref[rows, :] = (normed * gain + shift).astype(BF)
    own = w_scr[(zi - yi + 4) % 4, GD:, :256].astype(F32)[:8, :GD]
    qkv = dot(h1_ref[...], w_ref[...])
    kv_ref[:, :GD] = qkv[:, :GD].astype(BF)
    kv_ref[:, GD:] = (qkv[:, GD : 2 * GD] + own[7:8]).astype(BF)
    query = (qkv[:, 2 * GD :] + own[3:4]).astype(BF).astype(F32) * 0.125
    q_ref[...] = jnp.concatenate([query, jnp.zeros((ROWS, EXT - GD), F32)], axis=1).astype(BF)


def first_rows(at, toks, ws, cot, out_w):
    return pl.pallas_call(
        qkv_kernel,
        out_shape=(
            shape(ROWS, 2 * GD), shape(ROWS, EXT), shape(ROWS, D), shape(ROWS, D, dtype=F32),
            shape(D, 3 * GD), shape(8, D, dtype=F32), shape(320, D),
        ),
        in_specs=[SMEM] + [VM] * 10,
        out_specs=(VM,) * 7,
        scratch_shapes=[pltpu.VMEM((4, GD + 16, 3 * GD), BF)],
        compiler_params=PARAMS,
        cost_estimate=pl.CostEstimate(flops=5 * 10**8, bytes_accessed=6 * 10**6, transcendentals=0),
    )(at, *toks, *ws, cot, out_w)


def mlp_kernel(at_ref, *refs):
    h2s = refs[:4]
    both_ref, up_ref, down_ref, ub_ref, h2_ref, cot_ref, act_ref, dup_ref, dh_ref, sems = refs[4:]
    zi = at_ref[1]
    copies = [
        pltpu.make_async_copy(
            both_ref.at[(zi - s + 4) % 4, :128], cot_ref.at[128 * s : 128 * (s + 1)], sems.at[s]
        )
        for s in range(4)
    ]
    for copy in copies:
        copy.start()
    for copy in copies:
        copy.wait()
    for s in range(4):
        rows = slice(128 * s, 128 * (s + 1))
        h2 = h2s[s][...]
        h2_ref[rows, :] = h2
        up = dot(h2, up_ref[...]) + ub_ref[...].astype(F32)
        d_act = dot_t(cot_ref[rows, :], down_ref[...])
        square = up * up
        th = jnp.tanh(0.7978845608028654 * (up + 0.044715 * (square * up)))
        half = 0.5 * (1.0 + th)
        slope = half + 0.5 * up * (1.0 - th * th) * (
            0.7978845608028654 * (1.0 + 3 * 0.044715 * square)
        )
        act_ref[rows, :] = (up * half).astype(BF)
        d_up = (slope * d_act).astype(BF)
        dup_ref[rows, :] = d_up
        dh_ref[rows, :] = dot_t(d_up, up_ref[...]).astype(BF)


def feed_forward(at, h2s, both, w_up, w_down, ub):
    return pl.pallas_call(
        mlp_kernel,
        out_shape=(shape(ROWS, D),) * 5,
        in_specs=[SMEM] + [VM] * 4 + [ANY] + [VM] * 3,
        out_specs=(VM,) * 5,
        scratch_shapes=[pltpu.SemaphoreType.DMA((4,))],
        compiler_params=PARAMS,
        cost_estimate=pl.CostEstimate(flops=4 * 10**9, bytes_accessed=6 * 10**6, transcendentals=4 * 10**5),
    )(at, *h2s, both, w_up, w_down, ub)


def down_kernel(act_ref, wd_ref, early_ref, down_ref):
    down_ref[...] = dot(act_ref[...], wd_ref[...]).astype(BF)


def down_rows(act, w_down, early):
    return pl.pallas_call(
        down_kernel,
        out_shape=shape(ROWS, D),
        in_specs=[VM] * 2 + [ANY],
        out_specs=VM,
        compiler_params=PARAMS,
        cost_estimate=pl.CostEstimate(flops=10**9, bytes_accessed=3 * 10**6, transcendentals=0),
    )(act, w_down, early)


def hold_kernel(*refs):
    for s in range(3):
        refs[4 + s][...] = refs[s][...]


def hold_back(values, early):
    return pl.pallas_call(
        hold_kernel,
        out_shape=tuple(shape(*v.shape) for v in values),
        in_specs=[VM] * 3 + [ANY],
        out_specs=(VM,) * 3,
        compiler_params=PARAMS,
        cost_estimate=pl.CostEstimate(flops=1000, bytes_accessed=10**6, transcendentals=0),
    )(*values, early)


def wgrad_kernel(
    at_ref, h2_ref, dup_ref, act_ref, cot_ref, attn_ref, branch_ref, early_ref,
    keep_ref, give_ref, out_scr,
):
    yi, ci = at_ref[0], at_ref[2]
    g_up = t_dot(h2_ref[...], dup_ref[...])
    g_down = t_dot(act_ref[...], cot_ref[...])
    g_out = t_dot(attn_ref[...], branch_ref[...])
    for s in range(4):
        out_scr[s] = g_out[GD * s : GD * (s + 1)]
    vec = jnp.concatenate(
        [
            jnp.sum(dup_ref[...].astype(F32), axis=0, keepdims=True),
            jnp.sum(cot_ref[...].astype(F32), axis=0, keepdims=True),
            jnp.zeros((14, D), F32),
        ],
        axis=0,
    )
    for c in range(2):
        for j in range(4):
            b = 4 * c + j
            parts = []
            for z in range(4):
                parts.append(g_up[GD * z + 24 * b : GD * z + 24 * (b + 1)])
                parts.append(out_scr[(z - yi + 4) % 4, 24 * b : 24 * (b + 1)])
            parts += [g_down[96 * b : 96 * (b + 1)], vec]
            block = jnp.concatenate(parts, axis=0).astype(BF)
            slot = (j - yi + 4) % 4

            @pl.when(ci == c)
            def _():
                keep_ref[slot] = block

            @pl.when(ci != c)
            def _():
                give_ref[slot] = block


def weight_blocks(at, h2, d_up, act, cot, attn, d_branch, early):
    return pl.pallas_call(
        wgrad_kernel,
        out_shape=(shape(4, 304, D), shape(4, 304, D)),
        in_specs=[SMEM] + [VM] * 6 + [ANY],
        out_specs=(VM,) * 2,
        scratch_shapes=[pltpu.VMEM((4, GD, D), F32)],
        compiler_params=PARAMS,
        cost_estimate=pl.CostEstimate(flops=5 * 10**9, bytes_accessed=6 * 10**6, transcendentals=0),
    )(at, h2, d_up, act, cot, attn, d_branch, early)


def add_kernel(a_ref, b_ref, *outs):
    for s in range(4):
        outs[s][...] = (a_ref[s].astype(F32) + b_ref[s].astype(F32)).astype(BF)


def add_blocks(a, b):
    return pl.pallas_call(
        add_kernel,
        out_shape=(shape(*a.shape[1:]),) * 4,
        in_specs=[VM] * 2,
        out_specs=(VM,) * 4,
        compiler_params=PARAMS,
        cost_estimate=pl.CostEstimate(flops=10**6, bytes_accessed=6 * 10**6, transcendentals=0),
    )(a, b)


def mid_kernel(at_ref, *refs):
    blocks, (up_ref, down_ref, out_ref, vec_ref, scr) = refs[:8], refs[8:]
    yi, ci = at_ref[0], at_ref[2]
    for s in range(4):
        for c in range(2):
            scr[s, c] = blocks[2 * s + c][...]
    for c in range(2):
        for j in range(4):
            b = 4 * c + j
            block = scr[(yi - j + 4) % 4, (ci + c) % 2].astype(F32)
            for g in range(4):
                up_ref[24 * b : 24 * (b + 1), g * D : (g + 1) * D] = block[24 * g : 24 * (g + 1)]
            down_ref[96 * b : 96 * (b + 1), :] = block[96:192]
            out_ref[24 * b : 24 * (b + 1), :] = block[192:216]
            if b == 0:
                vec_ref[...] = block[216:224]


def mid_rows(at, blocks):
    return pl.pallas_call(
        mid_kernel,
        out_shape=(
            shape(GD, 4 * D, dtype=F32), shape(D, D, dtype=F32), shape(GD, D, dtype=F32),
            shape(8, D, dtype=F32),
        ),
        in_specs=[SMEM] + [VM] * 8,
        out_specs=(VM,) * 4,
        scratch_shapes=[pltpu.VMEM((4, 2, 232, D), BF)],
        compiler_params=PARAMS,
        cost_estimate=pl.CostEstimate(flops=10**6, bytes_accessed=8 * 10**6, transcendentals=0),
    )(at, *blocks)


def tail_kernel(
    at_ref, dkv_ref, dq_ref, h1_ref, n1_ref, w_ref, vec_ref, m0, m1, m2, m3, dh_ref, t_ref, rest_ref, scr
):
    yi, zi = at_ref[0], at_ref[1]
    scr[...] = (m0[...].astype(F32) + m2[...].astype(F32)) + (
        m1[...].astype(F32) + m3[...].astype(F32)
    )
    rest_ref[...] = scr[192:, :].astype(BF)
    for s in range(4):
        part = scr[pl.ds(pl.multiple_of((zi + s) % 4 * 48, 8), 48), :]
        t_ref[s, 192:240] = part[:, :640].astype(BF)
        t_ref[s, 240:, :128] = part[:, 640:].astype(BF)
        t_ref[s, 240:, 128:] = jnp.zeros((48, 512), BF)
    d_qkv = jnp.concatenate([dkv_ref[...], dq_ref[...]], axis=1)
    d_h1 = dot_t(d_qkv[:, : 3 * GD], w_ref[...])
    dh_ref[...] = d_h1.astype(BF)
    sums = jnp.sum(d_qkv.astype(F32), axis=0, keepdims=True)
    at_own = lambda v: jnp.concatenate([jnp.where(yi == k, v, 0.0) for k in range(4)], axis=1)
    vectors = jnp.concatenate(
        [
            jnp.sum(d_h1 * n1_ref[...], axis=0, keepdims=True),
            jnp.sum(d_h1, axis=0, keepdims=True),
            at_own(sums[:, 2 * GD : 3 * GD]),
            at_own(sums[:, GD : 2 * GD]),
            vec_ref[4:8, :],
        ],
        axis=0,
    ).astype(BF)
    row = lax.broadcasted_iota(jnp.int32, (8, 128), 0)
    lane = lax.broadcasted_iota(jnp.int32, (8, 128), 1)
    columns = t_dot(vectors, jnp.where(lane == row + 64, 1.0, 0.0).astype(BF))
    grad = t_dot(h1_ref[...], d_qkv)
    for g in range(4):
        rows = slice(g * GD, (g + 1) * GD)
        slot = (g - zi + 4) % 4
        t_ref[slot, :GD, :512] = grad[rows, :512].astype(BF)
        t_ref[slot, :GD, 512:] = (grad[rows, 512:] + columns[rows]).astype(BF)


def last_gradients(at, d_kv, d_q, h1, n1, w, vec, mid):
    return pl.pallas_call(
        tail_kernel,
        out_shape=(shape(ROWS, D), shape(4, 288, 640), shape(112, D)),
        in_specs=[SMEM] + [VM] * 10,
        out_specs=(VM,) * 3,
        scratch_shapes=[pltpu.VMEM((304, D), F32)],
        compiler_params=PARAMS,
        cost_estimate=pl.CostEstimate(flops=3 * 10**9, bytes_accessed=6 * 10**6, transcendentals=0),
    )(at, d_kv, d_q, h1, n1, w, vec, *mid)


def sum_kernel(at_ref, t_ref, r1, r2, r3, dh_ref, rest_ref, kept_ref, given_ref, same_ref, block_ref, scr):
    same_ref[...] = dh_ref[...]
    slots = (r1, r2, r3)
    for c in range(2):
        rows = slice(96 * c, 96 * (c + 1))
        a, b, d, e = (v.astype(F32) for v in [t_ref[0, rows]] + [r[rows] for r in slots])
        total = ((a + d) + (b + e)).astype(BF)

        @pl.when(at_ref[2] == c)
        def _():
            kept_ref[...] = total

        @pl.when(at_ref[2] != c)
        def _():
            given_ref[...] = total

    for s in range(4):
        part = (t_ref[0, GD:] if s == 0 else slots[s - 1][GD:]).astype(F32)
        scr[s, :, :640] = part[:48]
        scr[s, :, 640:] = part[48:, :128]
    up = [scr[(at_ref[1] - g + 4) % 4][:24] for g in range(4)]
    g_out = (scr[0] + scr[2])[24:] + (scr[1] + scr[3])[24:]
    rest = rest_ref[...].astype(F32)
    block_ref[...] = jnp.concatenate(up + [rest[:96], g_out, rest[96:]], axis=0).astype(BF)


def sum_slots(at, own, slots, d_h1, rest):
    return pl.pallas_call(
        sum_kernel,
        out_shape=(shape(96, 640), shape(96, 640), shape(ROWS, D), shape(232, D)),
        in_specs=[SMEM] + [VM] * 6,
        out_specs=(VM,) * 4,
        scratch_shapes=[pltpu.VMEM((4, 48, D), F32)],
        compiler_params=PARAMS,
        cost_estimate=pl.CostEstimate(flops=10**6, bytes_accessed=3 * 10**6, transcendentals=0),
    )(at, own, *slots, d_h1, rest)


def final_kernel(at_ref, *refs):
    slots, (grad_ref, vec_ref, scr) = refs[:4], refs[4:]
    for s in range(4):
        for c in range(2):
            scr[s, c] = slots[s][c]
    yi, ci = at_ref[0], at_ref[2]
    for c in range(2):
        rows = slice(96 * c, 96 * (c + 1))
        total = []
        for g in range(4):
            value = scr[(yi - g + 4) % 4, (ci + c) % 2].astype(F32)
            for i, part in enumerate((1, 2, 0)):
                start = part * D + g * GD
                grad_ref[rows, start : start + GD] = value[:, i * GD : (i + 1) * GD]
            total.append(value[:, 512:])
        vec_ref[rows, :] = (total[0] + total[1]) + (total[2] + total[3])


def final_rows(at, slots):
    return pl.pallas_call(
        final_kernel,
        out_shape=(shape(GD, 3 * D, dtype=F32), shape(GD, 128, dtype=F32)),
        in_specs=[SMEM] + [VM] * 4,
        out_specs=(VM, VM),
        scratch_shapes=[pltpu.VMEM((4, 2, 96, 640), BF)],
        compiler_params=PARAMS,
        cost_estimate=pl.CostEstimate(flops=10**6, bytes_accessed=3 * 10**6, transcendentals=0),
    )(at, *slots)


def gather(value, axes, axis=0):
    return lax.all_gather(value, axes, axis=axis, tiled=True)


def swap(value, axes):
    return lax.all_to_all(value, axes, 0, 0)


def send(value, axis, step):
    n = lax.axis_size(axis)
    return lax.ppermute(value, axis, [(i, (i + step) % n) for i in range(n)])


def spread(value, axis):
    return [value] + [send(value, axis, s) for s in range(1, 4)]


def exchange(slots, axis, step):
    return [slots[0]] + [send(slots[s], axis, s * step) for s in range(1, 4)]


def add_slots(slots):
    a, b, c, d = (v.astype(F32) for v in slots)
    return (a + c) + (b + d)


def group_of(value, index, size, axis=0):
    return lax.dynamic_slice_in_dim(value, (index % 4) * size, size, axis)


def local(
    tokens, qkv_w, out_w, up_w, down_w, norm_gains, biases, value_bias, up_bias, cotangent, block_place
):
    xi = lax.axis_index("x")
    yi = lax.axis_index("y")
    ci = lax.axis_index("core")
    zi = lax.axis_index("fsdp")
    tok_own = tokens[0]
    cot_own = cotangent[0]

    at = jnp.stack([yi, zi, ci]).astype(jnp.int32)
    ws = spread(prepare(at, qkv_w, norm_gains, biases, value_bias[None]), "fsdp")
    toks = spread(tok_own, "y")

    ids = jnp.arange(NBLK, dtype=jnp.int32)
    slot_x, slot_c, slot_y, blk = ids // 16, (ids // 8) % 2, (ids // 2) % 4, ids % 2
    pick = lambda at: jnp.sum(jnp.where(at[:, None] == ids[None, :], block_place[None, :], 0), axis=1)
    at_y = (yi - slot_y + 4) % 4
    key_place = pick(at_y * 16 + ((xi - slot_x + 4) % 4) * 4 + ((ci + slot_c) % 2) * 2 + blk)
    query_place = pick(at_y * 16 + slot_x * 4 + slot_c * 2 + blk)
    own_place = key_place[:8]
    rank = jnp.sum((own_place[None, :] > own_place[:, None]).astype(jnp.int32), axis=1)
    order = jnp.arange(8, dtype=jnp.int32)
    hit = rank[None, :] == order[:, None]
    own = jnp.sum(jnp.where(hit, order[None, :], 0), axis=1)
    place = jnp.sum(jnp.where(hit, own_place[None, :], 0), axis=1)

    w_up = swap(up_w.reshape(GD, 4, D).transpose(1, 0, 2), "fsdp").reshape(D, D)
    w_down = down_w

    kv_own, query, h1, n1y, w_qkv, small, both = first_rows(at, toks, ws, cot_own, out_w)
    both = lax.all_gather(both, "fsdp", axis=0)
    w_out = jnp.concatenate(
        [lax.dynamic_index_in_dim(both, (yi + s) % 4, 0, keepdims=False)[128:] for s in range(4)], axis=0
    )
    gain1, gain2 = small[0], small[1]
    out_bias, shift2, down_bias = small[4], small[5], small[6]
    with jax.named_scope("kv"):
        kv_all = [p for v in spread(kv_own, "x") for p in (v, send(v, "core", 1))]
    attn, o_exact, qe, ks, vs = attention_forward(key_place, own, place, query, kv_all, w_up)
    qe_all = gather(qe, XC)

    attn = attn[:, 64:]
    with jax.named_scope("attn_y"):
        attn_own = exchange([attn[128 * s : 128 * (s + 1)] for s in range(4)], "y", -1)
    attn_own = jnp.concatenate(attn_own, axis=1)
    x2 = tok_own.astype(F32) + (dot(attn_own, w_out) + out_bias)
    n2, s2 = normalize(x2)
    h2_own = (n2 * gain2 + shift2).astype(BF)

    with jax.named_scope("h2_z"):
        h2s = spread(h2_own, "fsdp")
    h2, cot_z, act, d_up, d_h2_part = feed_forward(
        at, h2s, both, w_up, w_down, up_bias[None]
    )
    back = lambda v: add_slots(exchange([v[128 * s : 128 * (s + 1)] for s in range(4)], "fsdp", -1))
    with jax.named_scope("d_h2_z"):
        d_h2 = back(d_h2_part)
    cot32 = cot_own.astype(F32)
    d_x2 = cot32 + norm_back(d_h2 * gain2, n2, s2)
    d_branch = d_x2.astype(BF)
    d_attn = dot_t(d_branch, w_out).astype(BF)
    with jax.named_scope("d_attn_y"):
        d_attn_own = exchange([d_attn[:, GD * s : GD * (s + 1)] for s in range(4)], "y", 1)
    d_attn_own = jnp.concatenate(d_attn_own, axis=0)
    de = delta_rows(d_attn_own, o_exact, (qe_all, both))
    with jax.named_scope("de"):
        arrived = spread(de, "x")[1:]
        d_q = attention_dq((0, 3), own, place, qe, de, ks, vs)
        arrived = hold_back(arrived, d_q)
        de_all = [p for v in (de, *arrived) for p in (v, send(v, "core", 1))]
    keep, give = weight_blocks(at, h2, d_up, act, cot_z, attn_own, d_branch, d_q)
    with jax.named_scope("mid"):
        mid = add_blocks(keep, send(give, "core", 1))
        mid = add_slots(exchange(mid, "y", 1)).astype(BF)
    with jax.named_scope("down"):
        layer_out = (x2 + back(down_rows(act, w_down, d_q)) + down_bias).astype(BF)
    d_q = attention_dq((1, 2), own, place, qe, de, ks, vs, (d_q,), arrived)
    d_kv = attention_dkv(
        query_place, key_place, own, place, kv_own, qe_all, de_all, (layer_out, mid)
    )
    with jax.named_scope("mid"):
        mid = spread(mid, "x")

    vec = jnp.stack([jnp.sum(d_h2 * n2, axis=0), jnp.sum(d_branch.astype(F32), axis=0), jnp.sum(d_h2, axis=0)])
    vec = jnp.pad(vec, ((4, 1), (0, 0)))
    d_h1_send, tail, rest = last_gradients(at, d_kv, d_q, h1, n1y, w_qkv, vec, mid)
    with jax.named_scope("tail_z"):
        received = [send(tail[s], "fsdp", s) for s in range(1, 4)]
    kept, given, d_h1_send, mid = sum_slots(at, tail, received, d_h1_send, rest)
    with jax.named_scope("mid"):
        mid = [p for v in spread(mid, "y") for p in (v, send(v, "core", 1))]
    grad_up, grad_down, grad_out, out_vec = mid_rows(at, mid)
    grad_up_bias = out_vec[0]
    grad_down_bias = lax.dynamic_slice(out_vec[1], (zi * GD,), (GD,))
    with jax.named_scope("d_h1_y"):
        d_h1 = add_slots(exchange([d_h1_send[128 * s : 128 * (s + 1)] for s in range(4)], "y", -1))
    n1, s1 = normalize(tok_own.astype(F32))
    input_grad = (d_x2 + norm_back(d_h1 * gain1, n1, s1)).astype(BF)

    with jax.named_scope("tail_core"):
        tail = (kept.astype(F32) + send(given, "core", 1).astype(F32)).astype(BF)
    with jax.named_scope("tail_x"):
        tail = add_slots(spread(tail, "x")).astype(BF)
    with jax.named_scope("tail_y"):
        tail = [jnp.stack([v, send(v, "core", 1)]) for v in spread(tail, "y")]
    grad_qkv, vectors = final_rows(at, tail)
    vectors = vectors[:, 64:71].T
    grad_gains = jnp.stack([vectors[0], vectors[4]])
    grad_biases = jnp.stack([vectors[1], vectors[2], vectors[5], vectors[6], grad_down_bias])
    grad_value_bias = vectors[3]
    return (
        layer_out[None], input_grad[None], grad_qkv, grad_out, grad_up, grad_down,
        grad_gains, grad_biases, grad_value_bias, grad_up_bias,
    )


def solution(mesh):
    grid = Mesh(mesh.devices.reshape(4, 4, 2, 4), ("y", "x", "core", "fsdp"))
    rows = P("fsdp", CTX, None)
    in_specs = (
        rows, P("fsdp", None), P("fsdp", None), P("fsdp", None), P("fsdp", None),
        P(None, "fsdp"), P(None, "fsdp"), P("fsdp"), P("fsdp"), rows, P(),
    )
    out_specs = (
        rows, rows, P("fsdp", None), P("fsdp", None), P("fsdp", None), P("fsdp", None),
        P(None, "fsdp"), P(None, "fsdp"), P("fsdp"), P("fsdp"),
    )
    return jax.shard_map(local, mesh=grid, in_specs=in_specs, out_specs=out_specs, check_vma=False)
```

```python
import functools

import jax
import jax.numpy as jnp
from jax import lax
from jax.experimental import pallas as pl
from jax.experimental.pallas import tpu as pltpu
from jax.sharding import Mesh
from jax.sharding import PartitionSpec as P

EPS = 1e-05
D = 768
GD = 192
NH = 3
HD = 64
ROWS = 512
LEN = 4096
BLK = 64
NBLK = 64
EXT = 256
TILE = 1024
CHUNK = 128
BF = jnp.bfloat16
F32 = jnp.float32
XC = ("x", "core")
CTX = ("y", "x", "core")


def dot(a, b):
    return lax.dot_general(a, b, (((1,), (0,)), ((), ())), preferred_element_type=F32)


def dot_t(a, b):
    return lax.dot_general(a, b, (((1,), (1,)), ((), ())), preferred_element_type=F32)


def t_dot(a, b):
    return lax.dot_general(a, b, (((0,), (0,)), ((), ())), preferred_element_type=F32)


def normalize(value):
    center = value - jnp.mean(value, axis=-1, keepdims=True)
    factor = lax.rsqrt(jnp.mean(center * center, axis=-1, keepdims=True) + EPS)
    return (center * factor, factor)


def norm_back(scaled, normed, factor):
    return factor * (
        scaled
        - jnp.mean(scaled, axis=-1, keepdims=True)
        - normed * jnp.mean(scaled * normed, axis=-1, keepdims=True)
    )


def lanes(rows):
    return lax.broadcasted_iota(jnp.int32, (rows, EXT), 1)


def head_mask(rows, h, high):
    lane = lanes(rows)
    if high:
        feat = (lane >= 64 + HD * h) & (lane < 64 + HD * (h + 1))
        ext = (lane >= 3 * h) & (lane < 3 * h + 3)
    else:
        feat = (lane >= HD * h) & (lane < HD * (h + 1))
        ext = (lane >= GD + 3 * h) & (lane < GD + 3 * h + 3)
    return feat | ext


def feature_mask(rows, h, high):
    lane = lanes(rows) - (64 if high else 0)
    return (lane >= HD * h) & (lane < HD * (h + 1))


def stack_heads(value, high):
    rows = value.shape[0]
    zero = jnp.zeros_like(value)
    return jnp.concatenate(
        [jnp.where(head_mask(rows, h, high), value, zero) for h in range(NH)], axis=0
    )


def merge_heads(stacked, high):
    rows = stacked.shape[0] // NH
    out = jnp.zeros((rows, EXT), F32)
    for h in range(NH):
        out = out + jnp.where(feature_mask(rows, h, high), stacked[h * rows : (h + 1) * rows], 0.0)
    return out


def pieces(value):
    first = value.astype(BF).astype(F32)
    second = (value - first).astype(BF).astype(F32)
    third = (value - first - second).astype(BF).astype(F32)
    return (first, second, third)


def add_extras(base, columns, high):
    rows = base.shape[0]
    lane = lanes(rows)
    start = 0 if high else GD
    for h in range(NH):
        for i, piece in enumerate(pieces(columns[h])):
            base = jnp.where(lane == start + 3 * h + i, piece, base)
    return base


def key_form(kv):
    lane = lanes(kv.shape[0])
    one = jnp.ones((kv.shape[0], EXT), BF)
    zero = jnp.zeros((kv.shape[0], EXT), BF)
    low = jnp.where(lane < GD, kv[:, :EXT], jnp.where(lane < GD + 9, one, zero))
    high = jnp.where(lane >= 64, kv[:, 128:384], jnp.where(lane < 9, one, zero))
    return (low, high)


def block_rows(index):
    return pl.ds(pl.multiple_of(index * BLK, BLK), BLK)


def stacked_pos(place_a, place_b):
    row = lax.broadcasted_iota(jnp.int32, (NH * CHUNK, 1), 0)
    place = jnp.where(row % CHUNK < BLK, place_a, place_b)
    return place * BLK + row % BLK


def col_pos(tile):
    return tile * TILE + lax.broadcasted_iota(jnp.int32, (NH * CHUNK, TILE), 1)


def fold(value, op):
    out = value[:, :128]
    for i in range(1, value.shape[1] // 128):
        out = op(out, value[:, i * 128 : (i + 1) * 128])
    return out


def tile_rows(t):
    return pl.ds(pl.multiple_of(t * TILE, TILE), TILE)


def fwd_kernel(
    kplace_ref, own_ref, place_ref, q_ref, *refs
):
    kv_refs = refs[:8]
    attn_ref, o_ref, qe_ref, ks_ref, vs_ref, s_scr, m_scr, l_scr, acc_scr, land, sems = refs[9:]
    copies = [pltpu.make_async_copy(kv_refs[k], land.at[k], sems.at[k]) for k in range(8)]
    for copy in copies:
        copy.start()
    for k in range(8):
        copies[k].wait()
        for b in range(8):
            low, high = key_form(land[k, b * BLK : (b + 1) * BLK, :])
            dst = block_rows(kplace_ref[8 * k + b])
            ks_ref[dst, :] = low
            vs_ref[dst, :] = high

    for c in range(ROWS // CHUNK):
        place_a, place_b = place_ref[2 * c], place_ref[2 * c + 1]
        blocks = (own_ref[2 * c], own_ref[2 * c + 1])
        query = jnp.concatenate([q_ref[block_rows(b), :] for b in blocks], axis=0)
        stacked = stack_heads(query, False)
        qpos = stacked_pos(place_a, place_b)
        tiles = place_a // (TILE // BLK) + 1
        m_scr[...] = jnp.full(m_scr.shape, -1e30, F32)

        def score_step(t, _):
            scores = dot_t(stacked, ks_ref[tile_rows(t), :])
            scores = jnp.where(col_pos(t) <= qpos, scores, -1e30)
            s_scr[t] = scores
            m_scr[...] = jnp.maximum(m_scr[...], fold(scores, jnp.maximum))
            return 0

        lax.fori_loop(0, tiles, score_step, 0)
        peak = jnp.max(m_scr[...], axis=1, keepdims=True)
        l_scr[...] = jnp.zeros(l_scr.shape, F32)
        acc_scr[...] = jnp.zeros(acc_scr.shape, F32)

        def value_step(t, _):
            prob = jnp.exp(s_scr[t] - peak)
            l_scr[...] = l_scr[...] + fold(prob, jnp.add)
            acc_scr[...] = acc_scr[...] + dot(prob.astype(BF), vs_ref[tile_rows(t), :])
            return 0

        lax.fori_loop(0, tiles, value_step, 0)
        total = jnp.sum(l_scr[...], axis=1, keepdims=True)
        log_total = peak + jnp.log(total)
        out = merge_heads(acc_scr[...] / total, True)
        ext = add_extras(
            query.astype(F32),
            [-log_total[h * CHUNK : (h + 1) * CHUNK] for h in range(NH)],
            False,
        ).astype(BF)
        for i, b in enumerate(blocks):
            rows = slice(i * BLK, (i + 1) * BLK)
            o_ref[block_rows(b), :] = out[rows]
            attn_ref[block_rows(b), :] = out[rows].astype(BF)
            qe_ref[block_rows(b), :] = ext[rows]


def dq_kernel(chunks, n_before, own_ref, place_ref, qe_ref, de_ref, ks_ref, vs_ref, *refs):
    *before, dq_ref, acc_scr = refs
    if n_before:
        dq_ref[...] = before[0][...]
    for c in chunks:
        place_a, place_b = place_ref[2 * c], place_ref[2 * c + 1]
        blocks = (own_ref[2 * c], own_ref[2 * c + 1])
        query = stack_heads(jnp.concatenate([qe_ref[block_rows(b), :] for b in blocks], axis=0), False)
        d_out = stack_heads(jnp.concatenate([de_ref[block_rows(b), :] for b in blocks], axis=0), True)
        qpos = stacked_pos(place_a, place_b)
        tiles = place_a // (TILE // BLK) + 1
        acc_scr[...] = jnp.zeros(acc_scr.shape, F32)

        def step(t, _):
            keys = ks_ref[tile_rows(t), :]
            prob = jnp.where(col_pos(t) <= qpos, jnp.exp(dot_t(query, keys)), 0.0)
            d_raw = (prob * dot_t(d_out, vs_ref[tile_rows(t), :])).astype(BF)
            acc_scr[...] = acc_scr[...] + dot(d_raw, keys)
            return 0

        lax.fori_loop(0, tiles, step, 0)
        out = (merge_heads(acc_scr[...], False) * 0.125).astype(BF)
        for i, b in enumerate(blocks):
            dq_ref[block_rows(b), :] = out[i * BLK : (i + 1) * BLK]


def dkv_kernel(qplace_ref, kplace_ref, own_ref, place_ref, kv_ref, qe_ref, *refs):
    de_refs, (dkv_ref, qs_scr, ds_scr, dk_scr, dv_scr, q_land, d_land, sems) = refs[:8], refs[8:]
    q_copy = pltpu.make_async_copy(qe_ref, q_land, sems.at[8])
    q_copy.start()
    copies = [pltpu.make_async_copy(de_refs[k], d_land.at[k], sems.at[k]) for k in range(8)]
    for copy in copies:
        copy.start()
    q_copy.wait()
    for b in range(NBLK):
        qs_scr[block_rows(qplace_ref[b]), :] = q_land[b * BLK : (b + 1) * BLK, :]
    for k in range(8):
        copies[k].wait()
        for b in range(8):
            ds_scr[block_rows(kplace_ref[8 * k + b]), :] = d_land[k, b * BLK : (b + 1) * BLK, :]

    for c in range(ROWS // CHUNK):
        place_a, place_b = place_ref[2 * c], place_ref[2 * c + 1]
        blocks = (own_ref[2 * c], own_ref[2 * c + 1])
        low, high = key_form(jnp.concatenate([kv_ref[block_rows(b), :] for b in blocks], axis=0))
        keys = stack_heads(low, False)
        values = stack_heads(high, True)
        kpos = stacked_pos(place_a, place_b)
        dk_scr[...] = jnp.zeros(dk_scr.shape, F32)
        dv_scr[...] = jnp.zeros(dv_scr.shape, F32)

        def step(t, _):
            query = qs_scr[tile_rows(t), :]
            d_out = ds_scr[tile_rows(t), :]
            prob = jnp.where(col_pos(t) >= kpos, jnp.exp(dot_t(keys, query)), 0.0)
            d_raw = (prob * dot_t(values, d_out)).astype(BF)
            dv_scr[...] = dv_scr[...] + dot(prob.astype(BF), d_out)
            dk_scr[...] = dk_scr[...] + dot(d_raw, query)
            return 0

        lax.fori_loop(place_b // (TILE // BLK), LEN // TILE, step, 0)
        d_keys = merge_heads(dk_scr[...], False)
        d_values = merge_heads(dv_scr[...], True)
        out = jnp.concatenate(
            [d_keys[:, :128], d_keys[:, 128:] + d_values[:, :128], d_values[:, 128:]], axis=1
        ).astype(BF)
        for i, b in enumerate(blocks):
            dkv_ref[block_rows(b), :] = out[i * BLK : (i + 1) * BLK]


def delta_kernel(d_ref, o_ref, early_a, early_b, de_ref):
    d_out = jnp.concatenate([jnp.zeros((ROWS, 64), F32), d_ref[...].astype(F32)], axis=1)
    product = d_out * o_ref[...]
    sums = [
        -jnp.sum(jnp.where(feature_mask(ROWS, h, True), product, 0.0), axis=1, keepdims=True)
        for h in range(NH)
    ]
    de_ref[...] = add_extras(d_out, sums, True).astype(BF)


SMEM = pl.BlockSpec(memory_space=pltpu.SMEM)
VM = pl.BlockSpec(memory_space=pltpu.VMEM)
ANY = pl.BlockSpec(memory_space=pl.ANY)
PARAMS = pltpu.CompilerParams(vmem_limit_bytes=48 * 1024 * 1024)


def shape(*dims, dtype=BF):
    return jax.ShapeDtypeStruct(dims, dtype)


def attention_forward(kplace, own, place, query, kv, early):
    return pl.pallas_call(
        fwd_kernel,
        out_shape=(
            shape(ROWS, EXT), shape(ROWS, EXT, dtype=F32), shape(ROWS, EXT),
            shape(LEN, EXT), shape(LEN, EXT),
        ),
        in_specs=[SMEM] * 3 + [VM] + [ANY] * 9,
        out_specs=(VM,) * 5,
        scratch_shapes=[
            pltpu.VMEM((LEN // TILE, NH * CHUNK, TILE), F32),
            pltpu.VMEM((NH * CHUNK, 128), F32),
            pltpu.VMEM((NH * CHUNK, 128), F32),
            pltpu.VMEM((NH * CHUNK, EXT), F32),
            pltpu.VMEM((8, ROWS, 2 * GD), BF),
            pltpu.SemaphoreType.DMA((8,)),
        ],
        compiler_params=PARAMS,
        cost_estimate=pl.CostEstimate(flops=16 * 10**9, bytes_accessed=10**7, transcendentals=4 * 10**6),
    )(kplace, own, place, query, *kv, early)


def attention_dq(chunks, own, place, qe, de, ks, vs, before=(), early=()):
    return pl.pallas_call(
        functools.partial(dq_kernel, chunks, len(before)),
        out_shape=shape(ROWS, EXT),
        in_specs=[SMEM] * 2 + [VM] * (4 + len(before)) + [ANY] * len(early),
        out_specs=VM,
        scratch_shapes=[pltpu.VMEM((NH * CHUNK, EXT), F32)],
        compiler_params=PARAMS,
        cost_estimate=pl.CostEstimate(flops=8 * 10**9, bytes_accessed=5 * 10**6, transcendentals=2 * 10**6),
    )(own, place, qe, de, ks, vs, *before, *early)


def attention_dkv(qplace, kplace, own, place, kv, qe, de):
    return pl.pallas_call(
        dkv_kernel,
        out_shape=shape(ROWS, 2 * GD),
        in_specs=[SMEM] * 4 + [VM] + [ANY] * 9,
        out_specs=VM,
        scratch_shapes=[
            pltpu.VMEM((LEN, EXT), BF),
            pltpu.VMEM((LEN, EXT), BF),
            pltpu.VMEM((NH * CHUNK, EXT), F32),
            pltpu.VMEM((NH * CHUNK, EXT), F32),
            pltpu.VMEM((LEN, EXT), BF),
            pltpu.VMEM((8, ROWS, EXT), BF),
            pltpu.SemaphoreType.DMA((9,)),
        ],
        compiler_params=PARAMS,
        cost_estimate=pl.CostEstimate(flops=15 * 10**9, bytes_accessed=10**7, transcendentals=4 * 10**6),
    )(qplace, kplace, own, place, kv, qe, *de)


def delta_rows(d_attn, o, early):
    return pl.pallas_call(
        delta_kernel,
        out_shape=shape(ROWS, EXT),
        in_specs=[VM] * 2 + [ANY] * 2,
        out_specs=VM,
        compiler_params=PARAMS,
        cost_estimate=pl.CostEstimate(flops=10**6, bytes_accessed=10**6, transcendentals=0),
    )(d_attn, o, *early)


def prep_kernel(at_ref, w_ref, gain_ref, bias_ref, vb_ref, cols_ref):
    for k in range(4):

        @pl.when(at_ref[0] == k)
        def _():
            for i, part in enumerate((1, 2, 0)):
                start = part * D + k * GD
                cols_ref[:GD, i * GD : (i + 1) * GD] = w_ref[:, start : start + GD]

    small = jnp.concatenate(
        [gain_ref[...].astype(F32), bias_ref[...].astype(F32), vb_ref[...].astype(F32), jnp.zeros((8, GD), F32)],
        axis=0,
    )
    cols_ref[GD:, :] = jnp.concatenate([small, jnp.zeros((16, 2 * GD), F32)], axis=1).astype(BF)


def prepare(at, w, gains, biases, vb):
    return pl.pallas_call(
        prep_kernel,
        out_shape=shape(GD + 16, 3 * GD),
        in_specs=[SMEM] + [VM] * 4,
        out_specs=VM,
        compiler_params=PARAMS,
        cost_estimate=pl.CostEstimate(flops=1000, bytes_accessed=10**6, transcendentals=0),
    )(at, w, gains, biases, vb)


def qkv_kernel(at_ref, *refs):
    toks, ws = refs[:4], refs[4:8]
    kv_ref, q_ref, h1_ref, n1_ref, w_ref, small_ref, w_scr = refs[8:]
    yi, zi = at_ref[0], at_ref[1]
    for s in range(4):
        w_scr[s] = ws[s][...]
    for g in range(4):
        slot = (zi - g + 4) % 4
        w_ref[g * GD : (g + 1) * GD, :] = w_scr[slot, :GD]
        small_ref[:, g * GD : (g + 1) * GD] = w_scr[slot, GD:, :256].astype(F32)[:8, :GD]
    gain, shift = small_ref[0:1, :], small_ref[2:3, :]
    for s in range(4):
        rows = slice(128 * s, 128 * (s + 1))
        normed, _ = normalize(toks[s][...].astype(F32))
        n1_ref[rows, :] = normed
        h1_ref[rows, :] = (normed * gain + shift).astype(BF)
    own = w_scr[(zi - yi + 4) % 4, GD:, :256].astype(F32)[:8, :GD]
    qkv = dot(h1_ref[...], w_ref[...])
    kv_ref[:, :GD] = qkv[:, :GD].astype(BF)
    kv_ref[:, GD:] = (qkv[:, GD : 2 * GD] + own[7:8]).astype(BF)
    query = (qkv[:, 2 * GD :] + own[3:4]).astype(BF).astype(F32) * 0.125
    q_ref[...] = jnp.concatenate([query, jnp.zeros((ROWS, EXT - GD), F32)], axis=1).astype(BF)


def both_kernel(cot_ref, out_ref, early_ref, both_ref):
    both_ref[:128, :] = cot_ref[...]
    both_ref[128:, :] = out_ref[...]


def both_rows(cot, out_w, early):
    return pl.pallas_call(
        both_kernel,
        out_shape=shape(320, D),
        in_specs=[VM] * 2 + [ANY],
        out_specs=VM,
        compiler_params=PARAMS,
        cost_estimate=pl.CostEstimate(flops=1000, bytes_accessed=10**6, transcendentals=0),
    )(cot, out_w, early)


def first_rows(at, toks, ws):
    return pl.pallas_call(
        qkv_kernel,
        out_shape=(
            shape(ROWS, 2 * GD), shape(ROWS, EXT), shape(ROWS, D), shape(ROWS, D, dtype=F32),
            shape(D, 3 * GD), shape(8, D, dtype=F32),
        ),
        in_specs=[SMEM] + [VM] * 8,
        out_specs=(VM,) * 6,
        scratch_shapes=[pltpu.VMEM((4, GD + 16, 3 * GD), BF)],
        compiler_params=PARAMS,
        cost_estimate=pl.CostEstimate(flops=5 * 10**8, bytes_accessed=6 * 10**6, transcendentals=0),
    )(at, *toks, *ws)


def mlp_kernel(at_ref, *refs):
    h2s = refs[:4]
    both_ref, up_ref, down_ref, ub_ref, h2_ref, cot_ref, act_ref, dup_ref, dh_ref, sems = refs[4:]
    zi = at_ref[1]
    copies = [
        pltpu.make_async_copy(
            both_ref.at[(zi - s + 4) % 4, :128], cot_ref.at[128 * s : 128 * (s + 1)], sems.at[s]
        )
        for s in range(4)
    ]
    for copy in copies:
        copy.start()
    for copy in copies:
        copy.wait()
    for s in range(4):
        rows = slice(128 * s, 128 * (s + 1))
        h2 = h2s[s][...]
        h2_ref[rows, :] = h2
        up = dot(h2, up_ref[...]) + ub_ref[...].astype(F32)
        d_act = dot_t(cot_ref[rows, :], down_ref[...])
        square = up * up
        th = jnp.tanh(0.7978845608028654 * (up + 0.044715 * (square * up)))
        half = 0.5 * (1.0 + th)
        slope = half + 0.5 * up * (1.0 - th * th) * (
            0.7978845608028654 * (1.0 + 3 * 0.044715 * square)
        )
        act_ref[rows, :] = (up * half).astype(BF)
        d_up = (slope * d_act).astype(BF)
        dup_ref[rows, :] = d_up
        dh_ref[rows, :] = dot_t(d_up, up_ref[...]).astype(BF)


def feed_forward(at, h2s, both, w_up, w_down, ub):
    return pl.pallas_call(
        mlp_kernel,
        out_shape=(shape(ROWS, D),) * 5,
        in_specs=[SMEM] + [VM] * 4 + [ANY] + [VM] * 3,
        out_specs=(VM,) * 5,
        scratch_shapes=[pltpu.SemaphoreType.DMA((4,))],
        compiler_params=PARAMS,
        cost_estimate=pl.CostEstimate(flops=4 * 10**9, bytes_accessed=6 * 10**6, transcendentals=4 * 10**5),
    )(at, *h2s, both, w_up, w_down, ub)


def down_kernel(act_ref, wd_ref, early_ref, down_ref):
    down_ref[...] = dot(act_ref[...], wd_ref[...]).astype(BF)


def down_rows(act, w_down, early):
    return pl.pallas_call(
        down_kernel,
        out_shape=shape(ROWS, D),
        in_specs=[VM] * 2 + [ANY],
        out_specs=VM,
        compiler_params=PARAMS,
        cost_estimate=pl.CostEstimate(flops=10**9, bytes_accessed=3 * 10**6, transcendentals=0),
    )(act, w_down, early)


def hold_kernel(*refs):
    for s in range(3):
        refs[4 + s][...] = refs[s][...]


def hold_back(values, early):
    return pl.pallas_call(
        hold_kernel,
        out_shape=tuple(shape(*v.shape) for v in values),
        in_specs=[VM] * 3 + [ANY],
        out_specs=(VM,) * 3,
        compiler_params=PARAMS,
        cost_estimate=pl.CostEstimate(flops=1000, bytes_accessed=10**6, transcendentals=0),
    )(*values, early)


def wgrad_kernel(
    at_ref, h2_ref, dup_ref, act_ref, cot_ref, attn_ref, branch_ref, early_ref,
    keep_ref, give_ref, out_scr,
):
    yi, ci = at_ref[0], at_ref[2]
    g_up = t_dot(h2_ref[...], dup_ref[...])
    g_down = t_dot(act_ref[...], cot_ref[...])
    g_out = t_dot(attn_ref[...], branch_ref[...])
    for s in range(4):
        out_scr[s] = g_out[GD * s : GD * (s + 1)]
    vec = jnp.concatenate(
        [
            jnp.sum(dup_ref[...].astype(F32), axis=0, keepdims=True),
            jnp.sum(cot_ref[...].astype(F32), axis=0, keepdims=True),
            jnp.zeros((14, D), F32),
        ],
        axis=0,
    )
    for c in range(2):
        for j in range(4):
            b = 4 * c + j
            parts = []
            for z in range(4):
                parts.append(g_up[GD * z + 24 * b : GD * z + 24 * (b + 1)])
                parts.append(out_scr[(z - yi + 4) % 4, 24 * b : 24 * (b + 1)])
            parts += [g_down[96 * b : 96 * (b + 1)], vec]
            block = jnp.concatenate(parts, axis=0).astype(BF)
            slot = (j - yi + 4) % 4

            @pl.when(ci == c)
            def _():
                keep_ref[slot] = block

            @pl.when(ci != c)
            def _():
                give_ref[slot] = block


def weight_blocks(at, h2, d_up, act, cot, attn, d_branch, early):
    return pl.pallas_call(
        wgrad_kernel,
        out_shape=(shape(4, 304, D), shape(4, 304, D)),
        in_specs=[SMEM] + [VM] * 6 + [ANY],
        out_specs=(VM,) * 2,
        scratch_shapes=[pltpu.VMEM((4, GD, D), F32)],
        compiler_params=PARAMS,
        cost_estimate=pl.CostEstimate(flops=5 * 10**9, bytes_accessed=6 * 10**6, transcendentals=0),
    )(at, h2, d_up, act, cot, attn, d_branch, early)


def add_kernel(a_ref, b_ref, *outs):
    for s in range(4):
        outs[s][...] = (a_ref[s].astype(F32) + b_ref[s].astype(F32)).astype(BF)


def add_blocks(a, b):
    return pl.pallas_call(
        add_kernel,
        out_shape=(shape(*a.shape[1:]),) * 4,
        in_specs=[VM] * 2,
        out_specs=(VM,) * 4,
        compiler_params=PARAMS,
        cost_estimate=pl.CostEstimate(flops=10**6, bytes_accessed=6 * 10**6, transcendentals=0),
    )(a, b)


def mid_kernel(blocks_ref, up_ref, down_ref, out_ref, vec_ref):
    for c in range(2):
        for j in range(4):
            b = 4 * c + j
            block = blocks_ref[2 * j + c].astype(F32)
            for g in range(4):
                up_ref[24 * b : 24 * (b + 1), g * D : (g + 1) * D] = block[24 * g : 24 * (g + 1)]
            down_ref[96 * b : 96 * (b + 1), :] = block[96:192]
            out_ref[24 * b : 24 * (b + 1), :] = block[192:216]
            if b == 0:
                vec_ref[...] = block[216:224]


def mid_rows(blocks):
    return pl.pallas_call(
        mid_kernel,
        out_shape=(
            shape(GD, 4 * D, dtype=F32), shape(D, D, dtype=F32), shape(GD, D, dtype=F32),
            shape(8, D, dtype=F32),
        ),
        in_specs=[VM],
        out_specs=(VM,) * 4,
        compiler_params=PARAMS,
        cost_estimate=pl.CostEstimate(flops=10**6, bytes_accessed=8 * 10**6, transcendentals=0),
    )(blocks)


def tail_kernel(
    at_ref, dkv_ref, dq_ref, h1_ref, n1_ref, w_ref, vec_ref, m0, m1, m2, m3, early_ref, dh_ref, t_ref, rest_ref, scr
):
    yi, zi = at_ref[0], at_ref[1]
    scr[...] = (m0[...].astype(F32) + m2[...].astype(F32)) + (
        m1[...].astype(F32) + m3[...].astype(F32)
    )
    rest_ref[...] = scr[192:, :].astype(BF)
    for s in range(4):
        part = scr[pl.ds(pl.multiple_of((zi + s) % 4 * 48, 8), 48), :]
        t_ref[s, 192:240] = part[:, :640].astype(BF)
        t_ref[s, 240:, :128] = part[:, 640:].astype(BF)
        t_ref[s, 240:, 128:] = jnp.zeros((48, 512), BF)
    d_qkv = jnp.concatenate([dkv_ref[...], dq_ref[...]], axis=1)
    d_h1 = dot_t(d_qkv[:, : 3 * GD], w_ref[...])
    dh_ref[...] = d_h1.astype(BF)
    sums = jnp.sum(d_qkv.astype(F32), axis=0, keepdims=True)
    at_own = lambda v: jnp.concatenate([jnp.where(yi == k, v, 0.0) for k in range(4)], axis=1)
    vectors = jnp.concatenate(
        [
            jnp.sum(d_h1 * n1_ref[...], axis=0, keepdims=True),
            jnp.sum(d_h1, axis=0, keepdims=True),
            at_own(sums[:, 2 * GD : 3 * GD]),
            at_own(sums[:, GD : 2 * GD]),
            vec_ref[4:8, :],
        ],
        axis=0,
    ).astype(BF)
    row = lax.broadcasted_iota(jnp.int32, (8, 128), 0)
    lane = lax.broadcasted_iota(jnp.int32, (8, 128), 1)
    columns = t_dot(vectors, jnp.where(lane == row + 64, 1.0, 0.0).astype(BF))
    grad = t_dot(h1_ref[...], d_qkv)
    for g in range(4):
        rows = slice(g * GD, (g + 1) * GD)
        slot = (g - zi + 4) % 4
        t_ref[slot, :GD, :512] = grad[rows, :512].astype(BF)
        t_ref[slot, :GD, 512:] = (grad[rows, 512:] + columns[rows]).astype(BF)


def last_gradients(at, d_kv, d_q, h1, n1, w, vec, mid, early):
    return pl.pallas_call(
        tail_kernel,
        out_shape=(shape(ROWS, D), shape(4, 288, 640), shape(112, D)),
        in_specs=[SMEM] + [VM] * 10 + [ANY],
        out_specs=(VM,) * 3,
        scratch_shapes=[pltpu.VMEM((304, D), F32)],
        compiler_params=PARAMS,
        cost_estimate=pl.CostEstimate(flops=3 * 10**9, bytes_accessed=6 * 10**6, transcendentals=0),
    )(at, d_kv, d_q, h1, n1, w, vec, *mid, early)


def sum_kernel(at_ref, t_ref, r1, r2, r3, dh_ref, rest_ref, kept_ref, given_ref, same_ref, block_ref, scr):
    same_ref[...] = dh_ref[...]
    slots = (r1, r2, r3)
    for c in range(2):
        rows = slice(96 * c, 96 * (c + 1))
        a, b, d, e = (v.astype(F32) for v in [t_ref[0, rows]] + [r[rows] for r in slots])
        total = ((a + d) + (b + e)).astype(BF)

        @pl.when(at_ref[2] == c)
        def _():
            kept_ref[...] = total

        @pl.when(at_ref[2] != c)
        def _():
            given_ref[...] = total

    for s in range(4):
        part = (t_ref[0, GD:] if s == 0 else slots[s - 1][GD:]).astype(F32)
        scr[s, :, :640] = part[:48]
        scr[s, :, 640:] = part[48:, :128]
    up = [scr[(at_ref[1] - g + 4) % 4][:24] for g in range(4)]
    g_out = (scr[0] + scr[2])[24:] + (scr[1] + scr[3])[24:]
    rest = rest_ref[...].astype(F32)
    block_ref[...] = jnp.concatenate(up + [rest[:96], g_out, rest[96:]], axis=0).astype(BF)


def sum_slots(at, own, slots, d_h1, rest):
    return pl.pallas_call(
        sum_kernel,
        out_shape=(shape(96, 640), shape(96, 640), shape(ROWS, D), shape(232, D)),
        in_specs=[SMEM] + [VM] * 6,
        out_specs=(VM,) * 4,
        scratch_shapes=[pltpu.VMEM((4, 48, D), F32)],
        compiler_params=PARAMS,
        cost_estimate=pl.CostEstimate(flops=10**6, bytes_accessed=3 * 10**6, transcendentals=0),
    )(at, own, *slots, d_h1, rest)


def final_kernel(at_ref, *refs):
    slots, (grad_ref, vec_ref, scr) = refs[:4], refs[4:]
    for s in range(4):
        for c in range(2):
            scr[s, c] = slots[s][c]
    yi, ci = at_ref[0], at_ref[2]
    for c in range(2):
        rows = slice(96 * c, 96 * (c + 1))
        total = []
        for g in range(4):
            value = scr[(yi - g + 4) % 4, (ci + c) % 2].astype(F32)
            for i, part in enumerate((1, 2, 0)):
                start = part * D + g * GD
                grad_ref[rows, start : start + GD] = value[:, i * GD : (i + 1) * GD]
            total.append(value[:, 512:])
        vec_ref[rows, :] = (total[0] + total[1]) + (total[2] + total[3])


def final_rows(at, slots):
    return pl.pallas_call(
        final_kernel,
        out_shape=(shape(GD, 3 * D, dtype=F32), shape(GD, 128, dtype=F32)),
        in_specs=[SMEM] + [VM] * 4,
        out_specs=(VM, VM),
        scratch_shapes=[pltpu.VMEM((4, 2, 96, 640), BF)],
        compiler_params=PARAMS,
        cost_estimate=pl.CostEstimate(flops=10**6, bytes_accessed=3 * 10**6, transcendentals=0),
    )(at, *slots)


def gather(value, axes, axis=0):
    return lax.all_gather(value, axes, axis=axis, tiled=True)


def swap(value, axes):
    return lax.all_to_all(value, axes, 0, 0)


def send(value, axis, step):
    n = lax.axis_size(axis)
    return lax.ppermute(value, axis, [(i, (i + step) % n) for i in range(n)])


def spread(value, axis):
    return [value] + [send(value, axis, s) for s in range(1, 4)]


def exchange(slots, axis, step):
    return [slots[0]] + [send(slots[s], axis, s * step) for s in range(1, 4)]


def add_slots(slots):
    a, b, c, d = (v.astype(F32) for v in slots)
    return (a + c) + (b + d)


def group_of(value, index, size, axis=0):
    return lax.dynamic_slice_in_dim(value, (index % 4) * size, size, axis)


def local(
    tokens, qkv_w, out_w, up_w, down_w, norm_gains, biases, value_bias, up_bias, cotangent, block_place
):
    xi = lax.axis_index("x")
    yi = lax.axis_index("y")
    ci = lax.axis_index("core")
    zi = lax.axis_index("fsdp")
    tok_own = tokens[0]
    cot_own = cotangent[0]

    at = jnp.stack([yi, zi, ci]).astype(jnp.int32)
    ws = spread(prepare(at, qkv_w, norm_gains, biases, value_bias[None]), "fsdp")
    toks = spread(tok_own, "y")

    ids = jnp.arange(NBLK, dtype=jnp.int32)
    slot_x, slot_c, slot_y, blk = ids // 16, (ids // 8) % 2, (ids // 2) % 4, ids % 2
    pick = lambda at: jnp.sum(jnp.where(at[:, None] == ids[None, :], block_place[None, :], 0), axis=1)
    at_y = (yi - slot_y + 4) % 4
    key_place = pick(at_y * 16 + ((xi - slot_x + 4) % 4) * 4 + ((ci + slot_c) % 2) * 2 + blk)
    query_place = pick(at_y * 16 + slot_x * 4 + slot_c * 2 + blk)
    own_place = key_place[:8]
    rank = jnp.sum((own_place[None, :] > own_place[:, None]).astype(jnp.int32), axis=1)
    order = jnp.arange(8, dtype=jnp.int32)
    hit = rank[None, :] == order[:, None]
    own = jnp.sum(jnp.where(hit, order[None, :], 0), axis=1)
    place = jnp.sum(jnp.where(hit, own_place[None, :], 0), axis=1)

    w_up = swap(up_w.reshape(GD, 4, D).transpose(1, 0, 2), "fsdp").reshape(D, D)
    w_down = down_w

    kv_own, query, h1, n1y, w_qkv, small = first_rows(at, toks, ws)
    both = both_rows(cot_own, out_w, kv_own)
    both = lax.all_gather(both, "fsdp", axis=0)
    w_out = jnp.concatenate(
        [lax.dynamic_index_in_dim(both, (yi + s) % 4, 0, keepdims=False)[128:] for s in range(4)], axis=0
    )
    gain1, gain2 = small[0], small[1]
    out_bias, shift2, down_bias = small[4], small[5], small[6]
    with jax.named_scope("kv"):
        kv_all = [p for v in spread(kv_own, "x") for p in (v, send(v, "core", 1))]
    attn, o_exact, qe, ks, vs = attention_forward(key_place, own, place, query, kv_all, w_up)
    qe_all = gather(qe, XC)

    attn = attn[:, 64:]
    with jax.named_scope("attn_y"):
        attn_own = exchange([attn[128 * s : 128 * (s + 1)] for s in range(4)], "y", -1)
    attn_own = jnp.concatenate(attn_own, axis=1)
    x2 = tok_own.astype(F32) + (dot(attn_own, w_out) + out_bias)
    n2, s2 = normalize(x2)
    h2_own = (n2 * gain2 + shift2).astype(BF)

    with jax.named_scope("h2_z"):
        h2s = spread(h2_own, "fsdp")
    h2, cot_z, act, d_up, d_h2_part = feed_forward(
        at, h2s, both, w_up, w_down, up_bias[None]
    )
    back = lambda v: add_slots(exchange([v[128 * s : 128 * (s + 1)] for s in range(4)], "fsdp", -1))
    with jax.named_scope("d_h2_z"):
        d_h2 = back(d_h2_part)
    cot32 = cot_own.astype(F32)
    d_x2 = cot32 + norm_back(d_h2 * gain2, n2, s2)
    d_branch = d_x2.astype(BF)
    d_attn = dot_t(d_branch, w_out).astype(BF)
    with jax.named_scope("d_attn_y"):
        d_attn_own = exchange([d_attn[:, GD * s : GD * (s + 1)] for s in range(4)], "y", 1)
    d_attn_own = jnp.concatenate(d_attn_own, axis=0)
    de = delta_rows(d_attn_own, o_exact, (qe_all, both))
    keep, give = weight_blocks(at, h2, d_up, act, cot_z, attn_own, d_branch, de)
    with jax.named_scope("mid"):
        mid = add_blocks(keep, send(give, "core", 1))
        mid = add_slots(exchange(mid, "y", 1)).astype(BF)
    with jax.named_scope("de"):
        arrived = spread(de, "x")[1:]
        d_q = attention_dq((0, 3), own, place, qe, de, ks, vs)
        arrived = hold_back(arrived, d_q)
        de_all = [p for v in (de, *arrived) for p in (v, send(v, "core", 1))]
    d_q = attention_dq((1, 2), own, place, qe, de, ks, vs, (d_q,), (*arrived, mid))
    with jax.named_scope("down"):
        layer_out = (x2 + back(down_rows(act, w_down, d_q)) + down_bias).astype(BF)
    d_kv = attention_dkv(query_place, key_place, own, place, kv_own, qe_all, de_all)
    with jax.named_scope("mid"):
        mid = spread(mid, "x")

    vec = jnp.stack([jnp.sum(d_h2 * n2, axis=0), jnp.sum(d_branch.astype(F32), axis=0), jnp.sum(d_h2, axis=0)])
    vec = jnp.pad(vec, ((4, 1), (0, 0)))
    d_h1_send, tail, rest = last_gradients(at, d_kv, d_q, h1, n1y, w_qkv, vec, mid, layer_out)
    with jax.named_scope("tail_z"):
        received = [send(tail[s], "fsdp", s) for s in range(1, 4)]
    kept, given, d_h1_send, mid = sum_slots(at, tail, received, d_h1_send, rest)
    with jax.named_scope("mid"):
        mid = lax.all_gather(mid, ("y", "core"), axis=0)
    grad_up, grad_down, grad_out, out_vec = mid_rows(mid)
    grad_up_bias = out_vec[0]
    grad_down_bias = lax.dynamic_slice(out_vec[1], (zi * GD,), (GD,))
    with jax.named_scope("d_h1_y"):
        d_h1 = add_slots(exchange([d_h1_send[128 * s : 128 * (s + 1)] for s in range(4)], "y", -1))
    n1, s1 = normalize(tok_own.astype(F32))
    input_grad = (d_x2 + norm_back(d_h1 * gain1, n1, s1)).astype(BF)

    with jax.named_scope("tail_core"):
        tail = (kept.astype(F32) + send(given, "core", 1).astype(F32)).astype(BF)
    with jax.named_scope("tail_x"):
        tail = add_slots(spread(tail, "x")).astype(BF)
    with jax.named_scope("tail_y"):
        tail = [jnp.stack([v, send(v, "core", 1)]) for v in spread(tail, "y")]
    grad_qkv, vectors = final_rows(at, tail)
    vectors = vectors[:, 64:71].T
    grad_gains = jnp.stack([vectors[0], vectors[4]])
    grad_biases = jnp.stack([vectors[1], vectors[2], vectors[5], vectors[6], grad_down_bias])
    grad_value_bias = vectors[3]
    return (
        layer_out[None], input_grad[None], grad_qkv, grad_out, grad_up, grad_down,
        grad_gains, grad_biases, grad_value_bias, grad_up_bias,
    )


def solution(mesh):
    grid = Mesh(mesh.devices.reshape(4, 4, 2, 4), ("y", "x", "core", "fsdp"))
    rows = P("fsdp", CTX, None)
    in_specs = (
        rows, P("fsdp", None), P("fsdp", None), P("fsdp", None), P("fsdp", None),
        P(None, "fsdp"), P(None, "fsdp"), P("fsdp"), P("fsdp"), rows, P(),
    )
    out_specs = (
        rows, rows, P("fsdp", None), P("fsdp", None), P("fsdp", None), P("fsdp", None),
        P(None, "fsdp"), P(None, "fsdp"), P("fsdp"), P("fsdp"),
    )
    return jax.shard_map(local, mesh=grid, in_specs=in_specs, out_specs=out_specs, check_vma=False)
```

```python
import functools

import jax
import jax.numpy as jnp
from jax import lax
from jax.experimental import pallas as pl
from jax.experimental.pallas import tpu as pltpu
from jax.sharding import Mesh
from jax.sharding import PartitionSpec as P

EPS = 1e-05
D = 768
GD = 192
NH = 3
HD = 64
ROWS = 512
LEN = 4096
BLK = 64
NBLK = 64
EXT = 256
TILE = 1024
CHUNK = 128
BF = jnp.bfloat16
F32 = jnp.float32
XC = ("x", "core")
CTX = ("y", "x", "core")


def dot(a, b):
    return lax.dot_general(a, b, (((1,), (0,)), ((), ())), preferred_element_type=F32)


def dot_t(a, b):
    return lax.dot_general(a, b, (((1,), (1,)), ((), ())), preferred_element_type=F32)


def t_dot(a, b):
    return lax.dot_general(a, b, (((0,), (0,)), ((), ())), preferred_element_type=F32)


def normalize(value):
    center = value - jnp.mean(value, axis=-1, keepdims=True)
    factor = lax.rsqrt(jnp.mean(center * center, axis=-1, keepdims=True) + EPS)
    return (center * factor, factor)


def norm_back(scaled, normed, factor):
    return factor * (
        scaled
        - jnp.mean(scaled, axis=-1, keepdims=True)
        - normed * jnp.mean(scaled * normed, axis=-1, keepdims=True)
    )


def lanes(rows):
    return lax.broadcasted_iota(jnp.int32, (rows, EXT), 1)


def head_mask(rows, h, high):
    lane = lanes(rows)
    if high:
        feat = (lane >= 64 + HD * h) & (lane < 64 + HD * (h + 1))
        ext = (lane >= 3 * h) & (lane < 3 * h + 3)
    else:
        feat = (lane >= HD * h) & (lane < HD * (h + 1))
        ext = (lane >= GD + 3 * h) & (lane < GD + 3 * h + 3)
    return feat | ext


def feature_mask(rows, h, high):
    lane = lanes(rows) - (64 if high else 0)
    return (lane >= HD * h) & (lane < HD * (h + 1))


def stack_heads(value, high):
    rows = value.shape[0]
    zero = jnp.zeros_like(value)
    return jnp.concatenate(
        [jnp.where(head_mask(rows, h, high), value, zero) for h in range(NH)], axis=0
    )


def merge_heads(stacked, high):
    rows = stacked.shape[0] // NH
    out = jnp.zeros((rows, EXT), F32)
    for h in range(NH):
        out = out + jnp.where(feature_mask(rows, h, high), stacked[h * rows : (h + 1) * rows], 0.0)
    return out


def pieces(value):
    first = value.astype(BF).astype(F32)
    second = (value - first).astype(BF).astype(F32)
    third = (value - first - second).astype(BF).astype(F32)
    return (first, second, third)


def add_extras(base, columns, high):
    rows = base.shape[0]
    lane = lanes(rows)
    start = 0 if high else GD
    for h in range(NH):
        for i, piece in enumerate(pieces(columns[h])):
            base = jnp.where(lane == start + 3 * h + i, piece, base)
    return base


def key_form(kv):
    lane = lanes(kv.shape[0])
    one = jnp.ones((kv.shape[0], EXT), BF)
    zero = jnp.zeros((kv.shape[0], EXT), BF)
    low = jnp.where(lane < GD, kv[:, :EXT], jnp.where(lane < GD + 9, one, zero))
    high = jnp.where(lane >= 64, kv[:, 128:384], jnp.where(lane < 9, one, zero))
    return (low, high)


def block_rows(index):
    return pl.ds(pl.multiple_of(index * BLK, BLK), BLK)


def stacked_pos(place_a, place_b):
    row = lax.broadcasted_iota(jnp.int32, (NH * CHUNK, 1), 0)
    place = jnp.where(row % CHUNK < BLK, place_a, place_b)
    return place * BLK + row % BLK


def col_pos(tile):
    return tile * TILE + lax.broadcasted_iota(jnp.int32, (NH * CHUNK, TILE), 1)


def fold(value, op):
    out = value[:, :128]
    for i in range(1, value.shape[1] // 128):
        out = op(out, value[:, i * 128 : (i + 1) * 128])
    return out


def tile_rows(t):
    return pl.ds(pl.multiple_of(t * TILE, TILE), TILE)


def fwd_kernel(
    kplace_ref, own_ref, place_ref, q_ref, *refs
):
    kv_refs = refs[:8]
    attn_ref, o_ref, qe_ref, ks_ref, vs_ref, s_scr, m_scr, l_scr, acc_scr, land, sems = refs[11:]
    copies = [pltpu.make_async_copy(kv_refs[k], land.at[k], sems.at[k]) for k in range(8)]
    for copy in copies:
        copy.start()
    for k in range(8):
        copies[k].wait()
        for b in range(8):
            low, high = key_form(land[k, b * BLK : (b + 1) * BLK, :])
            dst = block_rows(kplace_ref[8 * k + b])
            ks_ref[dst, :] = low
            vs_ref[dst, :] = high

    for c in range(ROWS // CHUNK):
        place_a, place_b = place_ref[2 * c], place_ref[2 * c + 1]
        blocks = (own_ref[2 * c], own_ref[2 * c + 1])
        query = jnp.concatenate([q_ref[block_rows(b), :] for b in blocks], axis=0)
        stacked = stack_heads(query, False)
        qpos = stacked_pos(place_a, place_b)
        tiles = place_a // (TILE // BLK) + 1
        m_scr[...] = jnp.full(m_scr.shape, -1e30, F32)

        def score_step(t, _):
            scores = dot_t(stacked, ks_ref[tile_rows(t), :])
            scores = jnp.where(col_pos(t) <= qpos, scores, -1e30)
            s_scr[t] = scores
            m_scr[...] = jnp.maximum(m_scr[...], fold(scores, jnp.maximum))
            return 0

        lax.fori_loop(0, tiles, score_step, 0)
        peak = jnp.max(m_scr[...], axis=1, keepdims=True)
        l_scr[...] = jnp.zeros(l_scr.shape, F32)
        acc_scr[...] = jnp.zeros(acc_scr.shape, F32)

        def value_step(t, _):
            prob = jnp.exp(s_scr[t] - peak)
            l_scr[...] = l_scr[...] + fold(prob, jnp.add)
            acc_scr[...] = acc_scr[...] + dot(prob.astype(BF), vs_ref[tile_rows(t), :])
            return 0

        lax.fori_loop(0, tiles, value_step, 0)
        total = jnp.sum(l_scr[...], axis=1, keepdims=True)
        log_total = peak + jnp.log(total)
        out = merge_heads(acc_scr[...] / total, True)
        ext = add_extras(
            query.astype(F32),
            [-log_total[h * CHUNK : (h + 1) * CHUNK] for h in range(NH)],
            False,
        ).astype(BF)
        for i, b in enumerate(blocks):
            rows = slice(i * BLK, (i + 1) * BLK)
            o_ref[block_rows(b), :] = out[rows]
            attn_ref[block_rows(b), :] = out[rows].astype(BF)
            qe_ref[block_rows(b), :] = ext[rows]


def dq_kernel(chunks, n_before, own_ref, place_ref, qe_ref, de_ref, ks_ref, vs_ref, *refs):
    *before, dq_ref, acc_scr = refs
    if n_before:
        dq_ref[...] = before[0][...]
    for c in chunks:
        place_a, place_b = place_ref[2 * c], place_ref[2 * c + 1]
        blocks = (own_ref[2 * c], own_ref[2 * c + 1])
        query = stack_heads(jnp.concatenate([qe_ref[block_rows(b), :] for b in blocks], axis=0), False)
        d_out = stack_heads(jnp.concatenate([de_ref[block_rows(b), :] for b in blocks], axis=0), True)
        qpos = stacked_pos(place_a, place_b)
        tiles = place_a // (TILE // BLK) + 1
        acc_scr[...] = jnp.zeros(acc_scr.shape, F32)

        def step(t, _):
            keys = ks_ref[tile_rows(t), :]
            prob = jnp.where(col_pos(t) <= qpos, jnp.exp(dot_t(query, keys)), 0.0)
            d_raw = (prob * dot_t(d_out, vs_ref[tile_rows(t), :])).astype(BF)
            acc_scr[...] = acc_scr[...] + dot(d_raw, keys)
            return 0

        lax.fori_loop(0, tiles, step, 0)
        out = (merge_heads(acc_scr[...], False) * 0.125).astype(BF)
        for i, b in enumerate(blocks):
            dq_ref[block_rows(b), :] = out[i * BLK : (i + 1) * BLK]


def dkv_kernel(qplace_ref, kplace_ref, own_ref, place_ref, kv_ref, qe_ref, *refs):
    de_refs, (dkv_ref, qs_scr, ds_scr, dk_scr, dv_scr, q_land, d_land, sems) = refs[:8], refs[8:]
    q_copy = pltpu.make_async_copy(qe_ref, q_land, sems.at[8])
    q_copy.start()
    copies = [pltpu.make_async_copy(de_refs[k], d_land.at[k], sems.at[k]) for k in range(8)]
    for copy in copies:
        copy.start()
    q_copy.wait()
    for b in range(NBLK):
        qs_scr[block_rows(qplace_ref[b]), :] = q_land[b * BLK : (b + 1) * BLK, :]
    for k in range(8):
        copies[k].wait()
        for b in range(8):
            ds_scr[block_rows(kplace_ref[8 * k + b]), :] = d_land[k, b * BLK : (b + 1) * BLK, :]

    for c in range(ROWS // CHUNK):
        place_a, place_b = place_ref[2 * c], place_ref[2 * c + 1]
        blocks = (own_ref[2 * c], own_ref[2 * c + 1])
        low, high = key_form(jnp.concatenate([kv_ref[block_rows(b), :] for b in blocks], axis=0))
        keys = stack_heads(low, False)
        values = stack_heads(high, True)
        kpos = stacked_pos(place_a, place_b)
        dk_scr[...] = jnp.zeros(dk_scr.shape, F32)
        dv_scr[...] = jnp.zeros(dv_scr.shape, F32)

        def step(t, _):
            query = qs_scr[tile_rows(t), :]
            d_out = ds_scr[tile_rows(t), :]
            prob = jnp.where(col_pos(t) >= kpos, jnp.exp(dot_t(keys, query)), 0.0)
            d_raw = (prob * dot_t(values, d_out)).astype(BF)
            dv_scr[...] = dv_scr[...] + dot(prob.astype(BF), d_out)
            dk_scr[...] = dk_scr[...] + dot(d_raw, query)
            return 0

        lax.fori_loop(place_b // (TILE // BLK), LEN // TILE, step, 0)
        d_keys = merge_heads(dk_scr[...], False)
        d_values = merge_heads(dv_scr[...], True)
        out = jnp.concatenate(
            [d_keys[:, :128], d_keys[:, 128:] + d_values[:, :128], d_values[:, 128:]], axis=1
        ).astype(BF)
        for i, b in enumerate(blocks):
            dkv_ref[block_rows(b), :] = out[i * BLK : (i + 1) * BLK]


def delta_kernel(d_ref, o_ref, early_ref, de_ref):
    d_out = jnp.concatenate([jnp.zeros((ROWS, 64), F32), d_ref[...].astype(F32)], axis=1)
    product = d_out * o_ref[...]
    sums = [
        -jnp.sum(jnp.where(feature_mask(ROWS, h, True), product, 0.0), axis=1, keepdims=True)
        for h in range(NH)
    ]
    de_ref[...] = add_extras(d_out, sums, True).astype(BF)


SMEM = pl.BlockSpec(memory_space=pltpu.SMEM)
VM = pl.BlockSpec(memory_space=pltpu.VMEM)
ANY = pl.BlockSpec(memory_space=pl.ANY)
PARAMS = pltpu.CompilerParams(vmem_limit_bytes=48 * 1024 * 1024)


def shape(*dims, dtype=BF):
    return jax.ShapeDtypeStruct(dims, dtype)


def attention_forward(kplace, own, place, query, kv, early):
    return pl.pallas_call(
        fwd_kernel,
        out_shape=(
            shape(ROWS, EXT), shape(ROWS, EXT, dtype=F32), shape(ROWS, EXT),
            shape(LEN, EXT), shape(LEN, EXT),
        ),
        in_specs=[SMEM] * 3 + [VM] + [ANY] * 11,
        out_specs=(VM,) * 5,
        scratch_shapes=[
            pltpu.VMEM((LEN // TILE, NH * CHUNK, TILE), F32),
            pltpu.VMEM((NH * CHUNK, 128), F32),
            pltpu.VMEM((NH * CHUNK, 128), F32),
            pltpu.VMEM((NH * CHUNK, EXT), F32),
            pltpu.VMEM((8, ROWS, 2 * GD), BF),
            pltpu.SemaphoreType.DMA((8,)),
        ],
        compiler_params=PARAMS,
        cost_estimate=pl.CostEstimate(flops=16 * 10**9, bytes_accessed=10**7, transcendentals=4 * 10**6),
    )(kplace, own, place, query, *kv, *early)


def attention_dq(chunks, own, place, qe, de, ks, vs, before=(), early=()):
    return pl.pallas_call(
        functools.partial(dq_kernel, chunks, len(before)),
        out_shape=shape(ROWS, EXT),
        in_specs=[SMEM] * 2 + [VM] * (4 + len(before)) + [ANY] * len(early),
        out_specs=VM,
        scratch_shapes=[pltpu.VMEM((NH * CHUNK, EXT), F32)],
        compiler_params=PARAMS,
        cost_estimate=pl.CostEstimate(flops=8 * 10**9, bytes_accessed=5 * 10**6, transcendentals=2 * 10**6),
    )(own, place, qe, de, ks, vs, *before, *early)


def attention_dkv(qplace, kplace, own, place, kv, qe, de):
    return pl.pallas_call(
        dkv_kernel,
        out_shape=shape(ROWS, 2 * GD),
        in_specs=[SMEM] * 4 + [VM] + [ANY] * 9,
        out_specs=VM,
        scratch_shapes=[
            pltpu.VMEM((LEN, EXT), BF),
            pltpu.VMEM((LEN, EXT), BF),
            pltpu.VMEM((NH * CHUNK, EXT), F32),
            pltpu.VMEM((NH * CHUNK, EXT), F32),
            pltpu.VMEM((LEN, EXT), BF),
            pltpu.VMEM((8, ROWS, EXT), BF),
            pltpu.SemaphoreType.DMA((9,)),
        ],
        compiler_params=PARAMS,
        cost_estimate=pl.CostEstimate(flops=15 * 10**9, bytes_accessed=10**7, transcendentals=4 * 10**6),
    )(qplace, kplace, own, place, kv, qe, *de)


def delta_rows(d_attn, o, early):
    return pl.pallas_call(
        delta_kernel,
        out_shape=shape(ROWS, EXT),
        in_specs=[VM] * 2 + [ANY],
        out_specs=VM,
        compiler_params=PARAMS,
        cost_estimate=pl.CostEstimate(flops=10**6, bytes_accessed=10**6, transcendentals=0),
    )(d_attn, o, early)


def prep_kernel(at_ref, w_ref, gain_ref, bias_ref, vb_ref, cols_ref):
    for k in range(4):

        @pl.when(at_ref[0] == k)
        def _():
            for i, part in enumerate((1, 2, 0)):
                start = part * D + k * GD
                cols_ref[:GD, i * GD : (i + 1) * GD] = w_ref[:, start : start + GD]

    small = jnp.concatenate(
        [gain_ref[...].astype(F32), bias_ref[...].astype(F32), vb_ref[...].astype(F32), jnp.zeros((8, GD), F32)],
        axis=0,
    )
    cols_ref[GD:, :] = jnp.concatenate([small, jnp.zeros((16, 2 * GD), F32)], axis=1).astype(BF)


def prepare(at, w, gains, biases, vb):
    return pl.pallas_call(
        prep_kernel,
        out_shape=shape(GD + 16, 3 * GD),
        in_specs=[SMEM] + [VM] * 4,
        out_specs=VM,
        compiler_params=PARAMS,
        cost_estimate=pl.CostEstimate(flops=1000, bytes_accessed=10**6, transcendentals=0),
    )(at, w, gains, biases, vb)


def qkv_kernel(at_ref, *refs):
    toks, ws = refs[:4], refs[4:8]
    kv_ref, q_ref, h1_ref, n1_ref, w_ref, small_ref, w_scr = refs[8:]
    yi, zi = at_ref[0], at_ref[1]
    for s in range(4):
        w_scr[s] = ws[s][...]
    for g in range(4):
        slot = (zi - g + 4) % 4
        w_ref[g * GD : (g + 1) * GD, :] = w_scr[slot, :GD]
        small_ref[:, g * GD : (g + 1) * GD] = w_scr[slot, GD:, :256].astype(F32)[:8, :GD]
    gain, shift = small_ref[0:1, :], small_ref[2:3, :]
    for s in range(4):
        rows = slice(128 * s, 128 * (s + 1))
        normed, _ = normalize(toks[s][...].astype(F32))
        n1_ref[rows, :] = normed
        h1_ref[rows, :] = (normed * gain + shift).astype(BF)
    own = w_scr[(zi - yi + 4) % 4, GD:, :256].astype(F32)[:8, :GD]
    qkv = dot(h1_ref[...], w_ref[...])
    kv_ref[:, :GD] = qkv[:, :GD].astype(BF)
    kv_ref[:, GD:] = (qkv[:, GD : 2 * GD] + own[7:8]).astype(BF)
    query = (qkv[:, 2 * GD :] + own[3:4]).astype(BF).astype(F32) * 0.125
    q_ref[...] = jnp.concatenate([query, jnp.zeros((ROWS, EXT - GD), F32)], axis=1).astype(BF)


def both_kernel(cot_ref, out_ref, early_ref, both_ref):
    both_ref[:128, :] = cot_ref[...]
    both_ref[128:, :] = out_ref[...]


def both_rows(cot, out_w, early):
    return pl.pallas_call(
        both_kernel,
        out_shape=shape(320, D),
        in_specs=[VM] * 2 + [ANY],
        out_specs=VM,
        compiler_params=PARAMS,
        cost_estimate=pl.CostEstimate(flops=1000, bytes_accessed=10**6, transcendentals=0),
    )(cot, out_w, early)


def first_rows(at, toks, ws):
    return pl.pallas_call(
        qkv_kernel,
        out_shape=(
            shape(ROWS, 2 * GD), shape(ROWS, EXT), shape(ROWS, D), shape(ROWS, D, dtype=F32),
            shape(D, 3 * GD), shape(8, D, dtype=F32),
        ),
        in_specs=[SMEM] + [VM] * 8,
        out_specs=(VM,) * 6,
        scratch_shapes=[pltpu.VMEM((4, GD + 16, 3 * GD), BF)],
        compiler_params=PARAMS,
        cost_estimate=pl.CostEstimate(flops=5 * 10**8, bytes_accessed=6 * 10**6, transcendentals=0),
    )(at, *toks, *ws)


def mlp_kernel(at_ref, *refs):
    h2s = refs[:4]
    ups = refs[4:8]
    both_ref, down_ref, ub_ref, h2_ref, cot_ref, act_ref, dup_ref, dh_ref, up_ref, sems = refs[8:]
    zi = at_ref[1]
    copies = [
        pltpu.make_async_copy(
            both_ref.at[(zi - s + 4) % 4, :128], cot_ref.at[128 * s : 128 * (s + 1)], sems.at[s]
        )
        for s in range(4)
    ]
    for copy in copies:
        copy.start()
    for s in range(4):
        up_ref[pl.ds(pl.multiple_of((zi - s + 4) % 4 * GD, GD), GD), :] = ups[s][...]
    for copy in copies:
        copy.wait()
    for s in range(4):
        rows = slice(128 * s, 128 * (s + 1))
        h2 = h2s[s][...]
        h2_ref[rows, :] = h2
        up = dot(h2, up_ref[...]) + ub_ref[...].astype(F32)
        d_act = dot_t(cot_ref[rows, :], down_ref[...])
        square = up * up
        th = jnp.tanh(0.7978845608028654 * (up + 0.044715 * (square * up)))
        half = 0.5 * (1.0 + th)
        slope = half + 0.5 * up * (1.0 - th * th) * (
            0.7978845608028654 * (1.0 + 3 * 0.044715 * square)
        )
        act_ref[rows, :] = (up * half).astype(BF)
        d_up = (slope * d_act).astype(BF)
        dup_ref[rows, :] = d_up
        dh_ref[rows, :] = dot_t(d_up, up_ref[...]).astype(BF)


def feed_forward(at, h2s, w_ups, both, w_down, ub):
    return pl.pallas_call(
        mlp_kernel,
        out_shape=(shape(ROWS, D),) * 5,
        in_specs=[SMEM] + [VM] * 8 + [ANY] + [VM] * 2,
        out_specs=(VM,) * 5,
        scratch_shapes=[pltpu.VMEM((D, D), BF), pltpu.SemaphoreType.DMA((4,))],
        compiler_params=PARAMS,
        cost_estimate=pl.CostEstimate(flops=4 * 10**9, bytes_accessed=6 * 10**6, transcendentals=4 * 10**5),
    )(at, *h2s, *w_ups, both, w_down, ub)


def down_kernel(act_ref, wd_ref, early_ref, down_ref):
    down_ref[...] = dot(act_ref[...], wd_ref[...]).astype(BF)


def down_rows(act, w_down, early):
    return pl.pallas_call(
        down_kernel,
        out_shape=shape(ROWS, D),
        in_specs=[VM] * 2 + [ANY],
        out_specs=VM,
        compiler_params=PARAMS,
        cost_estimate=pl.CostEstimate(flops=10**9, bytes_accessed=3 * 10**6, transcendentals=0),
    )(act, w_down, early)


def hold_kernel(*refs):
    for s in range(3):
        refs[4 + s][...] = refs[s][...]


def hold_back(values, early):
    return pl.pallas_call(
        hold_kernel,
        out_shape=tuple(shape(*v.shape) for v in values),
        in_specs=[VM] * 3 + [ANY],
        out_specs=(VM,) * 3,
        compiler_params=PARAMS,
        cost_estimate=pl.CostEstimate(flops=1000, bytes_accessed=10**6, transcendentals=0),
    )(*values, early)


def wgrad_kernel(
    at_ref, h2_ref, dup_ref, act_ref, cot_ref, attn_ref, branch_ref, early_ref,
    keep_ref, give_ref, out_scr,
):
    yi, ci = at_ref[0], at_ref[2]
    g_up = t_dot(h2_ref[...], dup_ref[...])
    g_down = t_dot(act_ref[...], cot_ref[...])
    g_out = t_dot(attn_ref[...], branch_ref[...])
    for s in range(4):
        out_scr[s] = g_out[GD * s : GD * (s + 1)]
    vec = jnp.concatenate(
        [
            jnp.sum(dup_ref[...].astype(F32), axis=0, keepdims=True),
            jnp.sum(cot_ref[...].astype(F32), axis=0, keepdims=True),
            jnp.zeros((14, D), F32),
        ],
        axis=0,
    )
    for c in range(2):
        for j in range(4):
            b = 4 * c + j
            parts = []
            for z in range(4):
                parts.append(g_up[GD * z + 24 * b : GD * z + 24 * (b + 1)])
                parts.append(out_scr[(z - yi + 4) % 4, 24 * b : 24 * (b + 1)])
            parts += [g_down[96 * b : 96 * (b + 1)], vec]
            block = jnp.concatenate(parts, axis=0).astype(BF)
            slot = (j - yi + 4) % 4

            @pl.when(ci == c)
            def _():
                keep_ref[slot] = block

            @pl.when(ci != c)
            def _():
                give_ref[slot] = block


def weight_blocks(at, h2, d_up, act, cot, attn, d_branch, early):
    return pl.pallas_call(
        wgrad_kernel,
        out_shape=(shape(4, 304, D), shape(4, 304, D)),
        in_specs=[SMEM] + [VM] * 6 + [ANY],
        out_specs=(VM,) * 2,
        scratch_shapes=[pltpu.VMEM((4, GD, D), F32)],
        compiler_params=PARAMS,
        cost_estimate=pl.CostEstimate(flops=5 * 10**9, bytes_accessed=6 * 10**6, transcendentals=0),
    )(at, h2, d_up, act, cot, attn, d_branch, early)


def add_kernel(a_ref, b_ref, *outs):
    for s in range(4):
        outs[s][...] = (a_ref[s].astype(F32) + b_ref[s].astype(F32)).astype(BF)


def add_blocks(a, b):
    return pl.pallas_call(
        add_kernel,
        out_shape=(shape(*a.shape[1:]),) * 4,
        in_specs=[VM] * 2,
        out_specs=(VM,) * 4,
        compiler_params=PARAMS,
        cost_estimate=pl.CostEstimate(flops=10**6, bytes_accessed=6 * 10**6, transcendentals=0),
    )(a, b)


def mid_kernel(blocks_ref, up_ref, down_ref, out_ref, vec_ref):
    for c in range(2):
        for j in range(4):
            b = 4 * c + j
            block = blocks_ref[2 * j + c].astype(F32)
            for g in range(4):
                up_ref[24 * b : 24 * (b + 1), g * D : (g + 1) * D] = block[24 * g : 24 * (g + 1)]
            down_ref[96 * b : 96 * (b + 1), :] = block[96:192]
            out_ref[24 * b : 24 * (b + 1), :] = block[192:216]
            if b == 0:
                vec_ref[...] = block[216:224]


def mid_rows(blocks):
    return pl.pallas_call(
        mid_kernel,
        out_shape=(
            shape(GD, 4 * D, dtype=F32), shape(D, D, dtype=F32), shape(GD, D, dtype=F32),
            shape(8, D, dtype=F32),
        ),
        in_specs=[VM],
        out_specs=(VM,) * 4,
        compiler_params=PARAMS,
        cost_estimate=pl.CostEstimate(flops=10**6, bytes_accessed=8 * 10**6, transcendentals=0),
    )(blocks)


def tail_kernel(
    at_ref, dkv_ref, dq_ref, h1_ref, n1_ref, w_ref, vec_ref, m0, m1, m2, m3, early_ref, dh_ref, t_ref, rest_ref, scr
):
    yi, zi = at_ref[0], at_ref[1]
    scr[...] = (m0[...].astype(F32) + m2[...].astype(F32)) + (
        m1[...].astype(F32) + m3[...].astype(F32)
    )
    rest_ref[...] = scr[192:, :].astype(BF)
    for s in range(4):
        part = scr[pl.ds(pl.multiple_of((zi + s) % 4 * 48, 8), 48), :]
        t_ref[s, 192:240] = part[:, :640].astype(BF)
        t_ref[s, 240:, :128] = part[:, 640:].astype(BF)
        t_ref[s, 240:, 128:] = jnp.zeros((48, 512), BF)
    d_qkv = jnp.concatenate([dkv_ref[...], dq_ref[...]], axis=1)
    d_h1 = dot_t(d_qkv[:, : 3 * GD], w_ref[...])
    dh_ref[...] = d_h1.astype(BF)
    sums = jnp.sum(d_qkv.astype(F32), axis=0, keepdims=True)
    at_own = lambda v: jnp.concatenate([jnp.where(yi == k, v, 0.0) for k in range(4)], axis=1)
    vectors = jnp.concatenate(
        [
            jnp.sum(d_h1 * n1_ref[...], axis=0, keepdims=True),
            jnp.sum(d_h1, axis=0, keepdims=True),
            at_own(sums[:, 2 * GD : 3 * GD]),
            at_own(sums[:, GD : 2 * GD]),
            vec_ref[4:8, :],
        ],
        axis=0,
    ).astype(BF)
    row = lax.broadcasted_iota(jnp.int32, (8, 128), 0)
    lane = lax.broadcasted_iota(jnp.int32, (8, 128), 1)
    columns = t_dot(vectors, jnp.where(lane == row + 64, 1.0, 0.0).astype(BF))
    grad = t_dot(h1_ref[...], d_qkv)
    for g in range(4):
        rows = slice(g * GD, (g + 1) * GD)
        slot = (g - zi + 4) % 4
        t_ref[slot, :GD, :512] = grad[rows, :512].astype(BF)
        t_ref[slot, :GD, 512:] = (grad[rows, 512:] + columns[rows]).astype(BF)


def last_gradients(at, d_kv, d_q, h1, n1, w, vec, mid, early):
    return pl.pallas_call(
        tail_kernel,
        out_shape=(shape(ROWS, D), shape(4, 288, 640), shape(112, D)),
        in_specs=[SMEM] + [VM] * 10 + [ANY],
        out_specs=(VM,) * 3,
        scratch_shapes=[pltpu.VMEM((304, D), F32)],
        compiler_params=PARAMS,
        cost_estimate=pl.CostEstimate(flops=3 * 10**9, bytes_accessed=6 * 10**6, transcendentals=0),
    )(at, d_kv, d_q, h1, n1, w, vec, *mid, early)


def sum_kernel(at_ref, t_ref, r1, r2, r3, dh_ref, rest_ref, kept_ref, given_ref, same_ref, block_ref, scr):
    same_ref[...] = dh_ref[...]
    slots = (r1, r2, r3)
    for c in range(2):
        rows = slice(96 * c, 96 * (c + 1))
        a, b, d, e = (v.astype(F32) for v in [t_ref[0, rows]] + [r[rows] for r in slots])
        total = ((a + d) + (b + e)).astype(BF)

        @pl.when(at_ref[2] == c)
        def _():
            kept_ref[...] = total

        @pl.when(at_ref[2] != c)
        def _():
            given_ref[...] = total

    for s in range(4):
        part = (t_ref[0, GD:] if s == 0 else slots[s - 1][GD:]).astype(F32)
        scr[s, :, :640] = part[:48]
        scr[s, :, 640:] = part[48:, :128]
    up = [scr[(at_ref[1] - g + 4) % 4][:24] for g in range(4)]
    g_out = (scr[0] + scr[2])[24:] + (scr[1] + scr[3])[24:]
    rest = rest_ref[...].astype(F32)
    block_ref[...] = jnp.concatenate(up + [rest[:96], g_out, rest[96:]], axis=0).astype(BF)


def sum_slots(at, own, slots, d_h1, rest):
    return pl.pallas_call(
        sum_kernel,
        out_shape=(shape(96, 640), shape(96, 640), shape(ROWS, D), shape(232, D)),
        in_specs=[SMEM] + [VM] * 6,
        out_specs=(VM,) * 4,
        scratch_shapes=[pltpu.VMEM((4, 48, D), F32)],
        compiler_params=PARAMS,
        cost_estimate=pl.CostEstimate(flops=10**6, bytes_accessed=3 * 10**6, transcendentals=0),
    )(at, own, *slots, d_h1, rest)


def final_kernel(at_ref, *refs):
    slots, (grad_ref, vec_ref, scr) = refs[:4], refs[4:]
    for s in range(4):
        for c in range(2):
            scr[s, c] = slots[s][c]
    yi, ci = at_ref[0], at_ref[2]
    for c in range(2):
        rows = slice(96 * c, 96 * (c + 1))
        total = []
        for g in range(4):
            value = scr[(yi - g + 4) % 4, (ci + c) % 2].astype(F32)
            for i, part in enumerate((1, 2, 0)):
                start = part * D + g * GD
                grad_ref[rows, start : start + GD] = value[:, i * GD : (i + 1) * GD]
            total.append(value[:, 512:])
        vec_ref[rows, :] = (total[0] + total[1]) + (total[2] + total[3])


def final_rows(at, slots):
    return pl.pallas_call(
        final_kernel,
        out_shape=(shape(GD, 3 * D, dtype=F32), shape(GD, 128, dtype=F32)),
        in_specs=[SMEM] + [VM] * 4,
        out_specs=(VM, VM),
        scratch_shapes=[pltpu.VMEM((4, 2, 96, 640), BF)],
        compiler_params=PARAMS,
        cost_estimate=pl.CostEstimate(flops=10**6, bytes_accessed=3 * 10**6, transcendentals=0),
    )(at, *slots)


def gather(value, axes, axis=0):
    return lax.all_gather(value, axes, axis=axis, tiled=True)


def swap(value, axes):
    return lax.all_to_all(value, axes, 0, 0)


def send(value, axis, step):
    n = lax.axis_size(axis)
    return lax.ppermute(value, axis, [(i, (i + step) % n) for i in range(n)])


def spread(value, axis):
    return [value] + [send(value, axis, s) for s in range(1, 4)]


def exchange(slots, axis, step):
    return [slots[0]] + [send(slots[s], axis, s * step) for s in range(1, 4)]


def add_slots(slots):
    a, b, c, d = (v.astype(F32) for v in slots)
    return (a + c) + (b + d)


def group_of(value, index, size, axis=0):
    return lax.dynamic_slice_in_dim(value, (index % 4) * size, size, axis)


def local(
    tokens, qkv_w, out_w, up_w, down_w, norm_gains, biases, value_bias, up_bias, cotangent, block_place
):
    xi = lax.axis_index("x")
    yi = lax.axis_index("y")
    ci = lax.axis_index("core")
    zi = lax.axis_index("fsdp")
    tok_own = tokens[0]
    cot_own = cotangent[0]

    at = jnp.stack([yi, zi, ci]).astype(jnp.int32)
    ws = spread(prepare(at, qkv_w, norm_gains, biases, value_bias[None]), "fsdp")
    toks = spread(tok_own, "y")

    ids = jnp.arange(NBLK, dtype=jnp.int32)
    slot_x, slot_c, slot_y, blk = ids // 16, (ids // 8) % 2, (ids // 2) % 4, ids % 2
    pick = lambda at: jnp.sum(jnp.where(at[:, None] == ids[None, :], block_place[None, :], 0), axis=1)
    at_y = (yi - slot_y + 4) % 4
    key_place = pick(at_y * 16 + ((xi - slot_x + 4) % 4) * 4 + ((ci + slot_c) % 2) * 2 + blk)
    query_place = pick(at_y * 16 + slot_x * 4 + slot_c * 2 + blk)
    own_place = key_place[:8]
    rank = jnp.sum((own_place[None, :] > own_place[:, None]).astype(jnp.int32), axis=1)
    order = jnp.arange(8, dtype=jnp.int32)
    hit = rank[None, :] == order[:, None]
    own = jnp.sum(jnp.where(hit, order[None, :], 0), axis=1)
    place = jnp.sum(jnp.where(hit, own_place[None, :], 0), axis=1)

    with jax.named_scope("w_up"):
        w_ups = exchange([group_of(up_w, zi + s, D, axis=1) for s in range(4)], "fsdp", 1)
    w_down = down_w

    kv_own, query, h1, n1y, w_qkv, small = first_rows(at, toks, ws)
    both = both_rows(cot_own, out_w, kv_own)
    both = lax.all_gather(both, "fsdp", axis=0)
    w_out = jnp.concatenate(
        [lax.dynamic_index_in_dim(both, (yi + s) % 4, 0, keepdims=False)[128:] for s in range(4)], axis=0
    )
    gain1, gain2 = small[0], small[1]
    out_bias, shift2, down_bias = small[4], small[5], small[6]
    with jax.named_scope("kv"):
        kv_all = [p for v in spread(kv_own, "x") for p in (v, send(v, "core", 1))]
    attn, o_exact, qe, ks, vs = attention_forward(key_place, own, place, query, kv_all, w_ups[1:])
    qe_all = gather(qe, XC)

    attn = attn[:, 64:]
    with jax.named_scope("attn_y"):
        attn_own = exchange([attn[128 * s : 128 * (s + 1)] for s in range(4)], "y", -1)
    attn_own = jnp.concatenate(attn_own, axis=1)
    x2 = tok_own.astype(F32) + (dot(attn_own, w_out) + out_bias)
    n2, s2 = normalize(x2)
    h2_own = (n2 * gain2 + shift2).astype(BF)

    with jax.named_scope("h2_z"):
        h2s = spread(h2_own, "fsdp")
    h2, cot_z, act, d_up, d_h2_part = feed_forward(
        at, h2s, w_ups, both, w_down, up_bias[None]
    )
    back = lambda v: add_slots(exchange([v[128 * s : 128 * (s + 1)] for s in range(4)], "fsdp", -1))
    with jax.named_scope("d_h2_z"):
        d_h2 = back(d_h2_part)
    cot32 = cot_own.astype(F32)
    d_x2 = cot32 + norm_back(d_h2 * gain2, n2, s2)
    d_branch = d_x2.astype(BF)
    d_attn = dot_t(d_branch, w_out).astype(BF)
    with jax.named_scope("d_attn_y"):
        d_attn_own = exchange([d_attn[:, GD * s : GD * (s + 1)] for s in range(4)], "y", 1)
    d_attn_own = jnp.concatenate(d_attn_own, axis=0)
    de = delta_rows(d_attn_own, o_exact, qe_all[:16])
    keep, give = weight_blocks(at, h2, d_up, act, cot_z, attn_own, d_branch, de)
    with jax.named_scope("mid"):
        mid = add_blocks(keep, send(give, "core", 1))
        mid = add_slots(exchange(mid, "y", 1)).astype(BF)
    with jax.named_scope("de"):
        arrived = spread(de, "x")[1:]
        d_q = attention_dq((0, 3), own, place, qe, de, ks, vs)
        arrived = hold_back(arrived, d_q)
        de_all = [p for v in (de, *arrived) for p in (v, send(v, "core", 1))]
    d_q = attention_dq((1, 2), own, place, qe, de, ks, vs, (d_q,), (*arrived, mid))
    with jax.named_scope("down"):
        layer_out = (x2 + back(down_rows(act, w_down, d_q)) + down_bias).astype(BF)
    d_kv = attention_dkv(query_place, key_place, own, place, kv_own, qe_all, de_all)
    with jax.named_scope("mid"):
        mid = spread(mid, "x")

    vec = jnp.stack([jnp.sum(d_h2 * n2, axis=0), jnp.sum(d_branch.astype(F32), axis=0), jnp.sum(d_h2, axis=0)])
    vec = jnp.pad(vec, ((4, 1), (0, 0)))
    d_h1_send, tail, rest = last_gradients(at, d_kv, d_q, h1, n1y, w_qkv, vec, mid, layer_out)
    with jax.named_scope("tail_z"):
        received = [send(tail[s], "fsdp", s) for s in range(1, 4)]
    kept, given, d_h1_send, mid = sum_slots(at, tail, received, d_h1_send, rest)
    with jax.named_scope("mid"):
        mid = lax.all_gather(mid, ("y", "core"), axis=0)
    grad_up, grad_down, grad_out, out_vec = mid_rows(mid)
    grad_up_bias = out_vec[0]
    grad_down_bias = lax.dynamic_slice(out_vec[1], (zi * GD,), (GD,))
    with jax.named_scope("d_h1_y"):
        d_h1 = add_slots(exchange([d_h1_send[128 * s : 128 * (s + 1)] for s in range(4)], "y", -1))
    n1, s1 = normalize(tok_own.astype(F32))
    input_grad = (d_x2 + norm_back(d_h1 * gain1, n1, s1)).astype(BF)

    with jax.named_scope("tail_core"):
        tail = (kept.astype(F32) + send(given, "core", 1).astype(F32)).astype(BF)
    with jax.named_scope("tail_x"):
        tail = add_slots(spread(tail, "x")).astype(BF)
    with jax.named_scope("tail_y"):
        tail = [jnp.stack([v, send(v, "core", 1)]) for v in spread(tail, "y")]
    grad_qkv, vectors = final_rows(at, tail)
    vectors = vectors[:, 64:71].T
    grad_gains = jnp.stack([vectors[0], vectors[4]])
    grad_biases = jnp.stack([vectors[1], vectors[2], vectors[5], vectors[6], grad_down_bias])
    grad_value_bias = vectors[3]
    return (
        layer_out[None], input_grad[None], grad_qkv, grad_out, grad_up, grad_down,
        grad_gains, grad_biases, grad_value_bias, grad_up_bias,
    )


def solution(mesh):
    grid = Mesh(mesh.devices.reshape(4, 4, 2, 4), ("y", "x", "core", "fsdp"))
    rows = P("fsdp", CTX, None)
    in_specs = (
        rows, P("fsdp", None), P("fsdp", None), P("fsdp", None), P("fsdp", None),
        P(None, "fsdp"), P(None, "fsdp"), P("fsdp"), P("fsdp"), rows, P(),
    )
    out_specs = (
        rows, rows, P("fsdp", None), P("fsdp", None), P("fsdp", None), P("fsdp", None),
        P(None, "fsdp"), P(None, "fsdp"), P("fsdp"), P("fsdp"),
    )
    return jax.shard_map(local, mesh=grid, in_specs=in_specs, out_specs=out_specs, check_vma=False)
```

```python
import functools

import jax
import jax.numpy as jnp
from jax import lax
from jax.experimental import pallas as pl
from jax.experimental.pallas import tpu as pltpu
from jax.sharding import Mesh
from jax.sharding import PartitionSpec as P

EPS = 1e-05
D = 768
GD = 192
NH = 3
HD = 64
ROWS = 512
LEN = 4096
BLK = 64
NBLK = 64
EXT = 256
TILE = 1024
CHUNK = 128
BF = jnp.bfloat16
F32 = jnp.float32
XC = ("x", "core")
CTX = ("y", "x", "core")


def dot(a, b):
    return lax.dot_general(a, b, (((1,), (0,)), ((), ())), preferred_element_type=F32)


def dot_t(a, b):
    return lax.dot_general(a, b, (((1,), (1,)), ((), ())), preferred_element_type=F32)


def t_dot(a, b):
    return lax.dot_general(a, b, (((0,), (0,)), ((), ())), preferred_element_type=F32)


def normalize(value):
    center = value - jnp.mean(value, axis=-1, keepdims=True)
    factor = lax.rsqrt(jnp.mean(center * center, axis=-1, keepdims=True) + EPS)
    return (center * factor, factor)


def norm_back(scaled, normed, factor):
    return factor * (
        scaled
        - jnp.mean(scaled, axis=-1, keepdims=True)
        - normed * jnp.mean(scaled * normed, axis=-1, keepdims=True)
    )


def lanes(rows):
    return lax.broadcasted_iota(jnp.int32, (rows, EXT), 1)


def head_mask(rows, h, high):
    lane = lanes(rows)
    if high:
        feat = (lane >= 64 + HD * h) & (lane < 64 + HD * (h + 1))
        ext = (lane >= 3 * h) & (lane < 3 * h + 3)
    else:
        feat = (lane >= HD * h) & (lane < HD * (h + 1))
        ext = (lane >= GD + 3 * h) & (lane < GD + 3 * h + 3)
    return feat | ext


def feature_mask(rows, h, high):
    lane = lanes(rows) - (64 if high else 0)
    return (lane >= HD * h) & (lane < HD * (h + 1))


def stack_heads(value, high):
    rows = value.shape[0]
    zero = jnp.zeros_like(value)
    return jnp.concatenate(
        [jnp.where(head_mask(rows, h, high), value, zero) for h in range(NH)], axis=0
    )


def merge_heads(stacked, high):
    rows = stacked.shape[0] // NH
    out = jnp.zeros((rows, EXT), F32)
    for h in range(NH):
        out = out + jnp.where(feature_mask(rows, h, high), stacked[h * rows : (h + 1) * rows], 0.0)
    return out


def pieces(value):
    first = value.astype(BF).astype(F32)
    second = (value - first).astype(BF).astype(F32)
    third = (value - first - second).astype(BF).astype(F32)
    return (first, second, third)


def add_extras(base, columns, high):
    rows = base.shape[0]
    lane = lanes(rows)
    start = 0 if high else GD
    for h in range(NH):
        for i, piece in enumerate(pieces(columns[h])):
            base = jnp.where(lane == start + 3 * h + i, piece, base)
    return base


def key_form(kv):
    lane = lanes(kv.shape[0])
    one = jnp.ones((kv.shape[0], EXT), BF)
    zero = jnp.zeros((kv.shape[0], EXT), BF)
    low = jnp.where(lane < GD, kv[:, :EXT], jnp.where(lane < GD + 9, one, zero))
    high = jnp.where(lane >= 64, kv[:, 128:384], jnp.where(lane < 9, one, zero))
    return (low, high)


def block_rows(index):
    return pl.ds(pl.multiple_of(index * BLK, BLK), BLK)


def stacked_pos(place_a, place_b):
    row = lax.broadcasted_iota(jnp.int32, (NH * CHUNK, 1), 0)
    place = jnp.where(row % CHUNK < BLK, place_a, place_b)
    return place * BLK + row % BLK


def col_pos(tile):
    return tile * TILE + lax.broadcasted_iota(jnp.int32, (NH * CHUNK, TILE), 1)


def fold(value, op):
    out = value[:, :128]
    for i in range(1, value.shape[1] // 128):
        out = op(out, value[:, i * 128 : (i + 1) * 128])
    return out


def tile_rows(t):
    return pl.ds(pl.multiple_of(t * TILE, TILE), TILE)


def fwd_kernel(
    kplace_ref, own_ref, place_ref, q_ref, *refs
):
    kv_refs = refs[:8]
    attn_ref, o_ref, qe_ref, ks_ref, vs_ref, s_scr, m_scr, l_scr, acc_scr, land, sems = refs[11:]
    copies = [pltpu.make_async_copy(kv_refs[k], land.at[k], sems.at[k]) for k in range(8)]
    for copy in copies:
        copy.start()
    for k in range(8):
        copies[k].wait()
        for b in range(8):
            low, high = key_form(land[k, b * BLK : (b + 1) * BLK, :])
            dst = block_rows(kplace_ref[8 * k + b])
            ks_ref[dst, :] = low
            vs_ref[dst, :] = high

    for c in range(ROWS // CHUNK):
        place_a, place_b = place_ref[2 * c], place_ref[2 * c + 1]
        blocks = (own_ref[2 * c], own_ref[2 * c + 1])
        query = jnp.concatenate([q_ref[block_rows(b), :] for b in blocks], axis=0)
        stacked = stack_heads(query, False)
        qpos = stacked_pos(place_a, place_b)
        tiles = place_a // (TILE // BLK) + 1
        m_scr[...] = jnp.full(m_scr.shape, -1e30, F32)

        def score_step(t, _):
            scores = dot_t(stacked, ks_ref[tile_rows(t), :])
            scores = jnp.where(col_pos(t) <= qpos, scores, -1e30)
            s_scr[t] = scores
            m_scr[...] = jnp.maximum(m_scr[...], fold(scores, jnp.maximum))
            return 0

        lax.fori_loop(0, tiles, score_step, 0)
        peak = jnp.max(m_scr[...], axis=1, keepdims=True)
        l_scr[...] = jnp.zeros(l_scr.shape, F32)
        acc_scr[...] = jnp.zeros(acc_scr.shape, F32)

        def value_step(t, _):
            prob = jnp.exp(s_scr[t] - peak)
            l_scr[...] = l_scr[...] + fold(prob, jnp.add)
            acc_scr[...] = acc_scr[...] + dot(prob.astype(BF), vs_ref[tile_rows(t), :])
            return 0

        lax.fori_loop(0, tiles, value_step, 0)
        total = jnp.sum(l_scr[...], axis=1, keepdims=True)
        log_total = peak + jnp.log(total)
        out = merge_heads(acc_scr[...] / total, True)
        ext = add_extras(
            query.astype(F32),
            [-log_total[h * CHUNK : (h + 1) * CHUNK] for h in range(NH)],
            False,
        ).astype(BF)
        for i, b in enumerate(blocks):
            rows = slice(i * BLK, (i + 1) * BLK)
            o_ref[block_rows(b), :] = out[rows]
            attn_ref[block_rows(b), :] = out[rows].astype(BF)
            qe_ref[block_rows(b), :] = ext[rows]


def dq_kernel(chunks, n_before, own_ref, place_ref, qe_ref, de_ref, ks_ref, vs_ref, *refs):
    *before, dq_ref, acc_scr = refs
    if n_before:
        dq_ref[...] = before[0][...]
    for c in chunks:
        place_a, place_b = place_ref[2 * c], place_ref[2 * c + 1]
        blocks = (own_ref[2 * c], own_ref[2 * c + 1])
        query = stack_heads(jnp.concatenate([qe_ref[block_rows(b), :] for b in blocks], axis=0), False)
        d_out = stack_heads(jnp.concatenate([de_ref[block_rows(b), :] for b in blocks], axis=0), True)
        qpos = stacked_pos(place_a, place_b)
        tiles = place_a // (TILE // BLK) + 1
        acc_scr[...] = jnp.zeros(acc_scr.shape, F32)

        def step(t, _):
            keys = ks_ref[tile_rows(t), :]
            prob = jnp.where(col_pos(t) <= qpos, jnp.exp(dot_t(query, keys)), 0.0)
            d_raw = (prob * dot_t(d_out, vs_ref[tile_rows(t), :])).astype(BF)
            acc_scr[...] = acc_scr[...] + dot(d_raw, keys)
            return 0

        lax.fori_loop(0, tiles, step, 0)
        out = (merge_heads(acc_scr[...], False) * 0.125).astype(BF)
        for i, b in enumerate(blocks):
            dq_ref[block_rows(b), :] = out[i * BLK : (i + 1) * BLK]


def dkv_kernel(qplace_ref, kplace_ref, own_ref, place_ref, kv_ref, qe_ref, *refs):
    de_refs, (dkv_ref, qs_scr, ds_scr, dk_scr, dv_scr, q_land, d_land, sems) = refs[:8], refs[8:]
    q_copy = pltpu.make_async_copy(qe_ref, q_land, sems.at[8])
    q_copy.start()
    copies = [pltpu.make_async_copy(de_refs[k], d_land.at[k], sems.at[k]) for k in range(8)]
    for copy in copies:
        copy.start()
    q_copy.wait()
    for b in range(NBLK):
        qs_scr[block_rows(qplace_ref[b]), :] = q_land[b * BLK : (b + 1) * BLK, :]
    for k in range(8):
        copies[k].wait()
        for b in range(8):
            ds_scr[block_rows(kplace_ref[8 * k + b]), :] = d_land[k, b * BLK : (b + 1) * BLK, :]

    for c in range(ROWS // CHUNK):
        place_a, place_b = place_ref[2 * c], place_ref[2 * c + 1]
        blocks = (own_ref[2 * c], own_ref[2 * c + 1])
        low, high = key_form(jnp.concatenate([kv_ref[block_rows(b), :] for b in blocks], axis=0))
        keys = stack_heads(low, False)
        values = stack_heads(high, True)
        kpos = stacked_pos(place_a, place_b)
        dk_scr[...] = jnp.zeros(dk_scr.shape, F32)
        dv_scr[...] = jnp.zeros(dv_scr.shape, F32)

        def step(t, _):
            query = qs_scr[tile_rows(t), :]
            d_out = ds_scr[tile_rows(t), :]
            prob = jnp.where(col_pos(t) >= kpos, jnp.exp(dot_t(keys, query)), 0.0)
            d_raw = (prob * dot_t(values, d_out)).astype(BF)
            dv_scr[...] = dv_scr[...] + dot(prob.astype(BF), d_out)
            dk_scr[...] = dk_scr[...] + dot(d_raw, query)
            return 0

        lax.fori_loop(place_b // (TILE // BLK), LEN // TILE, step, 0)
        d_keys = merge_heads(dk_scr[...], False)
        d_values = merge_heads(dv_scr[...], True)
        out = jnp.concatenate(
            [d_keys[:, :128], d_keys[:, 128:] + d_values[:, :128], d_values[:, 128:]], axis=1
        ).astype(BF)
        for i, b in enumerate(blocks):
            dkv_ref[block_rows(b), :] = out[i * BLK : (i + 1) * BLK]


def delta_kernel(d_ref, o_ref, early_ref, de_ref):
    d_out = jnp.concatenate([jnp.zeros((ROWS, 64), F32), d_ref[...].astype(F32)], axis=1)
    product = d_out * o_ref[...]
    sums = [
        -jnp.sum(jnp.where(feature_mask(ROWS, h, True), product, 0.0), axis=1, keepdims=True)
        for h in range(NH)
    ]
    de_ref[...] = add_extras(d_out, sums, True).astype(BF)


SMEM = pl.BlockSpec(memory_space=pltpu.SMEM)
VM = pl.BlockSpec(memory_space=pltpu.VMEM)
ANY = pl.BlockSpec(memory_space=pl.ANY)
PARAMS = pltpu.CompilerParams(vmem_limit_bytes=48 * 1024 * 1024)


def shape(*dims, dtype=BF):
    return jax.ShapeDtypeStruct(dims, dtype)


def attention_forward(kplace, own, place, query, kv, early):
    return pl.pallas_call(
        fwd_kernel,
        out_shape=(
            shape(ROWS, EXT), shape(ROWS, EXT, dtype=F32), shape(ROWS, EXT),
            shape(LEN, EXT), shape(LEN, EXT),
        ),
        in_specs=[SMEM] * 3 + [VM] + [ANY] * 11,
        out_specs=(VM,) * 5,
        scratch_shapes=[
            pltpu.VMEM((LEN // TILE, NH * CHUNK, TILE), F32),
            pltpu.VMEM((NH * CHUNK, 128), F32),
            pltpu.VMEM((NH * CHUNK, 128), F32),
            pltpu.VMEM((NH * CHUNK, EXT), F32),
            pltpu.VMEM((8, ROWS, 2 * GD), BF),
            pltpu.SemaphoreType.DMA((8,)),
        ],
        compiler_params=PARAMS,
        cost_estimate=pl.CostEstimate(flops=16 * 10**9, bytes_accessed=10**7, transcendentals=4 * 10**6),
    )(kplace, own, place, query, *kv, *early)


def attention_dq(chunks, own, place, qe, de, ks, vs, before=(), early=()):
    return pl.pallas_call(
        functools.partial(dq_kernel, chunks, len(before)),
        out_shape=shape(ROWS, EXT),
        in_specs=[SMEM] * 2 + [VM] * (4 + len(before)) + [ANY] * len(early),
        out_specs=VM,
        scratch_shapes=[pltpu.VMEM((NH * CHUNK, EXT), F32)],
        compiler_params=PARAMS,
        cost_estimate=pl.CostEstimate(flops=8 * 10**9, bytes_accessed=5 * 10**6, transcendentals=2 * 10**6),
    )(own, place, qe, de, ks, vs, *before, *early)


def attention_dkv(qplace, kplace, own, place, kv, qe, de):
    return pl.pallas_call(
        dkv_kernel,
        out_shape=shape(ROWS, 2 * GD),
        in_specs=[SMEM] * 4 + [VM] + [ANY] * 9,
        out_specs=VM,
        scratch_shapes=[
            pltpu.VMEM((LEN, EXT), BF),
            pltpu.VMEM((LEN, EXT), BF),
            pltpu.VMEM((NH * CHUNK, EXT), F32),
            pltpu.VMEM((NH * CHUNK, EXT), F32),
            pltpu.VMEM((LEN, EXT), BF),
            pltpu.VMEM((8, ROWS, EXT), BF),
            pltpu.SemaphoreType.DMA((9,)),
        ],
        compiler_params=PARAMS,
        cost_estimate=pl.CostEstimate(flops=15 * 10**9, bytes_accessed=10**7, transcendentals=4 * 10**6),
    )(qplace, kplace, own, place, kv, qe, *de)


def delta_rows(d_attn, o, early):
    return pl.pallas_call(
        delta_kernel,
        out_shape=shape(ROWS, EXT),
        in_specs=[VM] * 2 + [ANY],
        out_specs=VM,
        compiler_params=PARAMS,
        cost_estimate=pl.CostEstimate(flops=10**6, bytes_accessed=10**6, transcendentals=0),
    )(d_attn, o, early)


def prep_kernel(at_ref, w_ref, gain_ref, bias_ref, vb_ref, cols_ref):
    for k in range(4):

        @pl.when(at_ref[0] == k)
        def _():
            for i, part in enumerate((1, 2, 0)):
                start = part * D + k * GD
                cols_ref[:GD, i * GD : (i + 1) * GD] = w_ref[:, start : start + GD]

    small = jnp.concatenate(
        [gain_ref[...].astype(F32), bias_ref[...].astype(F32), vb_ref[...].astype(F32), jnp.zeros((8, GD), F32)],
        axis=0,
    )
    cols_ref[GD:, :] = jnp.concatenate([small, jnp.zeros((16, 2 * GD), F32)], axis=1).astype(BF)


def prepare(at, w, gains, biases, vb):
    return pl.pallas_call(
        prep_kernel,
        out_shape=shape(GD + 16, 3 * GD),
        in_specs=[SMEM] + [VM] * 4,
        out_specs=VM,
        compiler_params=PARAMS,
        cost_estimate=pl.CostEstimate(flops=1000, bytes_accessed=10**6, transcendentals=0),
    )(at, w, gains, biases, vb)


def qkv_kernel(at_ref, *refs):
    toks, ws = refs[:4], refs[4:8]
    kv_ref, q_ref, h1_ref, n1_ref, w_ref, small_ref, w_scr = refs[8:]
    yi, zi = at_ref[0], at_ref[1]
    for s in range(4):
        w_scr[s] = ws[s][...]
    for g in range(4):
        slot = (zi - g + 4) % 4
        w_ref[g * GD : (g + 1) * GD, :] = w_scr[slot, :GD]
        small_ref[:, g * GD : (g + 1) * GD] = w_scr[slot, GD:, :256].astype(F32)[:8, :GD]
    gain, shift = small_ref[0:1, :], small_ref[2:3, :]
    for s in range(4):
        rows = slice(128 * s, 128 * (s + 1))
        normed, _ = normalize(toks[s][...].astype(F32))
        n1_ref[rows, :] = normed
        h1_ref[rows, :] = (normed * gain + shift).astype(BF)
    own = w_scr[(zi - yi + 4) % 4, GD:, :256].astype(F32)[:8, :GD]
    qkv = dot(h1_ref[...], w_ref[...])
    kv_ref[:, :GD] = qkv[:, :GD].astype(BF)
    kv_ref[:, GD:] = (qkv[:, GD : 2 * GD] + own[7:8]).astype(BF)
    query = (qkv[:, 2 * GD :] + own[3:4]).astype(BF).astype(F32) * 0.125
    q_ref[...] = jnp.concatenate([query, jnp.zeros((ROWS, EXT - GD), F32)], axis=1).astype(BF)


def both_kernel(cot_ref, out_ref, early_ref, both_ref):
    both_ref[:128, :] = cot_ref[...]
    both_ref[128:, :] = out_ref[...]


def both_rows(cot, out_w, early):
    return pl.pallas_call(
        both_kernel,
        out_shape=shape(320, D),
        in_specs=[VM] * 2 + [ANY],
        out_specs=VM,
        compiler_params=PARAMS,
        cost_estimate=pl.CostEstimate(flops=1000, bytes_accessed=10**6, transcendentals=0),
    )(cot, out_w, early)


def first_rows(at, toks, ws):
    return pl.pallas_call(
        qkv_kernel,
        out_shape=(
            shape(ROWS, 2 * GD), shape(ROWS, EXT), shape(ROWS, D), shape(ROWS, D, dtype=F32),
            shape(D, 3 * GD), shape(8, D, dtype=F32),
        ),
        in_specs=[SMEM] + [VM] * 8,
        out_specs=(VM,) * 6,
        scratch_shapes=[pltpu.VMEM((4, GD + 16, 3 * GD), BF)],
        compiler_params=PARAMS,
        cost_estimate=pl.CostEstimate(flops=5 * 10**8, bytes_accessed=6 * 10**6, transcendentals=0),
    )(at, *toks, *ws)


def mlp_kernel(at_ref, *refs):
    h2s = refs[:4]
    ups = refs[4:8]
    both_ref, down_ref, ub_ref, h2_ref, cot_ref, act_ref, dup_ref, dh_ref, up_ref, sems = refs[8:]
    zi = at_ref[1]
    copies = [
        pltpu.make_async_copy(
            both_ref.at[(zi - s + 4) % 4, :128], cot_ref.at[128 * s : 128 * (s + 1)], sems.at[s]
        )
        for s in range(4)
    ]
    for copy in copies:
        copy.start()
    for s in range(4):
        up_ref[pl.ds(pl.multiple_of((zi - s + 4) % 4 * GD, GD), GD), :] = ups[s][...]
    for copy in copies:
        copy.wait()
    for s in range(4):
        rows = slice(128 * s, 128 * (s + 1))
        h2 = h2s[s][...]
        h2_ref[rows, :] = h2
        up = dot(h2, up_ref[...]) + ub_ref[...].astype(F32)
        d_act = dot_t(cot_ref[rows, :], down_ref[...])
        square = up * up
        th = jnp.tanh(0.7978845608028654 * (up + 0.044715 * (square * up)))
        half = 0.5 * (1.0 + th)
        slope = half + 0.5 * up * (1.0 - th * th) * (
            0.7978845608028654 * (1.0 + 3 * 0.044715 * square)
        )
        act_ref[rows, :] = (up * half).astype(BF)
        d_up = (slope * d_act).astype(BF)
        dup_ref[rows, :] = d_up
        dh_ref[rows, :] = dot_t(d_up, up_ref[...]).astype(BF)


def feed_forward(at, h2s, w_ups, both, w_down, ub):
    return pl.pallas_call(
        mlp_kernel,
        out_shape=(shape(ROWS, D),) * 5,
        in_specs=[SMEM] + [VM] * 8 + [ANY] + [VM] * 2,
        out_specs=(VM,) * 5,
        scratch_shapes=[pltpu.VMEM((D, D), BF), pltpu.SemaphoreType.DMA((4,))],
        compiler_params=PARAMS,
        cost_estimate=pl.CostEstimate(flops=4 * 10**9, bytes_accessed=6 * 10**6, transcendentals=4 * 10**5),
    )(at, *h2s, *w_ups, both, w_down, ub)


def down_kernel(act_ref, wd_ref, early_ref, down_ref):
    down_ref[...] = dot(act_ref[...], wd_ref[...]).astype(BF)


def down_rows(act, w_down, early):
    return pl.pallas_call(
        down_kernel,
        out_shape=shape(ROWS, D),
        in_specs=[VM] * 2 + [ANY],
        out_specs=VM,
        compiler_params=PARAMS,
        cost_estimate=pl.CostEstimate(flops=10**9, bytes_accessed=3 * 10**6, transcendentals=0),
    )(act, w_down, early)


def hold_kernel(*refs):
    for s in range(3):
        refs[4 + s][...] = refs[s][...]


def hold_back(values, early):
    return pl.pallas_call(
        hold_kernel,
        out_shape=tuple(shape(*v.shape) for v in values),
        in_specs=[VM] * 3 + [ANY],
        out_specs=(VM,) * 3,
        compiler_params=PARAMS,
        cost_estimate=pl.CostEstimate(flops=1000, bytes_accessed=10**6, transcendentals=0),
    )(*values, early)


def wgrad_kernel(
    at_ref, h2_ref, dup_ref, act_ref, cot_ref, attn_ref, branch_ref, early_ref,
    keep_ref, give_ref, out_scr,
):
    yi, ci = at_ref[0], at_ref[2]
    g_up = t_dot(h2_ref[...], dup_ref[...])
    g_down = t_dot(act_ref[...], cot_ref[...])
    g_out = t_dot(attn_ref[...], branch_ref[...])
    for s in range(4):
        out_scr[s] = g_out[GD * s : GD * (s + 1)]
    vec = jnp.concatenate(
        [
            jnp.sum(dup_ref[...].astype(F32), axis=0, keepdims=True),
            jnp.sum(cot_ref[...].astype(F32), axis=0, keepdims=True),
            jnp.zeros((14, D), F32),
        ],
        axis=0,
    )
    for c in range(2):
        for j in range(4):
            b = 4 * c + j
            parts = []
            for z in range(4):
                parts.append(g_up[GD * z + 24 * b : GD * z + 24 * (b + 1)])
                parts.append(out_scr[(z - yi + 4) % 4, 24 * b : 24 * (b + 1)])
            parts += [g_down[96 * b : 96 * (b + 1)], vec]
            block = jnp.concatenate(parts, axis=0).astype(BF)
            slot = (j - yi + 4) % 4

            @pl.when(ci == c)
            def _():
                keep_ref[slot] = block

            @pl.when(ci != c)
            def _():
                give_ref[slot] = block


def weight_blocks(at, h2, d_up, act, cot, attn, d_branch, early):
    return pl.pallas_call(
        wgrad_kernel,
        out_shape=(shape(4, 304, D), shape(4, 304, D)),
        in_specs=[SMEM] + [VM] * 6 + [ANY],
        out_specs=(VM,) * 2,
        scratch_shapes=[pltpu.VMEM((4, GD, D), F32)],
        compiler_params=PARAMS,
        cost_estimate=pl.CostEstimate(flops=5 * 10**9, bytes_accessed=6 * 10**6, transcendentals=0),
    )(at, h2, d_up, act, cot, attn, d_branch, early)


def add_kernel(a_ref, b_ref, *outs):
    for s in range(4):
        outs[s][...] = (a_ref[s].astype(F32) + b_ref[s].astype(F32)).astype(BF)


def add_blocks(a, b):
    return pl.pallas_call(
        add_kernel,
        out_shape=(shape(*a.shape[1:]),) * 4,
        in_specs=[VM] * 2,
        out_specs=(VM,) * 4,
        compiler_params=PARAMS,
        cost_estimate=pl.CostEstimate(flops=10**6, bytes_accessed=6 * 10**6, transcendentals=0),
    )(a, b)


def mid_kernel(blocks_ref, up_ref, down_ref, out_ref, vec_ref):
    for c in range(2):
        for j in range(4):
            b = 4 * c + j
            block = blocks_ref[2 * j + c].astype(F32)
            for g in range(4):
                up_ref[24 * b : 24 * (b + 1), g * D : (g + 1) * D] = block[24 * g : 24 * (g + 1)]
            down_ref[96 * b : 96 * (b + 1), :] = block[96:192]
            out_ref[24 * b : 24 * (b + 1), :] = block[192:216]
            if b == 0:
                vec_ref[...] = block[216:224]


def mid_rows(blocks):
    return pl.pallas_call(
        mid_kernel,
        out_shape=(
            shape(GD, 4 * D, dtype=F32), shape(D, D, dtype=F32), shape(GD, D, dtype=F32),
            shape(8, D, dtype=F32),
        ),
        in_specs=[VM],
        out_specs=(VM,) * 4,
        compiler_params=PARAMS,
        cost_estimate=pl.CostEstimate(flops=10**6, bytes_accessed=8 * 10**6, transcendentals=0),
    )(blocks)


def tail_kernel(
    at_ref, dkv_ref, dq_ref, h1_ref, n1_ref, w_ref, vec_ref, m0, m1, m2, m3, early_ref, dh_ref, t_ref, rest_ref, scr
):
    yi, zi = at_ref[0], at_ref[1]
    scr[...] = (m0[...].astype(F32) + m2[...].astype(F32)) + (
        m1[...].astype(F32) + m3[...].astype(F32)
    )
    rest_ref[...] = scr[192:, :].astype(BF)
    for s in range(4):
        part = scr[pl.ds(pl.multiple_of((zi + s) % 4 * 48, 8), 48), :]
        t_ref[s, 192:240] = part[:, :640].astype(BF)
        t_ref[s, 240:, :128] = part[:, 640:].astype(BF)
        t_ref[s, 240:, 128:] = jnp.zeros((48, 512), BF)
    d_qkv = jnp.concatenate([dkv_ref[...], dq_ref[...]], axis=1)
    d_h1 = dot_t(d_qkv[:, : 3 * GD], w_ref[...])
    dh_ref[...] = d_h1.astype(BF)
    sums = jnp.sum(d_qkv.astype(F32), axis=0, keepdims=True)
    at_own = lambda v: jnp.concatenate([jnp.where(yi == k, v, 0.0) for k in range(4)], axis=1)
    vectors = jnp.concatenate(
        [
            jnp.sum(d_h1 * n1_ref[...], axis=0, keepdims=True),
            jnp.sum(d_h1, axis=0, keepdims=True),
            at_own(sums[:, 2 * GD : 3 * GD]),
            at_own(sums[:, GD : 2 * GD]),
            vec_ref[4:8, :],
        ],
        axis=0,
    ).astype(BF)
    row = lax.broadcasted_iota(jnp.int32, (8, 128), 0)
    lane = lax.broadcasted_iota(jnp.int32, (8, 128), 1)
    columns = t_dot(vectors, jnp.where(lane == row + 64, 1.0, 0.0).astype(BF))
    grad = t_dot(h1_ref[...], d_qkv)
    for g in range(4):
        rows = slice(g * GD, (g + 1) * GD)
        slot = (g - zi + 4) % 4
        t_ref[slot, :GD, :512] = grad[rows, :512].astype(BF)
        t_ref[slot, :GD, 512:] = (grad[rows, 512:] + columns[rows]).astype(BF)


def last_gradients(at, d_kv, d_q, h1, n1, w, vec, mid, early):
    return pl.pallas_call(
        tail_kernel,
        out_shape=(shape(ROWS, D), shape(4, 288, 640), shape(112, D)),
        in_specs=[SMEM] + [VM] * 10 + [ANY],
        out_specs=(VM,) * 3,
        scratch_shapes=[pltpu.VMEM((304, D), F32)],
        compiler_params=PARAMS,
        cost_estimate=pl.CostEstimate(flops=3 * 10**9, bytes_accessed=6 * 10**6, transcendentals=0),
    )(at, d_kv, d_q, h1, n1, w, vec, *mid, early)


def sum_kernel(at_ref, t_ref, r1, r2, r3, dh_ref, rest_ref, kept_ref, given_ref, same_ref, block_ref, scr):
    same_ref[...] = dh_ref[...]
    slots = (r1, r2, r3)
    for c in range(2):
        rows = slice(96 * c, 96 * (c + 1))
        a, b, d, e = (v.astype(F32) for v in [t_ref[0, rows]] + [r[rows] for r in slots])
        total = ((a + d) + (b + e)).astype(BF)

        @pl.when(at_ref[2] == c)
        def _():
            kept_ref[...] = total

        @pl.when(at_ref[2] != c)
        def _():
            given_ref[...] = total

    for s in range(4):
        part = (t_ref[0, GD:] if s == 0 else slots[s - 1][GD:]).astype(F32)
        scr[s, :, :640] = part[:48]
        scr[s, :, 640:] = part[48:, :128]
    up = [scr[(at_ref[1] - g + 4) % 4][:24] for g in range(4)]
    g_out = (scr[0] + scr[2])[24:] + (scr[1] + scr[3])[24:]
    rest = rest_ref[...].astype(F32)
    block_ref[...] = jnp.concatenate(up + [rest[:96], g_out, rest[96:]], axis=0).astype(BF)


def sum_slots(at, own, slots, d_h1, rest):
    return pl.pallas_call(
        sum_kernel,
        out_shape=(shape(96, 640), shape(96, 640), shape(ROWS, D), shape(232, D)),
        in_specs=[SMEM] + [VM] * 6,
        out_specs=(VM,) * 4,
        scratch_shapes=[pltpu.VMEM((4, 48, D), F32)],
        compiler_params=PARAMS,
        cost_estimate=pl.CostEstimate(flops=10**6, bytes_accessed=3 * 10**6, transcendentals=0),
    )(at, own, *slots, d_h1, rest)


def final_kernel(at_ref, *refs):
    slots, (grad_ref, vec_ref, scr) = refs[:4], refs[4:]
    for s in range(4):
        for c in range(2):
            scr[s, c] = slots[s][c]
    yi, ci = at_ref[0], at_ref[2]
    for c in range(2):
        rows = slice(96 * c, 96 * (c + 1))
        total = []
        for g in range(4):
            value = scr[(yi - g + 4) % 4, (ci + c) % 2].astype(F32)
            for i, part in enumerate((1, 2, 0)):
                start = part * D + g * GD
                grad_ref[rows, start : start + GD] = value[:, i * GD : (i + 1) * GD]
            total.append(value[:, 512:])
        vec_ref[rows, :] = (total[0] + total[1]) + (total[2] + total[3])


def final_rows(at, slots):
    return pl.pallas_call(
        final_kernel,
        out_shape=(shape(GD, 3 * D, dtype=F32), shape(GD, 128, dtype=F32)),
        in_specs=[SMEM] + [VM] * 4,
        out_specs=(VM, VM),
        scratch_shapes=[pltpu.VMEM((4, 2, 96, 640), BF)],
        compiler_params=PARAMS,
        cost_estimate=pl.CostEstimate(flops=10**6, bytes_accessed=3 * 10**6, transcendentals=0),
    )(at, *slots)


def gather(value, axes, axis=0):
    return lax.all_gather(value, axes, axis=axis, tiled=True)


def swap(value, axes):
    return lax.all_to_all(value, axes, 0, 0)


def send(value, axis, step):
    n = lax.axis_size(axis)
    return lax.ppermute(value, axis, [(i, (i + step) % n) for i in range(n)])


def spread(value, axis):
    return [value] + [send(value, axis, s) for s in range(1, 4)]


def exchange(slots, axis, step):
    return [slots[0]] + [send(slots[s], axis, s * step) for s in range(1, 4)]


def add_slots(slots):
    a, b, c, d = (v.astype(F32) for v in slots)
    return (a + c) + (b + d)


def group_of(value, index, size, axis=0):
    return lax.dynamic_slice_in_dim(value, (index % 4) * size, size, axis)


def local(
    tokens, qkv_w, out_w, up_w, down_w, norm_gains, biases, value_bias, up_bias, cotangent, block_place
):
    xi = lax.axis_index("x")
    yi = lax.axis_index("y")
    ci = lax.axis_index("core")
    zi = lax.axis_index("fsdp")
    tok_own = tokens[0]
    cot_own = cotangent[0]

    at = jnp.stack([yi, zi, ci]).astype(jnp.int32)
    ws = spread(prepare(at, qkv_w, norm_gains, biases, value_bias[None]), "fsdp")
    toks = spread(tok_own, "y")

    ids = jnp.arange(NBLK, dtype=jnp.int32)
    slot_x, slot_c, slot_y, blk = ids // 16, (ids // 8) % 2, (ids // 2) % 4, ids % 2
    pick = lambda at: jnp.sum(jnp.where(at[:, None] == ids[None, :], block_place[None, :], 0), axis=1)
    at_y = (yi - slot_y + 4) % 4
    key_place = pick(at_y * 16 + ((xi - slot_x + 4) % 4) * 4 + ((ci + slot_c) % 2) * 2 + blk)
    query_place = pick(at_y * 16 + slot_x * 4 + slot_c * 2 + blk)
    own_place = key_place[:8]
    rank = jnp.sum((own_place[None, :] > own_place[:, None]).astype(jnp.int32), axis=1)
    order = jnp.arange(8, dtype=jnp.int32)
    hit = rank[None, :] == order[:, None]
    own = jnp.sum(jnp.where(hit, order[None, :], 0), axis=1)
    place = jnp.sum(jnp.where(hit, own_place[None, :], 0), axis=1)

    with jax.named_scope("w_up"):
        w_ups = exchange([group_of(up_w, zi + s, D, axis=1) for s in range(4)], "fsdp", 1)
    w_down = down_w

    kv_own, query, h1, n1y, w_qkv, small = first_rows(at, toks, ws)
    with jax.named_scope("kv"):
        kv_all = [p for v in spread(kv_own, "x") for p in (v, send(v, "core", 1))]
    both = both_rows(cot_own, out_w, kv_all[2])
    both = lax.all_gather(both, "fsdp", axis=0)
    w_out = jnp.concatenate(
        [lax.dynamic_index_in_dim(both, (yi + s) % 4, 0, keepdims=False)[128:] for s in range(4)], axis=0
    )
    gain1, gain2 = small[0], small[1]
    out_bias, shift2, down_bias = small[4], small[5], small[6]
    attn, o_exact, qe, ks, vs = attention_forward(key_place, own, place, query, kv_all, w_ups[1:])
    qe_all = gather(qe, XC)

    attn = attn[:, 64:]
    with jax.named_scope("attn_y"):
        attn_own = exchange([attn[128 * s : 128 * (s + 1)] for s in range(4)], "y", -1)
    attn_own = jnp.concatenate(attn_own, axis=1)
    x2 = tok_own.astype(F32) + (dot(attn_own, w_out) + out_bias)
    n2, s2 = normalize(x2)
    h2_own = (n2 * gain2 + shift2).astype(BF)

    with jax.named_scope("h2_z"):
        h2s = spread(h2_own, "fsdp")
    h2, cot_z, act, d_up, d_h2_part = feed_forward(
        at, h2s, w_ups, both, w_down, up_bias[None]
    )
    back = lambda v: add_slots(exchange([v[128 * s : 128 * (s + 1)] for s in range(4)], "fsdp", -1))
    with jax.named_scope("d_h2_z"):
        d_h2 = back(d_h2_part)
    cot32 = cot_own.astype(F32)
    d_x2 = cot32 + norm_back(d_h2 * gain2, n2, s2)
    d_branch = d_x2.astype(BF)
    d_attn = dot_t(d_branch, w_out).astype(BF)
    with jax.named_scope("d_attn_y"):
        d_attn_own = exchange([d_attn[:, GD * s : GD * (s + 1)] for s in range(4)], "y", 1)
    d_attn_own = jnp.concatenate(d_attn_own, axis=0)
    de = delta_rows(d_attn_own, o_exact, qe_all[:16])
    keep, give = weight_blocks(at, h2, d_up, act, cot_z, attn_own, d_branch, de)
    with jax.named_scope("mid"):
        mid = add_blocks(keep, send(give, "core", 1))
        mid = add_slots(exchange(mid, "y", 1)).astype(BF)
    with jax.named_scope("de"):
        arrived = spread(de, "x")[1:]
        d_q = attention_dq((0, 3), own, place, qe, de, ks, vs)
        arrived = hold_back(arrived, d_q)
        de_all = [p for v in (de, *arrived) for p in (v, send(v, "core", 1))]
    d_q = attention_dq((1, 2), own, place, qe, de, ks, vs, (d_q,), (*arrived, mid))
    with jax.named_scope("down"):
        layer_out = (x2 + back(down_rows(act, w_down, d_q)) + down_bias).astype(BF)
    d_kv = attention_dkv(query_place, key_place, own, place, kv_own, qe_all, de_all)
    with jax.named_scope("mid"):
        mid = spread(mid, "x")

    vec = jnp.stack([jnp.sum(d_h2 * n2, axis=0), jnp.sum(d_branch.astype(F32), axis=0), jnp.sum(d_h2, axis=0)])
    vec = jnp.pad(vec, ((4, 1), (0, 0)))
    d_h1_send, tail, rest = last_gradients(at, d_kv, d_q, h1, n1y, w_qkv, vec, mid, layer_out)
    with jax.named_scope("tail_z"):
        received = [send(tail[s], "fsdp", s) for s in range(1, 4)]
    kept, given, d_h1_send, mid = sum_slots(at, tail, received, d_h1_send, rest)
    with jax.named_scope("mid"):
        mid = lax.all_gather(mid, ("y", "core"), axis=0)
    grad_up, grad_down, grad_out, out_vec = mid_rows(mid)
    grad_up_bias = out_vec[0]
    grad_down_bias = lax.dynamic_slice(out_vec[1], (zi * GD,), (GD,))
    with jax.named_scope("d_h1_y"):
        d_h1 = add_slots(exchange([d_h1_send[128 * s : 128 * (s + 1)] for s in range(4)], "y", -1))
    n1, s1 = normalize(tok_own.astype(F32))
    input_grad = (d_x2 + norm_back(d_h1 * gain1, n1, s1)).astype(BF)

    with jax.named_scope("tail_core"):
        tail = (kept.astype(F32) + send(given, "core", 1).astype(F32)).astype(BF)
    with jax.named_scope("tail_x"):
        tail = add_slots(spread(tail, "x")).astype(BF)
    with jax.named_scope("tail_y"):
        tail = [jnp.stack([v, send(v, "core", 1)]) for v in spread(tail, "y")]
    grad_qkv, vectors = final_rows(at, tail)
    vectors = vectors[:, 64:71].T
    grad_gains = jnp.stack([vectors[0], vectors[4]])
    grad_biases = jnp.stack([vectors[1], vectors[2], vectors[5], vectors[6], grad_down_bias])
    grad_value_bias = vectors[3]
    return (
        layer_out[None], input_grad[None], grad_qkv, grad_out, grad_up, grad_down,
        grad_gains, grad_biases, grad_value_bias, grad_up_bias,
    )


def solution(mesh):
    grid = Mesh(mesh.devices.reshape(4, 4, 2, 4), ("y", "x", "core", "fsdp"))
    rows = P("fsdp", CTX, None)
    in_specs = (
        rows, P("fsdp", None), P("fsdp", None), P("fsdp", None), P("fsdp", None),
        P(None, "fsdp"), P(None, "fsdp"), P("fsdp"), P("fsdp"), rows, P(),
    )
    out_specs = (
        rows, rows, P("fsdp", None), P("fsdp", None), P("fsdp", None), P("fsdp", None),
        P(None, "fsdp"), P(None, "fsdp"), P("fsdp"), P("fsdp"),
    )
    return jax.shard_map(local, mesh=grid, in_specs=in_specs, out_specs=out_specs, check_vma=False)
```
